128 devices in a mesh: ctx: 32 (over z_lo, x, y), fsdp: 4 (over z_hi, core).
Axes of the slice: x: 4, y: 4, z: 4 (z_hi: 2, z_lo: 2; z = z_hi * 2 + z_lo), core: 2. Of those that a mesh axis runs over, the one named last changes fastest.
Arguments:
- inputs: bfloat16 [4, 4096, 1024], P('fsdp', 'ctx'), may hold values from -6 to 6
- cotangent: bfloat16 [4, 4096, 1024], P('fsdp', 'ctx'), may hold values from -6 to 6
- qkv_weight: bfloat16 [1024, 2048], P('fsdp'), may hold values from -0.1875 to 0.1875
- out_weight: bfloat16 [1024, 1024], P('fsdp'), may hold values from -1 to 1
- gate_weight: bfloat16 [1024, 4608], P('fsdp'), may hold values from -0.1875 to 0.1875
- up_weight: bfloat16 [1024, 4608], P('fsdp'), may hold values from -0.1875 to 0.1875
- down_weight: bfloat16 [4608, 1024], P('fsdp'), may hold values from -0.09375 to 0.09375
- gain_attn: float32 [1024], replicated, may hold values from 0.5 to 1.5
- gain_query: float32 [64], replicated, may hold values from 0.1 to 1.9
- gain_key: float32 [64], replicated, may hold values from 0.1 to 1.9
- gain_ffn: float32 [1024], replicated, may hold values from 0.5 to 1.5
- block_order: int32 [64], replicated, may hold values from 0 to 63, each once
- doc_starts: int32 [4, 4], P('fsdp'), may hold values from 0 to 4095, as said below
Outputs:
- outputs: bfloat16 [4, 4096, 1024], P('fsdp', 'ctx')
- grad_inputs: bfloat16 [4, 4096, 1024], P('fsdp', 'ctx')
- grad_qkv_weight: float32 [1024, 2048], P('fsdp')
- grad_out_weight: float32 [1024, 1024], P('fsdp')
- grad_gate_weight: float32 [1024, 4608], P('fsdp')
- grad_up_weight: float32 [1024, 4608], P('fsdp')
- grad_down_weight: float32 [4608, 1024], P('fsdp')
- grad_gain_attn: float32 [1024], replicated
- grad_gain_query: float32 [64], replicated
- grad_gain_key: float32 [64], replicated
- grad_gain_ffn: float32 [1024], replicated
The draws below stay inside these ranges and needn't reach their ends.
Inputs may be any that keep to these rules, and one draw needn't show every extreme that they name: `doc_starts`: for each sequence, 4 strictly increasing document starts: the first is 0, the last is 4095, all others lie at or after 4096 - 4096 // 4.
All inputs are finite; a program needn't handle non-finite values.
Results may differ from the reference program's by a relative error of at most 0.03.
Values may be sent and summed in bfloat16 or wider, within the bound.
A program may use at most 256 MiB of HBM per device.

```python
import math
import jax
import jax.numpy as jnp
from jax import lax

D = 1024
QUERY_HEADS = 16
KEY_VALUE_HEADS = 8
HEAD_SIZE = 64
FF = 4608
NDOC = 4
HALF = 64
NBLK = 64
SEQ = 4096
BATCH = 4
QKV = 2048


def draw_doc_starts(key, part):
    key = jax.random.fold_in(key, 7)
    tail_span = SEQ // 4

    def one_row(row_key):
        offsets = jnp.sort(jax.random.permutation(row_key, tail_span - 1)[:NDOC - 2])
        middle = (SEQ - tail_span + offsets).astype(jnp.int32)
        return jnp.concatenate([jnp.zeros((1,), jnp.int32), middle, jnp.full((1,), SEQ - 1, jnp.int32)])
    return jax.vmap(one_row)(jax.random.split(key, BATCH))


def steps_of(key, shape, pieces, least, top_value):
    factor_of = 1.0
    for dim, blocks in pieces:
        steps = jax.random.uniform(jax.random.fold_in(jax.random.fold_in(key, 6), dim), (blocks,), jnp.float32, least / len(pieces), top_value / len(pieces))
        factor_of = factor_of * jnp.repeat(jnp.exp(steps), shape[dim] // blocks).reshape((-1,) + (1,) * (len(shape) - 1 - dim))
    return factor_of


def bell_draw(rng, dims, deviation, limit, cuts=(), kind=jnp.bfloat16):
    values = deviation * jax.random.normal(rng, dims, jnp.float32)
    if cuts:
        values = values * steps_of(rng, dims, cuts, -0.22, 0.18)
    return jnp.clip(values, -limit, limit).astype(kind)


def setup_inputs(seed: int = 0) -> dict:
    keys = jax.random.split(jax.random.key(seed), 14)
    return {
        "inputs": bell_draw(keys[0], (BATCH, SEQ, D), 1.0, 6.0, ((0, 4), (1, 32))),
        "cotangent": bell_draw(keys[1], (BATCH, SEQ, D), 1.0, 6.0, ((0, 4), (1, 32))),
        "qkv_weight": bell_draw(keys[2], (D, QKV), D ** -0.5, 0.1875, ((0, 4),)),
        "out_weight": bell_draw(keys[3], (QUERY_HEADS * HEAD_SIZE, D), (QUERY_HEADS * HEAD_SIZE // 32) ** -0.5, 1.0, ((0, 4),)),
        "gate_weight": bell_draw(keys[4], (D, FF), D ** -0.5, 0.1875, ((0, 4),)),
        "up_weight": bell_draw(keys[5], (D, FF), D ** -0.5, 0.1875, ((0, 4),)),
        "down_weight": bell_draw(keys[6], (FF, D), FF ** -0.5, 0.09375, ((0, 4),)),
        "gain_attn": jnp.clip(1.0 + 0.1 * jax.random.normal(keys[7], (D,), jnp.float32), 0.5, 1.5),
        "gain_query": jnp.clip(1.0 + 0.18 * jax.random.normal(keys[8], (HEAD_SIZE,), jnp.float32), 0.1, 1.9),
        "gain_key": jnp.clip(1.0 + 0.18 * jax.random.normal(keys[9], (HEAD_SIZE,), jnp.float32), 0.1, 1.9),
        "gain_ffn": jnp.clip(1.0 + 0.1 * jax.random.normal(keys[10], (D,), jnp.float32), 0.5, 1.5),
        "block_order": jax.random.permutation(keys[11], NBLK).astype(jnp.int32),
        "doc_starts": draw_doc_starts(jax.random.fold_in(keys[13], 71), 0),
    }


@jax.custom_vjp
def reduced_precision(v):
    return lax.optimization_barrier(v.astype(jnp.bfloat16)).astype(jnp.float32)

@jax.custom_vjp
def low_back(v):
    return v

def low_keep(v):
    return (reduced_precision(v), None)

def low_pass(kept, grad):
    return (grad,)

def back_keep(v):
    return (v, None)

def back_low(kept, grad):
    return (reduced_precision(grad),)
reduced_precision.defvjp(low_keep, low_pass)
low_back.defvjp(back_keep, back_low)
EPSILON = 1e-05
ROPE_BASE = 1000000.0
NEGATIVE_FILLER = -1e+30

def matmul(left, right):
    return jnp.dot(left, right, precision=lax.Precision.HIGHEST)

def rms_norm(values, gain_row):
    return values * lax.rsqrt(lax.optimization_barrier(jnp.mean(values * values, axis=-1, keepdims=True)) + EPSILON) * gain_row

def rotate(values, positions):
    half_width = values.shape[-1] // 2
    frequency = ROPE_BASE ** (-2.0 * jnp.arange(half_width, dtype=jnp.float32) / values.shape[-1])
    angles = positions.astype(jnp.float32)[:, None] * frequency[None, :]
    cosine = jnp.cos(angles)[:, None, :]
    sine_part = jnp.sin(angles)[:, None, :]
    first_half = values[..., :half_width]
    second_half = values[..., half_width:]
    return jnp.concatenate([first_half * cosine - second_half * sine_part, second_half * cosine + first_half * sine_part], axis=-1)

def block_layer(inputs, positions, segments, qkv_weight, out_weight, gate_weight, up_weight, down_weight, gain_attn, gain_query, gain_key, gain_ffn):
    sequence_length = inputs.shape[0]
    query_groups = QUERY_HEADS // KEY_VALUE_HEADS
    normed = reduced_precision(rms_norm(inputs, gain_attn))
    output_projection = low_back(matmul(normed, qkv_weight))
    queries = output_projection[:, :QUERY_HEADS * HEAD_SIZE].reshape(sequence_length, QUERY_HEADS, HEAD_SIZE)
    unrotated_keys = output_projection[:, QUERY_HEADS * HEAD_SIZE:(QUERY_HEADS + KEY_VALUE_HEADS) * HEAD_SIZE].reshape(sequence_length, KEY_VALUE_HEADS, HEAD_SIZE)
    value_heads_block = reduced_precision(output_projection[:, (QUERY_HEADS + KEY_VALUE_HEADS) * HEAD_SIZE:].reshape(sequence_length, KEY_VALUE_HEADS, HEAD_SIZE))
    queries = reduced_precision(rotate(rms_norm(queries, gain_query), positions))
    keys_all = reduced_precision(rotate(rms_norm(unrotated_keys, gain_key), positions))
    keys_wide = jnp.repeat(keys_all, query_groups, axis=1)
    values_wide = jnp.repeat(value_heads_block, query_groups, axis=1)
    block_rows = math.gcd(sequence_length, 512)
    block_count = sequence_length // block_rows

    def attend_block(block_args):
        query_block, pos_block, seg_block = block_args
        scores = jnp.einsum('qhd,khd->hqk', query_block, keys_wide, precision=lax.Precision.HIGHEST)
        scores = low_back(scores * float(HEAD_SIZE) ** (-0.5))
        allowed = (positions[None, :] <= pos_block[:, None]) & (segments[None, :] == seg_block[:, None])
        scores = jnp.where(allowed[None], scores, NEGATIVE_FILLER)
        prob_rows = reduced_precision(jax.nn.softmax(scores, axis=-1))
        return jnp.einsum('hqk,khd->qhd', prob_rows, values_wide, precision=lax.Precision.HIGHEST)
    attention_output = lax.map(jax.checkpoint(attend_block), (queries.reshape(block_count, block_rows, QUERY_HEADS, HEAD_SIZE), positions.reshape(block_count, block_rows), segments.reshape(block_count, block_rows)))
    attention_output = low_back(reduced_precision(attention_output.reshape(sequence_length, QUERY_HEADS * HEAD_SIZE)))
    residual = inputs + low_back(matmul(attention_output, out_weight))
    normed_ffn = reduced_precision(rms_norm(residual, gain_ffn))
    gate_proj = low_back(matmul(normed_ffn, gate_weight))
    up_proj = low_back(matmul(normed_ffn, up_weight))
    hidden = reduced_precision(jax.nn.silu(gate_proj) * up_proj)
    return residual + matmul(hidden, down_weight)

def reference(inputs, cotangent, qkv_weight, out_weight, gate_weight, up_weight, down_weight, gain_attn, gain_query, gain_key, gain_ffn, block_order, doc_starts):
    row_ids = jnp.arange(SEQ, dtype=jnp.int32)
    positions = (block_order[row_ids // HALF] * HALF + row_ids % HALF).astype(jnp.int32)
    segments = (lax.optimization_barrier(jnp.sum((doc_starts[:, None, :] <= positions[None, :, None]).astype(jnp.int32), axis=-1)) - 1).astype(jnp.int32)

    def forward(batch_inputs, *weights):

        def one_seq(seq_pair):
            return block_layer(seq_pair[0], positions, seq_pair[1], *weights)
        return lax.map(one_seq, (batch_inputs, segments))
    floats = [array_in.astype(jnp.float32) for array_in in (inputs, qkv_weight, out_weight, gate_weight, up_weight, down_weight, gain_attn, gain_query, gain_key, gain_ffn)]
    outputs, pull_back = jax.vjp(forward, *floats)
    gradients = pull_back(cotangent.astype(jnp.float32))
    return (outputs.astype(jnp.bfloat16), gradients[0].astype(jnp.bfloat16), gradients[1], gradients[2], gradients[3], gradients[4], gradients[5], gradients[6], gradients[7], gradients[8], gradients[9])
```

```python
import functools
import math

import jax
import jax.numpy as jnp
from jax import lax
from jax.experimental import pallas as pl
from jax.experimental.pallas import tpu as pltpu
from jax.sharding import PartitionSpec as P

QUERY_HEADS = 16
KEY_VALUE_HEADS = 8
HEAD_SIZE = 64
FF = 4608
D = 1024
TOKENS = 128
RING = 32
QUARTER = 8
SLICE = 1152
HALF_FF = FF // 2
KEY_TILE = 512
SEQ = 4096

EPSILON = 1e-05
ROPE_BASE = 1000000.0
SCORE_TO_EXP2 = float(HEAD_SIZE) ** (-0.5) * math.log2(math.e)

MESH = pl.DeviceIdType.MESH
ANY = pl.BlockSpec(memory_space=pl.ANY)
VMEM = pl.BlockSpec(memory_space=pltpu.VMEM)
SMEM = pl.BlockSpec(memory_space=pltpu.SMEM)
BF16 = jnp.bfloat16
F32 = jnp.float32
MIB = 1 << 20


class Place:
    def __init__(self):
        self.ctx, self.fsdp = (lax.axis_index("ctx"), lax.axis_index("fsdp"))
        self.zl, self.x, self.y = (self.ctx // 16, (self.ctx // 4) % 4, self.ctx % 4)
        self.zh, self.core = (self.fsdp // 2, self.fsdp % 2)
        self.z = self.zh * 2 + self.zl

    def device(self, x=None, y=None, z=None, core=None):
        x = self.x if x is None else x
        y = self.y if y is None else y
        z = self.z if z is None else z
        core = self.core if core is None else core
        return ((z % 2) * 16 + x * 4 + y, (z // 2) * 2 + core)

    def sibling(self):
        return self.device(core=1 - self.core)

    def along(self, axis, step):
        coordinate = (getattr(self, axis) + step) % 4
        return coordinate, self.device(**{axis: coordinate})


class Wires:
    def __init__(self, sends, receives, locals_=None):
        self.sends, self.receives, self.locals_ = (sends, receives, locals_)
        self.pushed, self.moved = ([], 0)

    def push(self, source, target, device):
        at = len(self.pushed)
        copy = pltpu.make_async_remote_copy(
            src_ref=source,
            dst_ref=target,
            send_sem=self.sends.at[at],
            recv_sem=self.receives.at[at],
            device_id=device,
            device_id_type=MESH,
        )
        copy.start()
        self.pushed.append(copy)
        return copy

    def move(self, source, target):
        copy = pltpu.make_async_copy(source, target, self.locals_.at[self.moved])
        copy.start()
        self.moved += 1
        return copy

    def finish_sends(self):
        for copy in self.pushed:
            copy.wait_send()


def arrive(copies):
    for copy in copies:
        copy.wait_recv()


def greet(devices):
    barrier = pltpu.get_barrier_semaphore()
    for device in devices:
        pl.semaphore_signal(barrier, inc=1, device_id=device, device_id_type=MESH)
    pl.semaphore_wait(barrier, len(devices))


def wired_call(kernel, outs, ins, collective_id, name, copies, moves, scratch=(), in_specs=None,
               out_specs=None, vmem=32 * MIB):
    return pl.pallas_call(
        kernel,
        out_shape=outs,
        in_specs=[ANY] * len(ins) if in_specs is None else in_specs,
        out_specs=[ANY] * len(outs) if out_specs is None else out_specs,
        scratch_shapes=[
            *scratch,
            pltpu.SemaphoreType.DMA((copies,)),
            pltpu.SemaphoreType.DMA((copies,)),
            pltpu.SemaphoreType.DMA((max(moves, 1),)),
        ],
        compiler_params=pltpu.CompilerParams(
            collective_id=collective_id, has_side_effects=True, vmem_limit_bytes=vmem
        ),
        name=name,
    )(*ins)


def shape(*dims, dtype=BF16):
    return jax.ShapeDtypeStruct(dims, dtype)


def gather_weights_kernel(
    qkv, out, gate, up, down, qkv_all, out_all, gate_all, up_all, down_all, sends, receives, moves
):
    here = Place()
    wires = Wires(sends, receives, moves)
    zh, core, x, y = (here.zh, here.core, here.x, here.y)
    other = 1 - zh
    steps = (1, 3, 2)
    xs = [here.along("x", s)[1] for s in steps]
    ys = [here.along("y", s)[1] for s in steps]
    across = 3 - here.z
    cross = [here.device(z=across, core=(core + t) % 2) for t in range(2)]
    sibling = here.sibling()
    greet(xs + ys + cross + [sibling])

    def ff_columns(r, c):
        return pl.ds(pl.multiple_of(r * HALF_FF + c * SLICE, 128), SLICE)

    def down_columns():
        return pl.ds(pl.multiple_of(y * 256, 256), 256)

    crossed = {}
    crossed["qkv"] = [wires.push(qkv.at[x, y], qkv_all.at[zh, core, x, y], cross[0])]
    crossed["out"] = [wires.push(out.at[x, y], out_all.at[zh, core, x, y], cross[0])]
    for name, shard, whole in (("gate", gate, gate_all), ("up", up, up_all)):
        crossed[name] = [
            wires.push(
                shard.at[x, y, :, ff_columns(r, (core + t) % 2)],
                whole.at[zh, core, x, y, :, pl.ds(r * SLICE, SLICE)],
                cross[t],
            )
            for t in range(2)
            for r in range(2)
        ]
    crossed["down"] = [
        wires.push(
            down.at[x, :, :, down_columns()], down_all.at[zh, x, :, :, down_columns()], cross[0]
        )
    ]
    beside = [
        wires.push(qkv, qkv_all.at[zh, core], sibling),
        wires.push(out, out_all.at[zh, core], sibling),
    ]
    kept = [wires.move(qkv, qkv_all.at[zh, core]), wires.move(out, out_all.at[zh, core])]
    for shard, whole in ((gate, gate_all), (up, up_all)):
        for r in range(2):
            target = whole.at[zh, core, :, :, :, pl.ds(r * SLICE, SLICE)]
            beside.append(wires.push(shard.at[:, :, :, ff_columns(r, 1 - core)], target, sibling))
            kept.append(wires.move(shard.at[:, :, :, ff_columns(r, core)], target))
    kept.append(wires.move(down, down_all.at[zh]))

    def own_piece(name, half):
        if name == "down":
            return down_all.at[other, x, half, :, down_columns()]
        if name in ("gate", "up"):
            whole = gate_all if name == "gate" else up_all
            return whole.at[other, :, x, y, :, pl.ds(half * SLICE, SLICE)]
        whole, width = (qkv_all, 1024) if name == "qkv" else (out_all, 512)
        return whole.at[other, core, x, y, :, pl.ds(half * width, width)]

    def line(name, half):
        if name == "down":
            if half == 0:
                return down_all.at[other, :, 0, :, down_columns()]
            return down_all.at[other, x, 1]
        if name in ("gate", "up"):
            whole = gate_all if name == "gate" else up_all
            if half == 0:
                return whole.at[other, :, :, y, :, pl.ds(0, SLICE)]
            return whole.at[other, :, x, :, :, pl.ds(SLICE, SLICE)]
        whole, width = (qkv_all, 1024) if name == "qkv" else (out_all, 512)
        if half == 0:
            return whole.at[other, core, :, y, :, pl.ds(0, width)]
        return whole.at[other, core, x, :, :, pl.ds(width, width)]

    names = ("qkv", "out", "gate", "up", "down")
    first, second = ({}, {})
    for name in names:
        arrive(crossed[name])
        first[name] = [
            wires.push(own_piece(name, half), own_piece(name, half), device)
            for half, ring in ((0, xs), (1, ys))
            for device in ring
        ]
    for name in names:
        arrive(first[name])
        second[name] = [
            wires.push(line(name, half), line(name, half), device)
            for half, ring in ((0, ys), (1, xs))
            for device in ring
        ]
    for name, whole in (("qkv", qkv_all), ("out", out_all)):
        arrive(second[name])
        beside.append(wires.push(whole.at[other, core], whole.at[other, core], sibling))
    for name in names[2:]:
        arrive(second[name])
    arrive(beside)
    for copy in kept:
        copy.wait()
    wires.finish_sends()


def gather_weights(qkv, out, gate, up, down):
    rows = (4, 4, 16)
    ins = (
        qkv.reshape(*rows, 2048),
        out.reshape(*rows, D),
        gate.reshape(*rows, FF),
        up.reshape(*rows, FF),
        down.reshape(4, 2, 144, D),
    )
    outs = [
        shape(2, 2, *rows, 2048),
        shape(2, 2, *rows, D),
        shape(2, 2, *rows, HALF_FF),
        shape(2, 2, *rows, HALF_FF),
        shape(2, 4, 2, 144, D),
    ]
    copies = 3 + 8 + 6 + 30 + 30 + 2
    qkv, out, gate, up, down = wired_call(
        gather_weights_kernel, outs, ins, 1, "gather_weights", copies, 7
    )
    return (
        qkv.reshape(D, 2048),
        out.reshape(D, D),
        gate.reshape(D, HALF_FF),
        up.reshape(D, HALF_FF),
        down.reshape(HALF_FF, D),
    )


class RowsByShard:
    lead = (2, 2, 4, 4)

    def __init__(self, columns):
        self.columns = columns

    def order(self, at):
        return [at.get("zh"), at.get("zl"), at.get("x"), at.get("y")]

    def tail(self, at):
        return (slice(None), slice(None))

    def tail_dims(self, at):
        return (16, self.columns)


class RowsByPlane:
    lead = (2, 4, 4)

    def __init__(self, first, columns):
        self.first, self.columns = (first, columns)

    def order(self, at):
        return [at.get("zh"), at.get("x"), at.get("y")]

    def tail(self, at):
        if "zl" not in at:
            return (slice(None), pl.ds(self.first, self.columns))
        half = self.columns // 2
        return (slice(None), pl.ds(pl.multiple_of(self.first + half * at["zl"], 128), half))

    def tail_dims(self, at):
        return (16, self.columns // 2 if "zl" in at else self.columns)


class ColumnsByY:
    lead = (2, 4, 2)

    def __init__(self, rows):
        self.rows = rows

    def order(self, at):
        return [at.get("zh"), at.get("x"), at.get("zl")]

    def tail(self, at):
        if "y" not in at:
            return (slice(None), slice(None))
        return (slice(None), pl.ds(pl.multiple_of(at["y"] * 256, 256), 256))

    def tail_dims(self, at):
        return (self.rows, 256 if "y" in at else D)


def view(kind, ref, at, skip=0):
    lead = [slice(None) if i is None else i for i in kind.order(at)[skip:]]
    return ref.at[(*lead, *kind.tail(at))]


def open_dims(kind, at):
    return tuple(n for n, i in zip(kind.lead, kind.order(at)) if i is None)


def fix(at, axis, coordinate):
    if axis == "z":
        return {**at, "zh": coordinate // 2, "zl": coordinate % 2}
    return {**at, axis: coordinate}


PARTS = (
    (0, RowsByShard(HALF_FF), ("z", "x", "y")),
    (1, RowsByShard(HALF_FF), ("x", "y", "z")),
    (2, ColumnsByY(144), ("y", "z", "x")),
    (3, RowsByPlane(0, 1024), ("z", "x", "y")),
    (3, RowsByPlane(1024, 1024), ("x", "y", "z")),
    (4, ColumnsByY(32), ("y", "z", "x")),
)
STEPS = (1, 3, 2)


def slot_shapes():
    found = []
    for _, kind, order in PARTS:
        at = {}
        for axis in order:
            at = fix(at, axis, 0)
            found.append((3, *open_dims(kind, at), *kind.tail_dims(at)))
    return found


def add_up(kind, total, slots, at):
    dims = open_dims(kind, at)
    order = kind.order(at)
    tail = kind.tail(at)

    def body(i, _):
        inner, rest = ([], i)
        for n in reversed(dims):
            inner.insert(0, rest % n)
            rest = rest // n
        picks = iter(inner)
        where = (*[next(picks) if o is None else o for o in order], *tail)
        value = total[where].astype(F32)
        for j in range(3):
            value += slots[(j, *inner, slice(None), slice(None))].astype(F32)
        total[where] = value.astype(BF16)
        return 0

    lax.fori_loop(0, math.prod(dims), body, 0)


def reduce_weights_kernel(*refs):
    grads, gains = (refs[:5], refs[5])
    gate_near, up_near, gate_out, up_out, down_out, qkv_out, out_out, gains_out = refs[6:14]
    totals = refs[14:19]
    slots = refs[19:37]
    gain_slots, sends, receives, moves = refs[37:]
    nears = (gate_near, up_near, down_out, qkv_out, out_out)

    here = Place()
    wires = Wires(sends, receives, moves)
    core = here.core
    sibling = here.sibling()
    ring = {a: [here.along(a, s) for s in STEPS] for a in ("x", "y", "z")}
    greet([device for a in ("x", "y", "z") for _, device in ring[a]] + [sibling])

    gain_slots[0, core] = gains[...]
    gain_copies = [wires.push(gain_slots.at[0, core], gain_slots.at[0, core], sibling)]

    def next_gains(stage):
        arrive(gain_copies)
        total = gain_slots[stage, 0] + gain_slots[stage, 1]
        if stage > 0:
            total = total + gain_slots[stage, 2] + gain_slots[stage, 3]
        if stage == 3:
            gains_out[...] = total
            return
        axis = ("x", "y", "z")[stage]
        me = getattr(here, axis)
        gain_slots[stage + 1, me] = total
        source = gain_slots.at[stage + 1, me]
        gain_copies[:] = [wires.push(source, source, device) for _, device in ring[axis]]

    fixed = [{} for _ in PARTS]
    flying = [None] * len(PARTS)
    own = [None] * len(PARTS)
    for step in range(3):
        for p, (g, kind, order) in enumerate(PARTS):
            if step > 0:
                if own[p] is not None:
                    own[p].wait()
                    own[p] = None
                arrive(flying[p])
                add_up(kind, totals[g], slots[3 * p + step - 1], fixed[p])
            axis = order[step]
            source = grads[g] if step == 0 else totals[g]
            flying[p] = [
                wires.push(
                    view(kind, source, fix(fixed[p], axis, coordinate)),
                    slots[3 * p + step].at[j],
                    device,
                )
                for j, (coordinate, device) in enumerate(ring[axis])
            ]
            fixed[p] = fix(fixed[p], axis, getattr(here, axis))
            if step == 0:
                own[p] = wires.move(
                    view(kind, source, fixed[p]), view(kind, totals[g], fixed[p])
                )
        next_gains(step)
    next_gains(3)

    for p, (g, kind, order) in enumerate(PARTS):
        arrive(flying[p])
        add_up(kind, totals[g], slots[3 * p + 2], fixed[p])
        own[p] = wires.move(view(kind, totals[g], fixed[p]), view(kind, nears[g], fixed[p], 1))
    for step in (2, 1, 0):
        for p, (g, kind, order) in enumerate(PARTS):
            if step == 2:
                own[p].wait()
            else:
                arrive(flying[p])
            axis = order[step]
            piece = view(kind, nears[g], fixed[p], 1)
            if axis == "z":
                devices = [here.device(z=here.zh * 2 + 1 - here.zl)]
                gone = ("zl",)
            else:
                devices = [device for _, device in ring[axis]]
                gone = (axis,)
            flying[p] = [wires.push(piece, piece, device) for device in devices]
            fixed[p] = {a: i for a, i in fixed[p].items() if a not in gone}
    last = []
    kept = []
    for p, (near, final) in enumerate(((gate_near, gate_out), (up_near, up_out))):
        arrive(flying[p])
        for r in range(2):
            source = pl.ds(r * SLICE, SLICE)
            target = final.at[:, :, :, pl.ds(pl.multiple_of(r * HALF_FF + core * SLICE, 128), SLICE)]
            last.append(wires.push(near.at[1 - core, :, :, :, source], target, sibling))
            kept.append(wires.move(near.at[core, :, :, :, source], target))
    for p in range(2, len(PARTS)):
        arrive(flying[p])
    arrive(last)
    for copy in kept:
        copy.wait()
    wires.finish_sends()


def reduce_weights(gate, up, down, qkv, out, gains):
    dims = (
        (2, 2, 4, 4, 16, HALF_FF),
        (2, 2, 4, 4, 16, HALF_FF),
        (2, 4, 2, 144, D),
        (2, 4, 4, 16, 2048),
        (2, 4, 2, 32, D),
    )
    ins = [a.reshape(d) for a, d in zip((gate, up, down, qkv, out), dims)] + [gains]
    outs = [
        shape(*dims[0][1:]),
        shape(*dims[1][1:]),
        shape(4, 4, 16, FF),
        shape(4, 4, 16, FF),
        shape(*dims[2][1:]),
        shape(*dims[3][1:]),
        shape(*dims[4][1:]),
        shape(*gains.shape, dtype=F32),
    ]
    scratch = [pltpu.VMEM(d, BF16) for d in dims]
    scratch += [pltpu.VMEM(s, BF16) for s in slot_shapes()]
    scratch += [pltpu.VMEM((4, 4, *gains.shape), F32)]
    copies = 1 + 9 + 6 * 9 + 6 * 7 + 4
    done = wired_call(
        reduce_weights_kernel,
        outs,
        ins,
        2,
        "reduce_weights",
        copies,
        12 + 4,
        scratch,
        [ANY] * 5 + [VMEM],
        [ANY] * 7 + [VMEM],
        vmem=56 * MIB,
    )
    gate, up, down, qkv, out, gains = done[2:]
    return (
        qkv.reshape(256, 2048),
        out.reshape(256, D),
        gate.reshape(256, FF),
        up.reshape(256, FF),
        down.reshape(SLICE, D),
        gains,
    )


def head_columns(head):
    return pl.ds(pl.multiple_of(head * 128, 128), 128)


def to_heads_kernel(with_keys, *refs):
    if with_keys:
        query, key_value, query_out, key_value_out, sends, receives, moves = refs
    else:
        query, query_out, sends, receives, moves = refs
    here = Place()
    wires = Wires(sends, receives, moves)
    me = here.ctx
    quarter, seat = (me // QUARTER, me % QUARTER)
    near = [quarter * QUARTER + (seat + s) % QUARTER for s in range(1, QUARTER)]
    far = [(me + s) % RING for s in range(1, RING)]
    greet([(k, here.fsdp) for k in (far if with_keys else near)])
    copies = [
        wires.push(query.at[:, head_columns(k % QUARTER)], query_out.at[seat], (k, here.fsdp))
        for k in near
    ]
    kept = [wires.move(query.at[:, head_columns(seat)], query_out.at[seat])]
    if with_keys:
        copies += [
            wires.push(
                key_value.at[:, head_columns(k % QUARTER)], key_value_out.at[me], (k, here.fsdp)
            )
            for k in far
        ]
        kept.append(wires.move(key_value.at[:, head_columns(seat)], key_value_out.at[me]))
    arrive(copies)
    for copy in kept:
        copy.wait()
    wires.finish_sends()


def to_heads(query, key_value=None):
    ins = [query] + ([] if key_value is None else [key_value])
    outs = [shape(QUARTER, TOKENS, 128)]
    if key_value is not None:
        outs.append(shape(RING, TOKENS, 128))
    copies = 7 if key_value is None else 38
    return wired_call(
        functools.partial(to_heads_kernel, key_value is not None),
        outs,
        ins,
        3 if key_value is None else 4,
        "to_heads",
        copies,
        2,
    )


def to_tokens_kernel(with_keys, *refs):
    if with_keys:
        query, key_value, query_out, key_value_out, sends, receives, moves = refs
    else:
        query, query_out, sends, receives, moves = refs
    here = Place()
    wires = Wires(sends, receives, moves)
    me = here.ctx
    quarter, seat = (me // QUARTER, me % QUARTER)
    near = [quarter * QUARTER + (seat + s) % QUARTER for s in range(1, QUARTER)]
    far = [(me + s) % RING for s in range(1, RING)]
    greet([(k, here.fsdp) for k in (far if with_keys else near)])
    columns = query_out.at[:, head_columns(seat)]
    copies = [wires.push(query.at[k % QUARTER], columns, (k, here.fsdp)) for k in near]
    kept = [wires.move(query.at[seat], columns)]
    if with_keys:
        copies += [
            wires.push(key_value.at[k], key_value_out.at[me], (k, here.fsdp)) for k in far
        ]
        kept.append(wires.move(key_value.at[me], key_value_out.at[me]))
    arrive(copies)
    for copy in kept:
        copy.wait()
    wires.finish_sends()


def to_tokens(query, key_value=None):
    ins = [query] + ([] if key_value is None else [key_value])
    outs = [shape(TOKENS, D)]
    if key_value is not None:
        outs.append(shape(RING, TOKENS, 128))
    copies = 7 if key_value is None else 38
    return wired_call(
        functools.partial(to_tokens_kernel, key_value is not None),
        outs,
        ins,
        5 if key_value is None else 6,
        "to_tokens",
        copies,
        2,
    )


def half_columns(r, core):
    return pl.ds(pl.multiple_of(r * 512 + core * 256, 256), 256)


def share_kernel(whole, halved, *refs):
    n = whole + halved
    ins, outs = (refs[:n], refs[n : 2 * n])
    here = Place()
    wires = Wires(*refs[2 * n :])
    core = here.core
    sibling = here.sibling()
    greet([sibling])
    copies, kept = ([], [])
    for source, target in zip(ins[:whole], outs[:whole]):
        copies.append(wires.push(source, target.at[core], sibling))
        kept.append(wires.move(source, target.at[core]))
    for source, target in zip(ins[whole:], outs[whole:]):
        for r in range(2):
            place = target.at[core, :, pl.ds(r * 256, 256)]
            copies.append(wires.push(source.at[:, half_columns(r, 1 - core)], place, sibling))
            kept.append(wires.move(source.at[:, half_columns(r, core)], place))
    arrive(copies)
    for copy in kept:
        copy.wait()
    wires.finish_sends()


def share(whole, halved, collective_id):
    outs = [shape(2, *a.shape, dtype=a.dtype) for a in whole]
    outs += [shape(2, a.shape[0], 512, dtype=a.dtype) for a in halved]
    count = len(whole) + 2 * len(halved)
    done = wired_call(
        functools.partial(share_kernel, len(whole), len(halved)),
        outs,
        [*whole, *halved],
        collective_id,
        "share",
        count,
        count,
    )
    return [a.reshape(2 * a.shape[1], a.shape[2]) for a in done]


def hand_over_kernel(count, *refs):
    ins, outs = (refs[:count], refs[count : 2 * count])
    here = Place()
    wires = Wires(*refs[2 * count :])
    sibling = here.sibling()
    greet([sibling])
    copies = [wires.push(i.at[1 - here.core], o, sibling) for i, o in zip(ins, outs)]
    arrive(copies)
    wires.finish_sends()


def hand_over(partials, collective_id):
    return wired_call(
        functools.partial(hand_over_kernel, len(partials)),
        [shape(*a.shape[1:], dtype=a.dtype) for a in partials],
        partials,
        collective_id,
        "hand_over",
        len(partials),
        0,
    )


def nt(left, right):
    return lax.dot_general(left, right, (((1,), (1,)), ((), ())), preferred_element_type=F32)


def nn(left, right):
    return lax.dot_general(left, right, (((1,), (0,)), ((), ())), preferred_element_type=F32)


def by_position(order_ref, key_value_ref, sorted_ref):
    def body(j, _):
        sorted_ref[pl.ds(pl.multiple_of(order_ref[j] * 64, 64), 64), :] = key_value_ref[j]
        return 0

    lax.fori_loop(0, 64, body, 0)


def query_block(ref, t):
    block = ref[t].astype(F32)
    both = jnp.concatenate([block, pltpu.roll(block, 64, 1)], axis=0)
    low = lax.broadcasted_iota(jnp.int32, (128, 128), 1) < 64
    return jnp.where(low, both, 0.0)


def key_limits(order_ref, starts_ref, place_ref, t):
    first = order_ref[place_ref[0] * 16 + t] * 64
    begin = jnp.int32(0)
    for n in range(4):
        begin = jnp.maximum(begin, jnp.where(starts_ref[n] <= first, starts_ref[n], 0))
    return first, begin // KEY_TILE, (first + 63) // KEY_TILE + 1


def first_allowed(position, starts_ref):
    begin = jnp.zeros_like(position)
    for n in range(4):
        begin = jnp.maximum(begin, jnp.where(starts_ref[n] <= position, starts_ref[n], 0))
    return begin


def attend_kernel(
    order_ref, starts_ref, place_ref, query_ref, key_value_ref, out_ref, exact_ref, sum_ref,
    sorted_ref, value_ref,
):
    by_position(order_ref, key_value_ref, sorted_ref)

    def values(j, _):
        rows = pl.ds(pl.multiple_of(j * 256, 256), 256)
        block = pltpu.roll(sorted_ref[rows, :].astype(F32), 64, 1)
        low = lax.broadcasted_iota(jnp.int32, (256, 128), 1) < 64
        value_ref[rows, :] = jnp.where(low, block, 1.0).astype(BF16)
        return 0

    lax.fori_loop(0, SEQ // 256, values, 0)

    def block(t, _):
        first, begin_tile, end_tile = key_limits(order_ref, starts_ref, place_ref, t)
        queries = query_block(query_ref, t).astype(BF16)
        position = first + lax.broadcasted_iota(jnp.int32, (128, 1), 0) % 64
        begin = first_allowed(position, starts_ref)

        def tile(j, total):
            rows = pl.ds(pl.multiple_of(j * KEY_TILE, KEY_TILE), KEY_TILE)
            scores = nt(queries, sorted_ref[rows, :])
            key = j * KEY_TILE + lax.broadcasted_iota(jnp.int32, (128, KEY_TILE), 1)
            allowed = (key <= position) & (key >= begin)
            weight = jnp.where(allowed, jnp.exp2(scores * SCORE_TO_EXP2), 0.0)
            return total + nn(weight.astype(BF16), value_ref[rows, :])

        total = lax.fori_loop(begin_tile, end_tile, tile, jnp.zeros((128, 128), F32))
        sums = pltpu.roll(total, 64, 1)
        attended = total / sums
        low_pair = lax.broadcasted_iota(jnp.int32, (128, 128), 1) < 64
        low = lax.broadcasted_iota(jnp.int32, (64, 128), 1) < 64
        exact_ref[t] = jnp.where(low_pair, attended, 0.0)
        out_ref[t] = jnp.where(low, attended[:64], pltpu.roll(attended[64:], 64, 1)).astype(BF16)
        sum_ref[t] = jnp.transpose(total)[64:72]
        return 0

    lax.fori_loop(0, 16, block, 0)


def attend(order, starts, place, queries, key_values):
    return pl.pallas_call(
        attend_kernel,
        out_shape=[shape(16, 64, 128), shape(16, 128, 128, dtype=F32), shape(16, 8, 128, dtype=F32)],
        in_specs=[SMEM, SMEM, SMEM, VMEM, VMEM],
        out_specs=[VMEM] * 3,
        scratch_shapes=[pltpu.VMEM((SEQ, 128), BF16), pltpu.VMEM((SEQ, 128), BF16)],
        compiler_params=pltpu.CompilerParams(vmem_limit_bytes=32 * MIB),
        name="attend",
    )(order, starts, place, queries, key_values)


def attend_back_kernel(
    order_ref, starts_ref, place_ref, query_ref, key_value_ref, grad_ref, exact_ref, sum_ref,
    query_grad_ref, key_value_grad_ref, sorted_ref, across_ref, total_ref,
):
    by_position(order_ref, key_value_ref, sorted_ref)
    total_ref[...] = jnp.zeros_like(total_ref)

    def turn(j, _):
        rows = pl.ds(pl.multiple_of(j * 128, 128), 128)
        across_ref[:, rows] = jnp.transpose(sorted_ref[rows, :].astype(F32)).astype(BF16)
        return 0

    lax.fori_loop(0, SEQ // 128, turn, 0)

    def block(t, _):
        first, begin_tile, end_tile = key_limits(order_ref, starts_ref, place_ref, t)
        queries = query_block(query_ref, t)
        grads = query_block(grad_ref, t)
        delta = jnp.sum(jnp.transpose(grads * exact_ref[t]), axis=0, keepdims=True)
        total_exp2 = jnp.log2(sum_ref[t][0:1])
        both = jnp.concatenate([queries, pltpu.roll(grads, 64, 1)], axis=0).astype(BF16)
        position = first + lax.broadcasted_iota(jnp.int32, (1, 128), 1) % 64
        begin = first_allowed(position, starts_ref)

        def tile(j, query_grad):
            rows = pl.ds(pl.multiple_of(j * KEY_TILE, KEY_TILE), KEY_TILE)
            products = nt(sorted_ref[rows, :], both)
            key = j * KEY_TILE + lax.broadcasted_iota(jnp.int32, (KEY_TILE, 128), 0)
            allowed = (key <= position) & (key >= begin)
            prob = jnp.where(
                allowed, jnp.exp2(products[:, :128] * SCORE_TO_EXP2 - total_exp2), 0.0
            )
            score = (prob * (products[:, 128:] - delta)).astype(BF16)
            pair = jnp.concatenate([score, prob.astype(BF16)], axis=1)
            total_ref[rows, :] += nn(pair, both)
            return query_grad + nn(across_ref[:, rows], score)

        query_grad = lax.fori_loop(begin_tile, end_tile, tile, jnp.zeros((128, 128), F32))
        query_grad = jnp.transpose(query_grad) * float(HEAD_SIZE) ** (-0.5)
        low = lax.broadcasted_iota(jnp.int32, (64, 128), 1) < 64
        query_grad_ref[t] = jnp.where(
            low, query_grad[:64], pltpu.roll(query_grad[64:], 64, 1)
        ).astype(BF16)
        return 0

    lax.fori_loop(0, 16, block, 0)

    def put_back(j, _):
        rows = pl.ds(pl.multiple_of(order_ref[j] * 64, 64), 64)
        low = lax.broadcasted_iota(jnp.int32, (64, 128), 1) < 64
        scale = jnp.where(low, float(HEAD_SIZE) ** (-0.5), 1.0)
        key_value_grad_ref[j] = (total_ref[rows, :] * scale).astype(BF16)
        return 0

    lax.fori_loop(0, 64, put_back, 0)


def attend_back(order, starts, place, queries, key_values, grads, exact, sums):
    return pl.pallas_call(
        attend_back_kernel,
        out_shape=[shape(16, 64, 128), shape(64, 64, 128)],
        in_specs=[SMEM] * 3 + [VMEM] * 5,
        out_specs=[VMEM] * 2,
        scratch_shapes=[
            pltpu.VMEM((SEQ, 128), BF16),
            pltpu.VMEM((128, SEQ), BF16),
            pltpu.VMEM((SEQ, 128), F32),
        ],
        compiler_params=pltpu.CompilerParams(vmem_limit_bytes=40 * MIB),
        name="attend_back",
    )(order, starts, place, queries, key_values, grads, exact, sums)


def rms_norm(values, gain_row):
    return (
        values * lax.rsqrt(jnp.mean(values * values, axis=-1, keepdims=True) + EPSILON) * gain_row
    )


def rotate(values, positions):
    half_width = values.shape[-1] // 2
    frequency = ROPE_BASE ** (-2.0 * jnp.arange(half_width, dtype=F32) / values.shape[-1])
    angles = positions.astype(F32)[:, None] * frequency[None, :]
    cosine = jnp.cos(angles)[:, None, :]
    sine_part = jnp.sin(angles)[:, None, :]
    first_half = values[..., :half_width]
    second_half = values[..., half_width:]
    return jnp.concatenate(
        [
            first_half * cosine - second_half * sine_part,
            second_half * cosine + first_half * sine_part,
        ],
        axis=-1,
    )


def outer_sum(left, right):
    return lax.dot_general(
        left, right, (((0,), (0,)), ((), ())), preferred_element_type=F32
    ).astype(BF16)


def matmul(left, right):
    return jnp.dot(left, right, preferred_element_type=F32)


def positions_at(block_order, first_row, total_row_count, half_rows):
    row_ids = first_row + jnp.arange(total_row_count, dtype=jnp.int32)
    blocks = row_ids // half_rows
    lookup = jnp.arange(block_order.shape[0], dtype=jnp.int32)
    picked = jnp.sum(jnp.where(blocks[:, None] == lookup[None, :], block_order[None, :], 0), axis=1)
    return picked * half_rows + row_ids % half_rows


def per_device(
    inputs,
    cotangent,
    qkv_weight,
    out_weight,
    gate_weight,
    up_weight,
    down_weight,
    gain_attn,
    gain_query,
    gain_key,
    gain_ffn,
    block_order,
    doc_starts,
):
    cycle_index = lax.axis_index("ctx")
    core = lax.axis_index("fsdp") % 2
    qkv_all, out_all, gate_all, up_all, down_all = gather_weights(
        qkv_weight, out_weight, gate_weight, up_weight, down_weight
    )
    starts = doc_starts[0]
    place = (cycle_index // QUARTER).astype(jnp.int32).reshape(1)
    positions = positions_at(block_order, cycle_index * TOKENS, TOKENS, TOKENS // 2)

    resid_in = inputs[0].astype(F32)
    normed, norm_in_pull = jax.vjp(rms_norm, resid_in, gain_attn)
    normed_low = normed.astype(BF16)
    projected = matmul(normed_low, qkv_all)
    split_position = (QUERY_HEADS + KEY_VALUE_HEADS) * HEAD_SIZE

    def query_key(leading_columns, scale_query, scale_key):
        queries = leading_columns[:, : QUERY_HEADS * HEAD_SIZE].reshape(
            TOKENS, QUERY_HEADS, HEAD_SIZE
        )
        keys = leading_columns[:, QUERY_HEADS * HEAD_SIZE :].reshape(
            TOKENS, KEY_VALUE_HEADS, HEAD_SIZE
        )
        return (
            rotate(rms_norm(queries, scale_query), positions),
            rotate(rms_norm(keys, scale_key), positions),
        )

    (queries, keys), qk_pull = jax.vjp(
        query_key, projected[:, :split_position], gain_query, gain_key
    )
    values = projected[:, split_position:].reshape(TOKENS, KEY_VALUE_HEADS, HEAD_SIZE)
    key_values = jnp.concatenate([keys, values], axis=-1).astype(BF16).reshape(TOKENS, D)
    query_part, key_value_part = to_heads(queries.astype(BF16).reshape(TOKENS, D), key_values)
    query_part = query_part.reshape(16, 64, 128)
    key_value_part = key_value_part.reshape(64, 64, 128)
    attended, exact, sums = attend(block_order, starts, place, query_part, key_value_part)
    (attended_low,) = to_tokens(attended.reshape(QUARTER, TOKENS, 128))

    residual = resid_in + matmul(attended_low, out_all)
    normed_ffn, norm_ffn_pull = jax.vjp(rms_norm, residual, gain_ffn)
    grad_out = cotangent[0]
    ffn_pair, cotangent_pair, normed_half, attended_half = share(
        [normed_ffn.astype(BF16), grad_out], [normed_low, attended_low], 7
    )
    gate_proj = matmul(ffn_pair, gate_all)
    up_proj = matmul(ffn_pair, up_all)
    hidden, gating_pull = jax.vjp(
        lambda gate_in, up_in: jax.nn.silu(gate_in) * up_in, gate_proj, up_proj
    )
    hidden_low = hidden.astype(BF16)
    out_partial = matmul(hidden_low, down_all).reshape(2, TOKENS, D)
    grad_hidden = matmul(cotangent_pair, down_all.T)
    grad_gate, grad_up = gating_pull(grad_hidden)
    gate_low = grad_gate.astype(BF16)
    up_low = grad_up.astype(BF16)
    ffn_partial = (matmul(gate_low, gate_all.T) + matmul(up_low, up_all.T)).reshape(2, TOKENS, D)
    out_rest, ffn_rest = hand_over([out_partial, ffn_partial], 8)

    def mine(pair):
        return lax.dynamic_index_in_dim(pair, core, 0, keepdims=False)

    outputs = residual + mine(out_partial) + out_rest
    grad_resid_ffn, grad_gain_ffn = norm_ffn_pull(mine(ffn_partial) + ffn_rest)
    grad_resid = grad_out.astype(F32) + grad_resid_ffn
    branch_low = grad_resid.astype(BF16)
    grad_attended = matmul(branch_low, out_all.T).astype(BF16)
    (grad_part,) = to_heads(grad_attended)
    query_grad, key_value_grad = attend_back(
        block_order,
        starts,
        place,
        query_part,
        key_value_part,
        grad_part.reshape(16, 64, 128),
        exact,
        sums,
    )
    query_grad, key_value_grad = to_tokens(
        query_grad.reshape(QUARTER, TOKENS, 128), key_value_grad.reshape(RING, TOKENS, 128)
    )
    key_value_grad = key_value_grad.reshape(4, KEY_VALUE_HEADS, TOKENS, 128)
    key_value_grad = jnp.transpose(jnp.sum(key_value_grad.astype(F32), axis=0), (1, 0, 2))
    grad_front, grad_gain_query, grad_gain_key = qk_pull(
        (
            query_grad.astype(F32).reshape(TOKENS, QUERY_HEADS, HEAD_SIZE),
            key_value_grad[..., :HEAD_SIZE],
        )
    )
    grad_values = key_value_grad[..., HEAD_SIZE:].reshape(TOKENS, KEY_VALUE_HEADS * HEAD_SIZE)
    grad_projected = jnp.concatenate([grad_front, grad_values], axis=1).astype(BF16)
    grad_normed = matmul(grad_projected, qkv_all.T)
    grad_input_norm, grad_gain_attn = norm_in_pull(grad_normed)
    grad_inputs = (grad_resid + grad_input_norm).astype(BF16)

    projected_pair, branch_pair = share([grad_projected, branch_low], [], 9)
    gains = jnp.concatenate([grad_gain_attn, grad_gain_ffn, grad_gain_query, grad_gain_key])
    gains = jnp.pad(gains, (0, 24 * 128 - gains.shape[0])).reshape(24, 128)
    grad_qkv, grad_out_weight, grad_gate_weight, grad_up_weight, grad_down, gains = reduce_weights(
        outer_sum(ffn_pair, gate_low),
        outer_sum(ffn_pair, up_low),
        outer_sum(hidden_low, cotangent_pair),
        outer_sum(normed_half, projected_pair),
        outer_sum(attended_half, branch_pair),
        gains,
    )
    gains = gains.reshape(-1)
    return (
        outputs.astype(BF16)[None],
        grad_inputs[None],
        grad_qkv.astype(F32),
        grad_out_weight.astype(F32),
        grad_gate_weight.astype(F32),
        grad_up_weight.astype(F32),
        grad_down.astype(F32),
        gains[:D],
        gains[2 * D : 2 * D + HEAD_SIZE],
        gains[2 * D + HEAD_SIZE : 2 * D + 2 * HEAD_SIZE],
        gains[D : 2 * D],
    )


def solution(mesh):
    in_specs = (
        P("fsdp", "ctx", None),
        P("fsdp", "ctx", None),
        P("fsdp", None),
        P("fsdp", None),
        P("fsdp", None),
        P("fsdp", None),
        P("fsdp", None),
        P(),
        P(),
        P(),
        P(),
        P(),
        P("fsdp", None),
    )
    out_specs = (
        P("fsdp", "ctx", None),
        P("fsdp", "ctx", None),
        P("fsdp", None),
        P("fsdp", None),
        P("fsdp", None),
        P("fsdp", None),
        P("fsdp", None),
        P(),
        P(),
        P(),
        P(),
    )
    return jax.shard_map(
        per_device, mesh=mesh, in_specs=in_specs, out_specs=out_specs, check_vma=False
    )
```

```python
import functools
import math

import jax
import jax.numpy as jnp
from jax import lax
from jax.experimental import pallas as pl
from jax.experimental.pallas import tpu as pltpu
from jax.sharding import PartitionSpec as P

QUERY_HEADS = 16
KEY_VALUE_HEADS = 8
HEAD_SIZE = 64
FF = 4608
D = 1024
TOKENS = 128
RING = 32
QUARTER = 8
SLICE = 1152
HALF_FF = FF // 2
KEY_TILE = 512
SEQ = 4096

EPSILON = 1e-05
ROPE_BASE = 1000000.0
SCORE_TO_EXP2 = float(HEAD_SIZE) ** (-0.5) * math.log2(math.e)

MESH = pl.DeviceIdType.MESH
ANY = pl.BlockSpec(memory_space=pl.ANY)
VMEM = pl.BlockSpec(memory_space=pltpu.VMEM)
SMEM = pl.BlockSpec(memory_space=pltpu.SMEM)
BF16 = jnp.bfloat16
F32 = jnp.float32
MIB = 1 << 20


class Place:
    def __init__(self):
        self.ctx, self.fsdp = (lax.axis_index("ctx"), lax.axis_index("fsdp"))
        self.zl, self.x, self.y = (self.ctx // 16, (self.ctx // 4) % 4, self.ctx % 4)
        self.zh, self.core = (self.fsdp // 2, self.fsdp % 2)
        self.z = self.zh * 2 + self.zl

    def device(self, x=None, y=None, z=None, core=None):
        x = self.x if x is None else x
        y = self.y if y is None else y
        z = self.z if z is None else z
        core = self.core if core is None else core
        return ((z % 2) * 16 + x * 4 + y, (z // 2) * 2 + core)

    def sibling(self):
        return self.device(core=1 - self.core)

    def along(self, axis, step):
        coordinate = (getattr(self, axis) + step) % 4
        return coordinate, self.device(**{axis: coordinate})


class Wires:
    def __init__(self, sends, receives, locals_=None):
        self.sends, self.receives, self.locals_ = (sends, receives, locals_)
        self.pushed, self.moved = ([], 0)

    def push(self, source, target, device):
        at = len(self.pushed)
        copy = pltpu.make_async_remote_copy(
            src_ref=source,
            dst_ref=target,
            send_sem=self.sends.at[at],
            recv_sem=self.receives.at[at],
            device_id=device,
            device_id_type=MESH,
        )
        copy.start()
        self.pushed.append(copy)
        return copy

    def move(self, source, target):
        copy = pltpu.make_async_copy(source, target, self.locals_.at[self.moved])
        copy.start()
        self.moved += 1
        return copy

    def finish_sends(self):
        for copy in self.pushed:
            copy.wait_send()


def arrive(copies):
    for copy in copies:
        copy.wait_recv()


def greet(devices):
    barrier = pltpu.get_barrier_semaphore()
    for device in devices:
        pl.semaphore_signal(barrier, inc=1, device_id=device, device_id_type=MESH)
    pl.semaphore_wait(barrier, len(devices))


def wired_call(kernel, outs, ins, collective_id, name, copies, moves, scratch=(), in_specs=None,
               out_specs=None, vmem=32 * MIB):
    return pl.pallas_call(
        kernel,
        out_shape=outs,
        in_specs=[ANY] * len(ins) if in_specs is None else in_specs,
        out_specs=[ANY] * len(outs) if out_specs is None else out_specs,
        scratch_shapes=[
            *scratch,
            pltpu.SemaphoreType.DMA((copies,)),
            pltpu.SemaphoreType.DMA((copies,)),
            pltpu.SemaphoreType.DMA((max(moves, 1),)),
        ],
        compiler_params=pltpu.CompilerParams(
            collective_id=collective_id, has_side_effects=True, vmem_limit_bytes=vmem
        ),
        name=name,
    )(*ins)


def shape(*dims, dtype=BF16):
    return jax.ShapeDtypeStruct(dims, dtype)


def gather_weights_kernel(
    qkv, out, gate, up, down, qkv_all, out_all, gate_all, up_all, down_all, sends, receives, moves
):
    here = Place()
    wires = Wires(sends, receives, moves)
    zh, core, x, y = (here.zh, here.core, here.x, here.y)
    other = 1 - zh
    steps = (1, 3, 2)
    xs = [here.along("x", s)[1] for s in steps]
    ys = [here.along("y", s)[1] for s in steps]
    across = 3 - here.z
    cross = [here.device(z=across, core=(core + t) % 2) for t in range(2)]
    sibling = here.sibling()
    greet(xs + ys + cross + [sibling])

    def ff_columns(r, c):
        return pl.ds(pl.multiple_of(r * HALF_FF + c * SLICE, 128), SLICE)

    def down_columns():
        return pl.ds(pl.multiple_of(y * 256, 256), 256)

    crossed = {}
    crossed["qkv"] = [wires.push(qkv.at[x, y], qkv_all.at[zh, core, x, y], cross[0])]
    crossed["out"] = [wires.push(out.at[x, y], out_all.at[zh, core, x, y], cross[0])]
    for name, shard, whole in (("gate", gate, gate_all), ("up", up, up_all)):
        crossed[name] = [
            wires.push(
                shard.at[x, y, :, ff_columns(r, (core + t) % 2)],
                whole.at[zh, core, x, y, :, pl.ds(r * SLICE, SLICE)],
                cross[t],
            )
            for t in range(2)
            for r in range(2)
        ]
    crossed["down"] = [
        wires.push(
            down.at[x, :, :, down_columns()], down_all.at[zh, x, :, :, down_columns()], cross[0]
        )
    ]
    beside = [
        wires.push(qkv, qkv_all.at[zh, core], sibling),
        wires.push(out, out_all.at[zh, core], sibling),
    ]
    kept = [wires.move(qkv, qkv_all.at[zh, core]), wires.move(out, out_all.at[zh, core])]
    for shard, whole in ((gate, gate_all), (up, up_all)):
        for r in range(2):
            target = whole.at[zh, core, :, :, :, pl.ds(r * SLICE, SLICE)]
            beside.append(wires.push(shard.at[:, :, :, ff_columns(r, 1 - core)], target, sibling))
            kept.append(wires.move(shard.at[:, :, :, ff_columns(r, core)], target))
    kept.append(wires.move(down, down_all.at[zh]))

    def own_piece(name, half):
        if name == "down":
            return down_all.at[other, x, half, :, down_columns()]
        if name in ("gate", "up"):
            whole = gate_all if name == "gate" else up_all
            return whole.at[other, :, x, y, :, pl.ds(half * SLICE, SLICE)]
        whole, width = (qkv_all, 1024) if name == "qkv" else (out_all, 512)
        return whole.at[other, core, x, y, :, pl.ds(half * width, width)]

    def line(name, half):
        if name == "down":
            if half == 0:
                return down_all.at[other, :, 0, :, down_columns()]
            return down_all.at[other, x, 1]
        if name in ("gate", "up"):
            whole = gate_all if name == "gate" else up_all
            if half == 0:
                return whole.at[other, :, :, y, :, pl.ds(0, SLICE)]
            return whole.at[other, :, x, :, :, pl.ds(SLICE, SLICE)]
        whole, width = (qkv_all, 1024) if name == "qkv" else (out_all, 512)
        if half == 0:
            return whole.at[other, core, :, y, :, pl.ds(0, width)]
        return whole.at[other, core, x, :, :, pl.ds(width, width)]

    names = ("qkv", "out", "gate", "up", "down")
    first, second = ({}, {})
    for name in names:
        arrive(crossed[name])
        first[name] = [
            wires.push(own_piece(name, half), own_piece(name, half), device)
            for half, ring in ((0, xs), (1, ys))
            for device in ring
        ]
    for name in names:
        arrive(first[name])
        second[name] = [
            wires.push(line(name, half), line(name, half), device)
            for half, ring in ((0, ys), (1, xs))
            for device in ring
        ]
    for name, whole in (("qkv", qkv_all), ("out", out_all)):
        arrive(second[name])
        beside.append(wires.push(whole.at[other, core], whole.at[other, core], sibling))
    for name in names[2:]:
        arrive(second[name])
    arrive(beside)
    for copy in kept:
        copy.wait()
    wires.finish_sends()


def gather_weights(qkv, out, gate, up, down):
    rows = (4, 4, 16)
    ins = (
        qkv.reshape(*rows, 2048),
        out.reshape(*rows, D),
        gate.reshape(*rows, FF),
        up.reshape(*rows, FF),
        down.reshape(4, 2, 144, D),
    )
    outs = [
        shape(2, 2, *rows, 2048),
        shape(2, 2, *rows, D),
        shape(2, 2, *rows, HALF_FF),
        shape(2, 2, *rows, HALF_FF),
        shape(2, 4, 2, 144, D),
    ]
    copies = 3 + 8 + 6 + 30 + 30 + 2
    qkv, out, gate, up, down = wired_call(
        gather_weights_kernel, outs, ins, 1, "gather_weights", copies, 7
    )
    return (
        qkv.reshape(D, 2048),
        out.reshape(D, D),
        gate.reshape(D, HALF_FF),
        up.reshape(D, HALF_FF),
        down.reshape(HALF_FF, D),
    )


class RowsByShard:
    lead = (2, 2, 4, 4)

    def __init__(self, columns):
        self.columns = columns

    def order(self, at):
        return [at.get("zh"), at.get("zl"), at.get("x"), at.get("y")]

    def tail(self, at):
        return (slice(None), slice(None))

    def tail_dims(self, at):
        return (16, self.columns)


class RowsByPlane:
    lead = (2, 4, 4)

    def __init__(self, first, columns):
        self.first, self.columns = (first, columns)

    def order(self, at):
        return [at.get("zh"), at.get("x"), at.get("y")]

    def tail(self, at):
        if "zl" not in at:
            return (slice(None), pl.ds(self.first, self.columns))
        half = self.columns // 2
        return (slice(None), pl.ds(pl.multiple_of(self.first + half * at["zl"], 128), half))

    def tail_dims(self, at):
        return (16, self.columns // 2 if "zl" in at else self.columns)


class ColumnsByY:
    lead = (2, 4, 2)

    def __init__(self, rows):
        self.rows = rows

    def order(self, at):
        return [at.get("zh"), at.get("x"), at.get("zl")]

    def tail(self, at):
        if "y" not in at:
            return (slice(None), slice(None))
        return (slice(None), pl.ds(pl.multiple_of(at["y"] * 256, 256), 256))

    def tail_dims(self, at):
        return (self.rows, 256 if "y" in at else D)


def view(kind, ref, at, skip=0):
    lead = [slice(None) if i is None else i for i in kind.order(at)[skip:]]
    return ref.at[(*lead, *kind.tail(at))]


def open_dims(kind, at):
    return tuple(n for n, i in zip(kind.lead, kind.order(at)) if i is None)


def fix(at, axis, coordinate):
    if axis == "z":
        return {**at, "zh": coordinate // 2, "zl": coordinate % 2}
    return {**at, axis: coordinate}


PARTS = (
    (0, RowsByShard(HALF_FF), ("z", "x", "y")),
    (1, RowsByShard(HALF_FF), ("x", "y", "z")),
    (2, ColumnsByY(144), ("y", "z", "x")),
    (3, RowsByPlane(0, 1024), ("z", "x", "y")),
    (3, RowsByPlane(1024, 1024), ("x", "y", "z")),
    (4, ColumnsByY(32), ("y", "z", "x")),
)
STEPS = (1, 3, 2)


def slot_shapes():
    found = []
    for _, kind, order in PARTS:
        at = {}
        for axis in order:
            at = fix(at, axis, 0)
            found.append((3, *open_dims(kind, at), *kind.tail_dims(at)))
    return found


def add_up(kind, total, slots, at):
    dims = open_dims(kind, at)
    order = kind.order(at)
    tail = kind.tail(at)

    def body(i, _):
        inner, rest = ([], i)
        for n in reversed(dims):
            inner.insert(0, rest % n)
            rest = rest // n
        picks = iter(inner)
        where = (*[next(picks) if o is None else o for o in order], *tail)
        value = total[where].astype(F32)
        for j in range(3):
            value += slots[(j, *inner, slice(None), slice(None))].astype(F32)
        total[where] = value.astype(BF16)
        return 0

    lax.fori_loop(0, math.prod(dims), body, 0)


def reduce_weights_kernel(*refs):
    grads, gains = (refs[:5], refs[5])
    gate_near, up_near, gate_beside, up_beside, down_out, qkv_out, out_out, gains_out = refs[6:14]
    totals = refs[14:19]
    slots = refs[19:37]
    gain_slots, sends, receives, moves = refs[37:]
    nears = (gate_near, up_near, down_out, qkv_out, out_out)

    here = Place()
    wires = Wires(sends, receives, moves)
    core = here.core
    sibling = here.sibling()
    ring = {a: [here.along(a, s) for s in STEPS] for a in ("x", "y", "z")}
    greet([device for a in ("x", "y", "z") for _, device in ring[a]] + [sibling])

    gain_slots[0, core] = gains[...]
    gain_copies = [wires.push(gain_slots.at[0, core], gain_slots.at[0, core], sibling)]

    def next_gains(stage):
        arrive(gain_copies)
        total = gain_slots[stage, 0] + gain_slots[stage, 1]
        if stage > 0:
            total = total + gain_slots[stage, 2] + gain_slots[stage, 3]
        if stage == 3:
            gains_out[...] = total
            return
        axis = ("x", "y", "z")[stage]
        me = getattr(here, axis)
        gain_slots[stage + 1, me] = total
        source = gain_slots.at[stage + 1, me]
        gain_copies[:] = [wires.push(source, source, device) for _, device in ring[axis]]

    fixed = [{} for _ in PARTS]
    flying = [None] * len(PARTS)
    own = [None] * len(PARTS)
    for step in range(3):
        for p, (g, kind, order) in enumerate(PARTS):
            if step > 0:
                if own[p] is not None:
                    own[p].wait()
                    own[p] = None
                arrive(flying[p])
                add_up(kind, totals[g], slots[3 * p + step - 1], fixed[p])
            axis = order[step]
            source = grads[g] if step == 0 else totals[g]
            flying[p] = [
                wires.push(
                    view(kind, source, fix(fixed[p], axis, coordinate)),
                    slots[3 * p + step].at[j],
                    device,
                )
                for j, (coordinate, device) in enumerate(ring[axis])
            ]
            fixed[p] = fix(fixed[p], axis, getattr(here, axis))
            if step == 0:
                own[p] = wires.move(
                    view(kind, source, fixed[p]), view(kind, totals[g], fixed[p])
                )
        next_gains(step)
    next_gains(3)

    for p, (g, kind, order) in enumerate(PARTS):
        arrive(flying[p])
        add_up(kind, totals[g], slots[3 * p + 2], fixed[p])
        own[p] = wires.move(view(kind, totals[g], fixed[p]), view(kind, nears[g], fixed[p], 1))
    for step in (2, 1, 0):
        for p, (g, kind, order) in enumerate(PARTS):
            if step == 2:
                own[p].wait()
            else:
                arrive(flying[p])
            axis = order[step]
            piece = view(kind, nears[g], fixed[p], 1)
            if axis == "z":
                devices = [here.device(z=here.zh * 2 + 1 - here.zl)]
                gone = ("zl",)
            else:
                devices = [device for _, device in ring[axis]]
                gone = (axis,)
            flying[p] = [wires.push(piece, piece, device) for device in devices]
            fixed[p] = {a: i for a, i in fixed[p].items() if a not in gone}
    last = []
    for p, (near, beside) in enumerate(((gate_near, gate_beside), (up_near, up_beside))):
        arrive(flying[p])
        last.append(wires.push(near.at[1 - core], beside, sibling))
    for p in range(2, len(PARTS)):
        arrive(flying[p])
    arrive(last)
    wires.finish_sends()


def reduce_weights(gate, up, down, qkv, out, gains):
    dims = (
        (2, 2, 4, 4, 16, HALF_FF),
        (2, 2, 4, 4, 16, HALF_FF),
        (2, 4, 2, 144, D),
        (2, 4, 4, 16, 2048),
        (2, 4, 2, 32, D),
    )
    ins = [a.reshape(d) for a, d in zip((gate, up, down, qkv, out), dims)] + [gains]
    outs = [
        shape(*dims[0][1:]),
        shape(*dims[1][1:]),
        shape(*dims[0][2:]),
        shape(*dims[1][2:]),
        shape(*dims[2][1:]),
        shape(*dims[3][1:]),
        shape(*dims[4][1:]),
        shape(*gains.shape, dtype=F32),
    ]
    scratch = [pltpu.VMEM(d, BF16) for d in dims]
    scratch += [pltpu.VMEM(s, BF16) for s in slot_shapes()]
    scratch += [pltpu.VMEM((4, 4, *gains.shape), F32)]
    copies = 1 + 9 + 6 * 9 + 6 * 7 + 2
    done = wired_call(
        reduce_weights_kernel,
        outs,
        ins,
        2,
        "reduce_weights",
        copies,
        12,
        scratch,
        [ANY] * 5 + [VMEM],
        [ANY] * 7 + [VMEM],
        vmem=56 * MIB,
    )
    core = lax.axis_index("fsdp") % 2

    def joined(near, beside):
        own = lax.dynamic_index_in_dim(near, core, 0, keepdims=False).reshape(256, HALF_FF)
        beside = beside.reshape(256, HALF_FF)
        first, second = (jnp.where(core == 0, own, beside), jnp.where(core == 0, beside, own))
        pieces = [f[:, r * SLICE : (r + 1) * SLICE] for r in range(2) for f in (first, second)]
        return jnp.concatenate(pieces, axis=1)

    gate, up = (joined(done[0], done[2]), joined(done[1], done[3]))
    down, qkv, out, gains = done[4:]
    return (
        qkv.reshape(256, 2048),
        out.reshape(256, D),
        gate,
        up,
        down.reshape(SLICE, D),
        gains,
    )


def head_columns(head):
    return pl.ds(pl.multiple_of(head * 128, 128), 128)


def to_heads_kernel(with_keys, *refs):
    if with_keys:
        query, key_value, query_out, key_value_out, sends, receives, moves = refs
    else:
        query, query_out, sends, receives, moves = refs
    here = Place()
    wires = Wires(sends, receives, moves)
    me = here.ctx
    quarter, seat = (me // QUARTER, me % QUARTER)
    near = [quarter * QUARTER + (seat + s) % QUARTER for s in range(1, QUARTER)]
    far = [(me + s) % RING for s in range(1, RING)]
    greet([(k, here.fsdp) for k in (far if with_keys else near)])
    copies = [
        wires.push(query.at[:, head_columns(k % QUARTER)], query_out.at[seat], (k, here.fsdp))
        for k in near
    ]
    kept = [wires.move(query.at[:, head_columns(seat)], query_out.at[seat])]
    if with_keys:
        copies += [
            wires.push(
                key_value.at[:, head_columns(k % QUARTER)], key_value_out.at[me], (k, here.fsdp)
            )
            for k in far
        ]
        kept.append(wires.move(key_value.at[:, head_columns(seat)], key_value_out.at[me]))
    arrive(copies)
    for copy in kept:
        copy.wait()
    wires.finish_sends()


def to_heads(query, key_value=None):
    ins = [query] + ([] if key_value is None else [key_value])
    outs = [shape(QUARTER, TOKENS, 128)]
    if key_value is not None:
        outs.append(shape(RING, TOKENS, 128))
    copies = 7 if key_value is None else 38
    return wired_call(
        functools.partial(to_heads_kernel, key_value is not None),
        outs,
        ins,
        3 if key_value is None else 4,
        "to_heads",
        copies,
        2,
    )


def to_tokens_kernel(with_keys, *refs):
    if with_keys:
        query, key_value, query_out, key_value_out, sends, receives, moves = refs
    else:
        query, query_out, sends, receives, moves = refs
    here = Place()
    wires = Wires(sends, receives, moves)
    me = here.ctx
    quarter, seat = (me // QUARTER, me % QUARTER)
    near = [quarter * QUARTER + (seat + s) % QUARTER for s in range(1, QUARTER)]
    far = [(me + s) % RING for s in range(1, RING)]
    greet([(k, here.fsdp) for k in (far if with_keys else near)])
    columns = query_out.at[:, head_columns(seat)]
    copies = [wires.push(query.at[k % QUARTER], columns, (k, here.fsdp)) for k in near]
    kept = [wires.move(query.at[seat], columns)]
    if with_keys:
        copies += [
            wires.push(key_value.at[k], key_value_out.at[me], (k, here.fsdp)) for k in far
        ]
        kept.append(wires.move(key_value.at[me], key_value_out.at[me]))
    arrive(copies)
    for copy in kept:
        copy.wait()
    wires.finish_sends()


def to_tokens(query, key_value=None):
    ins = [query] + ([] if key_value is None else [key_value])
    outs = [shape(TOKENS, D)]
    if key_value is not None:
        outs.append(shape(RING, TOKENS, 128))
    copies = 7 if key_value is None else 38
    return wired_call(
        functools.partial(to_tokens_kernel, key_value is not None),
        outs,
        ins,
        5 if key_value is None else 6,
        "to_tokens",
        copies,
        2,
    )


def half_columns(r, core):
    return pl.ds(pl.multiple_of(r * 512 + core * 256, 256), 256)


def share_kernel(whole, halved, *refs):
    n = whole + halved
    ins, outs = (refs[:n], refs[n : 2 * n])
    here = Place()
    wires = Wires(*refs[2 * n :])
    core = here.core
    sibling = here.sibling()
    greet([sibling])
    copies, kept = ([], [])
    for source, target in zip(ins[:whole], outs[:whole]):
        copies.append(wires.push(source, target.at[core], sibling))
        kept.append(wires.move(source, target.at[core]))
    for source, target in zip(ins[whole:], outs[whole:]):
        for r in range(2):
            place = target.at[core, :, pl.ds(r * 256, 256)]
            copies.append(wires.push(source.at[:, half_columns(r, 1 - core)], place, sibling))
            kept.append(wires.move(source.at[:, half_columns(r, core)], place))
    arrive(copies)
    for copy in kept:
        copy.wait()
    wires.finish_sends()


def share(whole, halved, collective_id):
    outs = [shape(2, *a.shape, dtype=a.dtype) for a in whole]
    outs += [shape(2, a.shape[0], 512, dtype=a.dtype) for a in halved]
    count = len(whole) + 2 * len(halved)
    done = wired_call(
        functools.partial(share_kernel, len(whole), len(halved)),
        outs,
        [*whole, *halved],
        collective_id,
        "share",
        count,
        count,
    )
    return [a.reshape(2 * a.shape[1], a.shape[2]) for a in done]


def hand_over_kernel(count, *refs):
    ins, outs = (refs[:count], refs[count : 2 * count])
    here = Place()
    wires = Wires(*refs[2 * count :])
    sibling = here.sibling()
    greet([sibling])
    copies = [wires.push(i.at[1 - here.core], o, sibling) for i, o in zip(ins, outs)]
    arrive(copies)
    wires.finish_sends()


def hand_over(partials, collective_id):
    return wired_call(
        functools.partial(hand_over_kernel, len(partials)),
        [shape(*a.shape[1:], dtype=a.dtype) for a in partials],
        partials,
        collective_id,
        "hand_over",
        len(partials),
        0,
    )


def nt(left, right):
    return lax.dot_general(left, right, (((1,), (1,)), ((), ())), preferred_element_type=F32)


def nn(left, right):
    return lax.dot_general(left, right, (((1,), (0,)), ((), ())), preferred_element_type=F32)


def by_position(order_ref, key_value_ref, sorted_ref):
    def body(j, _):
        sorted_ref[pl.ds(pl.multiple_of(order_ref[j] * 64, 64), 64), :] = key_value_ref[j]
        return 0

    lax.fori_loop(0, 64, body, 0)


def query_block(ref, t):
    block = ref[t].astype(F32)
    both = jnp.concatenate([block, pltpu.roll(block, 64, 1)], axis=0)
    low = lax.broadcasted_iota(jnp.int32, (128, 128), 1) < 64
    return jnp.where(low, both, 0.0)


def key_limits(order_ref, starts_ref, place_ref, t):
    first = order_ref[place_ref[0] * 16 + t] * 64
    begin = jnp.int32(0)
    for n in range(4):
        begin = jnp.maximum(begin, jnp.where(starts_ref[n] <= first, starts_ref[n], 0))
    return first, begin // KEY_TILE, (first + 63) // KEY_TILE + 1


def first_allowed(position, starts_ref):
    begin = jnp.zeros_like(position)
    for n in range(4):
        begin = jnp.maximum(begin, jnp.where(starts_ref[n] <= position, starts_ref[n], 0))
    return begin


def attend_kernel(
    order_ref, starts_ref, place_ref, query_ref, key_value_ref, out_ref, exact_ref, sum_ref,
    sorted_ref, value_ref,
):
    by_position(order_ref, key_value_ref, sorted_ref)

    def values(j, _):
        rows = pl.ds(pl.multiple_of(j * 256, 256), 256)
        block = pltpu.roll(sorted_ref[rows, :].astype(F32), 64, 1)
        low = lax.broadcasted_iota(jnp.int32, (256, 128), 1) < 64
        value_ref[rows, :] = jnp.where(low, block, 1.0).astype(BF16)
        return 0

    lax.fori_loop(0, SEQ // 256, values, 0)

    def block(t, _):
        first, begin_tile, end_tile = key_limits(order_ref, starts_ref, place_ref, t)
        queries = query_block(query_ref, t).astype(BF16)
        position = first + lax.broadcasted_iota(jnp.int32, (128, 1), 0) % 64
        begin = first_allowed(position, starts_ref)

        def tile(j, total):
            rows = pl.ds(pl.multiple_of(j * KEY_TILE, KEY_TILE), KEY_TILE)
            scores = nt(queries, sorted_ref[rows, :])
            key = j * KEY_TILE + lax.broadcasted_iota(jnp.int32, (128, KEY_TILE), 1)
            allowed = (key <= position) & (key >= begin)
            weight = jnp.where(allowed, jnp.exp2(scores * SCORE_TO_EXP2), 0.0)
            return total + nn(weight.astype(BF16), value_ref[rows, :])

        total = lax.fori_loop(begin_tile, end_tile, tile, jnp.zeros((128, 128), F32))
        sums = pltpu.roll(total, 64, 1)
        attended = total / sums
        low_pair = lax.broadcasted_iota(jnp.int32, (128, 128), 1) < 64
        low = lax.broadcasted_iota(jnp.int32, (64, 128), 1) < 64
        exact_ref[t] = jnp.where(low_pair, attended, 0.0)
        out_ref[t] = jnp.where(low, attended[:64], pltpu.roll(attended[64:], 64, 1)).astype(BF16)
        sum_ref[t] = jnp.transpose(total)[64:72]
        return 0

    lax.fori_loop(0, 16, block, 0)


def attend(order, starts, place, queries, key_values):
    return pl.pallas_call(
        attend_kernel,
        out_shape=[shape(16, 64, 128), shape(16, 128, 128, dtype=F32), shape(16, 8, 128, dtype=F32)],
        in_specs=[SMEM, SMEM, SMEM, VMEM, VMEM],
        out_specs=[VMEM] * 3,
        scratch_shapes=[pltpu.VMEM((SEQ, 128), BF16), pltpu.VMEM((SEQ, 128), BF16)],
        compiler_params=pltpu.CompilerParams(vmem_limit_bytes=32 * MIB),
        name="attend",
    )(order, starts, place, queries, key_values)


def attend_back_kernel(
    order_ref, starts_ref, place_ref, query_ref, key_value_ref, grad_ref, exact_ref, sum_ref,
    query_grad_ref, key_value_grad_ref, sorted_ref, across_ref, total_ref,
):
    by_position(order_ref, key_value_ref, sorted_ref)
    total_ref[...] = jnp.zeros_like(total_ref)

    def turn(j, _):
        rows = pl.ds(pl.multiple_of(j * 128, 128), 128)
        across_ref[:, rows] = jnp.transpose(sorted_ref[rows, :].astype(F32)).astype(BF16)
        return 0

    lax.fori_loop(0, SEQ // 128, turn, 0)

    def block(t, _):
        first, begin_tile, end_tile = key_limits(order_ref, starts_ref, place_ref, t)
        queries = query_block(query_ref, t)
        grads = query_block(grad_ref, t)
        delta = jnp.sum(jnp.transpose(grads * exact_ref[t]), axis=0, keepdims=True)
        total_exp2 = jnp.log2(sum_ref[t][0:1])
        both = jnp.concatenate([queries, pltpu.roll(grads, 64, 1)], axis=0).astype(BF16)
        position = first + lax.broadcasted_iota(jnp.int32, (1, 128), 1) % 64
        begin = first_allowed(position, starts_ref)

        def tile(j, query_grad):
            rows = pl.ds(pl.multiple_of(j * KEY_TILE, KEY_TILE), KEY_TILE)
            products = nt(sorted_ref[rows, :], both)
            key = j * KEY_TILE + lax.broadcasted_iota(jnp.int32, (KEY_TILE, 128), 0)
            allowed = (key <= position) & (key >= begin)
            prob = jnp.where(
                allowed, jnp.exp2(products[:, :128] * SCORE_TO_EXP2 - total_exp2), 0.0
            )
            score = (prob * (products[:, 128:] - delta)).astype(BF16)
            pair = jnp.concatenate([score, prob.astype(BF16)], axis=1)
            total_ref[rows, :] += nn(pair, both)
            return query_grad + nn(across_ref[:, rows], score)

        query_grad = lax.fori_loop(begin_tile, end_tile, tile, jnp.zeros((128, 128), F32))
        query_grad = jnp.transpose(query_grad) * float(HEAD_SIZE) ** (-0.5)
        low = lax.broadcasted_iota(jnp.int32, (64, 128), 1) < 64
        query_grad_ref[t] = jnp.where(
            low, query_grad[:64], pltpu.roll(query_grad[64:], 64, 1)
        ).astype(BF16)
        return 0

    lax.fori_loop(0, 16, block, 0)

    def put_back(j, _):
        rows = pl.ds(pl.multiple_of(order_ref[j] * 64, 64), 64)
        low = lax.broadcasted_iota(jnp.int32, (64, 128), 1) < 64
        scale = jnp.where(low, float(HEAD_SIZE) ** (-0.5), 1.0)
        key_value_grad_ref[j] = (total_ref[rows, :] * scale).astype(BF16)
        return 0

    lax.fori_loop(0, 64, put_back, 0)


def attend_back(order, starts, place, queries, key_values, grads, exact, sums):
    return pl.pallas_call(
        attend_back_kernel,
        out_shape=[shape(16, 64, 128), shape(64, 64, 128)],
        in_specs=[SMEM] * 3 + [VMEM] * 5,
        out_specs=[VMEM] * 2,
        scratch_shapes=[
            pltpu.VMEM((SEQ, 128), BF16),
            pltpu.VMEM((128, SEQ), BF16),
            pltpu.VMEM((SEQ, 128), F32),
        ],
        compiler_params=pltpu.CompilerParams(vmem_limit_bytes=40 * MIB),
        name="attend_back",
    )(order, starts, place, queries, key_values, grads, exact, sums)


def rms_norm(values, gain_row):
    return (
        values * lax.rsqrt(jnp.mean(values * values, axis=-1, keepdims=True) + EPSILON) * gain_row
    )


def rotate(values, positions):
    half_width = values.shape[-1] // 2
    frequency = ROPE_BASE ** (-2.0 * jnp.arange(half_width, dtype=F32) / values.shape[-1])
    angles = positions.astype(F32)[:, None] * frequency[None, :]
    cosine = jnp.cos(angles)[:, None, :]
    sine_part = jnp.sin(angles)[:, None, :]
    first_half = values[..., :half_width]
    second_half = values[..., half_width:]
    return jnp.concatenate(
        [
            first_half * cosine - second_half * sine_part,
            second_half * cosine + first_half * sine_part,
        ],
        axis=-1,
    )


def outer_sum(left, right):
    return lax.dot_general(
        left, right, (((0,), (0,)), ((), ())), preferred_element_type=F32
    ).astype(BF16)


def matmul(left, right):
    return jnp.dot(left, right, preferred_element_type=F32)


def positions_at(block_order, first_row, total_row_count, half_rows):
    row_ids = first_row + jnp.arange(total_row_count, dtype=jnp.int32)
    blocks = row_ids // half_rows
    lookup = jnp.arange(block_order.shape[0], dtype=jnp.int32)
    picked = jnp.sum(jnp.where(blocks[:, None] == lookup[None, :], block_order[None, :], 0), axis=1)
    return picked * half_rows + row_ids % half_rows


def per_device(
    inputs,
    cotangent,
    qkv_weight,
    out_weight,
    gate_weight,
    up_weight,
    down_weight,
    gain_attn,
    gain_query,
    gain_key,
    gain_ffn,
    block_order,
    doc_starts,
):
    cycle_index = lax.axis_index("ctx")
    core = lax.axis_index("fsdp") % 2
    qkv_all, out_all, gate_all, up_all, down_all = gather_weights(
        qkv_weight, out_weight, gate_weight, up_weight, down_weight
    )
    starts = doc_starts[0]
    place = (cycle_index // QUARTER).astype(jnp.int32).reshape(1)
    positions = positions_at(block_order, cycle_index * TOKENS, TOKENS, TOKENS // 2)

    resid_in = inputs[0].astype(F32)
    normed, norm_in_pull = jax.vjp(rms_norm, resid_in, gain_attn)
    normed_low = normed.astype(BF16)
    projected = matmul(normed_low, qkv_all)
    split_position = (QUERY_HEADS + KEY_VALUE_HEADS) * HEAD_SIZE

    def query_key(leading_columns, scale_query, scale_key):
        queries = leading_columns[:, : QUERY_HEADS * HEAD_SIZE].reshape(
            TOKENS, QUERY_HEADS, HEAD_SIZE
        )
        keys = leading_columns[:, QUERY_HEADS * HEAD_SIZE :].reshape(
            TOKENS, KEY_VALUE_HEADS, HEAD_SIZE
        )
        return (
            rotate(rms_norm(queries, scale_query), positions),
            rotate(rms_norm(keys, scale_key), positions),
        )

    (queries, keys), qk_pull = jax.vjp(
        query_key, projected[:, :split_position], gain_query, gain_key
    )
    values = projected[:, split_position:].reshape(TOKENS, KEY_VALUE_HEADS, HEAD_SIZE)
    key_values = jnp.concatenate([keys, values], axis=-1).astype(BF16).reshape(TOKENS, D)
    query_part, key_value_part = to_heads(queries.astype(BF16).reshape(TOKENS, D), key_values)
    query_part = query_part.reshape(16, 64, 128)
    key_value_part = key_value_part.reshape(64, 64, 128)
    attended, exact, sums = attend(block_order, starts, place, query_part, key_value_part)
    (attended_low,) = to_tokens(attended.reshape(QUARTER, TOKENS, 128))

    residual = resid_in + matmul(attended_low, out_all)
    normed_ffn, norm_ffn_pull = jax.vjp(rms_norm, residual, gain_ffn)
    grad_out = cotangent[0]
    ffn_pair, cotangent_pair, normed_half, attended_half = share(
        [normed_ffn.astype(BF16), grad_out], [normed_low, attended_low], 7
    )
    gate_proj = matmul(ffn_pair, gate_all)
    up_proj = matmul(ffn_pair, up_all)
    hidden, gating_pull = jax.vjp(
        lambda gate_in, up_in: jax.nn.silu(gate_in) * up_in, gate_proj, up_proj
    )
    hidden_low = hidden.astype(BF16)
    out_partial = matmul(hidden_low, down_all).reshape(2, TOKENS, D)
    grad_hidden = matmul(cotangent_pair, down_all.T)
    grad_gate, grad_up = gating_pull(grad_hidden)
    gate_low = grad_gate.astype(BF16)
    up_low = grad_up.astype(BF16)
    ffn_partial = (matmul(gate_low, gate_all.T) + matmul(up_low, up_all.T)).reshape(2, TOKENS, D)
    out_rest, ffn_rest = hand_over([out_partial, ffn_partial], 8)

    def mine(pair):
        return lax.dynamic_index_in_dim(pair, core, 0, keepdims=False)

    outputs = residual + mine(out_partial) + out_rest
    grad_resid_ffn, grad_gain_ffn = norm_ffn_pull(mine(ffn_partial) + ffn_rest)
    grad_resid = grad_out.astype(F32) + grad_resid_ffn
    branch_low = grad_resid.astype(BF16)
    grad_attended = matmul(branch_low, out_all.T).astype(BF16)
    (grad_part,) = to_heads(grad_attended)
    query_grad, key_value_grad = attend_back(
        block_order,
        starts,
        place,
        query_part,
        key_value_part,
        grad_part.reshape(16, 64, 128),
        exact,
        sums,
    )
    query_grad, key_value_grad = to_tokens(
        query_grad.reshape(QUARTER, TOKENS, 128), key_value_grad.reshape(RING, TOKENS, 128)
    )
    key_value_grad = key_value_grad.reshape(4, KEY_VALUE_HEADS, TOKENS, 128)
    key_value_grad = jnp.transpose(jnp.sum(key_value_grad.astype(F32), axis=0), (1, 0, 2))
    grad_front, grad_gain_query, grad_gain_key = qk_pull(
        (
            query_grad.astype(F32).reshape(TOKENS, QUERY_HEADS, HEAD_SIZE),
            key_value_grad[..., :HEAD_SIZE],
        )
    )
    grad_values = key_value_grad[..., HEAD_SIZE:].reshape(TOKENS, KEY_VALUE_HEADS * HEAD_SIZE)
    grad_projected = jnp.concatenate([grad_front, grad_values], axis=1).astype(BF16)
    grad_normed = matmul(grad_projected, qkv_all.T)
    grad_input_norm, grad_gain_attn = norm_in_pull(grad_normed)
    grad_inputs = (grad_resid + grad_input_norm).astype(BF16)

    projected_pair, branch_pair = share([grad_projected, branch_low], [], 9)
    gains = jnp.concatenate([grad_gain_attn, grad_gain_ffn, grad_gain_query, grad_gain_key])
    gains = jnp.pad(gains, (0, 24 * 128 - gains.shape[0])).reshape(24, 128)
    grad_qkv, grad_out_weight, grad_gate_weight, grad_up_weight, grad_down, gains = reduce_weights(
        outer_sum(ffn_pair, gate_low),
        outer_sum(ffn_pair, up_low),
        outer_sum(hidden_low, cotangent_pair),
        outer_sum(normed_half, projected_pair),
        outer_sum(attended_half, branch_pair),
        gains,
    )
    gains = gains.reshape(-1)
    return (
        outputs.astype(BF16)[None],
        grad_inputs[None],
        grad_qkv.astype(F32),
        grad_out_weight.astype(F32),
        grad_gate_weight.astype(F32),
        grad_up_weight.astype(F32),
        grad_down.astype(F32),
        gains[:D],
        gains[2 * D : 2 * D + HEAD_SIZE],
        gains[2 * D + HEAD_SIZE : 2 * D + 2 * HEAD_SIZE],
        gains[D : 2 * D],
    )


def solution(mesh):
    in_specs = (
        P("fsdp", "ctx", None),
        P("fsdp", "ctx", None),
        P("fsdp", None),
        P("fsdp", None),
        P("fsdp", None),
        P("fsdp", None),
        P("fsdp", None),
        P(),
        P(),
        P(),
        P(),
        P(),
        P("fsdp", None),
    )
    out_specs = (
        P("fsdp", "ctx", None),
        P("fsdp", "ctx", None),
        P("fsdp", None),
        P("fsdp", None),
        P("fsdp", None),
        P("fsdp", None),
        P("fsdp", None),
        P(),
        P(),
        P(),
        P(),
    )
    return jax.shard_map(
        per_device, mesh=mesh, in_specs=in_specs, out_specs=out_specs, check_vma=False
    )
```

```python
import functools
import math

import jax
import jax.numpy as jnp
from jax import lax
from jax.experimental import pallas as pl
from jax.experimental.pallas import tpu as pltpu
from jax.sharding import PartitionSpec as P

QUERY_HEADS = 16
KEY_VALUE_HEADS = 8
HEAD_SIZE = 64
FF = 4608
D = 1024
TOKENS = 128
RING = 32
QUARTER = 8
SLICE = 1152
HALF_FF = FF // 2
KEY_TILE = 512
SEQ = 4096

EPSILON = 1e-05
ROPE_BASE = 1000000.0
SCORE_TO_EXP2 = float(HEAD_SIZE) ** (-0.5) * math.log2(math.e)

MESH = pl.DeviceIdType.MESH
ANY = pl.BlockSpec(memory_space=pl.ANY)
VMEM = pl.BlockSpec(memory_space=pltpu.VMEM)
SMEM = pl.BlockSpec(memory_space=pltpu.SMEM)
BF16 = jnp.bfloat16
F32 = jnp.float32
MIB = 1 << 20


class Place:
    def __init__(self):
        self.ctx, self.fsdp = (lax.axis_index("ctx"), lax.axis_index("fsdp"))
        self.zl, self.x, self.y = (self.ctx // 16, (self.ctx // 4) % 4, self.ctx % 4)
        self.zh, self.core = (self.fsdp // 2, self.fsdp % 2)
        self.z = self.zh * 2 + self.zl

    def device(self, x=None, y=None, z=None, core=None):
        x = self.x if x is None else x
        y = self.y if y is None else y
        z = self.z if z is None else z
        core = self.core if core is None else core
        return ((z % 2) * 16 + x * 4 + y, (z // 2) * 2 + core)

    def sibling(self):
        return self.device(core=1 - self.core)

    def along(self, axis, step):
        coordinate = (getattr(self, axis) + step) % 4
        return coordinate, self.device(**{axis: coordinate})


class Wires:
    def __init__(self, sends, receives, locals_=None):
        self.sends, self.receives, self.locals_ = (sends, receives, locals_)
        self.pushed, self.moved = ([], 0)

    def push(self, source, target, device):
        at = len(self.pushed)
        copy = pltpu.make_async_remote_copy(
            src_ref=source,
            dst_ref=target,
            send_sem=self.sends.at[at],
            recv_sem=self.receives.at[at],
            device_id=device,
            device_id_type=MESH,
        )
        copy.start()
        self.pushed.append(copy)
        return copy

    def move(self, source, target):
        copy = pltpu.make_async_copy(source, target, self.locals_.at[self.moved])
        copy.start()
        self.moved += 1
        return copy

    def finish_sends(self):
        for copy in self.pushed:
            copy.wait_send()


def arrive(copies):
    for copy in copies:
        copy.wait_recv()


def greet(devices):
    barrier = pltpu.get_barrier_semaphore()
    for device in devices:
        pl.semaphore_signal(barrier, inc=1, device_id=device, device_id_type=MESH)
    pl.semaphore_wait(barrier, len(devices))


def wired_call(kernel, outs, ins, collective_id, name, copies, moves, scratch=(), in_specs=None,
               out_specs=None, vmem=32 * MIB):
    return pl.pallas_call(
        kernel,
        out_shape=outs,
        in_specs=[ANY] * len(ins) if in_specs is None else in_specs,
        out_specs=[ANY] * len(outs) if out_specs is None else out_specs,
        scratch_shapes=[
            *scratch,
            pltpu.SemaphoreType.DMA((copies,)),
            pltpu.SemaphoreType.DMA((copies,)),
            pltpu.SemaphoreType.DMA((max(moves, 1),)),
        ],
        compiler_params=pltpu.CompilerParams(
            collective_id=collective_id, has_side_effects=True, vmem_limit_bytes=vmem
        ),
        name=name,
    )(*ins)


def shape(*dims, dtype=BF16):
    return jax.ShapeDtypeStruct(dims, dtype)


class Pieces:
    def view(self, ref, at, skip=0):
        lead = [slice(None) if i is None else i for i in self.order(at)[skip:]]
        return ref.at[(*lead, *self.tail(at))]

    def open_dims(self, at):
        return tuple(n for n, i in zip(self.lead, self.order(at)) if i is None)

    def tail(self, at):
        first, width = self.columns(at)
        if not isinstance(first, int):
            first = pl.multiple_of(first, 128)
        return (slice(None), pl.ds(first, width))

    def tail_dims(self, at):
        return (self.rows, self.columns(at)[1])


def halved(first, width, at):
    if "half" not in at:
        return first, width
    return first + at["half"] * (width // 2), width // 2


class RowsByShard(Pieces):
    lead, rows = ((2, 2, 4, 4), 16)

    def __init__(self, width):
        self.width = width

    def order(self, at):
        return [at.get("zh"), at.get("zl"), at.get("x"), at.get("y")]

    def columns(self, at):
        return halved(0, self.width, at)


class RowsByPlane(Pieces):
    lead, rows = ((2, 4, 4), 16)

    def __init__(self, first, width):
        self.first, self.width = (first, width)

    def order(self, at):
        return [at.get("zh"), at.get("x"), at.get("y")]

    def columns(self, at):
        if "zl" not in at:
            return halved(self.first, self.width, at)
        half = self.width // 2
        return halved(self.first + half * at["zl"], half, at)


class ColumnsByY(Pieces):
    lead = (2, 4, 2)

    def __init__(self, rows):
        self.rows = rows

    def order(self, at):
        return [at.get("zh"), at.get("x"), at.get("zl")]

    def columns(self, at):
        return halved(at["y"] * 256, 256, at) if "y" in at else halved(0, D, at)


class ShardsByCore(Pieces):
    lead, rows = ((2, 2, 4, 4), 16)

    def __init__(self, width):
        self.width = width

    def order(self, at):
        return [at.get("zh"), at.get("half"), at.get("x"), at.get("y")]

    def columns(self, at):
        half = self.width // 2
        return (half * at["zl"], half) if "zl" in at else (0, self.width)


class OneCore(RowsByPlane):
    lead = (2, 2, 4, 4)

    def __init__(self, width, core):
        super().__init__(0, width)
        self.core = core

    def order(self, at):
        return [at.get("zh"), self.core, at.get("x"), at.get("y")]


def fix(at, axis, coordinate):
    if axis == "z":
        return {**at, "zh": coordinate // 2, "zl": coordinate % 2}
    return {**at, axis: coordinate}


def without(at, axis):
    return {a: i for a, i in at.items() if a != ("zl" if axis == "z" else axis)}


def in_turn(tasks):
    while tasks:
        tasks = [task for task in tasks if next(task, "over") != "over"]


def spread(here, wires, kind, ref, at, order, skip=0):
    for axis in order:
        piece = kind.view(ref, at, skip)
        if axis == "z":
            copies = [wires.push(piece, piece, here.device(z=here.zh * 2 + 1 - here.zl))]
            yield
            arrive(copies)
        else:
            (_, right), (_, left) = (here.along(axis, 1), here.along(axis, 3))
            from_left = wires.push(piece, piece, right)
            from_right = wires.push(piece, piece, left)
            yield
            relays = []
            for half, copy, step, onward in ((0, from_left, 3, right), (1, from_right, 1, left)):
                arrive([copy])
                passing = fix(at, axis, here.along(axis, step)[0])
                passing = kind.view(ref, {**passing, "half": half}, skip)
                relays.append(wires.push(passing, passing, onward))
            yield
            arrive(relays)
        at = without(at, axis)


def gather_weights_kernel(
    qkv, out, gate, up, down, qkv_all, out_all, gate_all, up_all, down_all, sends, receives, moves
):
    here = Place()
    wires = Wires(sends, receives, moves)
    zh, core, x, y = (here.zh, here.core, here.x, here.y)
    there = 1 - here.zl
    across = 3 - here.z
    cross = [here.device(z=across, core=(core + t) % 2) for t in range(2)]
    sibling = here.sibling()
    greet([here.along(a, s)[1] for a in ("x", "y") for s in (1, 3)]
          + [here.device(z=here.zh * 2 + 1 - here.zl), *cross, sibling])

    def ff_columns(r, c):
        return pl.ds(pl.multiple_of(r * HALF_FF + c * SLICE, 128), SLICE)

    def part(width):
        return pl.ds(pl.multiple_of(there * width, 128), width)

    down_columns = pl.ds(pl.multiple_of(y * 256, 256), 256)
    held = {"zh": 1 - zh, "zl": here.zl, "x": x, "y": y}

    def fetch(kind, whole, crossed, order):
        yield
        arrive(crossed)
        yield from spread(here, wires, kind, whole, held, order)

    def fetch_narrow(shard, whole, width, order):
        kind = OneCore(width, core)
        columns = part(width // 2)
        source = shard.at[x, y, :, columns]
        crossed = [wires.push(source, whole.at[zh, core, x, y, :, columns], cross[0])]
        yield from fetch(kind, whole, crossed, order)
        beside = [wires.push(whole.at[1 - zh, core], whole.at[1 - zh, core], sibling)]
        yield
        arrive(beside)

    def fetch_wide(shard, whole, order):
        crossed = [
            wires.push(
                shard.at[x, y, :, ff_columns(there, (core + t) % 2)],
                whole.at[zh, core, x, y, :, part(SLICE)],
                cross[t],
            )
            for t in range(2)
        ]
        yield from fetch(ShardsByCore(HALF_FF), whole, crossed, order)

    def fetch_down(order):
        source = down.at[x, there, :, down_columns]
        crossed = [wires.push(source, down_all.at[zh, x, there, :, down_columns], cross[0])]
        yield from fetch(ColumnsByY(144), down_all, crossed, order)

    def from_this_chip():
        beside, kept = ([], [])
        for shard, whole in ((qkv, qkv_all), (out, out_all)):
            beside.append(wires.push(shard, whole.at[zh, core], sibling))
            kept.append(wires.move(shard, whole.at[zh, core]))
        for shard, whole in ((gate, gate_all), (up, up_all)):
            for r in range(2):
                target = whole.at[zh, core, :, :, :, pl.ds(r * SLICE, SLICE)]
                source = shard.at[:, :, :, ff_columns(r, 1 - core)]
                beside.append(wires.push(source, target, sibling))
                kept.append(wires.move(shard.at[:, :, :, ff_columns(r, core)], target))
        kept.append(wires.move(down, down_all.at[zh]))
        for _ in range(6):
            yield
        arrive(beside)
        for copy in kept:
            copy.wait()

    in_turn(
        [
            fetch_narrow(qkv, qkv_all, 2048, ("z", "y", "x")),
            fetch_wide(gate, gate_all, ("y", "x", "z")),
            fetch_wide(up, up_all, ("z", "y", "x")),
            fetch_down(("x", "z", "y")),
            fetch_narrow(out, out_all, D, ("x", "z", "y")),
            from_this_chip(),
        ]
    )
    wires.finish_sends()


def gather_weights(qkv, out, gate, up, down):
    rows = (4, 4, 16)
    ins = (
        qkv.reshape(*rows, 2048),
        out.reshape(*rows, D),
        gate.reshape(*rows, FF),
        up.reshape(*rows, FF),
        down.reshape(4, 2, 144, D),
    )
    outs = [
        shape(2, 2, *rows, 2048),
        shape(2, 2, *rows, D),
        shape(2, 2, *rows, HALF_FF),
        shape(2, 2, *rows, HALF_FF),
        shape(2, 4, 2, 144, D),
    ]
    copies = 7 + 6 + 5 * 9 + 2
    qkv, out, gate, up, down = wired_call(
        gather_weights_kernel, outs, ins, 1, "gather_weights", copies, 7
    )
    return (
        qkv.reshape(D, 2048),
        out.reshape(D, D),
        gate.reshape(D, HALF_FF),
        up.reshape(D, HALF_FF),
        down.reshape(HALF_FF, D),
    )


PARTS = (
    (0, RowsByShard(HALF_FF), ("z", "x", "y"), ("y", "x", "z")),
    (1, RowsByShard(HALF_FF), ("x", "y", "z"), ("z", "y", "x")),
    (2, ColumnsByY(144), ("y", "z", "x"), ("x", "z", "y")),
    (3, RowsByPlane(0, 1024), ("z", "x", "y"), ("z", "y", "x")),
    (3, RowsByPlane(1024, 1024), ("x", "y", "z"), ("x", "z", "y")),
    (4, ColumnsByY(32), ("y", "z", "x"), ("x", "z", "y")),
)


def slot_shapes():
    found = []
    for _, kind, order, _ in PARTS:
        at = {}
        for axis in order:
            at = fix(at, axis, 0)
            found.append((6, *kind.open_dims(at), *kind.tail_dims({**at, "half": 0})))
    return found


def each_block(kind, at, body):
    dims = kind.open_dims(at)

    def step(i, _):
        inner, rest = ([], i)
        for n in reversed(dims):
            inner.insert(0, rest % n)
            rest = rest // n
        picks = iter(inner)
        lead = [next(picks) if o is None else o for o in kind.order(at)]
        body((*lead, *kind.tail(at)), (*inner, slice(None), slice(None)))
        return 0

    lax.fori_loop(0, math.prod(dims), step, 0)


def reduce_one(here, wires, kind, grad, total, slots, order):
    at = {}
    for step, axis in enumerate(order):
        source, slot = (grad if step == 0 else total, slots[step])
        (right_place, right), (left_place, left) = (here.along(axis, 1), here.along(axis, 3))
        far_place, _ = here.along(axis, 2)
        mine = fix(at, axis, getattr(here, axis))

        def half_of(place, half):
            return {**fix(at, axis, place), "half": half}

        relays = [
            wires.push(kind.view(source, half_of(far_place, 0)), slot.at[4], right),
            wires.push(kind.view(source, half_of(far_place, 1)), slot.at[5], left),
        ]
        arriving = [
            wires.push(kind.view(source, half_of(right_place, 1)), slot.at[1], right),
            wires.push(kind.view(source, half_of(left_place, 0)), slot.at[2], left),
        ]
        kept = []
        if step == 0:
            for where in (half_of(right_place, 0), half_of(left_place, 1), mine):
                kept.append(wires.move(kind.view(source, where), kind.view(total, where)))
        yield
        for j, place, half, target, onward in (
            (4, right_place, 0, 0, right),
            (5, left_place, 1, 3, left),
        ):
            if kept:
                kept.pop(0).wait()
            arrive([relays[j - 4]])

            def pass_on(whole, part):
                value = slot[(j, *part)].astype(F32) + total[whole].astype(F32)
                slot[(j, *part)] = value.astype(BF16)

            each_block(kind, half_of(place, half), pass_on)
            arriving.append(wires.push(slot.at[j], slot.at[target], onward))
        yield
        if kept:
            kept.pop(0).wait()
        arrive(arriving)
        for half in range(2):

            def add_up(whole, part):
                value = total[whole].astype(F32) + slot[(half, *part)].astype(F32)
                total[whole] = (value + slot[(2 + half, *part)].astype(F32)).astype(BF16)

            each_block(kind, {**mine, "half": half}, add_up)
        at = mine


def reduce_weights_kernel(*refs):
    grads, gains = (refs[:5], refs[5])
    gate_near, up_near, gate_beside, up_beside, down_out, qkv_out, out_out, gains_out = refs[6:14]
    totals = refs[14:19]
    slots = refs[19:37]
    gain_slots, sends, receives, moves = refs[37:]
    nears = (gate_near, up_near, down_out, qkv_out, out_out)
    besides = (gate_beside, up_beside)

    here = Place()
    wires = Wires(sends, receives, moves)
    core = here.core
    sibling = here.sibling()
    greet([here.along(a, s)[1] for a in ("x", "y", "z") for s in (1, 3, 2)] + [sibling])

    def all_gains():
        total = gains[...]
        for stage, axis in enumerate(("core", "x", "y", "z")):
            me = getattr(here, axis)
            gain_slots[stage, me] = total
            source = gain_slots.at[stage, me]
            if axis == "core":
                others = [sibling]
            else:
                others = [here.along(axis, s)[1] for s in (1, 3, 2)]
            copies = [wires.push(source, source, device) for device in others]
            yield
            yield
            arrive(copies)
            total = gain_slots[stage, 0] + gain_slots[stage, 1]
            if axis != "core":
                total = total + gain_slots[stage, 2] + gain_slots[stage, 3]
        gains_out[...] = total

    def one(p):
        g, kind, order, back = PARTS[p]
        yield from reduce_one(
            here, wires, kind, grads[g], totals[g], slots[3 * p : 3 * p + 3], order
        )
        at = {"zh": here.zh, "zl": here.zl, "x": here.x, "y": here.y}
        own = wires.move(kind.view(totals[g], at), kind.view(nears[g], at, 1))
        yield
        own.wait()
        yield from spread(here, wires, kind, nears[g], at, back, 1)
        if g < 2:
            copies = [wires.push(nears[g].at[1 - core], besides[g], sibling)]
            yield
            arrive(copies)

    in_turn([all_gains()] + [one(p) for p in range(len(PARTS))])
    wires.finish_sends()


def reduce_weights(gate, up, down, qkv, out, gains):
    dims = (
        (2, 2, 4, 4, 16, HALF_FF),
        (2, 2, 4, 4, 16, HALF_FF),
        (2, 4, 2, 144, D),
        (2, 4, 4, 16, 2048),
        (2, 4, 2, 32, D),
    )
    ins = [a.reshape(d) for a, d in zip((gate, up, down, qkv, out), dims)] + [gains]
    outs = [
        shape(*dims[0][1:]),
        shape(*dims[1][1:]),
        shape(*dims[0][2:]),
        shape(*dims[1][2:]),
        shape(*dims[2][1:]),
        shape(*dims[3][1:]),
        shape(*dims[4][1:]),
        shape(*gains.shape, dtype=F32),
    ]
    scratch = [pltpu.VMEM(d, BF16) for d in dims]
    scratch += [pltpu.VMEM(s, BF16) for s in slot_shapes()]
    scratch += [pltpu.VMEM((4, 4, *gains.shape), F32)]
    copies = 10 + 6 * 18 + 6 * 9 + 2
    done = wired_call(
        reduce_weights_kernel,
        outs,
        ins,
        2,
        "reduce_weights",
        copies,
        6 * 4,
        scratch,
        [ANY] * 5 + [VMEM],
        [ANY] * 7 + [VMEM],
        vmem=56 * MIB,
    )
    core = lax.axis_index("fsdp") % 2

    def joined(near, beside):
        own = lax.dynamic_index_in_dim(near, core, 0, keepdims=False).reshape(256, HALF_FF)
        beside = beside.reshape(256, HALF_FF)
        first, second = (jnp.where(core == 0, own, beside), jnp.where(core == 0, beside, own))
        pieces = [f[:, r * SLICE : (r + 1) * SLICE] for r in range(2) for f in (first, second)]
        return jnp.concatenate(pieces, axis=1)

    gate, up = (joined(done[0], done[2]), joined(done[1], done[3]))
    down, qkv, out, gains = done[4:]
    return (
        qkv.reshape(256, 2048),
        out.reshape(256, D),
        gate,
        up,
        down.reshape(SLICE, D),
        gains,
    )


def head_columns(head):
    return pl.ds(pl.multiple_of(head * 128, 128), 128)


def to_heads_kernel(with_keys, *refs):
    if with_keys:
        query, key_value, query_out, key_value_out, sends, receives, moves = refs
    else:
        query, query_out, sends, receives, moves = refs
    here = Place()
    wires = Wires(sends, receives, moves)
    me = here.ctx
    quarter, seat = (me // QUARTER, me % QUARTER)
    near = [quarter * QUARTER + (seat + s) % QUARTER for s in range(1, QUARTER)]
    far = [(me + s) % RING for s in range(1, RING)]
    greet([(k, here.fsdp) for k in (far if with_keys else near)])
    copies = [
        wires.push(query.at[:, head_columns(k % QUARTER)], query_out.at[seat], (k, here.fsdp))
        for k in near
    ]
    kept = [wires.move(query.at[:, head_columns(seat)], query_out.at[seat])]
    if with_keys:
        copies += [
            wires.push(
                key_value.at[:, head_columns(k % QUARTER)], key_value_out.at[me], (k, here.fsdp)
            )
            for k in far
        ]
        kept.append(wires.move(key_value.at[:, head_columns(seat)], key_value_out.at[me]))
    arrive(copies)
    for copy in kept:
        copy.wait()
    wires.finish_sends()


def to_heads(query, key_value=None):
    ins = [query] + ([] if key_value is None else [key_value])
    outs = [shape(QUARTER, TOKENS, 128)]
    if key_value is not None:
        outs.append(shape(RING, TOKENS, 128))
    copies = 7 if key_value is None else 38
    return wired_call(
        functools.partial(to_heads_kernel, key_value is not None),
        outs,
        ins,
        3 if key_value is None else 4,
        "to_heads",
        copies,
        2,
    )


def to_tokens_kernel(with_keys, *refs):
    if with_keys:
        query, key_value, query_out, key_value_out, sends, receives, moves = refs
    else:
        query, query_out, sends, receives, moves = refs
    here = Place()
    wires = Wires(sends, receives, moves)
    me = here.ctx
    quarter, seat = (me // QUARTER, me % QUARTER)
    near = [quarter * QUARTER + (seat + s) % QUARTER for s in range(1, QUARTER)]
    far = [(me + s) % RING for s in range(1, RING)]
    greet([(k, here.fsdp) for k in (far if with_keys else near)])
    columns = query_out.at[:, head_columns(seat)]
    copies = [wires.push(query.at[k % QUARTER], columns, (k, here.fsdp)) for k in near]
    kept = [wires.move(query.at[seat], columns)]
    if with_keys:
        copies += [
            wires.push(key_value.at[k], key_value_out.at[me], (k, here.fsdp)) for k in far
        ]
        kept.append(wires.move(key_value.at[me], key_value_out.at[me]))
    arrive(copies)
    for copy in kept:
        copy.wait()
    wires.finish_sends()


def to_tokens(query, key_value=None):
    ins = [query] + ([] if key_value is None else [key_value])
    outs = [shape(TOKENS, D)]
    if key_value is not None:
        outs.append(shape(RING, TOKENS, 128))
    copies = 7 if key_value is None else 38
    return wired_call(
        functools.partial(to_tokens_kernel, key_value is not None),
        outs,
        ins,
        5 if key_value is None else 6,
        "to_tokens",
        copies,
        2,
    )


def half_columns(r, core):
    return pl.ds(pl.multiple_of(r * 512 + core * 256, 256), 256)


def share_kernel(whole, halved, *refs):
    n = whole + halved
    ins, outs = (refs[:n], refs[n : 2 * n])
    here = Place()
    wires = Wires(*refs[2 * n :])
    core = here.core
    sibling = here.sibling()
    greet([sibling])
    copies, kept = ([], [])
    for source, target in zip(ins[:whole], outs[:whole]):
        copies.append(wires.push(source, target.at[core], sibling))
        kept.append(wires.move(source, target.at[core]))
    for source, target in zip(ins[whole:], outs[whole:]):
        for r in range(2):
            place = target.at[core, :, pl.ds(r * 256, 256)]
            copies.append(wires.push(source.at[:, half_columns(r, 1 - core)], place, sibling))
            kept.append(wires.move(source.at[:, half_columns(r, core)], place))
    arrive(copies)
    for copy in kept:
        copy.wait()
    wires.finish_sends()


def share(whole, halved, collective_id):
    outs = [shape(2, *a.shape, dtype=a.dtype) for a in whole]
    outs += [shape(2, a.shape[0], 512, dtype=a.dtype) for a in halved]
    count = len(whole) + 2 * len(halved)
    done = wired_call(
        functools.partial(share_kernel, len(whole), len(halved)),
        outs,
        [*whole, *halved],
        collective_id,
        "share",
        count,
        count,
    )
    return [a.reshape(2 * a.shape[1], a.shape[2]) for a in done]


def hand_over_kernel(count, *refs):
    ins, outs = (refs[:count], refs[count : 2 * count])
    here = Place()
    wires = Wires(*refs[2 * count :])
    sibling = here.sibling()
    greet([sibling])
    copies = [wires.push(i.at[1 - here.core], o, sibling) for i, o in zip(ins, outs)]
    arrive(copies)
    wires.finish_sends()


def hand_over(partials, collective_id):
    return wired_call(
        functools.partial(hand_over_kernel, len(partials)),
        [shape(*a.shape[1:], dtype=a.dtype) for a in partials],
        partials,
        collective_id,
        "hand_over",
        len(partials),
        0,
    )


def nt(left, right):
    return lax.dot_general(left, right, (((1,), (1,)), ((), ())), preferred_element_type=F32)


def nn(left, right):
    return lax.dot_general(left, right, (((1,), (0,)), ((), ())), preferred_element_type=F32)


def by_position(order_ref, key_value_ref, sorted_ref):
    def body(j, _):
        sorted_ref[pl.ds(pl.multiple_of(order_ref[j] * 64, 64), 64), :] = key_value_ref[j]
        return 0

    lax.fori_loop(0, 64, body, 0)


def query_block(ref, t):
    block = ref[t].astype(F32)
    both = jnp.concatenate([block, pltpu.roll(block, 64, 1)], axis=0)
    low = lax.broadcasted_iota(jnp.int32, (128, 128), 1) < 64
    return jnp.where(low, both, 0.0)


def key_limits(order_ref, starts_ref, place_ref, t):
    first = order_ref[place_ref[0] * 16 + t] * 64
    begin = jnp.int32(0)
    for n in range(4):
        begin = jnp.maximum(begin, jnp.where(starts_ref[n] <= first, starts_ref[n], 0))
    return first, begin // KEY_TILE, (first + 63) // KEY_TILE + 1


def first_allowed(position, starts_ref):
    begin = jnp.zeros_like(position)
    for n in range(4):
        begin = jnp.maximum(begin, jnp.where(starts_ref[n] <= position, starts_ref[n], 0))
    return begin


def attend_kernel(
    order_ref, starts_ref, place_ref, query_ref, key_value_ref, out_ref, exact_ref, sum_ref,
    sorted_ref, value_ref,
):
    by_position(order_ref, key_value_ref, sorted_ref)

    def values(j, _):
        rows = pl.ds(pl.multiple_of(j * 256, 256), 256)
        block = pltpu.roll(sorted_ref[rows, :].astype(F32), 64, 1)
        low = lax.broadcasted_iota(jnp.int32, (256, 128), 1) < 64
        value_ref[rows, :] = jnp.where(low, block, 1.0).astype(BF16)
        return 0

    lax.fori_loop(0, SEQ // 256, values, 0)

    def block(t, _):
        first, begin_tile, end_tile = key_limits(order_ref, starts_ref, place_ref, t)
        queries = query_block(query_ref, t).astype(BF16)
        position = first + lax.broadcasted_iota(jnp.int32, (128, 1), 0) % 64
        begin = first_allowed(position, starts_ref)

        def tile(j, total):
            rows = pl.ds(pl.multiple_of(j * KEY_TILE, KEY_TILE), KEY_TILE)
            scores = nt(queries, sorted_ref[rows, :])
            key = j * KEY_TILE + lax.broadcasted_iota(jnp.int32, (128, KEY_TILE), 1)
            allowed = (key <= position) & (key >= begin)
            weight = jnp.where(allowed, jnp.exp2(scores * SCORE_TO_EXP2), 0.0)
            return total + nn(weight.astype(BF16), value_ref[rows, :])

        total = lax.fori_loop(begin_tile, end_tile, tile, jnp.zeros((128, 128), F32))
        sums = pltpu.roll(total, 64, 1)
        attended = total / sums
        low_pair = lax.broadcasted_iota(jnp.int32, (128, 128), 1) < 64
        low = lax.broadcasted_iota(jnp.int32, (64, 128), 1) < 64
        exact_ref[t] = jnp.where(low_pair, attended, 0.0)
        out_ref[t] = jnp.where(low, attended[:64], pltpu.roll(attended[64:], 64, 1)).astype(BF16)
        sum_ref[t] = jnp.transpose(total)[64:72]
        return 0

    lax.fori_loop(0, 16, block, 0)


def attend(order, starts, place, queries, key_values):
    return pl.pallas_call(
        attend_kernel,
        out_shape=[shape(16, 64, 128), shape(16, 128, 128, dtype=F32), shape(16, 8, 128, dtype=F32)],
        in_specs=[SMEM, SMEM, SMEM, VMEM, VMEM],
        out_specs=[VMEM] * 3,
        scratch_shapes=[pltpu.VMEM((SEQ, 128), BF16), pltpu.VMEM((SEQ, 128), BF16)],
        compiler_params=pltpu.CompilerParams(vmem_limit_bytes=32 * MIB),
        name="attend",
    )(order, starts, place, queries, key_values)


def attend_back_kernel(
    order_ref, starts_ref, place_ref, query_ref, key_value_ref, grad_ref, exact_ref, sum_ref,
    query_grad_ref, key_value_grad_ref, sorted_ref, across_ref, total_ref,
):
    by_position(order_ref, key_value_ref, sorted_ref)
    total_ref[...] = jnp.zeros_like(total_ref)

    def turn(j, _):
        rows = pl.ds(pl.multiple_of(j * 128, 128), 128)
        across_ref[:, rows] = jnp.transpose(sorted_ref[rows, :].astype(F32)).astype(BF16)
        return 0

    lax.fori_loop(0, SEQ // 128, turn, 0)

    def block(t, _):
        first, begin_tile, end_tile = key_limits(order_ref, starts_ref, place_ref, t)
        queries = query_block(query_ref, t)
        grads = query_block(grad_ref, t)
        delta = jnp.sum(jnp.transpose(grads * exact_ref[t]), axis=0, keepdims=True)
        total_exp2 = jnp.log2(sum_ref[t][0:1])
        both = jnp.concatenate([queries, pltpu.roll(grads, 64, 1)], axis=0).astype(BF16)
        position = first + lax.broadcasted_iota(jnp.int32, (1, 128), 1) % 64
        begin = first_allowed(position, starts_ref)

        def tile(j, query_grad):
            rows = pl.ds(pl.multiple_of(j * KEY_TILE, KEY_TILE), KEY_TILE)
            products = nt(sorted_ref[rows, :], both)
            key = j * KEY_TILE + lax.broadcasted_iota(jnp.int32, (KEY_TILE, 128), 0)
            allowed = (key <= position) & (key >= begin)
            prob = jnp.where(
                allowed, jnp.exp2(products[:, :128] * SCORE_TO_EXP2 - total_exp2), 0.0
            )
            score = (prob * (products[:, 128:] - delta)).astype(BF16)
            pair = jnp.concatenate([score, prob.astype(BF16)], axis=1)
            total_ref[rows, :] += nn(pair, both)
            return query_grad + nn(across_ref[:, rows], score)

        query_grad = lax.fori_loop(begin_tile, end_tile, tile, jnp.zeros((128, 128), F32))
        query_grad = jnp.transpose(query_grad) * float(HEAD_SIZE) ** (-0.5)
        low = lax.broadcasted_iota(jnp.int32, (64, 128), 1) < 64
        query_grad_ref[t] = jnp.where(
            low, query_grad[:64], pltpu.roll(query_grad[64:], 64, 1)
        ).astype(BF16)
        return 0

    lax.fori_loop(0, 16, block, 0)

    def put_back(j, _):
        rows = pl.ds(pl.multiple_of(order_ref[j] * 64, 64), 64)
        low = lax.broadcasted_iota(jnp.int32, (64, 128), 1) < 64
        scale = jnp.where(low, float(HEAD_SIZE) ** (-0.5), 1.0)
        key_value_grad_ref[j] = (total_ref[rows, :] * scale).astype(BF16)
        return 0

    lax.fori_loop(0, 64, put_back, 0)


def attend_back(order, starts, place, queries, key_values, grads, exact, sums):
    return pl.pallas_call(
        attend_back_kernel,
        out_shape=[shape(16, 64, 128), shape(64, 64, 128)],
        in_specs=[SMEM] * 3 + [VMEM] * 5,
        out_specs=[VMEM] * 2,
        scratch_shapes=[
            pltpu.VMEM((SEQ, 128), BF16),
            pltpu.VMEM((128, SEQ), BF16),
            pltpu.VMEM((SEQ, 128), F32),
        ],
        compiler_params=pltpu.CompilerParams(vmem_limit_bytes=40 * MIB),
        name="attend_back",
    )(order, starts, place, queries, key_values, grads, exact, sums)


def rms_norm(values, gain_row):
    return (
        values * lax.rsqrt(jnp.mean(values * values, axis=-1, keepdims=True) + EPSILON) * gain_row
    )


def rotate(values, positions):
    half_width = values.shape[-1] // 2
    frequency = ROPE_BASE ** (-2.0 * jnp.arange(half_width, dtype=F32) / values.shape[-1])
    angles = positions.astype(F32)[:, None] * frequency[None, :]
    cosine = jnp.cos(angles)[:, None, :]
    sine_part = jnp.sin(angles)[:, None, :]
    first_half = values[..., :half_width]
    second_half = values[..., half_width:]
    return jnp.concatenate(
        [
            first_half * cosine - second_half * sine_part,
            second_half * cosine + first_half * sine_part,
        ],
        axis=-1,
    )


def outer_sum(left, right):
    return lax.dot_general(
        left, right, (((0,), (0,)), ((), ())), preferred_element_type=F32
    ).astype(BF16)


def matmul(left, right):
    return jnp.dot(left, right, preferred_element_type=F32)


def positions_at(block_order, first_row, total_row_count, half_rows):
    row_ids = first_row + jnp.arange(total_row_count, dtype=jnp.int32)
    blocks = row_ids // half_rows
    lookup = jnp.arange(block_order.shape[0], dtype=jnp.int32)
    picked = jnp.sum(jnp.where(blocks[:, None] == lookup[None, :], block_order[None, :], 0), axis=1)
    return picked * half_rows + row_ids % half_rows


def per_device(
    inputs,
    cotangent,
    qkv_weight,
    out_weight,
    gate_weight,
    up_weight,
    down_weight,
    gain_attn,
    gain_query,
    gain_key,
    gain_ffn,
    block_order,
    doc_starts,
):
    cycle_index = lax.axis_index("ctx")
    core = lax.axis_index("fsdp") % 2
    qkv_all, out_all, gate_all, up_all, down_all = gather_weights(
        qkv_weight, out_weight, gate_weight, up_weight, down_weight
    )
    starts = doc_starts[0]
    place = (cycle_index // QUARTER).astype(jnp.int32).reshape(1)
    positions = positions_at(block_order, cycle_index * TOKENS, TOKENS, TOKENS // 2)

    resid_in = inputs[0].astype(F32)
    normed, norm_in_pull = jax.vjp(rms_norm, resid_in, gain_attn)
    normed_low = normed.astype(BF16)
    projected = matmul(normed_low, qkv_all)
    split_position = (QUERY_HEADS + KEY_VALUE_HEADS) * HEAD_SIZE

    def query_key(leading_columns, scale_query, scale_key):
        queries = leading_columns[:, : QUERY_HEADS * HEAD_SIZE].reshape(
            TOKENS, QUERY_HEADS, HEAD_SIZE
        )
        keys = leading_columns[:, QUERY_HEADS * HEAD_SIZE :].reshape(
            TOKENS, KEY_VALUE_HEADS, HEAD_SIZE
        )
        return (
            rotate(rms_norm(queries, scale_query), positions),
            rotate(rms_norm(keys, scale_key), positions),
        )

    (queries, keys), qk_pull = jax.vjp(
        query_key, projected[:, :split_position], gain_query, gain_key
    )
    values = projected[:, split_position:].reshape(TOKENS, KEY_VALUE_HEADS, HEAD_SIZE)
    key_values = jnp.concatenate([keys, values], axis=-1).astype(BF16).reshape(TOKENS, D)
    query_part, key_value_part = to_heads(queries.astype(BF16).reshape(TOKENS, D), key_values)
    query_part = query_part.reshape(16, 64, 128)
    key_value_part = key_value_part.reshape(64, 64, 128)
    attended, exact, sums = attend(block_order, starts, place, query_part, key_value_part)
    (attended_low,) = to_tokens(attended.reshape(QUARTER, TOKENS, 128))

    residual = resid_in + matmul(attended_low, out_all)
    normed_ffn, norm_ffn_pull = jax.vjp(rms_norm, residual, gain_ffn)
    grad_out = cotangent[0]
    ffn_pair, cotangent_pair, normed_half, attended_half = share(
        [normed_ffn.astype(BF16), grad_out], [normed_low, attended_low], 7
    )
    gate_proj = matmul(ffn_pair, gate_all)
    up_proj = matmul(ffn_pair, up_all)
    hidden, gating_pull = jax.vjp(
        lambda gate_in, up_in: jax.nn.silu(gate_in) * up_in, gate_proj, up_proj
    )
    hidden_low = hidden.astype(BF16)
    out_partial = matmul(hidden_low, down_all).reshape(2, TOKENS, D)
    grad_hidden = matmul(cotangent_pair, down_all.T)
    grad_gate, grad_up = gating_pull(grad_hidden)
    gate_low = grad_gate.astype(BF16)
    up_low = grad_up.astype(BF16)
    ffn_partial = (matmul(gate_low, gate_all.T) + matmul(up_low, up_all.T)).reshape(2, TOKENS, D)
    out_rest, ffn_rest = hand_over([out_partial, ffn_partial], 8)

    def mine(pair):
        return lax.dynamic_index_in_dim(pair, core, 0, keepdims=False)

    outputs = residual + mine(out_partial) + out_rest
    grad_resid_ffn, grad_gain_ffn = norm_ffn_pull(mine(ffn_partial) + ffn_rest)
    grad_resid = grad_out.astype(F32) + grad_resid_ffn
    branch_low = grad_resid.astype(BF16)
    grad_attended = matmul(branch_low, out_all.T).astype(BF16)
    (grad_part,) = to_heads(grad_attended)
    query_grad, key_value_grad = attend_back(
        block_order,
        starts,
        place,
        query_part,
        key_value_part,
        grad_part.reshape(16, 64, 128),
        exact,
        sums,
    )
    query_grad, key_value_grad = to_tokens(
        query_grad.reshape(QUARTER, TOKENS, 128), key_value_grad.reshape(RING, TOKENS, 128)
    )
    key_value_grad = key_value_grad.reshape(4, KEY_VALUE_HEADS, TOKENS, 128)
    key_value_grad = jnp.transpose(jnp.sum(key_value_grad.astype(F32), axis=0), (1, 0, 2))
    grad_front, grad_gain_query, grad_gain_key = qk_pull(
        (
            query_grad.astype(F32).reshape(TOKENS, QUERY_HEADS, HEAD_SIZE),
            key_value_grad[..., :HEAD_SIZE],
        )
    )
    grad_values = key_value_grad[..., HEAD_SIZE:].reshape(TOKENS, KEY_VALUE_HEADS * HEAD_SIZE)
    grad_projected = jnp.concatenate([grad_front, grad_values], axis=1).astype(BF16)
    grad_normed = matmul(grad_projected, qkv_all.T)
    grad_input_norm, grad_gain_attn = norm_in_pull(grad_normed)
    grad_inputs = (grad_resid + grad_input_norm).astype(BF16)

    projected_pair, branch_pair = share([grad_projected, branch_low], [], 9)
    gains = jnp.concatenate([grad_gain_attn, grad_gain_ffn, grad_gain_query, grad_gain_key])
    gains = jnp.pad(gains, (0, 24 * 128 - gains.shape[0])).reshape(24, 128)
    grad_qkv, grad_out_weight, grad_gate_weight, grad_up_weight, grad_down, gains = reduce_weights(
        outer_sum(ffn_pair, gate_low),
        outer_sum(ffn_pair, up_low),
        outer_sum(hidden_low, cotangent_pair),
        outer_sum(normed_half, projected_pair),
        outer_sum(attended_half, branch_pair),
        gains,
    )
    gains = gains.reshape(-1)
    return (
        outputs.astype(BF16)[None],
        grad_inputs[None],
        grad_qkv.astype(F32),
        grad_out_weight.astype(F32),
        grad_gate_weight.astype(F32),
        grad_up_weight.astype(F32),
        grad_down.astype(F32),
        gains[:D],
        gains[2 * D : 2 * D + HEAD_SIZE],
        gains[2 * D + HEAD_SIZE : 2 * D + 2 * HEAD_SIZE],
        gains[D : 2 * D],
    )


def solution(mesh):
    in_specs = (
        P("fsdp", "ctx", None),
        P("fsdp", "ctx", None),
        P("fsdp", None),
        P("fsdp", None),
        P("fsdp", None),
        P("fsdp", None),
        P("fsdp", None),
        P(),
        P(),
        P(),
        P(),
        P(),
        P("fsdp", None),
    )
    out_specs = (
        P("fsdp", "ctx", None),
        P("fsdp", "ctx", None),
        P("fsdp", None),
        P("fsdp", None),
        P("fsdp", None),
        P("fsdp", None),
        P("fsdp", None),
        P(),
        P(),
        P(),
        P(),
    )
    return jax.shard_map(
        per_device, mesh=mesh, in_specs=in_specs, out_specs=out_specs, check_vma=False
    )
```

```python
import functools
import math

import jax
import jax.numpy as jnp
from jax import lax
from jax.experimental import pallas as pl
from jax.experimental.pallas import tpu as pltpu
from jax.sharding import PartitionSpec as P

QUERY_HEADS = 16
KEY_VALUE_HEADS = 8
HEAD_SIZE = 64
FF = 4608
D = 1024
TOKENS = 128
RING = 32
QUARTER = 8
SLICE = 1152
HALF_FF = FF // 2
KEY_TILE = 1024
KEY_TILE_BACK = 1024
SEQ = 4096

EPSILON = 1e-05
ROPE_BASE = 1000000.0
SCORE_TO_EXP2 = float(HEAD_SIZE) ** (-0.5) * math.log2(math.e)

MESH = pl.DeviceIdType.MESH
ANY = pl.BlockSpec(memory_space=pl.ANY)
VMEM = pl.BlockSpec(memory_space=pltpu.VMEM)
SMEM = pl.BlockSpec(memory_space=pltpu.SMEM)
BF16 = jnp.bfloat16
F32 = jnp.float32
MIB = 1 << 20


class Place:
    def __init__(self):
        self.ctx, self.fsdp = (lax.axis_index("ctx"), lax.axis_index("fsdp"))
        self.zl, self.x, self.y = (self.ctx // 16, (self.ctx // 4) % 4, self.ctx % 4)
        self.zh, self.core = (self.fsdp // 2, self.fsdp % 2)
        self.z = self.zh * 2 + self.zl

    def device(self, x=None, y=None, z=None, core=None):
        x = self.x if x is None else x
        y = self.y if y is None else y
        z = self.z if z is None else z
        core = self.core if core is None else core
        return ((z % 2) * 16 + x * 4 + y, (z // 2) * 2 + core)

    def sibling(self):
        return self.device(core=1 - self.core)

    def along(self, axis, step):
        coordinate = (getattr(self, axis) + step) % 4
        return coordinate, self.device(**{axis: coordinate})


class Wires:
    def __init__(self, sends, receives, locals_=None):
        self.sends, self.receives, self.locals_ = (sends, receives, locals_)
        self.pushed, self.moved = ([], 0)

    def push(self, source, target, device):
        at = len(self.pushed)
        copy = pltpu.make_async_remote_copy(
            src_ref=source,
            dst_ref=target,
            send_sem=self.sends.at[at],
            recv_sem=self.receives.at[at],
            device_id=device,
            device_id_type=MESH,
        )
        copy.start()
        self.pushed.append(copy)
        return copy

    def move(self, source, target):
        copy = pltpu.make_async_copy(source, target, self.locals_.at[self.moved])
        copy.start()
        self.moved += 1
        return copy

    def finish_sends(self):
        for copy in self.pushed:
            copy.wait_send()


def arrive(copies):
    for copy in copies:
        copy.wait_recv()


def greet(devices):
    barrier = pltpu.get_barrier_semaphore()
    for device in devices:
        pl.semaphore_signal(barrier, inc=1, device_id=device, device_id_type=MESH)
    pl.semaphore_wait(barrier, len(devices))


def wired_call(kernel, outs, ins, collective_id, name, copies, moves, scratch=(), in_specs=None,
               out_specs=None, vmem=32 * MIB):
    return pl.pallas_call(
        kernel,
        out_shape=outs,
        in_specs=[ANY] * len(ins) if in_specs is None else in_specs,
        out_specs=[ANY] * len(outs) if out_specs is None else out_specs,
        scratch_shapes=[
            *scratch,
            pltpu.SemaphoreType.DMA((copies,)),
            pltpu.SemaphoreType.DMA((copies,)),
            pltpu.SemaphoreType.DMA((max(moves, 1),)),
        ],
        compiler_params=pltpu.CompilerParams(
            collective_id=collective_id, has_side_effects=True, vmem_limit_bytes=vmem
        ),
        name=name,
    )(*ins)


def shape(*dims, dtype=BF16):
    return jax.ShapeDtypeStruct(dims, dtype)


class Pieces:
    def view(self, ref, at, skip=0):
        lead = [slice(None) if i is None else i for i in self.order(at)[skip:]]
        return ref.at[(*lead, *self.tail(at))]

    def open_dims(self, at):
        return tuple(n for n, i in zip(self.lead, self.order(at)) if i is None)

    def tail(self, at):
        first, width = self.columns(at)
        if not isinstance(first, int):
            first = pl.multiple_of(first, 128)
        return (slice(None), pl.ds(first, width))

    def tail_dims(self, at):
        return (self.rows, self.columns(at)[1])


def halved(first, width, at):
    if "half" not in at:
        return first, width
    return first + at["half"] * (width // 2), width // 2


class RowsByShard(Pieces):
    lead, rows = ((2, 2, 4, 4), 16)

    def __init__(self, width):
        self.width = width

    def order(self, at):
        return [at.get("zh"), at.get("zl"), at.get("x"), at.get("y")]

    def columns(self, at):
        return halved(0, self.width, at)


class RowsByPlane(Pieces):
    lead, rows = ((2, 4, 4), 16)

    def __init__(self, first, width):
        self.first, self.width = (first, width)

    def order(self, at):
        return [at.get("zh"), at.get("x"), at.get("y")]

    def columns(self, at):
        if "zl" not in at:
            return halved(self.first, self.width, at)
        half = self.width // 2
        return halved(self.first + half * at["zl"], half, at)


class ColumnsByY(Pieces):
    lead = (2, 4, 2)

    def __init__(self, rows):
        self.rows = rows

    def order(self, at):
        return [at.get("zh"), at.get("x"), at.get("zl")]

    def columns(self, at):
        return halved(at["y"] * 256, 256, at) if "y" in at else halved(0, D, at)


class ShardsByCore(Pieces):
    lead, rows = ((2, 2, 4, 4), 16)

    def __init__(self, width):
        self.width = width

    def order(self, at):
        return [at.get("zh"), at.get("half"), at.get("x"), at.get("y")]

    def columns(self, at):
        half = self.width // 2
        return (half * at["zl"], half) if "zl" in at else (0, self.width)


class OneCore(RowsByPlane):
    lead = (2, 2, 4, 4)

    def __init__(self, width, core):
        super().__init__(0, width)
        self.core = core

    def order(self, at):
        return [at.get("zh"), self.core, at.get("x"), at.get("y")]


def fix(at, axis, coordinate):
    if axis == "z":
        return {**at, "zh": coordinate // 2, "zl": coordinate % 2}
    return {**at, axis: coordinate}


def without(at, axis):
    return {a: i for a, i in at.items() if a != ("zl" if axis == "z" else axis)}


def in_turn(tasks):
    while tasks:
        tasks = [task for task in tasks if next(task, "over") != "over"]


def spread(here, wires, kind, ref, at, order, skip=0):
    for axis in order:
        piece = kind.view(ref, at, skip)
        if axis == "z":
            copies = [wires.push(piece, piece, here.device(z=here.zh * 2 + 1 - here.zl))]
            yield
            arrive(copies)
        else:
            (_, right), (_, left) = (here.along(axis, 1), here.along(axis, 3))
            from_left = wires.push(piece, piece, right)
            from_right = wires.push(piece, piece, left)
            yield
            relays = []
            for half, copy, step, onward in ((0, from_left, 3, right), (1, from_right, 1, left)):
                arrive([copy])
                passing = fix(at, axis, here.along(axis, step)[0])
                passing = kind.view(ref, {**passing, "half": half}, skip)
                relays.append(wires.push(passing, passing, onward))
            yield
            arrive(relays)
        at = without(at, axis)


class Fetch:
    def __init__(self, here, wires):
        self.here, self.wires = (here, wires)
        self.zh, self.core, self.x, self.y = (here.zh, here.core, here.x, here.y)
        self.there = 1 - here.zl
        self.cross = [here.device(z=3 - here.z, core=(here.core + t) % 2) for t in range(2)]
        self.sibling = here.sibling()
        self.held = {"zh": 1 - here.zh, "zl": here.zl, "x": here.x, "y": here.y}

    def greet(self):
        here = self.here
        greet([here.along(a, s)[1] for a in ("x", "y") for s in (1, 3)]
              + [here.device(z=here.zh * 2 + 1 - here.zl), *self.cross, self.sibling])

    def part(self, width):
        return pl.ds(pl.multiple_of(self.there * width, 128), width)

    def ff_columns(self, r, c):
        return pl.ds(pl.multiple_of(r * HALF_FF + c * SLICE, 128), SLICE)

    def rest(self, kind, whole, crossed, order):
        yield
        arrive(crossed)
        yield from spread(self.here, self.wires, kind, whole, self.held, order)

    def narrow(self, shard, whole, width, order):
        columns = self.part(width // 2)
        source = shard.at[self.x, self.y, :, columns]
        target = whole.at[self.zh, self.core, self.x, self.y, :, columns]
        crossed = [self.wires.push(source, target, self.cross[0])]
        yield from self.rest(OneCore(width, self.core), whole, crossed, order)
        passed = whole.at[1 - self.zh, self.core]
        beside = [self.wires.push(passed, passed, self.sibling)]
        yield
        arrive(beside)

    def wide(self, shard, whole, order):
        crossed = [
            self.wires.push(
                shard.at[self.x, self.y, :, self.ff_columns(self.there, (self.core + t) % 2)],
                whole.at[self.zh, self.core, self.x, self.y, :, self.part(SLICE)],
                self.cross[t],
            )
            for t in range(2)
        ]
        yield from self.rest(ShardsByCore(HALF_FF), whole, crossed, order)

    def down(self, shard, whole, order):
        columns = pl.ds(pl.multiple_of(self.y * 256, 256), 256)
        source = shard.at[self.x, self.there, :, columns]
        target = whole.at[self.zh, self.x, self.there, :, columns]
        crossed = [self.wires.push(source, target, self.cross[0])]
        yield from self.rest(ColumnsByY(144), whole, crossed, order)

    def from_this_chip(self, narrow=(), wide=(), down=()):
        beside, kept = ([], [])
        for shard, whole in narrow:
            target = whole.at[self.zh, self.core]
            beside.append(self.wires.push(shard, target, self.sibling))
            kept.append(self.wires.move(shard, target))
        for shard, whole in wide:
            for r in range(2):
                target = whole.at[self.zh, self.core, :, :, :, pl.ds(r * SLICE, SLICE)]
                theirs = shard.at[:, :, :, self.ff_columns(r, 1 - self.core)]
                mine = shard.at[:, :, :, self.ff_columns(r, self.core)]
                beside.append(self.wires.push(theirs, target, self.sibling))
                kept.append(self.wires.move(mine, target))
        for shard, whole in down:
            kept.append(self.wires.move(shard, whole.at[self.zh]))
        for _ in range(6):
            yield
        arrive(beside)
        for copy in kept:
            copy.wait()


def gather_narrow_kernel(qkv, out, qkv_all, out_all, sends, receives, moves):
    wires = Wires(sends, receives, moves)
    fetch = Fetch(Place(), wires)
    fetch.greet()
    in_turn(
        [
            fetch.narrow(qkv, qkv_all, 2048, ("z", "y", "x")),
            fetch.narrow(out, out_all, D, ("x", "z", "y")),
            fetch.from_this_chip(narrow=((qkv, qkv_all), (out, out_all))),
        ]
    )
    wires.finish_sends()


def gather_narrow(qkv, out):
    rows = (4, 4, 16)
    qkv, out = wired_call(
        gather_narrow_kernel,
        [shape(2, 2, *rows, 2048), shape(2, 2, *rows, D)],
        (qkv.reshape(*rows, 2048), out.reshape(*rows, D)),
        1,
        "gather_narrow",
        2 * 11 + 2,
        2,
    )
    return qkv.reshape(D, 2048), out.reshape(D, D)


WIDE = (
    (0, RowsByShard(HALF_FF), ("z", "x", "y"), ("y", "x", "z")),
    (1, RowsByShard(HALF_FF), ("x", "y", "z"), ("z", "y", "x")),
    (2, ColumnsByY(144), ("y", "z", "x"), ("x", "z", "y")),
)
NARROW = (
    (0, RowsByPlane(0, 1024), ("z", "x", "y"), ("z", "y", "x")),
    (0, RowsByPlane(1024, 1024), ("x", "y", "z"), ("x", "z", "y")),
    (1, ColumnsByY(32), ("y", "z", "x"), ("x", "z", "y")),
)
WIDE_DIMS = ((2, 2, 4, 4, 16, HALF_FF), (2, 2, 4, 4, 16, HALF_FF), (2, 4, 2, 144, D))
NARROW_DIMS = ((2, 4, 4, 16, 2048), (2, 4, 2, 32, D))
PIECE_DIMS = ((16, HALF_FF), (16, HALF_FF), (144, 256))


def slot_shapes(parts):
    found = []
    for _, kind, order, _ in parts:
        at = {}
        for axis in order:
            at = fix(at, axis, 0)
            found.append((6, *kind.open_dims(at), *kind.tail_dims({**at, "half": 0})))
    return found


def each_block(kind, at, body):
    dims = kind.open_dims(at)

    def step(i, _):
        inner, rest = ([], i)
        for n in reversed(dims):
            inner.insert(0, rest % n)
            rest = rest // n
        picks = iter(inner)
        lead = [next(picks) if o is None else o for o in kind.order(at)]
        body((*lead, *kind.tail(at)), (*inner, slice(None), slice(None)))
        return 0

    lax.fori_loop(0, math.prod(dims), step, 0)


def reduce_one(here, wires, kind, grad, total, slots, order):
    at = {}
    for step, axis in enumerate(order):
        source, slot = (grad if step == 0 else total, slots[step])
        (right_place, right), (left_place, left) = (here.along(axis, 1), here.along(axis, 3))
        far_place, _ = here.along(axis, 2)
        mine = fix(at, axis, getattr(here, axis))

        def half_of(place, half):
            return {**fix(at, axis, place), "half": half}

        relays = [
            wires.push(kind.view(source, half_of(far_place, 0)), slot.at[4], right),
            wires.push(kind.view(source, half_of(far_place, 1)), slot.at[5], left),
        ]
        arriving = [
            wires.push(kind.view(source, half_of(right_place, 1)), slot.at[1], right),
            wires.push(kind.view(source, half_of(left_place, 0)), slot.at[2], left),
        ]
        kept = []
        if step == 0:
            for where in (half_of(right_place, 0), half_of(left_place, 1), mine):
                kept.append(wires.move(kind.view(source, where), kind.view(total, where)))
        yield
        for j, place, half, target, onward in (
            (4, right_place, 0, 0, right),
            (5, left_place, 1, 3, left),
        ):
            if kept:
                kept.pop(0).wait()
            arrive([relays[j - 4]])

            def pass_on(whole, part):
                value = slot[(j, *part)].astype(F32) + total[whole].astype(F32)
                slot[(j, *part)] = value.astype(BF16)

            each_block(kind, half_of(place, half), pass_on)
            arriving.append(wires.push(slot.at[j], slot.at[target], onward))
        yield
        if kept:
            kept.pop(0).wait()
        arrive(arriving)
        for half in range(2):

            def add_up(whole, part):
                value = total[whole].astype(F32) + slot[(half, *part)].astype(F32)
                total[whole] = (value + slot[(2 + half, *part)].astype(F32)).astype(BF16)

            each_block(kind, {**mine, "half": half}, add_up)
        at = mine


def reduce_weights_kernel(*refs):
    pieces, grads, gains = (refs[:3], refs[3:5], refs[5])
    gate_near, up_near, gate_beside, up_beside, down_out, qkv_out, out_out, gains_out = refs[6:14]
    totals = refs[14:16]
    slots = refs[16:25]
    gain_slots, sends, receives, moves = refs[25:]
    wide_near = (gate_near, up_near, down_out)
    narrow_near = (qkv_out, out_out)
    besides = (gate_beside, up_beside)

    here = Place()
    wires = Wires(sends, receives, moves)
    core = here.core
    sibling = here.sibling()
    greet([here.along(a, s)[1] for a in ("x", "y", "z") for s in (1, 3, 2)] + [sibling])
    at = {"zh": here.zh, "zl": here.zl, "x": here.x, "y": here.y}

    def all_gains():
        total = gains[...]
        for stage, axis in enumerate(("core", "x", "y", "z")):
            me = getattr(here, axis)
            gain_slots[stage, me] = total
            source = gain_slots.at[stage, me]
            if axis == "core":
                others = [sibling]
            else:
                others = [here.along(axis, s)[1] for s in (1, 3, 2)]
            copies = [wires.push(source, source, device) for device in others]
            yield
            yield
            arrive(copies)
            total = gain_slots[stage, 0] + gain_slots[stage, 1]
            if axis != "core":
                total = total + gain_slots[stage, 2] + gain_slots[stage, 3]
        gains_out[...] = total

    def narrow(p):
        g, kind, order, back = NARROW[p]
        yield from reduce_one(
            here, wires, kind, grads[g], totals[g], slots[3 * p : 3 * p + 3], order
        )
        own = wires.move(kind.view(totals[g], at), kind.view(narrow_near[g], at, 1))
        yield
        own.wait()
        yield from spread(here, wires, kind, narrow_near[g], at, back, 1)

    def wide(p):
        _, kind, _, back = WIDE[p]
        own = wires.move(pieces[p], kind.view(wide_near[p], at, 1))
        own.wait()
        yield from spread(here, wires, kind, wide_near[p], at, back, 1)
        if p < 2:
            copies = [wires.push(wide_near[p].at[1 - core], besides[p], sibling)]
            yield
            arrive(copies)

    in_turn([narrow(p) for p in range(3)] + [wide(p) for p in range(3)] + [all_gains()])
    wires.finish_sends()


def reduce_weights(pieces, qkv, out, gains):
    ins = [*pieces, qkv.reshape(NARROW_DIMS[0]), out.reshape(NARROW_DIMS[1]), gains]
    outs = [
        shape(*WIDE_DIMS[0][1:]),
        shape(*WIDE_DIMS[1][1:]),
        shape(*WIDE_DIMS[0][2:]),
        shape(*WIDE_DIMS[1][2:]),
        shape(*WIDE_DIMS[2][1:]),
        shape(*NARROW_DIMS[0][1:]),
        shape(*NARROW_DIMS[1][1:]),
        shape(*gains.shape, dtype=F32),
    ]
    scratch = [pltpu.VMEM(d, BF16) for d in NARROW_DIMS]
    scratch += [pltpu.VMEM(s, BF16) for s in slot_shapes(NARROW)]
    scratch += [pltpu.VMEM((4, 4, *gains.shape), F32)]
    done = wired_call(
        reduce_weights_kernel,
        outs,
        ins,
        2,
        "reduce_weights",
        10 + 3 * 18 + 6 * 9 + 2,
        3 * 4 + 3,
        scratch,
        [ANY] * 5 + [VMEM],
        [ANY] * 7 + [VMEM],
        vmem=40 * MIB,
    )
    core = lax.axis_index("fsdp") % 2

    def joined(near, beside):
        own = lax.dynamic_index_in_dim(near, core, 0, keepdims=False).reshape(256, HALF_FF)
        beside = beside.reshape(256, HALF_FF)
        first, second = (jnp.where(core == 0, own, beside), jnp.where(core == 0, beside, own))
        pieces = [f[:, r * SLICE : (r + 1) * SLICE] for r in range(2) for f in (first, second)]
        return jnp.concatenate(pieces, axis=1)

    gate, up = (joined(done[0], done[2]), joined(done[1], done[3]))
    down, qkv, out, gains = done[4:]
    return (
        qkv.reshape(256, 2048),
        out.reshape(256, D),
        gate,
        up,
        down.reshape(SLICE, D),
        gains,
    )


def head_columns(head):
    return pl.ds(pl.multiple_of(head * 128, 128), 128)


def to_heads_kernel(with_keys, *refs):
    if with_keys:
        query, key_value, query_out, key_value_out, sends, receives, moves = refs
    else:
        query, query_out, sends, receives, moves = refs
    here = Place()
    wires = Wires(sends, receives, moves)
    me = here.ctx
    quarter, seat = (me // QUARTER, me % QUARTER)
    near = [quarter * QUARTER + (seat + s) % QUARTER for s in range(1, QUARTER)]
    far = [(me + s) % RING for s in range(1, RING)]
    greet([(k, here.fsdp) for k in (far if with_keys else near)])
    copies = [
        wires.push(query.at[:, head_columns(k % QUARTER)], query_out.at[seat], (k, here.fsdp))
        for k in near
    ]
    kept = [wires.move(query.at[:, head_columns(seat)], query_out.at[seat])]
    if with_keys:
        copies += [
            wires.push(
                key_value.at[:, head_columns(k % QUARTER)], key_value_out.at[me], (k, here.fsdp)
            )
            for k in far
        ]
        kept.append(wires.move(key_value.at[:, head_columns(seat)], key_value_out.at[me]))
    arrive(copies)
    for copy in kept:
        copy.wait()
    wires.finish_sends()


def to_heads(query, key_value=None):
    ins = [query] + ([] if key_value is None else [key_value])
    outs = [shape(QUARTER, TOKENS, 128)]
    if key_value is not None:
        outs.append(shape(RING, TOKENS, 128))
    copies = 7 if key_value is None else 38
    return wired_call(
        functools.partial(to_heads_kernel, key_value is not None),
        outs,
        ins,
        3 if key_value is None else 4,
        "to_heads",
        copies,
        2,
    )


def to_tokens_kernel(with_keys, *refs):
    if with_keys:
        query, key_value, query_out, key_value_out, sends, receives, moves = refs
    else:
        query, query_out, sends, receives, moves = refs
    here = Place()
    wires = Wires(sends, receives, moves)
    me = here.ctx
    quarter, seat = (me // QUARTER, me % QUARTER)
    near = [quarter * QUARTER + (seat + s) % QUARTER for s in range(1, QUARTER)]
    far = [(me + s) % RING for s in range(1, RING)]
    greet([(k, here.fsdp) for k in (far if with_keys else near)])
    columns = query_out.at[:, head_columns(seat)]
    copies = [wires.push(query.at[k % QUARTER], columns, (k, here.fsdp)) for k in near]
    kept = [wires.move(query.at[seat], columns)]
    if with_keys:
        copies += [
            wires.push(key_value.at[k], key_value_out.at[me], (k, here.fsdp)) for k in far
        ]
        kept.append(wires.move(key_value.at[me], key_value_out.at[me]))
    arrive(copies)
    for copy in kept:
        copy.wait()
    wires.finish_sends()


def to_tokens(query, key_value=None):
    ins = [query] + ([] if key_value is None else [key_value])
    outs = [shape(TOKENS, D)]
    if key_value is not None:
        outs.append(shape(RING, TOKENS, 128))
    copies = 7 if key_value is None else 38
    return wired_call(
        functools.partial(to_tokens_kernel, key_value is not None),
        outs,
        ins,
        5 if key_value is None else 6,
        "to_tokens",
        copies,
        2,
    )


def half_columns(r, core):
    return pl.ds(pl.multiple_of(r * 512 + core * 256, 256), 256)


def share_kernel(whole, halved, *refs):
    n = whole + halved
    ins, outs = (refs[:n], refs[n : 2 * n])
    here = Place()
    wires = Wires(*refs[2 * n :])
    core = here.core
    sibling = here.sibling()
    greet([sibling])
    copies, kept = ([], [])
    for source, target in zip(ins[:whole], outs[:whole]):
        copies.append(wires.push(source, target.at[core], sibling))
        kept.append(wires.move(source, target.at[core]))
    for source, target in zip(ins[whole:], outs[whole:]):
        for r in range(2):
            place = target.at[core, :, pl.ds(r * 256, 256)]
            copies.append(wires.push(source.at[:, half_columns(r, 1 - core)], place, sibling))
            kept.append(wires.move(source.at[:, half_columns(r, core)], place))
    arrive(copies)
    for copy in kept:
        copy.wait()
    wires.finish_sends()


def share(whole, halved, collective_id):
    outs = [shape(2, *a.shape, dtype=a.dtype) for a in whole]
    outs += [shape(2, a.shape[0], 512, dtype=a.dtype) for a in halved]
    count = len(whole) + 2 * len(halved)
    done = wired_call(
        functools.partial(share_kernel, len(whole), len(halved)),
        outs,
        [*whole, *halved],
        collective_id,
        "share",
        count,
        count,
    )
    return [a.reshape(2 * a.shape[1], a.shape[2]) for a in done]


def hand_over_kernel(count, *refs):
    ins, outs = (refs[:count], refs[count : 2 * count])
    here = Place()
    wires = Wires(*refs[2 * count :])
    sibling = here.sibling()
    greet([sibling])
    copies = [wires.push(i.at[1 - here.core], o, sibling) for i, o in zip(ins, outs)]
    arrive(copies)
    wires.finish_sends()


def hand_over(partials, collective_id):
    return wired_call(
        functools.partial(hand_over_kernel, len(partials)),
        [shape(*a.shape[1:], dtype=a.dtype) for a in partials],
        partials,
        collective_id,
        "hand_over",
        len(partials),
        0,
    )


def nt(left, right):
    return lax.dot_general(left, right, (((1,), (1,)), ((), ())), preferred_element_type=F32)


def nn(left, right):
    return lax.dot_general(left, right, (((1,), (0,)), ((), ())), preferred_element_type=F32)


def query_block(ref, t):
    block = ref[t].astype(F32)
    both = jnp.concatenate([block, pltpu.roll(block, 64, 1)], axis=0)
    low = lax.broadcasted_iota(jnp.int32, (128, 128), 1) < 64
    return jnp.where(low, both, 0.0)


def query_pair(ref, u):
    return [query_block(ref, 2 * u), query_block(ref, 2 * u + 1)]


def first_allowed(position, starts_ref):
    begin = jnp.zeros_like(position)
    for n in range(4):
        begin = jnp.maximum(begin, jnp.where(starts_ref[n] <= position, starts_ref[n], 0))
    return begin


def heads_beside(rows):
    low = lax.broadcasted_iota(jnp.int32, (64, 128), 1) < 64
    return jnp.where(low, rows[:64], pltpu.roll(rows[64:], 64, 1)).astype(BF16)


def attend_task(
    counts, starts_ref, query_at_ref, key_at_ref, query_ref, key_value_ref, out_ref, exact_ref,
    sum_ref, value_ref,
):
    def values(j, _):
        rows = pl.ds(pl.multiple_of(j * 256, 256), 256)
        block = pltpu.roll(key_value_ref[rows, :].astype(F32), 64, 1)
        low = lax.broadcasted_iota(jnp.int32, (256, 128), 1) < 64
        value_ref[rows, :] = jnp.where(low, block, 1.0).astype(BF16)
        return 0

    def blocks(u, _):
        queries = jnp.concatenate(query_pair(query_ref, u), axis=0).astype(BF16)
        position = query_at_ref[pl.ds(pl.multiple_of(u * 256, 256), 256), :]
        begin = first_allowed(position, starts_ref)

        def tile(j, total):
            rows = pl.ds(pl.multiple_of(j * KEY_TILE, KEY_TILE), KEY_TILE)
            scores = nt(queries, key_value_ref[rows, :])
            key = key_at_ref[:, rows]
            allowed = (key <= position) & (key >= begin)
            weight = jnp.where(allowed, jnp.exp2(scores * SCORE_TO_EXP2), 0.0)
            return total + nn(weight.astype(BF16), value_ref[rows, :])

        total = lax.fori_loop(0, SEQ // KEY_TILE, tile, jnp.zeros((256, 128), F32))
        attended = total / pltpu.roll(total, 64, 1)
        low = lax.broadcasted_iota(jnp.int32, (256, 128), 1) < 64
        attended = jnp.where(low, attended, 0.0)
        for n in range(2):
            rows = slice(128 * n, 128 * n + 128)
            exact_ref[2 * u + n] = attended[rows]
            out_ref[2 * u + n] = heads_beside(attended[rows])
            sum_ref[2 * u + n] = jnp.transpose(total[rows])[64:72]
        return 0

    lax.fori_loop(0, SEQ // 256, values, 0)
    first = 0
    for count in counts:
        lax.fori_loop(first, first + count, blocks, 0)
        first += count
        yield


def attend_kernel(
    starts, query_at, key_at, query, key_value, gate, up, down, attended, exact, sums, gate_all,
    up_all, down_all, value_ref, sends, receives, moves,
):
    wires = Wires(sends, receives, moves)
    fetch = Fetch(Place(), wires)
    fetch.greet()
    in_turn(
        [
            fetch.wide(gate, gate_all, ("y", "x", "z")),
            fetch.wide(up, up_all, ("z", "y", "x")),
            fetch.down(down, down_all, ("x", "z", "y")),
            fetch.from_this_chip(wide=((gate, gate_all), (up, up_all)), down=((down, down_all),)),
            attend_task(
                (2, 1, 1, 1, 2, 1), starts, query_at, key_at, query, key_value, attended, exact,
                sums, value_ref,
            ),
        ]
    )
    wires.finish_sends()


def attend(starts, query_at, key_at, queries, key_values, gate, up, down):
    rows = (4, 4, 16)
    ins = (
        starts,
        query_at.reshape(-1, 1),
        key_at.reshape(1, -1),
        queries,
        key_values,
        gate.reshape(*rows, FF),
        up.reshape(*rows, FF),
        down.reshape(4, 2, 144, D),
    )
    outs = [
        shape(16, 64, 128),
        shape(16, 128, 128, dtype=F32),
        shape(16, 8, 128, dtype=F32),
        shape(2, 2, *rows, HALF_FF),
        shape(2, 2, *rows, HALF_FF),
        shape(2, 4, 2, 144, D),
    ]
    attended, exact, sums, gate, up, down = wired_call(
        attend_kernel,
        outs,
        ins,
        10,
        "attend",
        2 * 11 + 10 + 4,
        5,
        [pltpu.VMEM((SEQ, 128), BF16)],
        [SMEM] + [VMEM] * 4 + [ANY] * 3,
        [VMEM] * 3 + [ANY] * 3,
        vmem=40 * MIB,
    )
    weights = (gate.reshape(D, HALF_FF), up.reshape(D, HALF_FF), down.reshape(HALF_FF, D))
    return attended, exact, sums, weights


def attend_back_task(
    counts, starts_ref, query_at_ref, key_at_ref, query_ref, key_value_ref, grad_ref, exact_ref,
    sum_ref, query_grad_ref, key_value_grad_ref, across_ref, total_ref,
):
    total_ref[...] = jnp.zeros_like(total_ref)

    def turn(j, _):
        rows = pl.ds(pl.multiple_of(j * 128, 128), 128)
        across_ref[:, rows] = jnp.transpose(key_value_ref[rows, :].astype(F32)).astype(BF16)
        return 0

    def blocks(u, _):
        queries, grads = (query_pair(query_ref, u), query_pair(grad_ref, u))
        delta = [
            jnp.sum(jnp.transpose(grad * exact_ref[2 * u + n]), axis=0, keepdims=True)
            for n, grad in enumerate(grads)
        ]
        delta = jnp.concatenate(delta, axis=1)
        total_exp2 = jnp.concatenate(
            [jnp.log2(sum_ref[2 * u + n][0:1]) for n in range(2)], axis=1
        )
        grads = [pltpu.roll(grad, 64, 1) for grad in grads]
        both = jnp.concatenate(queries + grads, axis=0).astype(BF16)
        position = query_at_ref[:, pl.ds(pl.multiple_of(u * 256, 256), 256)]
        begin = first_allowed(position, starts_ref)

        def tile(j, query_grad):
            rows = pl.ds(pl.multiple_of(j * KEY_TILE_BACK, KEY_TILE_BACK), KEY_TILE_BACK)
            products = nt(key_value_ref[rows, :], both)
            key = key_at_ref[rows, :]
            allowed = (key <= position) & (key >= begin)
            prob = jnp.where(
                allowed, jnp.exp2(products[:, :256] * SCORE_TO_EXP2 - total_exp2), 0.0
            )
            score = (prob * (products[:, 256:] - delta)).astype(BF16)
            side = jnp.concatenate([score, prob.astype(BF16)], axis=1)
            total_ref[rows, :] += nn(side, both)
            return query_grad + nn(across_ref[:, rows], score)

        query_grad = lax.fori_loop(
            0, SEQ // KEY_TILE_BACK, tile, jnp.zeros((128, 256), F32)
        )
        for n in range(2):
            rows = jnp.transpose(query_grad[:, 128 * n : 128 * n + 128])
            query_grad_ref[2 * u + n] = heads_beside(rows * float(HEAD_SIZE) ** (-0.5))
        return 0

    def put_back(j, _):
        rows = pl.ds(pl.multiple_of(j * 256, 256), 256)
        low = lax.broadcasted_iota(jnp.int32, (256, 128), 1) < 64
        scale = jnp.where(low, float(HEAD_SIZE) ** (-0.5), 1.0)
        key_value_grad_ref[rows, :] = (total_ref[rows, :] * scale).astype(BF16)
        return 0

    lax.fori_loop(0, SEQ // 128, turn, 0)
    first = 0
    for count in counts:
        lax.fori_loop(first, first + count, blocks, 0)
        first += count
        yield
    lax.fori_loop(0, SEQ // 256, put_back, 0)


def attend_back_kernel(*refs):
    attention, grads = (refs[:8], refs[8:11])
    outs, pieces = (refs[11:13], refs[13:16])
    scratch, totals, slots = (refs[16:18], refs[18:21], refs[21:30])
    here = Place()
    wires = Wires(*refs[30:])
    greet([here.along(a, s)[1] for a in ("x", "y", "z") for s in (1, 3)])
    at = {"zh": here.zh, "zl": here.zl, "x": here.x, "y": here.y}

    def reduce(p):
        _, kind, order, _ = WIDE[p]
        yield from reduce_one(
            here, wires, kind, grads[p], totals[p], slots[3 * p : 3 * p + 3], order
        )
        own = wires.move(kind.view(totals[p], at), pieces[p])
        yield
        own.wait()

    in_turn(
        [reduce(p) for p in range(3)]
        + [attend_back_task((3, 3, 1, 1), *attention, *outs, *scratch)]
    )
    wires.finish_sends()


def attend_back(starts, query_at, key_at, queries, key_values, grads, exact, sums, wide):
    ins = [starts, query_at.reshape(1, -1), key_at.reshape(-1, 1), queries, key_values, grads]
    ins += [exact, sums, *(a.reshape(d) for a, d in zip(wide, WIDE_DIMS))]
    scratch = [pltpu.VMEM((128, SEQ), BF16), pltpu.VMEM((SEQ, 128), F32)]
    scratch += [pltpu.VMEM(d, BF16) for d in WIDE_DIMS]
    scratch += [pltpu.VMEM(s, BF16) for s in slot_shapes(WIDE)]
    query_grad, key_value_grad, *pieces = wired_call(
        attend_back_kernel,
        [shape(16, 64, 128), shape(SEQ, 128), *(shape(*d) for d in PIECE_DIMS)],
        ins,
        11,
        "attend_back",
        3 * 18,
        3 * 4,
        scratch,
        [SMEM] + [VMEM] * 7 + [ANY] * 3,
        [VMEM] * 2 + [ANY] * 3,
        vmem=56 * MIB,
    )
    return query_grad, key_value_grad, pieces


def rms_norm(values, gain_row):
    return (
        values * lax.rsqrt(jnp.mean(values * values, axis=-1, keepdims=True) + EPSILON) * gain_row
    )


def rotate(values, positions):
    half_width = values.shape[-1] // 2
    frequency = ROPE_BASE ** (-2.0 * jnp.arange(half_width, dtype=F32) / values.shape[-1])
    angles = positions.astype(F32)[:, None] * frequency[None, :]
    cosine = jnp.cos(angles)[:, None, :]
    sine_part = jnp.sin(angles)[:, None, :]
    first_half = values[..., :half_width]
    second_half = values[..., half_width:]
    return jnp.concatenate(
        [
            first_half * cosine - second_half * sine_part,
            second_half * cosine + first_half * sine_part,
        ],
        axis=-1,
    )


def outer_sum(left, right):
    return lax.dot_general(
        left, right, (((0,), (0,)), ((), ())), preferred_element_type=F32
    ).astype(BF16)


def matmul(left, right):
    return jnp.dot(left, right, preferred_element_type=F32)


def positions_at(block_order, first_row, total_row_count, half_rows):
    row_ids = first_row + jnp.arange(total_row_count, dtype=jnp.int32)
    blocks = row_ids // half_rows
    lookup = jnp.arange(block_order.shape[0], dtype=jnp.int32)
    picked = jnp.sum(jnp.where(blocks[:, None] == lookup[None, :], block_order[None, :], 0), axis=1)
    return picked * half_rows + row_ids % half_rows


def per_device(
    inputs,
    cotangent,
    qkv_weight,
    out_weight,
    gate_weight,
    up_weight,
    down_weight,
    gain_attn,
    gain_query,
    gain_key,
    gain_ffn,
    block_order,
    doc_starts,
):
    cycle_index = lax.axis_index("ctx")
    core = lax.axis_index("fsdp") % 2
    qkv_all, out_all = gather_narrow(qkv_weight, out_weight)
    starts = doc_starts[0]
    positions = positions_at(block_order, cycle_index * TOKENS, TOKENS, TOKENS // 2)
    key_at = positions_at(block_order, 0, SEQ, TOKENS // 2)
    first_query = (cycle_index // QUARTER) * QUARTER * TOKENS
    query_at = lax.dynamic_slice_in_dim(key_at, first_query, QUARTER * TOKENS).reshape(16, 1, 64)
    query_at = jnp.broadcast_to(query_at, (16, 2, 64))
    places = (starts, query_at, key_at)

    resid_in = inputs[0].astype(F32)
    normed, norm_in_pull = jax.vjp(rms_norm, resid_in, gain_attn)
    normed_low = normed.astype(BF16)
    projected = matmul(normed_low, qkv_all)
    split_position = (QUERY_HEADS + KEY_VALUE_HEADS) * HEAD_SIZE

    def query_key(leading_columns, scale_query, scale_key):
        queries = leading_columns[:, : QUERY_HEADS * HEAD_SIZE].reshape(
            TOKENS, QUERY_HEADS, HEAD_SIZE
        )
        keys = leading_columns[:, QUERY_HEADS * HEAD_SIZE :].reshape(
            TOKENS, KEY_VALUE_HEADS, HEAD_SIZE
        )
        return (
            rotate(rms_norm(queries, scale_query), positions),
            rotate(rms_norm(keys, scale_key), positions),
        )

    (queries, keys), qk_pull = jax.vjp(
        query_key, projected[:, :split_position], gain_query, gain_key
    )
    values = projected[:, split_position:].reshape(TOKENS, KEY_VALUE_HEADS, HEAD_SIZE)
    key_values = jnp.concatenate([keys, values], axis=-1).astype(BF16).reshape(TOKENS, D)
    query_part, key_value_part = to_heads(queries.astype(BF16).reshape(TOKENS, D), key_values)
    query_part = query_part.reshape(16, 64, 128)
    key_value_part = key_value_part.reshape(SEQ, 128)
    attended, exact, sums, (gate_all, up_all, down_all) = attend(
        *places, query_part, key_value_part, gate_weight, up_weight, down_weight
    )
    (attended_low,) = to_tokens(attended.reshape(QUARTER, TOKENS, 128))

    residual = resid_in + matmul(attended_low, out_all)
    normed_ffn, norm_ffn_pull = jax.vjp(rms_norm, residual, gain_ffn)
    grad_out = cotangent[0]
    ffn_pair, cotangent_pair, normed_half, attended_half = share(
        [normed_ffn.astype(BF16), grad_out], [normed_low, attended_low], 7
    )
    gate_proj = matmul(ffn_pair, gate_all)
    up_proj = matmul(ffn_pair, up_all)
    hidden, gating_pull = jax.vjp(
        lambda gate_in, up_in: jax.nn.silu(gate_in) * up_in, gate_proj, up_proj
    )
    hidden_low = hidden.astype(BF16)
    out_partial = matmul(hidden_low, down_all).reshape(2, TOKENS, D)
    grad_hidden = matmul(cotangent_pair, down_all.T)
    grad_gate, grad_up = gating_pull(grad_hidden)
    gate_low = grad_gate.astype(BF16)
    up_low = grad_up.astype(BF16)
    ffn_partial = (matmul(gate_low, gate_all.T) + matmul(up_low, up_all.T)).reshape(2, TOKENS, D)
    out_rest, ffn_rest = hand_over([out_partial, ffn_partial], 8)

    def mine(pair):
        return lax.dynamic_index_in_dim(pair, core, 0, keepdims=False)

    outputs = residual + mine(out_partial) + out_rest
    grad_resid_ffn, grad_gain_ffn = norm_ffn_pull(mine(ffn_partial) + ffn_rest)
    grad_resid = grad_out.astype(F32) + grad_resid_ffn
    branch_low = grad_resid.astype(BF16)
    grad_attended = matmul(branch_low, out_all.T).astype(BF16)
    (grad_part,) = to_heads(grad_attended)
    query_grad, key_value_grad, pieces = attend_back(
        *places,
        query_part,
        key_value_part,
        grad_part.reshape(16, 64, 128),
        exact,
        sums,
        (
            outer_sum(ffn_pair, gate_low),
            outer_sum(ffn_pair, up_low),
            outer_sum(hidden_low, cotangent_pair),
        ),
    )
    query_grad, key_value_grad = to_tokens(
        query_grad.reshape(QUARTER, TOKENS, 128), key_value_grad.reshape(RING, TOKENS, 128)
    )
    key_value_grad = key_value_grad.reshape(4, KEY_VALUE_HEADS, TOKENS, 128)
    key_value_grad = jnp.transpose(jnp.sum(key_value_grad.astype(F32), axis=0), (1, 0, 2))
    grad_front, grad_gain_query, grad_gain_key = qk_pull(
        (
            query_grad.astype(F32).reshape(TOKENS, QUERY_HEADS, HEAD_SIZE),
            key_value_grad[..., :HEAD_SIZE],
        )
    )
    grad_values = key_value_grad[..., HEAD_SIZE:].reshape(TOKENS, KEY_VALUE_HEADS * HEAD_SIZE)
    grad_projected = jnp.concatenate([grad_front, grad_values], axis=1).astype(BF16)
    grad_normed = matmul(grad_projected, qkv_all.T)
    grad_input_norm, grad_gain_attn = norm_in_pull(grad_normed)
    grad_inputs = (grad_resid + grad_input_norm).astype(BF16)

    projected_pair, branch_pair = share([grad_projected, branch_low], [], 9)
    gains = jnp.concatenate([grad_gain_attn, grad_gain_ffn, grad_gain_query, grad_gain_key])
    gains = jnp.pad(gains, (0, 24 * 128 - gains.shape[0])).reshape(24, 128)
    grad_qkv, grad_out_weight, grad_gate_weight, grad_up_weight, grad_down, gains = reduce_weights(
        pieces,
        outer_sum(normed_half, projected_pair),
        outer_sum(attended_half, branch_pair),
        gains,
    )
    gains = gains.reshape(-1)
    return (
        outputs.astype(BF16)[None],
        grad_inputs[None],
        grad_qkv.astype(F32),
        grad_out_weight.astype(F32),
        grad_gate_weight.astype(F32),
        grad_up_weight.astype(F32),
        grad_down.astype(F32),
        gains[:D],
        gains[2 * D : 2 * D + HEAD_SIZE],
        gains[2 * D + HEAD_SIZE : 2 * D + 2 * HEAD_SIZE],
        gains[D : 2 * D],
    )


def solution(mesh):
    in_specs = (
        P("fsdp", "ctx", None),
        P("fsdp", "ctx", None),
        P("fsdp", None),
        P("fsdp", None),
        P("fsdp", None),
        P("fsdp", None),
        P("fsdp", None),
        P(),
        P(),
        P(),
        P(),
        P(),
        P("fsdp", None),
    )
    out_specs = (
        P("fsdp", "ctx", None),
        P("fsdp", "ctx", None),
        P("fsdp", None),
        P("fsdp", None),
        P("fsdp", None),
        P("fsdp", None),
        P("fsdp", None),
        P(),
        P(),
        P(),
        P(),
    )
    return jax.shard_map(
        per_device, mesh=mesh, in_specs=in_specs, out_specs=out_specs, check_vma=False
    )
```

```python
import functools
import math

import jax
import jax.numpy as jnp
from jax import lax
from jax.experimental import pallas as pl
from jax.experimental.pallas import tpu as pltpu
from jax.sharding import PartitionSpec as P

QUERY_HEADS = 16
KEY_VALUE_HEADS = 8
HEAD_SIZE = 64
FF = 4608
D = 1024
TOKENS = 128
RING = 32
QUARTER = 8
SLICE = 1152
HALF_FF = FF // 2
KEY_TILE = 1024
KEY_TILE_BACK = 1024
SEQ = 4096

EPSILON = 1e-05
ROPE_BASE = 1000000.0
SCORE_TO_EXP2 = float(HEAD_SIZE) ** (-0.5) * math.log2(math.e)

MESH = pl.DeviceIdType.MESH
ANY = pl.BlockSpec(memory_space=pl.ANY)
VMEM = pl.BlockSpec(memory_space=pltpu.VMEM)
SMEM = pl.BlockSpec(memory_space=pltpu.SMEM)
BF16 = jnp.bfloat16
F32 = jnp.float32
MIB = 1 << 20
STEPS = (1, 3, 2)


class Place:
    def __init__(self):
        self.ctx, self.fsdp = (lax.axis_index("ctx"), lax.axis_index("fsdp"))
        self.zl, self.x, self.y = (self.ctx // 16, (self.ctx // 4) % 4, self.ctx % 4)
        self.zh, self.core = (self.fsdp // 2, self.fsdp % 2)
        self.z = self.zh * 2 + self.zl

    def device(self, x=None, y=None, z=None, core=None):
        x = self.x if x is None else x
        y = self.y if y is None else y
        z = self.z if z is None else z
        core = self.core if core is None else core
        return ((z % 2) * 16 + x * 4 + y, (z // 2) * 2 + core)

    def sibling(self):
        return self.device(core=1 - self.core)

    def along(self, axis, step):
        coordinate = (getattr(self, axis) + step) % 4
        return coordinate, self.device(**{axis: coordinate})


class Wires:
    def __init__(self, sends, receives, locals_=None):
        self.sends, self.receives, self.locals_ = (sends, receives, locals_)
        self.pushed, self.moved = ([], 0)

    def push(self, source, target, device):
        at = len(self.pushed)
        copy = pltpu.make_async_remote_copy(
            src_ref=source,
            dst_ref=target,
            send_sem=self.sends.at[at],
            recv_sem=self.receives.at[at],
            device_id=device,
            device_id_type=MESH,
        )
        copy.start()
        self.pushed.append(copy)
        return copy

    def move(self, source, target):
        copy = pltpu.make_async_copy(source, target, self.locals_.at[self.moved])
        copy.start()
        self.moved += 1
        return copy

    def finish_sends(self):
        for copy in self.pushed:
            copy.wait_send()


def arrive(copies):
    for copy in copies:
        copy.wait_recv()


def greet(devices):
    barrier = pltpu.get_barrier_semaphore()
    for device in devices:
        pl.semaphore_signal(barrier, inc=1, device_id=device, device_id_type=MESH)
    pl.semaphore_wait(barrier, len(devices))


def wired_call(kernel, outs, ins, collective_id, name, copies, moves, scratch=(), in_specs=None,
               out_specs=None, vmem=32 * MIB, aliases=None):
    return pl.pallas_call(
        kernel,
        out_shape=outs,
        in_specs=[ANY] * len(ins) if in_specs is None else in_specs,
        out_specs=[ANY] * len(outs) if out_specs is None else out_specs,
        scratch_shapes=[
            *scratch,
            pltpu.SemaphoreType.DMA((copies,)),
            pltpu.SemaphoreType.DMA((copies,)),
            pltpu.SemaphoreType.DMA((max(moves, 1),)),
        ],
        compiler_params=pltpu.CompilerParams(
            collective_id=collective_id, has_side_effects=True, vmem_limit_bytes=vmem
        ),
        name=name,
        input_output_aliases=aliases or {},
    )(*ins)


def shape(*dims, dtype=BF16):
    return jax.ShapeDtypeStruct(dims, dtype)


class Pieces:
    def view(self, ref, at, skip=0):
        lead = [slice(None) if i is None else i for i in self.order(at)[skip:]]
        return ref.at[(*lead, *self.tail(at))]

    def open_dims(self, at):
        return tuple(n for n, i in zip(self.lead, self.order(at)) if i is None)

    def tail(self, at):
        first, width = self.columns(at)
        if not isinstance(first, int):
            first = pl.multiple_of(first, 128)
        return (slice(None), pl.ds(first, width))

    def tail_dims(self, at):
        return (self.rows, self.columns(at)[1])


def halved(first, width, at):
    if "half" not in at:
        return first, width
    return first + at["half"] * (width // 2), width // 2


class RowsByShard(Pieces):
    lead, rows = ((2, 2, 4, 4), 16)

    def __init__(self, width):
        self.width = width

    def order(self, at):
        return [at.get("zh"), at.get("zl"), at.get("x"), at.get("y")]

    def columns(self, at):
        return halved(0, self.width, at)


class RowsByPlane(Pieces):
    lead, rows = ((2, 4, 4), 16)

    def __init__(self, first, width):
        self.first, self.width = (first, width)

    def order(self, at):
        return [at.get("zh"), at.get("x"), at.get("y")]

    def columns(self, at):
        if "zl" not in at:
            return halved(self.first, self.width, at)
        half = self.width // 2
        return halved(self.first + half * at["zl"], half, at)


class ColumnsByY(Pieces):
    lead = (2, 4, 2)

    def __init__(self, rows):
        self.rows = rows

    def order(self, at):
        return [at.get("zh"), at.get("x"), at.get("zl")]

    def columns(self, at):
        return halved(at["y"] * 256, 256, at) if "y" in at else halved(0, D, at)


class ShardsByCore(Pieces):
    lead, rows = ((2, 2, 4, 4), 16)

    def __init__(self, width):
        self.width = width

    def order(self, at):
        return [at.get("zh"), at.get("half"), at.get("x"), at.get("y")]

    def columns(self, at):
        half = self.width // 2
        return (half * at["zl"], half) if "zl" in at else (0, self.width)


class OneCore(RowsByPlane):
    lead = (2, 2, 4, 4)

    def __init__(self, first, width, core):
        super().__init__(first, width)
        self.core = core

    def order(self, at):
        return [at.get("zh"), self.core, at.get("x"), at.get("y")]


def fix(at, axis, coordinate):
    if axis == "z":
        return {**at, "zh": coordinate // 2, "zl": coordinate % 2}
    return {**at, axis: coordinate}


def without(at, axis):
    return {a: i for a, i in at.items() if a != ("zl" if axis == "z" else axis)}


def in_turn(tasks):
    while tasks:
        tasks = [task for task in tasks if next(task, "over") != "over"]


def spread(here, wires, kind, ref, at, order, skip=0, direct=""):
    for axis in order:
        piece = kind.view(ref, at, skip)
        if axis == "z":
            copies = [wires.push(piece, piece, here.device(z=here.zh * 2 + 1 - here.zl))]
            yield
            arrive(copies)
        elif axis in direct:
            copies = [wires.push(piece, piece, here.along(axis, s)[1]) for s in STEPS]
            yield
            arrive(copies)
        else:
            (_, right), (_, left) = (here.along(axis, 1), here.along(axis, 3))
            from_left = wires.push(piece, piece, right)
            from_right = wires.push(piece, piece, left)
            yield
            relays = []
            for half, copy, step, onward in ((0, from_left, 3, right), (1, from_right, 1, left)):
                arrive([copy])
                passing = fix(at, axis, here.along(axis, step)[0])
                passing = kind.view(ref, {**passing, "half": half}, skip)
                relays.append(wires.push(passing, passing, onward))
            yield
            arrive(relays)
        at = without(at, axis)


def greet_rings(here, others=()):
    rings = [here.along(a, s)[1] for a in ("x", "y", "z") for s in STEPS]
    greet([*rings, here.sibling(), *others])


class Fetch:
    def __init__(self, here, wires):
        self.here, self.wires = (here, wires)
        self.zh, self.core, self.x, self.y = (here.zh, here.core, here.x, here.y)
        self.there = 1 - here.zl
        self.cross = [here.device(z=3 - here.z, core=(here.core + t) % 2) for t in range(2)]
        self.sibling = here.sibling()
        self.held = {"zh": 1 - here.zh, "zl": here.zl, "x": here.x, "y": here.y}

    def part(self, width):
        return pl.ds(pl.multiple_of(self.there * width, 128), width)

    def ff_columns(self, r, c):
        return pl.ds(pl.multiple_of(r * HALF_FF + c * SLICE, 128), SLICE)

    def rest(self, kind, whole, crossed, order, direct):
        yield
        arrive(crossed)
        yield from spread(
            self.here, self.wires, kind, whole, self.held, order, direct=direct
        )

    def narrow(self, shard, whole, first, width, order):
        columns = pl.ds(first, width)
        source = shard.at[self.x, self.y, :, columns]
        target = whole.at[self.zh, self.core, self.x, self.y, :, columns]
        crossed = [self.wires.push(source, target, self.cross[0])]
        yield
        arrive(crossed)
        held = without(self.held, "z")
        kind = OneCore(first, width, self.core)
        yield from spread(self.here, self.wires, kind, whole, held, order, direct="xy")
        passed = whole.at[1 - self.zh, self.core, :, :, :, columns]
        beside = [self.wires.push(passed, passed, self.sibling)]
        yield
        arrive(beside)

    def wide(self, shard, whole, order):
        crossed = [
            self.wires.push(
                shard.at[self.x, self.y, :, self.ff_columns(self.there, (self.core + t) % 2)],
                whole.at[self.zh, self.core, self.x, self.y, :, self.part(SLICE)],
                self.cross[t],
            )
            for t in range(2)
        ]
        yield from self.rest(ShardsByCore(HALF_FF), whole, crossed, order, "y")

    def down(self, shard, whole, order):
        columns = pl.ds(pl.multiple_of(self.y * 256, 256), 256)
        source = shard.at[self.x, self.there, :, columns]
        target = whole.at[self.zh, self.x, self.there, :, columns]
        crossed = [self.wires.push(source, target, self.cross[0])]
        yield from self.rest(ColumnsByY(144), whole, crossed, order, "x")

    def from_this_chip(self, narrow=(), wide=(), down=()):
        beside, kept = ([], [])
        for shard, whole in narrow:
            target = whole.at[self.zh, self.core]
            beside.append(self.wires.push(shard, target, self.sibling))
            kept.append(self.wires.move(shard, target))
        for shard, whole in wide:
            for r in range(2):
                target = whole.at[self.zh, self.core, :, :, :, pl.ds(r * SLICE, SLICE)]
                theirs = shard.at[:, :, :, self.ff_columns(r, 1 - self.core)]
                mine = shard.at[:, :, :, self.ff_columns(r, self.core)]
                beside.append(self.wires.push(theirs, target, self.sibling))
                kept.append(self.wires.move(mine, target))
        for shard, whole in down:
            kept.append(self.wires.move(shard, whole.at[self.zh]))
        for _ in range(6):
            yield
        arrive(beside)
        for copy in kept:
            copy.wait()


WIDE_FETCH = (
    (ShardsByCore(HALF_FF), ("y", "x", "z")),
    (ShardsByCore(HALF_FF), ("z", "y", "x")),
    (ColumnsByY(144), ("x", "z", "y")),
)


def gather_kernel(
    qkv, out, gate, up, down, qkv_all, out_all, gate_all, up_all, down_all, sends, receives, moves
):
    wires = Wires(sends, receives, moves)
    here = Place()
    fetch = Fetch(here, wires)
    greet_rings(here, fetch.cross)
    in_turn(
        [
            fetch.narrow(qkv, qkv_all, 0, 1024, ("x", "y")),
            fetch.narrow(qkv, qkv_all, 1024, 1024, ("y", "x")),
            fetch.narrow(out, out_all, 0, D, ("x", "y")),
            fetch.wide(gate, gate_all, WIDE_FETCH[0][1][:2]),
            fetch.wide(up, up_all, WIDE_FETCH[1][1][:2]),
            fetch.down(down, down_all, WIDE_FETCH[2][1][:2]),
            fetch.from_this_chip(
                ((qkv, qkv_all), (out, out_all)),
                ((gate, gate_all), (up, up_all)),
                ((down, down_all),),
            ),
        ]
    )
    wires.finish_sends()


def gather(qkv, out, gate, up, down):
    rows = (4, 4, 16)
    qkv, out, *wide = wired_call(
        gather_kernel,
        [
            shape(2, 2, *rows, 2048),
            shape(2, 2, *rows, D),
            shape(2, 2, *rows, HALF_FF),
            shape(2, 2, *rows, HALF_FF),
            shape(2, 4, 2, 144, D),
        ],
        (
            qkv.reshape(*rows, 2048),
            out.reshape(*rows, D),
            gate.reshape(*rows, FF),
            up.reshape(*rows, FF),
            down.reshape(4, 2, 144, D),
        ),
        1,
        "gather",
        3 * 8 + 9 + 6 + 5 + 6,
        7,
    )
    return qkv.reshape(D, 2048), out.reshape(D, D), wide


def fetch_last(here, wires, wide):
    for (kind, order), whole in zip(WIDE_FETCH, wide):
        at = {"zh": 1 - here.zh, "zl": here.zl, "x": here.x, "y": here.y}
        for axis in order[:2]:
            at = without(at, axis)
        yield spread(here, wires, kind, whole, at, order[2:])


WIDE = (
    (0, RowsByShard(HALF_FF), ("z", "x", "y"), ("y", "x", "z")),
    (1, RowsByShard(HALF_FF), ("x", "y", "z"), ("z", "y", "x")),
    (2, ColumnsByY(144), ("y", "z", "x"), ("x", "z", "y")),
    (3, ColumnsByY(32), ("y", "z", "x"), ("x", "z", "y")),
)
NARROW = (
    (0, RowsByPlane(0, 1024), ("z", "x", "y"), ("z", "y", "x")),
    (0, RowsByPlane(1024, 1024), ("x", "y", "z"), ("x", "z", "y")),
)
FIRST_DIRECT = ("y", "y", "x", "x")
WIDE_DIMS = (
    (2, 2, 4, 4, 16, HALF_FF),
    (2, 2, 4, 4, 16, HALF_FF),
    (2, 4, 2, 144, D),
    (2, 4, 2, 32, D),
)
QKV_DIMS = (2, 4, 4, 16, 2048)
PIECE_DIMS = ((16, HALF_FF), (16, HALF_FF), (144, 256), (32, 256))


def slot_shapes(parts):
    found = []
    for _, kind, order, _ in parts:
        at = {}
        for axis in order:
            at = fix(at, axis, 0)
            found.append((6, *kind.open_dims(at), *kind.tail_dims({**at, "half": 0})))
    return found


def each_block(kind, at, body):
    dims = kind.open_dims(at)

    def step(i, _):
        inner, rest = ([], i)
        for n in reversed(dims):
            inner.insert(0, rest % n)
            rest = rest // n
        picks = iter(inner)
        lead = [next(picks) if o is None else o for o in kind.order(at)]
        body((*lead, *kind.tail(at)), (*inner, slice(None), slice(None)))
        return 0

    lax.fori_loop(0, math.prod(dims), step, 0)


def reduce_one(here, wires, kind, grad, total, slots, order, direct_from):
    at = {}
    for step, axis in enumerate(order):
        source, slot = (grad if step == 0 else total, slots[step])
        (right_place, right), (left_place, left) = (here.along(axis, 1), here.along(axis, 3))
        far_place, _ = here.along(axis, 2)
        mine = fix(at, axis, getattr(here, axis))

        def half_of(place, half):
            return {**fix(at, axis, place), "half": half}

        if step >= direct_from:
            copies = [
                wires.push(
                    kind.view(source, half_of(here.along(axis, s)[0], half)),
                    slot.at[2 * j + half],
                    here.along(axis, s)[1],
                )
                for j, s in enumerate(STEPS)
                for half in range(2)
            ]
            yield
            arrive(copies)
            for half in range(2):

                def add_all(whole, part):
                    value = total[whole].astype(F32)
                    for j in range(3):
                        value += slot[(2 * j + half, *part)].astype(F32)
                    total[whole] = value.astype(BF16)

                each_block(kind, {**mine, "half": half}, add_all)
            at = mine
            continue
        relays = [
            wires.push(kind.view(source, half_of(far_place, 0)), slot.at[4], right),
            wires.push(kind.view(source, half_of(far_place, 1)), slot.at[5], left),
        ]
        arriving = [
            wires.push(kind.view(source, half_of(right_place, 1)), slot.at[1], right),
            wires.push(kind.view(source, half_of(left_place, 0)), slot.at[2], left),
        ]
        kept = []
        if step == 0:
            for where in (half_of(right_place, 0), half_of(left_place, 1), mine):
                kept.append(wires.move(kind.view(source, where), kind.view(total, where)))
        yield
        for j, place, half, target, onward in (
            (4, right_place, 0, 0, right),
            (5, left_place, 1, 3, left),
        ):
            if kept:
                kept.pop(0).wait()
            arrive([relays[j - 4]])

            def pass_on(whole, part):
                value = slot[(j, *part)].astype(F32) + total[whole].astype(F32)
                slot[(j, *part)] = value.astype(BF16)

            each_block(kind, half_of(place, half), pass_on)
            arriving.append(wires.push(slot.at[j], slot.at[target], onward))
        yield
        if kept:
            kept.pop(0).wait()
        arrive(arriving)
        for half in range(2):

            def add_up(whole, part):
                value = total[whole].astype(F32) + slot[(half, *part)].astype(F32)
                total[whole] = (value + slot[(2 + half, *part)].astype(F32)).astype(BF16)

            each_block(kind, {**mine, "half": half}, add_up)
        at = mine


def reduce_weights_kernel(*refs):
    grad, gains = refs[4:6]
    nears, (gate_beside, up_beside, qkv_out, gains_out) = (refs[6:10], refs[10:14])
    total, slots = (refs[14], refs[15:21])
    gain_slots, sends, receives, moves = refs[21:]
    besides = (gate_beside, up_beside)

    here = Place()
    wires = Wires(sends, receives, moves)
    core = here.core
    sibling = here.sibling()
    greet_rings(here)
    held = {"zh": here.zh, "zl": here.zl, "x": here.x, "y": here.y}

    def all_gains():
        sums = gains[...]
        for stage, axis in enumerate(("core", "x", "y", "z")):
            me = getattr(here, axis)
            gain_slots[stage, me] = sums
            source = gain_slots.at[stage, me]
            if axis == "core":
                others = [sibling]
            else:
                others = [here.along(axis, s)[1] for s in STEPS]
            copies = [wires.push(source, source, device) for device in others]
            yield
            arrive(copies)
            sums = gain_slots[stage, 0] + gain_slots[stage, 1]
            if axis != "core":
                sums = sums + gain_slots[stage, 2] + gain_slots[stage, 3]
        gains_out[...] = sums

    def narrow(p):
        _, kind, order, back = NARROW[p]
        yield from reduce_one(
            here, wires, kind, grad, total, slots[3 * p : 3 * p + 3], order, 1
        )
        own = wires.move(kind.view(total, held), kind.view(qkv_out, held, 1))
        own.wait()
        yield from spread(here, wires, kind, qkv_out, held, back, 1, direct="xy")

    def wide(p):
        _, kind, _, back = WIDE[p]
        at = held
        for axis in back[:2]:
            at = without(at, axis)
        yield from spread(here, wires, kind, nears[p], at, back[2:], 1)
        if p < 2:
            copies = [wires.push(nears[p].at[1 - core], besides[p], sibling)]
            yield
            arrive(copies)

    in_turn([narrow(p) for p in range(2)] + [wide(p) for p in range(4)] + [all_gains()])
    wires.finish_sends()


def reduce_weights(nears, qkv, gains):
    outs = [
        *(shape(*d[1:]) for d in WIDE_DIMS),
        shape(*WIDE_DIMS[0][2:]),
        shape(*WIDE_DIMS[1][2:]),
        shape(*QKV_DIMS[1:]),
        shape(*gains.shape, dtype=F32),
    ]
    scratch = [pltpu.VMEM(QKV_DIMS, BF16)]
    scratch += [pltpu.VMEM(s, BF16) for s in slot_shapes(NARROW)]
    scratch += [pltpu.VMEM((4, 4, *gains.shape), F32)]
    gate, up, down, out, gate_beside, up_beside, qkv, gains = wired_call(
        reduce_weights_kernel,
        outs,
        [*nears, qkv.reshape(QKV_DIMS), gains],
        2,
        "reduce_weights",
        10 + 2 * (18 + 7) + 1 + 3 * 4 + 2,
        2 * 4,
        scratch,
        [ANY] * 5 + [VMEM],
        [ANY] * 7 + [VMEM],
        vmem=40 * MIB,
        aliases={i: i for i in range(4)},
    )
    core = lax.axis_index("fsdp") % 2

    def joined(near, beside):
        own = lax.dynamic_index_in_dim(near, core, 0, keepdims=False).reshape(256, HALF_FF)
        beside = beside.reshape(256, HALF_FF)
        first, second = (jnp.where(core == 0, own, beside), jnp.where(core == 0, beside, own))
        pieces = [f[:, r * SLICE : (r + 1) * SLICE] for r in range(2) for f in (first, second)]
        return jnp.concatenate(pieces, axis=1)

    gate, up = (joined(gate, gate_beside), joined(up, up_beside))
    return (
        qkv.reshape(256, 2048),
        out.reshape(256, D),
        gate,
        up,
        down.reshape(SLICE, D),
        gains,
    )


def head_columns(head):
    return pl.ds(pl.multiple_of(head * 128, 128), 128)


def seats(here):
    me = here.ctx
    quarter, seat = (me // QUARTER, me % QUARTER)
    near = [quarter * QUARTER + (seat + s) % QUARTER for s in range(1, QUARTER)]
    far = [(me + s) % RING for s in range(1, RING)]
    return me, seat, near, far


def to_heads_kernel(query, key_value, query_out, key_value_out, sends, receives, moves):
    here = Place()
    wires = Wires(sends, receives, moves)
    me, seat, near, far = seats(here)
    greet([(k, here.fsdp) for k in far])
    copies = [
        wires.push(query.at[:, head_columns(k % QUARTER)], query_out.at[seat], (k, here.fsdp))
        for k in near
    ]
    copies += [
        wires.push(key_value.at[:, head_columns(k % QUARTER)], key_value_out.at[me], (k, here.fsdp))
        for k in far
    ]
    kept = [
        wires.move(query.at[:, head_columns(seat)], query_out.at[seat]),
        wires.move(key_value.at[:, head_columns(seat)], key_value_out.at[me]),
    ]
    arrive(copies)
    for copy in kept:
        copy.wait()
    wires.finish_sends()


def to_heads(query, key_value):
    outs = [shape(QUARTER, TOKENS, 128), shape(RING, TOKENS, 128)]
    return wired_call(to_heads_kernel, outs, [query, key_value], 3, "to_heads", 38, 2)


def grad_to_heads_kernel(grad, branch, grad_out, branch_pair, sends, receives, moves):
    here = Place()
    wires = Wires(sends, receives, moves)
    _, seat, near, _ = seats(here)
    greet([(k, here.fsdp) for k in near] + [here.sibling()])
    copies = [
        wires.push(grad.at[:, head_columns(k % QUARTER)], grad_out.at[seat], (k, here.fsdp))
        for k in near
    ]
    copies.append(wires.push(branch, branch_pair.at[here.core], here.sibling()))
    kept = [
        wires.move(grad.at[:, head_columns(seat)], grad_out.at[seat]),
        wires.move(branch, branch_pair.at[here.core]),
    ]
    arrive(copies)
    for copy in kept:
        copy.wait()
    wires.finish_sends()


def grad_to_heads(grad, branch):
    outs = [shape(QUARTER, TOKENS, 128), shape(2, TOKENS, D)]
    return wired_call(grad_to_heads_kernel, outs, [grad, branch], 4, "grad_to_heads", 8, 2)


def to_tokens_kernel(query, query_out, sends, receives, moves):
    here = Place()
    wires = Wires(sends, receives, moves)
    _, seat, near, _ = seats(here)
    greet([(k, here.fsdp) for k in near])
    columns = query_out.at[:, head_columns(seat)]
    copies = [wires.push(query.at[k % QUARTER], columns, (k, here.fsdp)) for k in near]
    kept = wires.move(query.at[seat], columns)
    arrive(copies)
    kept.wait()
    wires.finish_sends()


def to_tokens(query):
    return wired_call(to_tokens_kernel, [shape(TOKENS, D)], [query], 5, "to_tokens", 7, 1)[0]


def grads_to_tokens_kernel(*refs):
    query, key_value, pieces = (refs[0], refs[1], refs[2:6])
    query_out, key_value_out, nears = (refs[6], refs[7], refs[8:12])
    here = Place()
    wires = Wires(*refs[12:])
    me, seat, near, far = seats(here)
    greet([(k, here.fsdp) for k in far])
    held = {"zh": here.zh, "zl": here.zl, "x": here.x, "y": here.y}

    def back():
        columns = query_out.at[:, head_columns(seat)]
        copies = [wires.push(query.at[k % QUARTER], columns, (k, here.fsdp)) for k in near]
        copies += [
            wires.push(key_value.at[k], key_value_out.at[me], (k, here.fsdp)) for k in far
        ]
        kept = [
            wires.move(query.at[seat], columns),
            wires.move(key_value.at[me], key_value_out.at[me]),
        ]
        for _ in range(3):
            yield
        arrive(copies)
        for copy in kept:
            copy.wait()

    def share(p):
        _, kind, _, order = WIDE[p]
        own = wires.move(pieces[p], kind.view(nears[p], held, 1))
        own.wait()
        yield from spread(
            here, wires, kind, nears[p], held, order[:2], 1, direct=FIRST_DIRECT[p]
        )

    in_turn([share(p) for p in range(4)] + [back()])
    wires.finish_sends()


def grads_to_tokens(query, key_value, pieces):
    query_grad, key_value_grad, *nears = wired_call(
        grads_to_tokens_kernel,
        [shape(TOKENS, D), shape(RING, TOKENS, 128), *(shape(*d[1:]) for d in WIDE_DIMS)],
        [query, key_value, *pieces],
        6,
        "grads_to_tokens",
        38 + 7 + 4 + 4 + 4,
        6,
    )
    return query_grad, key_value_grad, nears


def half_columns(r, core):
    return pl.ds(pl.multiple_of(r * 512 + core * 256, 256), 256)


def share_kernel(whole, halved, *refs):
    n = whole + halved
    ins, outs = (refs[:n], refs[n : 2 * n])
    here = Place()
    wires = Wires(*refs[2 * n :])
    core = here.core
    sibling = here.sibling()
    greet([sibling])
    copies, kept = ([], [])
    for source, target in zip(ins[:whole], outs[:whole]):
        copies.append(wires.push(source, target.at[core], sibling))
        kept.append(wires.move(source, target.at[core]))
    for source, target in zip(ins[whole:], outs[whole:]):
        for r in range(2):
            place = target.at[core, :, pl.ds(r * 256, 256)]
            copies.append(wires.push(source.at[:, half_columns(r, 1 - core)], place, sibling))
            kept.append(wires.move(source.at[:, half_columns(r, core)], place))
    arrive(copies)
    for copy in kept:
        copy.wait()
    wires.finish_sends()


def share(whole, halved, collective_id):
    outs = [shape(2, *a.shape, dtype=a.dtype) for a in whole]
    outs += [shape(2, a.shape[0], 512, dtype=a.dtype) for a in halved]
    count = len(whole) + 2 * len(halved)
    done = wired_call(
        functools.partial(share_kernel, len(whole), len(halved)),
        outs,
        [*whole, *halved],
        collective_id,
        "share",
        count,
        count,
    )
    return [a.reshape(2 * a.shape[1], a.shape[2]) for a in done]


def hand_over_kernel(count, *refs):
    ins, outs = (refs[:count], refs[count : 2 * count])
    here = Place()
    wires = Wires(*refs[2 * count :])
    sibling = here.sibling()
    greet([sibling])
    copies = [wires.push(i.at[1 - here.core], o, sibling) for i, o in zip(ins, outs)]
    arrive(copies)
    wires.finish_sends()


def hand_over(partials, collective_id):
    return wired_call(
        functools.partial(hand_over_kernel, len(partials)),
        [shape(*a.shape[1:], dtype=a.dtype) for a in partials],
        partials,
        collective_id,
        "hand_over",
        len(partials),
        0,
    )


def nt(left, right):
    return lax.dot_general(left, right, (((1,), (1,)), ((), ())), preferred_element_type=F32)


def nn(left, right):
    return lax.dot_general(left, right, (((1,), (0,)), ((), ())), preferred_element_type=F32)


def query_block(ref, t):
    block = ref[t].astype(F32)
    both = jnp.concatenate([block, pltpu.roll(block, 64, 1)], axis=0)
    low = lax.broadcasted_iota(jnp.int32, (128, 128), 1) < 64
    return jnp.where(low, both, 0.0)


def query_pair(ref, u):
    return [query_block(ref, 2 * u), query_block(ref, 2 * u + 1)]


def first_allowed(position, starts_ref):
    begin = jnp.zeros_like(position)
    for n in range(4):
        begin = jnp.maximum(begin, jnp.where(starts_ref[n] <= position, starts_ref[n], 0))
    return begin


def heads_beside(rows):
    low = lax.broadcasted_iota(jnp.int32, (64, 128), 1) < 64
    return jnp.where(low, rows[:64], pltpu.roll(rows[64:], 64, 1)).astype(BF16)


def attend_task(
    counts, first_block, starts_ref, order_ref, query_ref, key_value_ref, out_ref, exact_ref,
    sum_ref, value_ref, key_at_ref,
):
    def key_places(j, _):
        lane = lax.broadcasted_iota(jnp.int32, (1, 128), 1)
        block = jnp.where(lane < 64, order_ref[2 * j], order_ref[2 * j + 1])
        key_at_ref[:, pl.ds(pl.multiple_of(j * 128, 128), 128)] = block * 64 + lane % 64
        return 0

    def values(j, _):
        rows = pl.ds(pl.multiple_of(j * 256, 256), 256)
        block = pltpu.roll(key_value_ref[rows, :].astype(F32), 64, 1)
        low = lax.broadcasted_iota(jnp.int32, (256, 128), 1) < 64
        value_ref[rows, :] = jnp.where(low, block, 1.0).astype(BF16)
        return 0

    def blocks(u, _):
        queries = jnp.concatenate(query_pair(query_ref, u), axis=0).astype(BF16)
        inner = lax.broadcasted_iota(jnp.int32, (128, 1), 0) % 64
        block = first_block + 2 * u
        position = jnp.concatenate(
            [order_ref[block] * 64 + inner, order_ref[block + 1] * 64 + inner], axis=0
        )
        begin = first_allowed(position, starts_ref)

        def tile(j, total):
            rows = pl.ds(pl.multiple_of(j * KEY_TILE, KEY_TILE), KEY_TILE)
            scores = nt(queries, key_value_ref[rows, :])
            key = key_at_ref[:, rows]
            allowed = (key <= position) & (key >= begin)
            weight = jnp.where(allowed, jnp.exp2(scores * SCORE_TO_EXP2), 0.0)
            return total + nn(weight.astype(BF16), value_ref[rows, :])

        total = lax.fori_loop(0, SEQ // KEY_TILE, tile, jnp.zeros((256, 128), F32))
        attended = total / pltpu.roll(total, 64, 1)
        low = lax.broadcasted_iota(jnp.int32, (256, 128), 1) < 64
        attended = jnp.where(low, attended, 0.0)
        for n in range(2):
            rows = slice(128 * n, 128 * n + 128)
            exact_ref[2 * u + n] = attended[rows]
            out_ref[2 * u + n] = heads_beside(attended[rows])
            sum_ref[2 * u + n] = jnp.transpose(total[rows])[64:72]
        return 0

    lax.fori_loop(0, SEQ // 256, values, 0)
    lax.fori_loop(0, SEQ // 128, key_places, 0)
    first = 0
    for count in counts:
        lax.fori_loop(first, first + count, blocks, 0)
        first += count
        yield


def attend_kernel(
    starts, order, query, key_value, gate_in, up_in, down_in, attended, exact, sums, gate_all,
    up_all, down_all, value_ref, key_at_ref, sends, receives, moves,
):
    wires = Wires(sends, receives, moves)
    here = Place()
    greet_rings(here)
    in_turn(
        [
            *fetch_last(here, wires, (gate_all, up_all, down_all)),
            attend_task(
                (6, 2), here.ctx // QUARTER * 16, starts, order, query, key_value, attended, exact,
                sums, value_ref, key_at_ref,
            ),
        ]
    )
    wires.finish_sends()


def attend(starts, order, queries, key_values, wide):
    outs = [
        shape(16, 64, 128),
        shape(16, 128, 128, dtype=F32),
        shape(16, 8, 128, dtype=F32),
        *(shape(*a.shape) for a in wide),
    ]
    attended, exact, sums, gate, up, down = wired_call(
        attend_kernel,
        outs,
        [starts, order, queries, key_values, *wide],
        10,
        "attend",
        1 + 4 + 4,
        1,
        [pltpu.VMEM((SEQ, 128), BF16), pltpu.VMEM((1, SEQ), jnp.int32)],
        [SMEM] * 2 + [VMEM] * 2 + [ANY] * 3,
        [VMEM] * 3 + [ANY] * 3,
        vmem=40 * MIB,
        aliases={4 + i: 3 + i for i in range(3)},
    )
    weights = (gate.reshape(D, HALF_FF), up.reshape(D, HALF_FF), down.reshape(HALF_FF, D))
    return attended, exact, sums, weights


def attend_back_task(
    counts, first_block, starts_ref, order_ref, query_ref, key_value_ref, grad_ref, exact_ref,
    sum_ref, query_grad_ref, key_value_grad_ref, across_ref, total_ref, key_at_ref,
):
    total_ref[...] = jnp.zeros_like(total_ref)

    def key_places(j, _):
        inner = lax.broadcasted_iota(jnp.int32, (64, 1), 0)
        key_at_ref[pl.ds(pl.multiple_of(j * 64, 64), 64), :] = order_ref[j] * 64 + inner
        return 0

    def turn(j, _):
        rows = pl.ds(pl.multiple_of(j * 128, 128), 128)
        across_ref[:, rows] = jnp.transpose(key_value_ref[rows, :].astype(F32)).astype(BF16)
        return 0

    def blocks(u, _):
        queries, grads = (query_pair(query_ref, u), query_pair(grad_ref, u))
        delta = [
            jnp.sum(jnp.transpose(grad * exact_ref[2 * u + n]), axis=0, keepdims=True)
            for n, grad in enumerate(grads)
        ]
        delta = jnp.concatenate(delta, axis=1)
        total_exp2 = jnp.concatenate(
            [jnp.log2(sum_ref[2 * u + n][0:1]) for n in range(2)], axis=1
        )
        grads = [pltpu.roll(grad, 64, 1) for grad in grads]
        both = jnp.concatenate(queries + grads, axis=0).astype(BF16)
        inner = lax.broadcasted_iota(jnp.int32, (1, 128), 1) % 64
        block = first_block + 2 * u
        position = jnp.concatenate(
            [order_ref[block] * 64 + inner, order_ref[block + 1] * 64 + inner], axis=1
        )
        begin = first_allowed(position, starts_ref)

        def tile(j, query_grad):
            rows = pl.ds(pl.multiple_of(j * KEY_TILE_BACK, KEY_TILE_BACK), KEY_TILE_BACK)
            products = nt(key_value_ref[rows, :], both)
            key = key_at_ref[rows, :]
            allowed = (key <= position) & (key >= begin)
            prob = jnp.where(
                allowed, jnp.exp2(products[:, :256] * SCORE_TO_EXP2 - total_exp2), 0.0
            )
            score = (prob * (products[:, 256:] - delta)).astype(BF16)
            side = jnp.concatenate([score, prob.astype(BF16)], axis=1)
            total_ref[rows, :] += nn(side, both)
            return query_grad + nn(across_ref[:, rows], score)

        query_grad = lax.fori_loop(
            0, SEQ // KEY_TILE_BACK, tile, jnp.zeros((128, 256), F32)
        )
        for n in range(2):
            rows = jnp.transpose(query_grad[:, 128 * n : 128 * n + 128])
            query_grad_ref[2 * u + n] = heads_beside(rows * float(HEAD_SIZE) ** (-0.5))
        return 0

    def put_back(j, _):
        rows = pl.ds(pl.multiple_of(j * 256, 256), 256)
        low = lax.broadcasted_iota(jnp.int32, (256, 128), 1) < 64
        scale = jnp.where(low, float(HEAD_SIZE) ** (-0.5), 1.0)
        key_value_grad_ref[rows, :] = (total_ref[rows, :] * scale).astype(BF16)
        return 0

    lax.fori_loop(0, SEQ // 128, turn, 0)
    lax.fori_loop(0, 64, key_places, 0)
    first = 0
    for count in counts:
        lax.fori_loop(first, first + count, blocks, 0)
        first += count
        yield
    lax.fori_loop(0, SEQ // 256, put_back, 0)


def attend_back_kernel(*refs):
    attention, grads = (refs[:7], refs[7:11])
    outs, pieces = (refs[11:13], refs[13:17])
    scratch, totals, slots = (refs[17:20], refs[20:24], refs[24:36])
    here = Place()
    wires = Wires(*refs[36:])
    greet_rings(here)
    at = {"zh": here.zh, "zl": here.zl, "x": here.x, "y": here.y}

    def reduce(p):
        _, kind, order, _ = WIDE[p]
        yield from reduce_one(
            here, wires, kind, grads[p], totals[p], slots[3 * p : 3 * p + 3], order, 2
        )
        own = wires.move(kind.view(totals[p], at), pieces[p])
        yield
        own.wait()

    first_block = here.ctx // QUARTER * 16
    in_turn(
        [reduce(p) for p in range(4)]
        + [attend_back_task((3, 3, 1, 1), first_block, *attention, *outs, *scratch)]
    )
    wires.finish_sends()


def attend_back(starts, order, queries, key_values, grads, exact, sums, wide):
    ins = [starts, order, queries, key_values, grads]
    ins += [exact, sums, *(a.reshape(d) for a, d in zip(wide, WIDE_DIMS))]
    scratch = [
        pltpu.VMEM((128, SEQ), BF16),
        pltpu.VMEM((SEQ, 128), F32),
        pltpu.VMEM((SEQ, 1), jnp.int32),
    ]
    scratch += [pltpu.VMEM(d, BF16) for d in WIDE_DIMS]
    scratch += [pltpu.VMEM(s, BF16) for s in slot_shapes(WIDE)]
    query_grad, key_value_grad, *pieces = wired_call(
        attend_back_kernel,
        [shape(16, 64, 128), shape(SEQ, 128), *(shape(*d) for d in PIECE_DIMS)],
        ins,
        11,
        "attend_back",
        4 * 18,
        4 * 4,
        scratch,
        [SMEM] * 2 + [VMEM] * 5 + [ANY] * 4,
        [VMEM] * 2 + [ANY] * 4,
        vmem=58 * MIB,
    )
    return query_grad, key_value_grad, pieces


def rms_norm(values, gain_row):
    return (
        values * lax.rsqrt(jnp.mean(values * values, axis=-1, keepdims=True) + EPSILON) * gain_row
    )


def rotate(values, positions):
    half_width = values.shape[-1] // 2
    frequency = ROPE_BASE ** (-2.0 * jnp.arange(half_width, dtype=F32) / values.shape[-1])
    angles = positions.astype(F32)[:, None] * frequency[None, :]
    cosine = jnp.cos(angles)[:, None, :]
    sine_part = jnp.sin(angles)[:, None, :]
    first_half = values[..., :half_width]
    second_half = values[..., half_width:]
    return jnp.concatenate(
        [
            first_half * cosine - second_half * sine_part,
            second_half * cosine + first_half * sine_part,
        ],
        axis=-1,
    )


def outer_sum(left, right):
    return lax.dot_general(
        left, right, (((0,), (0,)), ((), ())), preferred_element_type=F32
    ).astype(BF16)


def matmul(left, right):
    return jnp.dot(left, right, preferred_element_type=F32)


def positions_at(block_order, first_row, total_row_count, half_rows):
    row_ids = first_row + jnp.arange(total_row_count, dtype=jnp.int32)
    blocks = row_ids // half_rows
    lookup = jnp.arange(block_order.shape[0], dtype=jnp.int32)
    picked = jnp.sum(jnp.where(blocks[:, None] == lookup[None, :], block_order[None, :], 0), axis=1)
    return picked * half_rows + row_ids % half_rows


def per_device(
    inputs,
    cotangent,
    qkv_weight,
    out_weight,
    gate_weight,
    up_weight,
    down_weight,
    gain_attn,
    gain_query,
    gain_key,
    gain_ffn,
    block_order,
    doc_starts,
):
    cycle_index = lax.axis_index("ctx")
    core = lax.axis_index("fsdp") % 2
    qkv_all, out_all, wide = gather(
        qkv_weight, out_weight, gate_weight, up_weight, down_weight
    )
    places = (doc_starts[0], block_order)
    positions = positions_at(block_order, cycle_index * TOKENS, TOKENS, TOKENS // 2)

    resid_in = inputs[0].astype(F32)
    normed, norm_in_pull = jax.vjp(rms_norm, resid_in, gain_attn)
    normed_low = normed.astype(BF16)
    projected = matmul(normed_low, qkv_all)
    split_position = (QUERY_HEADS + KEY_VALUE_HEADS) * HEAD_SIZE

    def query_key(leading_columns, scale_query, scale_key):
        queries = leading_columns[:, : QUERY_HEADS * HEAD_SIZE].reshape(
            TOKENS, QUERY_HEADS, HEAD_SIZE
        )
        keys = leading_columns[:, QUERY_HEADS * HEAD_SIZE :].reshape(
            TOKENS, KEY_VALUE_HEADS, HEAD_SIZE
        )
        return (
            rotate(rms_norm(queries, scale_query), positions),
            rotate(rms_norm(keys, scale_key), positions),
        )

    (queries, keys), qk_pull = jax.vjp(
        query_key, projected[:, :split_position], gain_query, gain_key
    )
    values = projected[:, split_position:].reshape(TOKENS, KEY_VALUE_HEADS, HEAD_SIZE)
    key_values = jnp.concatenate([keys, values], axis=-1).astype(BF16).reshape(TOKENS, D)
    query_part, key_value_part = to_heads(queries.astype(BF16).reshape(TOKENS, D), key_values)
    query_part = query_part.reshape(16, 64, 128)
    key_value_part = key_value_part.reshape(SEQ, 128)
    attended, exact, sums, (gate_all, up_all, down_all) = attend(
        *places, query_part, key_value_part, wide
    )
    attended_low = to_tokens(attended.reshape(QUARTER, TOKENS, 128))

    residual = resid_in + matmul(attended_low, out_all)
    normed_ffn, norm_ffn_pull = jax.vjp(rms_norm, residual, gain_ffn)
    grad_out = cotangent[0]
    ffn_pair, cotangent_pair, normed_half, attended_half = share(
        [normed_ffn.astype(BF16), grad_out], [normed_low, attended_low], 7
    )
    gate_proj = matmul(ffn_pair, gate_all)
    up_proj = matmul(ffn_pair, up_all)
    hidden, gating_pull = jax.vjp(
        lambda gate_in, up_in: jax.nn.silu(gate_in) * up_in, gate_proj, up_proj
    )
    hidden_low = hidden.astype(BF16)
    out_partial = matmul(hidden_low, down_all).reshape(2, TOKENS, D)
    grad_hidden = matmul(cotangent_pair, down_all.T)
    grad_gate, grad_up = gating_pull(grad_hidden)
    gate_low = grad_gate.astype(BF16)
    up_low = grad_up.astype(BF16)
    ffn_partial = (matmul(gate_low, gate_all.T) + matmul(up_low, up_all.T)).reshape(2, TOKENS, D)
    out_rest, ffn_rest = hand_over([out_partial, ffn_partial], 8)

    def mine(pair):
        return lax.dynamic_index_in_dim(pair, core, 0, keepdims=False)

    outputs = residual + mine(out_partial) + out_rest
    grad_resid_ffn, grad_gain_ffn = norm_ffn_pull(mine(ffn_partial) + ffn_rest)
    grad_resid = grad_out.astype(F32) + grad_resid_ffn
    branch_low = grad_resid.astype(BF16)
    grad_attended = matmul(branch_low, out_all.T).astype(BF16)
    grad_part, branch_pair = grad_to_heads(grad_attended, branch_low)
    query_grad, key_value_grad, pieces = attend_back(
        *places,
        query_part,
        key_value_part,
        grad_part.reshape(16, 64, 128),
        exact,
        sums,
        (
            outer_sum(ffn_pair, gate_low),
            outer_sum(ffn_pair, up_low),
            outer_sum(hidden_low, cotangent_pair),
            outer_sum(attended_half, branch_pair.reshape(2 * TOKENS, D)),
        ),
    )
    query_grad, key_value_grad, nears = grads_to_tokens(
        query_grad.reshape(QUARTER, TOKENS, 128),
        key_value_grad.reshape(RING, TOKENS, 128),
        pieces,
    )
    key_value_grad = key_value_grad.reshape(4, KEY_VALUE_HEADS, TOKENS, 128)
    key_value_grad = jnp.transpose(jnp.sum(key_value_grad.astype(F32), axis=0), (1, 0, 2))
    grad_front, grad_gain_query, grad_gain_key = qk_pull(
        (
            query_grad.astype(F32).reshape(TOKENS, QUERY_HEADS, HEAD_SIZE),
            key_value_grad[..., :HEAD_SIZE],
        )
    )
    grad_values = key_value_grad[..., HEAD_SIZE:].reshape(TOKENS, KEY_VALUE_HEADS * HEAD_SIZE)
    grad_projected = jnp.concatenate([grad_front, grad_values], axis=1).astype(BF16)
    grad_normed = matmul(grad_projected, qkv_all.T)
    grad_input_norm, grad_gain_attn = norm_in_pull(grad_normed)
    grad_inputs = (grad_resid + grad_input_norm).astype(BF16)

    (projected_pair,) = share([grad_projected], [], 9)
    gains = jnp.concatenate([grad_gain_attn, grad_gain_ffn, grad_gain_query, grad_gain_key])
    gains = jnp.pad(gains, (0, 24 * 128 - gains.shape[0])).reshape(24, 128)
    grad_qkv, grad_out_weight, grad_gate_weight, grad_up_weight, grad_down, gains = reduce_weights(
        nears, outer_sum(normed_half, projected_pair), gains
    )
    gains = gains.reshape(-1)
    return (
        outputs.astype(BF16)[None],
        grad_inputs[None],
        grad_qkv.astype(F32),
        grad_out_weight.astype(F32),
        grad_gate_weight.astype(F32),
        grad_up_weight.astype(F32),
        grad_down.astype(F32),
        gains[:D],
        gains[2 * D : 2 * D + HEAD_SIZE],
        gains[2 * D + HEAD_SIZE : 2 * D + 2 * HEAD_SIZE],
        gains[D : 2 * D],
    )


def solution(mesh):
    in_specs = (
        P("fsdp", "ctx", None),
        P("fsdp", "ctx", None),
        P("fsdp", None),
        P("fsdp", None),
        P("fsdp", None),
        P("fsdp", None),
        P("fsdp", None),
        P(),
        P(),
        P(),
        P(),
        P(),
        P("fsdp", None),
    )
    out_specs = (
        P("fsdp", "ctx", None),
        P("fsdp", "ctx", None),
        P("fsdp", None),
        P("fsdp", None),
        P("fsdp", None),
        P("fsdp", None),
        P("fsdp", None),
        P(),
        P(),
        P(),
        P(),
    )
    return jax.shard_map(
        per_device, mesh=mesh, in_specs=in_specs, out_specs=out_specs, check_vma=False
    )
```

```python
import functools
import math

import jax
import jax.numpy as jnp
from jax import lax
from jax.experimental import pallas as pl
from jax.experimental.pallas import tpu as pltpu
from jax.sharding import PartitionSpec as P

QUERY_HEADS = 16
KEY_VALUE_HEADS = 8
HEAD_SIZE = 64
FF = 4608
D = 1024
TOKENS = 128
RING = 32
QUARTER = 8
SLICE = 1152
HALF_FF = FF // 2
KEY_TILE = 1024
KEY_TILE_BACK = 1024
SEQ = 4096

EPSILON = 1e-05
ROPE_BASE = 1000000.0
SCORE_TO_EXP2 = float(HEAD_SIZE) ** (-0.5) * math.log2(math.e)

MESH = pl.DeviceIdType.MESH
ANY = pl.BlockSpec(memory_space=pl.ANY)
HBM = pl.BlockSpec(memory_space=pltpu.MemorySpace.HBM)
VMEM = pl.BlockSpec(memory_space=pltpu.VMEM)
SMEM = pl.BlockSpec(memory_space=pltpu.SMEM)
BF16 = jnp.bfloat16
F32 = jnp.float32
MIB = 1 << 20
STEPS = (1, 3, 2)


class Place:
    def __init__(self):
        self.ctx, self.fsdp = (lax.axis_index("ctx"), lax.axis_index("fsdp"))
        self.zl, self.x, self.y = (self.ctx // 16, (self.ctx // 4) % 4, self.ctx % 4)
        self.zh, self.core = (self.fsdp // 2, self.fsdp % 2)
        self.z = self.zh * 2 + self.zl

    def device(self, x=None, y=None, z=None, core=None):
        x = self.x if x is None else x
        y = self.y if y is None else y
        z = self.z if z is None else z
        core = self.core if core is None else core
        return ((z % 2) * 16 + x * 4 + y, (z // 2) * 2 + core)

    def sibling(self):
        return self.device(core=1 - self.core)

    def along(self, axis, step):
        coordinate = (getattr(self, axis) + step) % 4
        return coordinate, self.device(**{axis: coordinate})


class Wires:
    def __init__(self, sends, receives, locals_=None):
        self.sends, self.receives, self.locals_ = (sends, receives, locals_)
        self.pushed, self.moved = ([], 0)

    def push(self, source, target, device):
        at = len(self.pushed)
        copy = pltpu.make_async_remote_copy(
            src_ref=source,
            dst_ref=target,
            send_sem=self.sends.at[at],
            recv_sem=self.receives.at[at],
            device_id=device,
            device_id_type=MESH,
        )
        copy.start()
        self.pushed.append(copy)
        return copy

    def move(self, source, target):
        copy = pltpu.make_async_copy(source, target, self.locals_.at[self.moved])
        copy.start()
        self.moved += 1
        return copy

    def finish_sends(self):
        for copy in self.pushed:
            copy.wait_send()


def arrive(copies):
    for copy in copies:
        copy.wait_recv()


def greet(devices):
    barrier = pltpu.get_barrier_semaphore()
    for device in devices:
        pl.semaphore_signal(barrier, inc=1, device_id=device, device_id_type=MESH)
    pl.semaphore_wait(barrier, len(devices))


def wired_call(kernel, outs, ins, collective_id, name, copies, moves, scratch=(), in_specs=None,
               out_specs=None, vmem=32 * MIB, aliases=None):
    return pl.pallas_call(
        kernel,
        out_shape=outs,
        in_specs=[ANY] * len(ins) if in_specs is None else in_specs,
        out_specs=[ANY] * len(outs) if out_specs is None else out_specs,
        scratch_shapes=[
            *scratch,
            pltpu.SemaphoreType.DMA((copies,)),
            pltpu.SemaphoreType.DMA((copies,)),
            pltpu.SemaphoreType.DMA((max(moves, 1),)),
        ],
        compiler_params=pltpu.CompilerParams(
            collective_id=collective_id, has_side_effects=True, vmem_limit_bytes=vmem
        ),
        name=name,
        input_output_aliases=aliases or {},
    )(*ins)


def shape(*dims, dtype=BF16):
    return jax.ShapeDtypeStruct(dims, dtype)


class Pieces:
    def view(self, ref, at, skip=0):
        lead = [slice(None) if i is None else i for i in self.order(at)[skip:]]
        return ref.at[(*lead, *self.tail(at))]

    def open_dims(self, at):
        return tuple(n for n, i in zip(self.lead, self.order(at)) if i is None)

    def tail(self, at):
        first, width = self.columns(at)
        if not isinstance(first, int):
            first = pl.multiple_of(first, 128)
        return (slice(None), pl.ds(first, width))

    def tail_dims(self, at):
        return (self.rows, self.columns(at)[1])


def halved(first, width, at):
    if "half" not in at:
        return first, width
    return first + at["half"] * (width // 2), width // 2


class RowsByShard(Pieces):
    lead, rows = ((2, 2, 4, 4), 16)

    def __init__(self, width):
        self.width = width

    def order(self, at):
        return [at.get("zh"), at.get("zl"), at.get("x"), at.get("y")]

    def columns(self, at):
        return halved(0, self.width, at)


class RowsByPlane(Pieces):
    lead, rows = ((2, 4, 4), 16)

    def __init__(self, first, width):
        self.first, self.width = (first, width)

    def order(self, at):
        return [at.get("zh"), at.get("x"), at.get("y")]

    def columns(self, at):
        if "zl" not in at:
            return halved(self.first, self.width, at)
        half = self.width // 2
        return halved(self.first + half * at["zl"], half, at)


class ColumnsByY(Pieces):
    lead = (2, 4, 2)

    def __init__(self, rows):
        self.rows = rows

    def order(self, at):
        return [at.get("zh"), at.get("x"), at.get("zl")]

    def columns(self, at):
        return halved(at["y"] * 256, 256, at) if "y" in at else halved(0, D, at)


class ShardsByCore(Pieces):
    lead, rows = ((2, 2, 4, 4), 16)

    def __init__(self, width):
        self.width = width

    def order(self, at):
        return [at.get("zh"), at.get("half"), at.get("x"), at.get("y")]

    def columns(self, at):
        half = self.width // 2
        return (half * at["zl"], half) if "zl" in at else (0, self.width)


class OneCore(RowsByPlane):
    lead = (2, 2, 4, 4)

    def __init__(self, first, width, core):
        super().__init__(first, width)
        self.core = core

    def order(self, at):
        return [at.get("zh"), self.core, at.get("x"), at.get("y")]


def fix(at, axis, coordinate):
    if axis == "z":
        return {**at, "zh": coordinate // 2, "zl": coordinate % 2}
    return {**at, axis: coordinate}


def without(at, axis):
    return {a: i for a, i in at.items() if a != ("zl" if axis == "z" else axis)}


def in_turn(tasks):
    while tasks:
        tasks = [task for task in tasks if next(task, "over") != "over"]


def later(task, rounds):
    next(task)
    for _ in range(rounds + 1):
        yield
    yield from task


def spread(here, wires, kind, ref, at, order, skip=0, direct=""):
    for axis in order:
        piece = kind.view(ref, at, skip)
        if axis == "z":
            copies = [wires.push(piece, piece, here.device(z=here.zh * 2 + 1 - here.zl))]
            yield
            arrive(copies)
        elif axis in direct:
            copies = [wires.push(piece, piece, here.along(axis, s)[1]) for s in STEPS]
            yield
            arrive(copies)
        else:
            (_, right), (_, left) = (here.along(axis, 1), here.along(axis, 3))
            from_left = wires.push(piece, piece, right)
            from_right = wires.push(piece, piece, left)
            yield
            relays = []
            for half, copy, step, onward in ((0, from_left, 3, right), (1, from_right, 1, left)):
                arrive([copy])
                passing = fix(at, axis, here.along(axis, step)[0])
                passing = kind.view(ref, {**passing, "half": half}, skip)
                relays.append(wires.push(passing, passing, onward))
            yield
            arrive(relays)
        at = without(at, axis)


def greet_rings(here, others=()):
    rings = [here.along(a, s)[1] for a in ("x", "y", "z") for s in STEPS]
    greet([*rings, here.sibling(), *others])


class Fetch:
    def __init__(self, here, wires):
        self.here, self.wires = (here, wires)
        self.zh, self.core, self.x, self.y = (here.zh, here.core, here.x, here.y)
        self.there = 1 - here.zl
        self.cross = [here.device(z=3 - here.z, core=(here.core + t) % 2) for t in range(2)]
        self.sibling = here.sibling()
        self.held = {"zh": 1 - here.zh, "zl": here.zl, "x": here.x, "y": here.y}

    def part(self, width):
        return pl.ds(pl.multiple_of(self.there * width, 128), width)

    def ff_columns(self, r, c):
        return pl.ds(pl.multiple_of(r * HALF_FF + c * SLICE, 128), SLICE)

    def rest(self, kind, whole, crossed, order, direct):
        yield
        arrive(crossed)
        yield from spread(
            self.here, self.wires, kind, whole, self.held, order, direct=direct
        )

    def narrow(self, shard, whole, first, width, order):
        columns = pl.ds(first, width)
        source = shard.at[self.x, self.y, :, columns]
        target = whole.at[self.zh, self.core, self.x, self.y, :, columns]
        crossed = [self.wires.push(source, target, self.cross[0])]
        yield
        arrive(crossed)
        held = without(self.held, "z")
        kind = OneCore(first, width, self.core)
        yield from spread(self.here, self.wires, kind, whole, held, order, direct="xy")
        passed = whole.at[1 - self.zh, self.core, :, :, :, columns]
        beside = [self.wires.push(passed, passed, self.sibling)]
        yield
        arrive(beside)

    def wide(self, shard, whole, order):
        crossed = [
            self.wires.push(
                shard.at[self.x, self.y, :, self.ff_columns(self.there, (self.core + t) % 2)],
                whole.at[self.zh, self.core, self.x, self.y, :, self.part(SLICE)],
                self.cross[t],
            )
            for t in range(2)
        ]
        yield from self.rest(ShardsByCore(HALF_FF), whole, crossed, order, "y")

    def down(self, shard, whole, order):
        columns = pl.ds(pl.multiple_of(self.y * 256, 256), 256)
        source = shard.at[self.x, self.there, :, columns]
        target = whole.at[self.zh, self.x, self.there, :, columns]
        crossed = [self.wires.push(source, target, self.cross[0])]
        yield from self.rest(ColumnsByY(144), whole, crossed, order, "x")

    def from_this_chip(self, narrow=(), wide=(), down=()):
        beside, kept = ([], [])
        for shard, whole in narrow:
            target = whole.at[self.zh, self.core]
            beside.append(self.wires.push(shard, target, self.sibling))
            kept.append(self.wires.move(shard, target))
        for shard, whole in wide:
            for r in range(2):
                target = whole.at[self.zh, self.core, :, :, :, pl.ds(r * SLICE, SLICE)]
                theirs = shard.at[:, :, :, self.ff_columns(r, 1 - self.core)]
                mine = shard.at[:, :, :, self.ff_columns(r, self.core)]
                beside.append(self.wires.push(theirs, target, self.sibling))
                kept.append(self.wires.move(mine, target))
        for shard, whole in down:
            kept.append(self.wires.move(shard, whole.at[self.zh]))
        for _ in range(6):
            yield
        arrive(beside)
        for copy in kept:
            copy.wait()


WIDE_FETCH = (
    (ShardsByCore(HALF_FF), ("y", "x", "z")),
    (ShardsByCore(HALF_FF), ("z", "y", "x")),
    (ColumnsByY(144), ("x", "z", "y")),
)


def gather_kernel(
    qkv, out, gate, up, down, qkv_all, out_all, gate_all, up_all, down_all, sends, receives, moves
):
    wires = Wires(sends, receives, moves)
    here = Place()
    fetch = Fetch(here, wires)
    greet_rings(here, fetch.cross)
    in_turn(
        [
            fetch.narrow(qkv, qkv_all, 0, 1024, ("x", "y")),
            fetch.narrow(qkv, qkv_all, 1024, 1024, ("y", "x")),
            fetch.narrow(out, out_all, 0, D, ("x", "y")),
            fetch.wide(gate, gate_all, WIDE_FETCH[0][1][:2]),
            fetch.wide(up, up_all, WIDE_FETCH[1][1][:2]),
            fetch.down(down, down_all, WIDE_FETCH[2][1][:2]),
            fetch.from_this_chip(
                ((qkv, qkv_all), (out, out_all)),
                ((gate, gate_all), (up, up_all)),
                ((down, down_all),),
            ),
        ]
    )
    wires.finish_sends()


def gather(qkv, out, gate, up, down):
    rows = (4, 4, 16)
    qkv, out, *wide = wired_call(
        gather_kernel,
        [
            shape(2, 2, *rows, 2048),
            shape(2, 2, *rows, D),
            shape(2, 2, *rows, HALF_FF),
            shape(2, 2, *rows, HALF_FF),
            shape(2, 4, 2, 144, D),
        ],
        (
            qkv.reshape(*rows, 2048),
            out.reshape(*rows, D),
            gate.reshape(*rows, FF),
            up.reshape(*rows, FF),
            down.reshape(4, 2, 144, D),
        ),
        1,
        "gather",
        3 * 8 + 9 + 6 + 5 + 6,
        7,
        in_specs=[HBM] * 5,
        out_specs=[ANY] * 2 + [HBM] * 3,
    )
    return qkv.reshape(D, 2048), out.reshape(D, D), wide


def fetch_last(here, wires, wide):
    tasks = []
    for (kind, order), whole in zip(WIDE_FETCH, wide):
        at = {"zh": 1 - here.zh, "zl": here.zl, "x": here.x, "y": here.y}
        for axis in order[:2]:
            at = without(at, axis)
        task = spread(here, wires, kind, whole, at, order[2:])
        tasks.append(later(task, 1) if order[2] == "z" else task)
    return tasks


WIDE = (
    (0, RowsByShard(HALF_FF), ("z", "x", "y"), ("y", "x", "z")),
    (1, RowsByShard(HALF_FF), ("x", "y", "z"), ("z", "y", "x")),
    (2, ColumnsByY(144), ("y", "z", "x"), ("x", "z", "y")),
    (3, ColumnsByY(32), ("y", "z", "x"), ("x", "z", "y")),
)
NARROW = (
    (0, RowsByPlane(0, 1024), ("z", "x", "y"), ("z", "y", "x")),
    (0, RowsByPlane(1024, 1024), ("x", "y", "z"), ("x", "z", "y")),
)
FIRST_DIRECT = ("y", "y", "x", "x")
WIDE_DIMS = (
    (2, 2, 4, 4, 16, HALF_FF),
    (2, 2, 4, 4, 16, HALF_FF),
    (2, 4, 2, 144, D),
    (2, 4, 2, 32, D),
)
QKV_DIMS = (2, 4, 4, 16, 2048)
PIECE_DIMS = ((16, HALF_FF), (16, HALF_FF), (144, 256), (32, 256))


def slot_shapes(parts):
    found = []
    for _, kind, order, _ in parts:
        at = {}
        for axis in order:
            at = fix(at, axis, 0)
            found.append((6, *kind.open_dims(at), *kind.tail_dims({**at, "half": 0})))
    return found


def each_block(kind, at, body):
    dims = kind.open_dims(at)

    def step(i, _):
        inner, rest = ([], i)
        for n in reversed(dims):
            inner.insert(0, rest % n)
            rest = rest // n
        picks = iter(inner)
        lead = [next(picks) if o is None else o for o in kind.order(at)]
        body((*lead, *kind.tail(at)), (*inner, slice(None), slice(None)))
        return 0

    lax.fori_loop(0, math.prod(dims), step, 0)


def reduce_one(here, wires, kind, grad, total, slots, order, direct_from):
    at = {}
    for step, axis in enumerate(order):
        source, slot = (grad if step == 0 else total, slots[step])
        (right_place, right), (left_place, left) = (here.along(axis, 1), here.along(axis, 3))
        far_place, _ = here.along(axis, 2)
        mine = fix(at, axis, getattr(here, axis))

        def half_of(place, half):
            return {**fix(at, axis, place), "half": half}

        if step >= direct_from:
            copies = [
                wires.push(
                    kind.view(source, half_of(here.along(axis, s)[0], half)),
                    slot.at[2 * j + half],
                    here.along(axis, s)[1],
                )
                for j, s in enumerate(STEPS)
                for half in range(2)
            ]
            yield
            arrive(copies)
            for half in range(2):

                def add_all(whole, part):
                    value = total[whole].astype(F32)
                    for j in range(3):
                        value += slot[(2 * j + half, *part)].astype(F32)
                    total[whole] = value.astype(BF16)

                each_block(kind, {**mine, "half": half}, add_all)
            at = mine
            continue
        relays = [
            wires.push(kind.view(source, half_of(far_place, 0)), slot.at[4], right),
            wires.push(kind.view(source, half_of(far_place, 1)), slot.at[5], left),
        ]
        arriving = [
            wires.push(kind.view(source, half_of(right_place, 1)), slot.at[1], right),
            wires.push(kind.view(source, half_of(left_place, 0)), slot.at[2], left),
        ]
        kept = []
        if step == 0:
            for where in (half_of(right_place, 0), half_of(left_place, 1), mine):
                kept.append(wires.move(kind.view(source, where), kind.view(total, where)))
        yield
        for j, place, half, target, onward in (
            (4, right_place, 0, 0, right),
            (5, left_place, 1, 3, left),
        ):
            if kept:
                kept.pop(0).wait()
            arrive([relays[j - 4]])

            def pass_on(whole, part):
                value = slot[(j, *part)].astype(F32) + total[whole].astype(F32)
                slot[(j, *part)] = value.astype(BF16)

            each_block(kind, half_of(place, half), pass_on)
            arriving.append(wires.push(slot.at[j], slot.at[target], onward))
        yield
        if kept:
            kept.pop(0).wait()
        arrive(arriving)
        for half in range(2):

            def add_up(whole, part):
                value = total[whole].astype(F32) + slot[(half, *part)].astype(F32)
                total[whole] = (value + slot[(2 + half, *part)].astype(F32)).astype(BF16)

            each_block(kind, {**mine, "half": half}, add_up)
        at = mine


def reduce_weights_kernel(*refs):
    grad, gains = refs[4:6]
    nears, (gate_beside, up_beside, qkv_out, gains_out) = (refs[6:10], refs[10:14])
    total, slots = (refs[14], refs[15:21])
    gain_slots, sends, receives, moves = refs[21:]
    besides = (gate_beside, up_beside)

    here = Place()
    wires = Wires(sends, receives, moves)
    core = here.core
    sibling = here.sibling()
    greet_rings(here)
    held = {"zh": here.zh, "zl": here.zl, "x": here.x, "y": here.y}

    def all_gains():
        sums = gains[...]
        for stage, axis in enumerate(("core", "x", "y", "z")):
            me = getattr(here, axis)
            gain_slots[stage, me] = sums
            source = gain_slots.at[stage, me]
            if axis == "core":
                others = [sibling]
            else:
                others = [here.along(axis, s)[1] for s in STEPS]
            copies = [wires.push(source, source, device) for device in others]
            yield
            arrive(copies)
            sums = gain_slots[stage, 0] + gain_slots[stage, 1]
            if axis != "core":
                sums = sums + gain_slots[stage, 2] + gain_slots[stage, 3]
        gains_out[...] = sums

    def narrow(p):
        _, kind, order, back = NARROW[p]
        yield from reduce_one(
            here, wires, kind, grad, total, slots[3 * p : 3 * p + 3], order, 1
        )
        own = wires.move(kind.view(total, held), kind.view(qkv_out, held, 1))
        own.wait()
        yield from spread(here, wires, kind, qkv_out, held, back, 1, direct="xy")

    def wide(p):
        _, kind, _, back = WIDE[p]
        at = held
        for axis in back[:2]:
            at = without(at, axis)
        yield from spread(here, wires, kind, nears[p], at, back[2:], 1)
        if p < 2:
            copies = [wires.push(nears[p].at[1 - core], besides[p], sibling)]
            yield
            arrive(copies)

    in_turn(
        [narrow(p) for p in range(2)]
        + [later(wide(p), rounds) for p, rounds in ((1, 2), (2, 2), (3, 1), (0, 4))]
        + [all_gains()]
    )
    wires.finish_sends()


def reduce_weights(nears, qkv, gains):
    outs = [
        *(shape(*d[1:]) for d in WIDE_DIMS),
        shape(*WIDE_DIMS[0][2:]),
        shape(*WIDE_DIMS[1][2:]),
        shape(*QKV_DIMS[1:]),
        shape(*gains.shape, dtype=F32),
    ]
    scratch = [pltpu.VMEM(QKV_DIMS, BF16)]
    scratch += [pltpu.VMEM(s, BF16) for s in slot_shapes(NARROW)]
    scratch += [pltpu.VMEM((4, 4, *gains.shape), F32)]
    gate, up, down, out, gate_beside, up_beside, qkv, gains = wired_call(
        reduce_weights_kernel,
        outs,
        [*nears, qkv.reshape(QKV_DIMS), gains],
        2,
        "reduce_weights",
        10 + 2 * (18 + 7) + 1 + 3 * 4 + 2,
        2 * 4,
        scratch,
        [HBM] * 4 + [ANY] + [VMEM],
        [HBM] * 7 + [VMEM],
        vmem=40 * MIB,
        aliases={i: i for i in range(4)},
    )
    core = lax.axis_index("fsdp") % 2

    def joined(near, beside):
        own = lax.dynamic_index_in_dim(near, core, 0, keepdims=False).reshape(256, HALF_FF)
        beside = beside.reshape(256, HALF_FF)
        first, second = (jnp.where(core == 0, own, beside), jnp.where(core == 0, beside, own))
        pieces = [f[:, r * SLICE : (r + 1) * SLICE] for r in range(2) for f in (first, second)]
        return jnp.concatenate(pieces, axis=1)

    gate, up = (joined(gate, gate_beside), joined(up, up_beside))
    return (
        qkv.reshape(256, 2048),
        out.reshape(256, D),
        gate,
        up,
        down.reshape(SLICE, D),
        gains,
    )


def head_columns(head):
    return pl.ds(pl.multiple_of(head * 128, 128), 128)


def seats(here):
    me = here.ctx
    quarter, seat = (me // QUARTER, me % QUARTER)
    near = [quarter * QUARTER + (seat + s) % QUARTER for s in range(1, QUARTER)]
    far = [(me + s) % RING for s in range(1, RING)]
    return me, seat, near, far


def to_heads_kernel(query, key_value, query_out, key_value_out, sends, receives, moves):
    here = Place()
    wires = Wires(sends, receives, moves)
    me, seat, near, far = seats(here)
    greet([(k, here.fsdp) for k in far])
    copies = [
        wires.push(query.at[:, head_columns(k % QUARTER)], query_out.at[seat], (k, here.fsdp))
        for k in near
    ]
    copies += [
        wires.push(key_value.at[:, head_columns(k % QUARTER)], key_value_out.at[me], (k, here.fsdp))
        for k in far
    ]
    kept = [
        wires.move(query.at[:, head_columns(seat)], query_out.at[seat]),
        wires.move(key_value.at[:, head_columns(seat)], key_value_out.at[me]),
    ]
    arrive(copies)
    for copy in kept:
        copy.wait()
    wires.finish_sends()


def to_heads(query, key_value):
    outs = [shape(QUARTER, TOKENS, 128), shape(RING, TOKENS, 128)]
    return wired_call(to_heads_kernel, outs, [query, key_value], 3, "to_heads", 38, 2)


def grad_to_heads_kernel(grad, branch, grad_out, branch_pair, sends, receives, moves):
    here = Place()
    wires = Wires(sends, receives, moves)
    _, seat, near, _ = seats(here)
    greet([(k, here.fsdp) for k in near] + [here.sibling()])
    copies = [
        wires.push(grad.at[:, head_columns(k % QUARTER)], grad_out.at[seat], (k, here.fsdp))
        for k in near
    ]
    copies.append(wires.push(branch, branch_pair.at[here.core], here.sibling()))
    kept = [
        wires.move(grad.at[:, head_columns(seat)], grad_out.at[seat]),
        wires.move(branch, branch_pair.at[here.core]),
    ]
    arrive(copies)
    for copy in kept:
        copy.wait()
    wires.finish_sends()


def grad_to_heads(grad, branch):
    outs = [shape(QUARTER, TOKENS, 128), shape(2, TOKENS, D)]
    return wired_call(grad_to_heads_kernel, outs, [grad, branch], 4, "grad_to_heads", 8, 2)


def to_tokens_kernel(query, query_out, sends, receives, moves):
    here = Place()
    wires = Wires(sends, receives, moves)
    _, seat, near, _ = seats(here)
    greet([(k, here.fsdp) for k in near])
    columns = query_out.at[:, head_columns(seat)]
    copies = [wires.push(query.at[k % QUARTER], columns, (k, here.fsdp)) for k in near]
    kept = wires.move(query.at[seat], columns)
    arrive(copies)
    kept.wait()
    wires.finish_sends()


def to_tokens(query):
    return wired_call(to_tokens_kernel, [shape(TOKENS, D)], [query], 5, "to_tokens", 7, 1)[0]


def grads_to_tokens_kernel(*refs):
    query, key_value, pieces = (refs[0], refs[1], refs[2:6])
    query_out, key_value_out, nears = (refs[6], refs[7], refs[8:12])
    here = Place()
    wires = Wires(*refs[12:])
    me, seat, near, far = seats(here)
    greet([(k, here.fsdp) for k in far])
    held = {"zh": here.zh, "zl": here.zl, "x": here.x, "y": here.y}

    def back():
        columns = query_out.at[:, head_columns(seat)]
        copies = [wires.push(query.at[k % QUARTER], columns, (k, here.fsdp)) for k in near]
        copies += [
            wires.push(key_value.at[k], key_value_out.at[me], (k, here.fsdp)) for k in far
        ]
        kept = [
            wires.move(query.at[seat], columns),
            wires.move(key_value.at[me], key_value_out.at[me]),
        ]
        for _ in range(3):
            yield
        arrive(copies)
        for copy in kept:
            copy.wait()

    def share(p):
        _, kind, _, order = WIDE[p]
        own = wires.move(pieces[p], kind.view(nears[p], held, 1))
        own.wait()
        yield from spread(
            here, wires, kind, nears[p], held, order[:2], 1, direct=FIRST_DIRECT[p]
        )

    in_turn([share(p) for p in range(4)] + [back()])
    wires.finish_sends()


def grads_to_tokens(query, key_value, pieces):
    query_grad, key_value_grad, *nears = wired_call(
        grads_to_tokens_kernel,
        [shape(TOKENS, D), shape(RING, TOKENS, 128), *(shape(*d[1:]) for d in WIDE_DIMS)],
        [query, key_value, *pieces],
        6,
        "grads_to_tokens",
        38 + 7 + 4 + 4 + 4,
        6,
        in_specs=[ANY] * 2 + [HBM] * 4,
        out_specs=[ANY] * 2 + [HBM] * 4,
    )
    return query_grad, key_value_grad, nears


def half_columns(r, core):
    return pl.ds(pl.multiple_of(r * 512 + core * 256, 256), 256)


def share_kernel(whole, halved, *refs):
    n = whole + halved
    ins, outs = (refs[:n], refs[n : 2 * n])
    here = Place()
    wires = Wires(*refs[2 * n :])
    core = here.core
    sibling = here.sibling()
    greet([sibling])
    copies, kept = ([], [])
    for source, target in zip(ins[:whole], outs[:whole]):
        copies.append(wires.push(source, target.at[core], sibling))
        kept.append(wires.move(source, target.at[core]))
    for source, target in zip(ins[whole:], outs[whole:]):
        for r in range(2):
            place = target.at[core, :, pl.ds(r * 256, 256)]
            copies.append(wires.push(source.at[:, half_columns(r, 1 - core)], place, sibling))
            kept.append(wires.move(source.at[:, half_columns(r, core)], place))
    arrive(copies)
    for copy in kept:
        copy.wait()
    wires.finish_sends()


def share(whole, halved, collective_id):
    outs = [shape(2, *a.shape, dtype=a.dtype) for a in whole]
    outs += [shape(2, a.shape[0], 512, dtype=a.dtype) for a in halved]
    count = len(whole) + 2 * len(halved)
    done = wired_call(
        functools.partial(share_kernel, len(whole), len(halved)),
        outs,
        [*whole, *halved],
        collective_id,
        "share",
        count,
        count,
    )
    return [a.reshape(2 * a.shape[1], a.shape[2]) for a in done]


def hand_over_kernel(count, *refs):
    ins, outs = (refs[:count], refs[count : 2 * count])
    here = Place()
    wires = Wires(*refs[2 * count :])
    sibling = here.sibling()
    greet([sibling])
    copies = [wires.push(i.at[1 - here.core], o, sibling) for i, o in zip(ins, outs)]
    arrive(copies)
    wires.finish_sends()


def hand_over(partials, collective_id):
    return wired_call(
        functools.partial(hand_over_kernel, len(partials)),
        [shape(*a.shape[1:], dtype=a.dtype) for a in partials],
        partials,
        collective_id,
        "hand_over",
        len(partials),
        0,
    )


def nt(left, right):
    return lax.dot_general(left, right, (((1,), (1,)), ((), ())), preferred_element_type=F32)


def nn(left, right):
    return lax.dot_general(left, right, (((1,), (0,)), ((), ())), preferred_element_type=F32)


def query_block(ref, t):
    block = ref[t].astype(F32)
    both = jnp.concatenate([block, pltpu.roll(block, 64, 1)], axis=0)
    low = lax.broadcasted_iota(jnp.int32, (128, 128), 1) < 64
    return jnp.where(low, both, 0.0)


def query_pair(ref, u):
    return [query_block(ref, 2 * u), query_block(ref, 2 * u + 1)]


def first_allowed(position, starts_ref):
    begin = jnp.zeros_like(position)
    for n in range(4):
        begin = jnp.maximum(begin, jnp.where(starts_ref[n] <= position, starts_ref[n], 0))
    return begin


def heads_beside(rows):
    low = lax.broadcasted_iota(jnp.int32, (64, 128), 1) < 64
    return jnp.where(low, rows[:64], pltpu.roll(rows[64:], 64, 1)).astype(BF16)


def attend_task(
    counts, first_block, starts_ref, order_ref, query_ref, key_value_ref, out_ref, exact_ref,
    sum_ref, value_ref, key_at_ref,
):
    def key_places(j, _):
        lane = lax.broadcasted_iota(jnp.int32, (1, 128), 1)
        block = jnp.where(lane < 64, order_ref[2 * j], order_ref[2 * j + 1])
        key_at_ref[:, pl.ds(pl.multiple_of(j * 128, 128), 128)] = block * 64 + lane % 64
        return 0

    def values(j, _):
        rows = pl.ds(pl.multiple_of(j * 256, 256), 256)
        block = pltpu.roll(key_value_ref[rows, :].astype(F32), 64, 1)
        low = lax.broadcasted_iota(jnp.int32, (256, 128), 1) < 64
        value_ref[rows, :] = jnp.where(low, block, 1.0).astype(BF16)
        return 0

    def blocks(u, _):
        queries = jnp.concatenate(query_pair(query_ref, u), axis=0).astype(BF16)
        inner = lax.broadcasted_iota(jnp.int32, (128, 1), 0) % 64
        block = first_block + 2 * u
        position = jnp.concatenate(
            [order_ref[block] * 64 + inner, order_ref[block + 1] * 64 + inner], axis=0
        )
        begin = first_allowed(position, starts_ref)

        def tile(j, total):
            rows = pl.ds(pl.multiple_of(j * KEY_TILE, KEY_TILE), KEY_TILE)
            scores = nt(queries, key_value_ref[rows, :])
            key = key_at_ref[:, rows]
            allowed = (key <= position) & (key >= begin)
            weight = jnp.where(allowed, jnp.exp2(scores * SCORE_TO_EXP2), 0.0)
            return total + nn(weight.astype(BF16), value_ref[rows, :])

        total = lax.fori_loop(0, SEQ // KEY_TILE, tile, jnp.zeros((256, 128), F32))
        attended = total / pltpu.roll(total, 64, 1)
        low = lax.broadcasted_iota(jnp.int32, (256, 128), 1) < 64
        attended = jnp.where(low, attended, 0.0)
        for n in range(2):
            rows = slice(128 * n, 128 * n + 128)
            exact_ref[2 * u + n] = attended[rows]
            out_ref[2 * u + n] = heads_beside(attended[rows])
            sum_ref[2 * u + n] = jnp.transpose(total[rows])[64:72]
        return 0

    lax.fori_loop(0, SEQ // 256, values, 0)
    lax.fori_loop(0, SEQ // 128, key_places, 0)
    first = 0
    for count in counts:
        lax.fori_loop(first, first + count, blocks, 0)
        first += count
        yield


def attend_kernel(
    starts, order, query, key_value, gate_in, up_in, down_in, attended, exact, sums, gate_all,
    up_all, down_all, value_ref, key_at_ref, sends, receives, moves,
):
    wires = Wires(sends, receives, moves)
    here = Place()
    greet_rings(here)
    in_turn(
        [
            *fetch_last(here, wires, (gate_all, up_all, down_all))[::-1],
            attend_task(
                (6, 2), here.ctx // QUARTER * 16, starts, order, query, key_value, attended, exact,
                sums, value_ref, key_at_ref,
            ),
        ]
    )
    wires.finish_sends()


def attend(starts, order, queries, key_values, wide):
    outs = [
        shape(16, 64, 128),
        shape(16, 128, 128, dtype=F32),
        shape(16, 8, 128, dtype=F32),
        *(shape(*a.shape) for a in wide),
    ]
    attended, exact, sums, gate, up, down = wired_call(
        attend_kernel,
        outs,
        [starts, order, queries, key_values, *wide],
        10,
        "attend",
        1 + 4 + 4,
        1,
        [pltpu.VMEM((SEQ, 128), BF16), pltpu.VMEM((1, SEQ), jnp.int32)],
        [SMEM] * 2 + [VMEM] * 2 + [HBM] * 3,
        [VMEM] * 3 + [HBM] * 3,
        vmem=40 * MIB,
        aliases={4 + i: 3 + i for i in range(3)},
    )
    weights = (gate.reshape(D, HALF_FF), up.reshape(D, HALF_FF), down.reshape(HALF_FF, D))
    return attended, exact, sums, weights


def attend_back_task(
    counts, first_block, starts_ref, order_ref, query_ref, key_value_ref, grad_ref, exact_ref,
    sum_ref, query_grad_ref, key_value_grad_ref, across_ref, total_ref, key_at_ref,
):
    total_ref[...] = jnp.zeros_like(total_ref)

    def key_places(j, _):
        inner = lax.broadcasted_iota(jnp.int32, (64, 1), 0)
        key_at_ref[pl.ds(pl.multiple_of(j * 64, 64), 64), :] = order_ref[j] * 64 + inner
        return 0

    def turn(j, _):
        rows = pl.ds(pl.multiple_of(j * 128, 128), 128)
        across_ref[:, rows] = jnp.transpose(key_value_ref[rows, :].astype(F32)).astype(BF16)
        return 0

    def blocks(u, _):
        queries, grads = (query_pair(query_ref, u), query_pair(grad_ref, u))
        delta = [
            jnp.sum(jnp.transpose(grad * exact_ref[2 * u + n]), axis=0, keepdims=True)
            for n, grad in enumerate(grads)
        ]
        delta = jnp.concatenate(delta, axis=1)
        total_exp2 = jnp.concatenate(
            [jnp.log2(sum_ref[2 * u + n][0:1]) for n in range(2)], axis=1
        )
        grads = [pltpu.roll(grad, 64, 1) for grad in grads]
        both = jnp.concatenate(queries + grads, axis=0).astype(BF16)
        inner = lax.broadcasted_iota(jnp.int32, (1, 128), 1) % 64
        block = first_block + 2 * u
        position = jnp.concatenate(
            [order_ref[block] * 64 + inner, order_ref[block + 1] * 64 + inner], axis=1
        )
        begin = first_allowed(position, starts_ref)

        def tile(j, query_grad):
            rows = pl.ds(pl.multiple_of(j * KEY_TILE_BACK, KEY_TILE_BACK), KEY_TILE_BACK)
            products = nt(key_value_ref[rows, :], both)
            key = key_at_ref[rows, :]
            allowed = (key <= position) & (key >= begin)
            prob = jnp.where(
                allowed, jnp.exp2(products[:, :256] * SCORE_TO_EXP2 - total_exp2), 0.0
            )
            score = (prob * (products[:, 256:] - delta)).astype(BF16)
            side = jnp.concatenate([score, prob.astype(BF16)], axis=1)
            total_ref[rows, :] += nn(side, both)
            return query_grad + nn(across_ref[:, rows], score)

        query_grad = lax.fori_loop(
            0, SEQ // KEY_TILE_BACK, tile, jnp.zeros((128, 256), F32)
        )
        for n in range(2):
            rows = jnp.transpose(query_grad[:, 128 * n : 128 * n + 128])
            query_grad_ref[2 * u + n] = heads_beside(rows * float(HEAD_SIZE) ** (-0.5))
        return 0

    def put_back(j, _):
        rows = pl.ds(pl.multiple_of(j * 256, 256), 256)
        low = lax.broadcasted_iota(jnp.int32, (256, 128), 1) < 64
        scale = jnp.where(low, float(HEAD_SIZE) ** (-0.5), 1.0)
        key_value_grad_ref[rows, :] = (total_ref[rows, :] * scale).astype(BF16)
        return 0

    lax.fori_loop(0, SEQ // 128, turn, 0)
    lax.fori_loop(0, 64, key_places, 0)
    first = 0
    for count in counts:
        lax.fori_loop(first, first + count, blocks, 0)
        first += count
        yield
    lax.fori_loop(0, SEQ // 256, put_back, 0)


def attend_back_kernel(*refs):
    attention, grads = (refs[:7], refs[7:11])
    outs, pieces = (refs[11:13], refs[13:17])
    scratch, totals, slots = (refs[17:20], refs[20:24], refs[24:36])
    here = Place()
    wires = Wires(*refs[36:])
    greet_rings(here)
    at = {"zh": here.zh, "zl": here.zl, "x": here.x, "y": here.y}

    def reduce(p):
        _, kind, order, _ = WIDE[p]
        yield from reduce_one(
            here, wires, kind, grads[p], totals[p], slots[3 * p : 3 * p + 3], order, 2
        )
        own = wires.move(kind.view(totals[p], at), pieces[p])
        yield
        own.wait()

    first_block = here.ctx // QUARTER * 16
    in_turn(
        [reduce(p) for p in range(4)]
        + [attend_back_task((3, 3, 1, 1), first_block, *attention, *outs, *scratch)]
    )
    wires.finish_sends()


def attend_back(starts, order, queries, key_values, grads, exact, sums, wide):
    ins = [starts, order, queries, key_values, grads]
    ins += [exact, sums, *(a.reshape(d) for a, d in zip(wide, WIDE_DIMS))]
    scratch = [
        pltpu.VMEM((128, SEQ), BF16),
        pltpu.VMEM((SEQ, 128), F32),
        pltpu.VMEM((SEQ, 1), jnp.int32),
    ]
    scratch += [pltpu.VMEM(d, BF16) for d in WIDE_DIMS]
    scratch += [pltpu.VMEM(s, BF16) for s in slot_shapes(WIDE)]
    query_grad, key_value_grad, *pieces = wired_call(
        attend_back_kernel,
        [shape(16, 64, 128), shape(SEQ, 128), *(shape(*d) for d in PIECE_DIMS)],
        ins,
        11,
        "attend_back",
        4 * 18,
        4 * 4,
        scratch,
        [SMEM] * 2 + [VMEM] * 5 + [HBM] * 4,
        [VMEM] * 2 + [HBM] * 4,
        vmem=58 * MIB,
    )
    return query_grad, key_value_grad, pieces


def low_lanes():
    return lax.broadcasted_iota(jnp.int32, (TOKENS, 128), 1) < 64


def head_mean(values):
    low = low_lanes()
    first = jnp.sum(jnp.where(low, values, 0.0), axis=1, keepdims=True)
    second = jnp.sum(jnp.where(low, 0.0, values), axis=1, keepdims=True)
    return jnp.where(low, first, second) * (1.0 / HEAD_SIZE)


def other_half(values):
    first = lax.broadcasted_iota(jnp.int32, (TOKENS, 128), 1) % 64 < 32
    return jnp.where(first, pltpu.roll(values, 96, 1), pltpu.roll(values, 32, 1))


def chunk(j):
    return slice(128 * j, 128 * j + 128)


def project_kernel(
    x_ref, gain_ref, weight_ref, query_gain_ref, key_gain_ref, cosine_ref, sine_ref, normed_ref,
    query_ref, key_value_ref, projected_ref,
):
    x = x_ref[...].astype(F32)
    normed = x * lax.rsqrt(jnp.mean(x * x, axis=-1, keepdims=True) + EPSILON) * gain_ref[...]
    normed_ref[...] = normed.astype(BF16)
    projected = nn(normed_ref[...], weight_ref[...])
    projected_ref[...] = projected[:, :1536]
    low = low_lanes()

    def turned(j, gain):
        values = projected[:, chunk(j)]
        values = values * lax.rsqrt(head_mean(values * values) + EPSILON) * gain
        return values * cosine_ref[...] + other_half(values) * sine_ref[...]

    for j in range(8):
        query_ref[:, chunk(j)] = turned(j, query_gain_ref[...]).astype(BF16)
    for j in range(4):
        keys = turned(8 + j, key_gain_ref[...])
        values = projected[:, chunk(12 + j)]
        first = jnp.where(low, keys, pltpu.roll(values, 64, 1))
        second = jnp.where(low, pltpu.roll(keys, 64, 1), values)
        key_value_ref[:, chunk(2 * j)] = first.astype(BF16)
        key_value_ref[:, chunk(2 * j + 1)] = second.astype(BF16)


def project(x, gain, weight, query_gain, key_gain, cosine, sine):
    return pl.pallas_call(
        project_kernel,
        out_shape=[
            shape(TOKENS, D),
            shape(TOKENS, D),
            shape(TOKENS, D),
            shape(TOKENS, 1536, dtype=F32),
        ],
        in_specs=[VMEM] * 7,
        out_specs=[VMEM] * 4,
        compiler_params=pltpu.CompilerParams(vmem_limit_bytes=32 * MIB),
        name="project",
    )(x, gain, weight, query_gain, key_gain, cosine, sine)


def project_back_kernel(
    query_grad_ref, key_value_grad_ref, projected_ref, x_ref, grad_resid_ref, gain_ref, weight_ref,
    query_gain_ref, key_gain_ref, cosine_ref, sine_ref, ffn_gain_grad_ref, grad_projected_ref,
    grad_inputs_ref, gains_ref,
):
    low = low_lanes()

    def back(j, grad, gain):
        grad = grad * cosine_ref[...] + other_half(grad * sine_ref[...])
        values = projected_ref[:, chunk(j)]
        scale = lax.rsqrt(head_mean(values * values) + EPSILON)
        unit = values * scale
        gain_grad = jnp.sum(grad * unit, axis=0, keepdims=True)
        grad = grad * gain
        grad = scale * (grad - unit * head_mean(grad * unit))
        grad_projected_ref[:, chunk(j)] = grad.astype(BF16)
        return gain_grad

    query_gain_grad = jnp.zeros((1, 128), F32)
    for j in range(8):
        grad = query_grad_ref[:, chunk(j)].astype(F32)
        query_gain_grad += back(j, grad, query_gain_ref[...])
    key_gain_grad = jnp.zeros((1, 128), F32)
    for j in range(4):
        first, second = [
            sum(key_value_grad_ref[8 * q + 2 * j + n].astype(F32) for q in range(4))
            for n in range(2)
        ]
        keys = jnp.where(low, first, pltpu.roll(second, 64, 1))
        values = jnp.where(low, pltpu.roll(first, 64, 1), second)
        key_gain_grad += back(8 + j, keys, key_gain_ref[...])
        grad_projected_ref[:, chunk(12 + j)] = values.astype(BF16)

    grad = nt(grad_projected_ref[...], weight_ref[...])
    x = x_ref[...].astype(F32)
    scale = lax.rsqrt(jnp.mean(x * x, axis=-1, keepdims=True) + EPSILON)
    unit = x * scale
    gain_grad = jnp.sum(grad * unit, axis=0, keepdims=True)
    grad = grad * gain_ref[...]
    grad = scale * (grad - unit * jnp.mean(grad * unit, axis=-1, keepdims=True))
    grad_inputs_ref[...] = (grad_resid_ref[...] + grad).astype(BF16)

    gains_ref[...] = jnp.zeros_like(gains_ref)
    for j in range(8):
        gains_ref[j : j + 1, :] = gain_grad[:, chunk(j)]
        gains_ref[8 + j : 9 + j, :] = ffn_gain_grad_ref[:, chunk(j)]
    gains_ref[16:17, :] = query_gain_grad + pltpu.roll(query_gain_grad, 64, 1)
    gains_ref[17:18, :] = key_gain_grad + pltpu.roll(key_gain_grad, 64, 1)


def project_back(*ins):
    return pl.pallas_call(
        project_back_kernel,
        out_shape=[shape(TOKENS, 2048), shape(TOKENS, D), shape(24, 128, dtype=F32)],
        in_specs=[VMEM] * 12,
        out_specs=[VMEM] * 3,
        compiler_params=pltpu.CompilerParams(vmem_limit_bytes=40 * MIB),
        name="project_back",
    )(*ins)


def rms_norm(values, gain_row):
    return (
        values * lax.rsqrt(jnp.mean(values * values, axis=-1, keepdims=True) + EPSILON) * gain_row
    )


def rope_tables(positions):
    lane = jnp.arange(128, dtype=jnp.int32)
    frequency = ROPE_BASE ** (-2.0 * (lane % 32).astype(F32) / HEAD_SIZE)
    angles = positions.astype(F32)[:, None] * frequency[None, :]
    sign = jnp.where(lane % 64 < 32, -1.0, 1.0)
    return jnp.cos(angles), jnp.sin(angles) * sign[None, :]


def outer_sum(left, right):
    return lax.dot_general(
        left, right, (((0,), (0,)), ((), ())), preferred_element_type=F32
    ).astype(BF16)


def matmul(left, right):
    return jnp.dot(left, right, preferred_element_type=F32)


def positions_at(block_order, first_row, total_row_count, half_rows):
    row_ids = first_row + jnp.arange(total_row_count, dtype=jnp.int32)
    blocks = row_ids // half_rows
    lookup = jnp.arange(block_order.shape[0], dtype=jnp.int32)
    picked = jnp.sum(jnp.where(blocks[:, None] == lookup[None, :], block_order[None, :], 0), axis=1)
    return picked * half_rows + row_ids % half_rows


def per_device(
    inputs,
    cotangent,
    qkv_weight,
    out_weight,
    gate_weight,
    up_weight,
    down_weight,
    gain_attn,
    gain_query,
    gain_key,
    gain_ffn,
    block_order,
    doc_starts,
):
    cycle_index = lax.axis_index("ctx")
    core = lax.axis_index("fsdp") % 2
    qkv_all, out_all, wide = gather(
        qkv_weight, out_weight, gate_weight, up_weight, down_weight
    )
    places = (doc_starts[0], block_order)
    positions = positions_at(block_order, cycle_index * TOKENS, TOKENS, TOKENS // 2)

    resid_in = inputs[0].astype(F32)
    gain_row = gain_attn.reshape(1, D)
    head_gains = [jnp.concatenate([g, g]).reshape(1, 128) for g in (gain_query, gain_key)]
    tables = rope_tables(positions)
    normed_low, queries, key_values, projected = project(
        inputs[0], gain_row, qkv_all, *head_gains, *tables
    )
    query_part, key_value_part = to_heads(queries, key_values)
    query_part = query_part.reshape(16, 64, 128)
    key_value_part = key_value_part.reshape(SEQ, 128)
    attended, exact, sums, (gate_all, up_all, down_all) = attend(
        *places, query_part, key_value_part, wide
    )
    attended_low = to_tokens(attended.reshape(QUARTER, TOKENS, 128))

    residual = resid_in + matmul(attended_low, out_all)
    normed_ffn, norm_ffn_pull = jax.vjp(rms_norm, residual, gain_ffn)
    grad_out = cotangent[0]
    ffn_pair, cotangent_pair, normed_half, attended_half = share(
        [normed_ffn.astype(BF16), grad_out], [normed_low, attended_low], 7
    )
    gate_proj = matmul(ffn_pair, gate_all)
    up_proj = matmul(ffn_pair, up_all)
    hidden, gating_pull = jax.vjp(
        lambda gate_in, up_in: jax.nn.silu(gate_in) * up_in, gate_proj, up_proj
    )
    hidden_low = hidden.astype(BF16)
    out_partial = matmul(hidden_low, down_all).reshape(2, TOKENS, D)
    grad_hidden = matmul(cotangent_pair, down_all.T)
    grad_gate, grad_up = gating_pull(grad_hidden)
    gate_low = grad_gate.astype(BF16)
    up_low = grad_up.astype(BF16)
    ffn_partial = (matmul(gate_low, gate_all.T) + matmul(up_low, up_all.T)).reshape(2, TOKENS, D)
    out_rest, ffn_rest = hand_over([out_partial, ffn_partial], 8)

    def mine(pair):
        return lax.dynamic_index_in_dim(pair, core, 0, keepdims=False)

    outputs = residual + mine(out_partial) + out_rest
    grad_resid_ffn, grad_gain_ffn = norm_ffn_pull(mine(ffn_partial) + ffn_rest)
    grad_resid = grad_out.astype(F32) + grad_resid_ffn
    branch_low = grad_resid.astype(BF16)
    grad_attended = matmul(branch_low, out_all.T).astype(BF16)
    grad_part, branch_pair = grad_to_heads(grad_attended, branch_low)
    query_grad, key_value_grad, pieces = attend_back(
        *places,
        query_part,
        key_value_part,
        grad_part.reshape(16, 64, 128),
        exact,
        sums,
        (
            outer_sum(ffn_pair, gate_low),
            outer_sum(ffn_pair, up_low),
            outer_sum(hidden_low, cotangent_pair),
            outer_sum(attended_half, branch_pair.reshape(2 * TOKENS, D)),
        ),
    )
    query_grad, key_value_grad, nears = grads_to_tokens(
        query_grad.reshape(QUARTER, TOKENS, 128),
        key_value_grad.reshape(RING, TOKENS, 128),
        pieces,
    )
    grad_projected, grad_inputs, gains = project_back(
        query_grad,
        key_value_grad,
        projected,
        inputs[0],
        grad_resid,
        gain_row,
        qkv_all,
        *head_gains,
        *tables,
        grad_gain_ffn.reshape(1, D),
    )

    (projected_pair,) = share([grad_projected], [], 9)
    grad_qkv, grad_out_weight, grad_gate_weight, grad_up_weight, grad_down, gains = reduce_weights(
        nears, outer_sum(normed_half, projected_pair), gains
    )
    gains = gains.reshape(-1)
    return (
        outputs.astype(BF16)[None],
        grad_inputs[None],
        grad_qkv.astype(F32),
        grad_out_weight.astype(F32),
        grad_gate_weight.astype(F32),
        grad_up_weight.astype(F32),
        grad_down.astype(F32),
        gains[:D],
        gains[2 * D : 2 * D + HEAD_SIZE],
        gains[2 * D + 128 : 2 * D + 128 + HEAD_SIZE],
        gains[D : 2 * D],
    )


def solution(mesh):
    in_specs = (
        P("fsdp", "ctx", None),
        P("fsdp", "ctx", None),
        P("fsdp", None),
        P("fsdp", None),
        P("fsdp", None),
        P("fsdp", None),
        P("fsdp", None),
        P(),
        P(),
        P(),
        P(),
        P(),
        P("fsdp", None),
    )
    out_specs = (
        P("fsdp", "ctx", None),
        P("fsdp", "ctx", None),
        P("fsdp", None),
        P("fsdp", None),
        P("fsdp", None),
        P("fsdp", None),
        P("fsdp", None),
        P(),
        P(),
        P(),
        P(),
    )
    return jax.shard_map(
        per_device, mesh=mesh, in_specs=in_specs, out_specs=out_specs, check_vma=False
    )
```

```python
import functools
import math

import jax
import jax.numpy as jnp
from jax import lax
from jax.experimental import pallas as pl
from jax.experimental.pallas import tpu as pltpu
from jax.sharding import PartitionSpec as P

QUERY_HEADS = 16
KEY_VALUE_HEADS = 8
HEAD_SIZE = 64
FF = 4608
D = 1024
TOKENS = 128
RING = 32
QUARTER = 8
SLICE = 1152
HALF_FF = FF // 2
KEY_TILE = 1024
KEY_TILE_BACK = 1024
SEQ = 4096

EPSILON = 1e-05
ROPE_BASE = 1000000.0
SCORE_TO_EXP2 = float(HEAD_SIZE) ** (-0.5) * math.log2(math.e)

MESH = pl.DeviceIdType.MESH
ANY = pl.BlockSpec(memory_space=pl.ANY)
HBM = pl.BlockSpec(memory_space=pltpu.MemorySpace.HBM)
VMEM = pl.BlockSpec(memory_space=pltpu.VMEM)
SMEM = pl.BlockSpec(memory_space=pltpu.SMEM)
BF16 = jnp.bfloat16
F32 = jnp.float32
MIB = 1 << 20
STEPS = (1, 3, 2)


class Place:
    def __init__(self):
        self.ctx, self.fsdp = (lax.axis_index("ctx"), lax.axis_index("fsdp"))
        self.zl, self.x, self.y = (self.ctx // 16, (self.ctx // 4) % 4, self.ctx % 4)
        self.zh, self.core = (self.fsdp // 2, self.fsdp % 2)
        self.z = self.zh * 2 + self.zl

    def device(self, x=None, y=None, z=None, core=None):
        x = self.x if x is None else x
        y = self.y if y is None else y
        z = self.z if z is None else z
        core = self.core if core is None else core
        return ((z % 2) * 16 + x * 4 + y, (z // 2) * 2 + core)

    def sibling(self):
        return self.device(core=1 - self.core)

    def along(self, axis, step):
        coordinate = (getattr(self, axis) + step) % 4
        return coordinate, self.device(**{axis: coordinate})


class Wires:
    def __init__(self, sends, receives, locals_=None):
        self.sends, self.receives, self.locals_ = (sends, receives, locals_)
        self.pushed, self.moved = ([], 0)

    def push(self, source, target, device):
        at = len(self.pushed)
        copy = pltpu.make_async_remote_copy(
            src_ref=source,
            dst_ref=target,
            send_sem=self.sends.at[at],
            recv_sem=self.receives.at[at],
            device_id=device,
            device_id_type=MESH,
        )
        copy.start()
        self.pushed.append(copy)
        return copy

    def move(self, source, target):
        copy = pltpu.make_async_copy(source, target, self.locals_.at[self.moved])
        copy.start()
        self.moved += 1
        return copy

    def finish_sends(self):
        for copy in self.pushed:
            copy.wait_send()


def arrive(copies):
    for copy in copies:
        copy.wait_recv()


def greet(devices):
    barrier = pltpu.get_barrier_semaphore()
    for device in devices:
        pl.semaphore_signal(barrier, inc=1, device_id=device, device_id_type=MESH)
    pl.semaphore_wait(barrier, len(devices))


def wired_call(kernel, outs, ins, collective_id, name, copies, moves, scratch=(), in_specs=None,
               out_specs=None, vmem=32 * MIB, aliases=None):
    return pl.pallas_call(
        kernel,
        out_shape=outs,
        in_specs=[ANY] * len(ins) if in_specs is None else in_specs,
        out_specs=[ANY] * len(outs) if out_specs is None else out_specs,
        scratch_shapes=[
            *scratch,
            pltpu.SemaphoreType.DMA((copies,)),
            pltpu.SemaphoreType.DMA((copies,)),
            pltpu.SemaphoreType.DMA((max(moves, 1),)),
        ],
        compiler_params=pltpu.CompilerParams(
            collective_id=collective_id, has_side_effects=True, vmem_limit_bytes=vmem
        ),
        name=name,
        input_output_aliases=aliases or {},
    )(*ins)


def shape(*dims, dtype=BF16):
    return jax.ShapeDtypeStruct(dims, dtype)


class Pieces:
    def view(self, ref, at, skip=0):
        lead = [slice(None) if i is None else i for i in self.order(at)[skip:]]
        return ref.at[(*lead, *self.tail(at))]

    def open_dims(self, at):
        return tuple(n for n, i in zip(self.lead, self.order(at)) if i is None)

    def tail(self, at):
        first, width = self.columns(at)
        if not isinstance(first, int):
            first = pl.multiple_of(first, 128)
        return (slice(None), pl.ds(first, width))

    def tail_dims(self, at):
        return (self.rows, self.columns(at)[1])


def halved(first, width, at):
    if "half" not in at:
        return first, width
    return first + at["half"] * (width // 2), width // 2


class RowsByShard(Pieces):
    lead, rows = ((2, 2, 4, 4), 16)

    def __init__(self, width):
        self.width = width

    def order(self, at):
        return [at.get("zh"), at.get("zl"), at.get("x"), at.get("y")]

    def columns(self, at):
        return halved(0, self.width, at)


class RowsByPlane(Pieces):
    lead, rows = ((2, 4, 4), 16)

    def __init__(self, first, width):
        self.first, self.width = (first, width)

    def order(self, at):
        return [at.get("zh"), at.get("x"), at.get("y")]

    def columns(self, at):
        if "zl" not in at:
            return halved(self.first, self.width, at)
        half = self.width // 2
        return halved(self.first + half * at["zl"], half, at)


class ColumnsByY(Pieces):
    lead = (2, 4, 2)

    def __init__(self, rows):
        self.rows = rows

    def order(self, at):
        return [at.get("zh"), at.get("x"), at.get("zl")]

    def columns(self, at):
        return halved(at["y"] * 256, 256, at) if "y" in at else halved(0, D, at)


class ShardsByCore(Pieces):
    lead, rows = ((2, 2, 4, 4), 16)

    def __init__(self, width):
        self.width = width

    def order(self, at):
        return [at.get("zh"), at.get("half"), at.get("x"), at.get("y")]

    def columns(self, at):
        half = self.width // 2
        return (half * at["zl"], half) if "zl" in at else (0, self.width)


class OneCore(RowsByPlane):
    lead = (2, 2, 4, 4)

    def __init__(self, first, width, core):
        super().__init__(first, width)
        self.core = core

    def order(self, at):
        return [at.get("zh"), self.core, at.get("x"), at.get("y")]


def fix(at, axis, coordinate):
    if axis == "z":
        return {**at, "zh": coordinate // 2, "zl": coordinate % 2}
    return {**at, axis: coordinate}


def without(at, axis):
    return {a: i for a, i in at.items() if a != ("zl" if axis == "z" else axis)}


def in_turn(tasks):
    while tasks:
        tasks = [task for task in tasks if next(task, "over") != "over"]


def later(task, rounds):
    next(task)
    for _ in range(rounds + 1):
        yield
    yield from task


def spread(here, wires, kind, ref, at, order, skip=0, direct=""):
    for axis in order:
        piece = kind.view(ref, at, skip)
        if axis == "z":
            copies = [wires.push(piece, piece, here.device(z=here.zh * 2 + 1 - here.zl))]
            yield
            arrive(copies)
        elif axis in direct:
            copies = [wires.push(piece, piece, here.along(axis, s)[1]) for s in STEPS]
            yield
            arrive(copies)
        else:
            (_, right), (_, left) = (here.along(axis, 1), here.along(axis, 3))
            from_left = wires.push(piece, piece, right)
            from_right = wires.push(piece, piece, left)
            yield
            relays = []
            for half, copy, step, onward in ((0, from_left, 3, right), (1, from_right, 1, left)):
                arrive([copy])
                passing = fix(at, axis, here.along(axis, step)[0])
                passing = kind.view(ref, {**passing, "half": half}, skip)
                relays.append(wires.push(passing, passing, onward))
            yield
            arrive(relays)
        at = without(at, axis)


def greet_rings(here, others=()):
    rings = [here.along(a, s)[1] for a in ("x", "y", "z") for s in STEPS]
    greet([*rings, here.sibling(), *others])


class Fetch:
    def __init__(self, here, wires):
        self.here, self.wires = (here, wires)
        self.zh, self.core, self.x, self.y = (here.zh, here.core, here.x, here.y)
        self.there = 1 - here.zl
        self.cross = [here.device(z=3 - here.z, core=(here.core + t) % 2) for t in range(2)]
        self.sibling = here.sibling()
        self.held = {"zh": 1 - here.zh, "zl": here.zl, "x": here.x, "y": here.y}

    def part(self, width):
        return pl.ds(pl.multiple_of(self.there * width, 128), width)

    def ff_columns(self, r, c):
        return pl.ds(pl.multiple_of(r * HALF_FF + c * SLICE, 128), SLICE)

    def rest(self, kind, whole, crossed, order, direct):
        yield
        arrive(crossed)
        yield from spread(
            self.here, self.wires, kind, whole, self.held, order, direct=direct
        )

    def narrow(self, shard, whole, first, width, order):
        columns = pl.ds(first, width)
        source = shard.at[self.x, self.y, :, columns]
        target = whole.at[self.zh, self.core, self.x, self.y, :, columns]
        crossed = [self.wires.push(source, target, self.cross[0])]
        yield
        arrive(crossed)
        held = without(self.held, "z")
        kind = OneCore(first, width, self.core)
        yield from spread(self.here, self.wires, kind, whole, held, order, direct="xy")
        passed = whole.at[1 - self.zh, self.core, :, :, :, columns]
        beside = [self.wires.push(passed, passed, self.sibling)]
        yield
        arrive(beside)

    def wide(self, shard, whole, order):
        crossed = [
            self.wires.push(
                shard.at[self.x, self.y, :, self.ff_columns(self.there, (self.core + t) % 2)],
                whole.at[self.zh, self.core, self.x, self.y, :, self.part(SLICE)],
                self.cross[t],
            )
            for t in range(2)
        ]
        yield from self.rest(ShardsByCore(HALF_FF), whole, crossed, order, "y")

    def down(self, shard, whole, order):
        columns = pl.ds(pl.multiple_of(self.y * 256, 256), 256)
        source = shard.at[self.x, self.there, :, columns]
        target = whole.at[self.zh, self.x, self.there, :, columns]
        crossed = [self.wires.push(source, target, self.cross[0])]
        yield from self.rest(ColumnsByY(144), whole, crossed, order, "x")

    def from_this_chip(self, narrow=(), wide=(), down=()):
        beside, kept = ([], [])
        for shard, whole in narrow:
            target = whole.at[self.zh, self.core]
            beside.append(self.wires.push(shard, target, self.sibling))
            kept.append(self.wires.move(shard, target))
        for shard, whole in wide:
            for r in range(2):
                target = whole.at[self.zh, self.core, :, :, :, pl.ds(r * SLICE, SLICE)]
                theirs = shard.at[:, :, :, self.ff_columns(r, 1 - self.core)]
                mine = shard.at[:, :, :, self.ff_columns(r, self.core)]
                beside.append(self.wires.push(theirs, target, self.sibling))
                kept.append(self.wires.move(mine, target))
        for shard, whole in down:
            kept.append(self.wires.move(shard, whole.at[self.zh]))
        for _ in range(6):
            yield
        arrive(beside)
        for copy in kept:
            copy.wait()


WIDE_FETCH = (
    (ShardsByCore(HALF_FF), ("y", "x", "z")),
    (ShardsByCore(HALF_FF), ("z", "y", "x")),
    (ColumnsByY(144), ("x", "z", "y")),
)


def gather_kernel(
    qkv, out, gate, up, down, qkv_all, out_all, gate_all, up_all, down_all, sends, receives, moves
):
    wires = Wires(sends, receives, moves)
    here = Place()
    fetch = Fetch(here, wires)
    greet_rings(here, fetch.cross)
    in_turn(
        [
            fetch.narrow(qkv, qkv_all, 0, 1024, ("x", "y")),
            fetch.narrow(qkv, qkv_all, 1024, 1024, ("y", "x")),
            fetch.narrow(out, out_all, 0, D, ("x", "y")),
            fetch.wide(gate, gate_all, WIDE_FETCH[0][1][:2]),
            fetch.wide(up, up_all, WIDE_FETCH[1][1][:2]),
            fetch.down(down, down_all, WIDE_FETCH[2][1][:2]),
            fetch.from_this_chip(
                ((qkv, qkv_all), (out, out_all)),
                ((gate, gate_all), (up, up_all)),
                ((down, down_all),),
            ),
        ]
    )
    wires.finish_sends()


def gather(qkv, out, gate, up, down):
    rows = (4, 4, 16)
    qkv, out, *wide = wired_call(
        gather_kernel,
        [
            shape(2, 2, *rows, 2048),
            shape(2, 2, *rows, D),
            shape(2, 2, *rows, HALF_FF),
            shape(2, 2, *rows, HALF_FF),
            shape(2, 4, 2, 144, D),
        ],
        (
            qkv.reshape(*rows, 2048),
            out.reshape(*rows, D),
            gate.reshape(*rows, FF),
            up.reshape(*rows, FF),
            down.reshape(4, 2, 144, D),
        ),
        1,
        "gather",
        3 * 8 + 9 + 6 + 5 + 6,
        7,
        in_specs=[HBM] * 5,
        out_specs=[ANY] * 2 + [HBM] * 3,
        vmem=60 * MIB,
    )
    return qkv.reshape(D, 2048), out.reshape(D, D), wide


def fetch_last(here, wires, wide):
    tasks = []
    for (kind, order), whole in zip(WIDE_FETCH, wide):
        at = {"zh": 1 - here.zh, "zl": here.zl, "x": here.x, "y": here.y}
        for axis in order[:2]:
            at = without(at, axis)
        task = spread(here, wires, kind, whole, at, order[2:])
        tasks.append(later(task, 1) if order[2] == "z" else task)
    return tasks


WIDE = (
    (0, RowsByShard(HALF_FF), ("z", "x", "y"), ("y", "x", "z")),
    (1, RowsByShard(HALF_FF), ("x", "y", "z"), ("z", "y", "x")),
    (2, ColumnsByY(144), ("y", "z", "x"), ("x", "z", "y")),
)
NARROW = (
    (0, RowsByPlane(0, 1024), ("z", "x", "y"), ("z", "y", "x")),
    (0, RowsByPlane(1024, 1024), ("x", "y", "z"), ("x", "z", "y")),
    (1, ColumnsByY(32), ("y", "z", "x"), ("z", "x", "y")),
)
FIRST_DIRECT = ("y", "y", "x")
WIDE_DIMS = ((2, 2, 4, 4, 16, HALF_FF), (2, 2, 4, 4, 16, HALF_FF), (2, 4, 2, 144, D))
NARROW_DIMS = ((2, 4, 4, 16, 2048), (2, 4, 2, 32, D))
PIECE_DIMS = ((16, HALF_FF), (16, HALF_FF), (144, 256))


def slot_shapes(parts):
    found = []
    for _, kind, order, _ in parts:
        at = {}
        for axis in order:
            at = fix(at, axis, 0)
            found.append((6, *kind.open_dims(at), *kind.tail_dims({**at, "half": 0})))
    return found


def each_block(kind, at, body):
    dims = kind.open_dims(at)

    def step(i, _):
        inner, rest = ([], i)
        for n in reversed(dims):
            inner.insert(0, rest % n)
            rest = rest // n
        picks = iter(inner)
        lead = [next(picks) if o is None else o for o in kind.order(at)]
        body((*lead, *kind.tail(at)), (*inner, slice(None), slice(None)))
        return 0

    lax.fori_loop(0, math.prod(dims), step, 0)


def reduce_one(here, wires, kind, grad, total, slots, order, direct_from):
    at = {}
    for step, axis in enumerate(order):
        source, slot = (grad if step == 0 else total, slots[step])
        (right_place, right), (left_place, left) = (here.along(axis, 1), here.along(axis, 3))
        far_place, _ = here.along(axis, 2)
        mine = fix(at, axis, getattr(here, axis))

        def half_of(place, half):
            return {**fix(at, axis, place), "half": half}

        if step >= direct_from:
            copies = [
                wires.push(
                    kind.view(source, half_of(here.along(axis, s)[0], half)),
                    slot.at[2 * j + half],
                    here.along(axis, s)[1],
                )
                for j, s in enumerate(STEPS)
                for half in range(2)
            ]
            yield
            arrive(copies)
            for half in range(2):

                def add_all(whole, part):
                    value = total[whole].astype(F32)
                    for j in range(3):
                        value += slot[(2 * j + half, *part)].astype(F32)
                    total[whole] = value.astype(BF16)

                each_block(kind, {**mine, "half": half}, add_all)
            at = mine
            continue
        relays = [
            wires.push(kind.view(source, half_of(far_place, 0)), slot.at[4], right),
            wires.push(kind.view(source, half_of(far_place, 1)), slot.at[5], left),
        ]
        arriving = [
            wires.push(kind.view(source, half_of(right_place, 1)), slot.at[1], right),
            wires.push(kind.view(source, half_of(left_place, 0)), slot.at[2], left),
        ]
        kept = []
        if step == 0:
            for where in (half_of(right_place, 0), half_of(left_place, 1), mine):
                kept.append(wires.move(kind.view(source, where), kind.view(total, where)))
        yield
        for j, place, half, target, onward in (
            (4, right_place, 0, 0, right),
            (5, left_place, 1, 3, left),
        ):
            if kept:
                kept.pop(0).wait()
            arrive([relays[j - 4]])

            def pass_on(whole, part):
                value = slot[(j, *part)].astype(F32) + total[whole].astype(F32)
                slot[(j, *part)] = value.astype(BF16)

            each_block(kind, half_of(place, half), pass_on)
            arriving.append(wires.push(slot.at[j], slot.at[target], onward))
        yield
        if kept:
            kept.pop(0).wait()
        arrive(arriving)
        for half in range(2):

            def add_up(whole, part):
                value = total[whole].astype(F32) + slot[(half, *part)].astype(F32)
                total[whole] = (value + slot[(2 + half, *part)].astype(F32)).astype(BF16)

            each_block(kind, {**mine, "half": half}, add_up)
        at = mine


def reduce_weights_kernel(*refs):
    grads, gains = (refs[3:5], refs[5])
    nears, boths, narrow_outs, gains_out = (refs[6:9], refs[9:11], refs[11:13], refs[13])
    totals, slots = (refs[14:16], refs[16:25])
    gain_slots, sends, receives, moves = refs[25:]

    here = Place()
    wires = Wires(sends, receives, moves)
    core = here.core
    sibling = here.sibling()
    greet_rings(here)
    held = {"zh": here.zh, "zl": here.zl, "x": here.x, "y": here.y}

    def all_gains():
        sums = gains[...]
        for stage, axis in enumerate(("core", "x", "y", "z")):
            me = getattr(here, axis)
            gain_slots[stage, me] = sums
            source = gain_slots.at[stage, me]
            if axis == "core":
                others = [sibling]
            else:
                others = [here.along(axis, s)[1] for s in STEPS]
            copies = [wires.push(source, source, device) for device in others]
            yield
            arrive(copies)
            sums = gain_slots[stage, 0] + gain_slots[stage, 1]
            if axis != "core":
                sums = sums + gain_slots[stage, 2] + gain_slots[stage, 3]
        gains_out[...] = sums

    def narrow(p):
        g, kind, order, back = NARROW[p]
        yield from reduce_one(
            here, wires, kind, grads[g], totals[g], slots[3 * p : 3 * p + 3], order, 1
        )
        out = narrow_outs[g]
        own = wires.move(kind.view(totals[g], held), kind.view(out, held, 1))
        own.wait()
        yield from spread(here, wires, kind, out, held, back, 1, direct="xy")

    def wide(p):
        _, kind, _, back = WIDE[p]
        at = held
        for axis in back[:2]:
            at = without(at, axis)
        yield from spread(here, wires, kind, nears[p], at, back[2:], 1)
        if p < 2:
            copies = [wires.push(nears[p].at[1 - core], boths[p].at[core], sibling)]
            own = wires.move(nears[p].at[core], boths[p].at[core])
            yield
            arrive(copies)
            own.wait()

    in_turn(
        [narrow(p) for p in range(3)]
        + [later(wide(p), rounds) for p, rounds in ((1, 2), (2, 2), (0, 4))]
        + [all_gains()]
    )
    wires.finish_sends()


def reduce_weights(nears, qkv, out, gains):
    outs = [
        *(shape(*d[1:]) for d in WIDE_DIMS),
        shape(*WIDE_DIMS[0][1:]),
        shape(*WIDE_DIMS[1][1:]),
        *(shape(*d[1:]) for d in NARROW_DIMS),
        shape(*gains.shape, dtype=F32),
    ]
    scratch = [pltpu.VMEM(d, BF16) for d in NARROW_DIMS]
    scratch += [pltpu.VMEM(s, BF16) for s in slot_shapes(NARROW)]
    scratch += [pltpu.VMEM((4, 4, *gains.shape), F32)]
    narrow = [a.reshape(d) for a, d in zip((qkv, out), NARROW_DIMS)]
    _, _, down, gate, up, qkv, out, gains = wired_call(
        reduce_weights_kernel,
        outs,
        [*nears, *narrow, gains],
        2,
        "reduce_weights",
        10 + 3 * (18 + 7) + 1 + 2 * 4 + 2,
        3 * 4 + 2,
        scratch,
        [HBM] * 3 + [ANY] * 2 + [VMEM],
        [HBM] * 7 + [VMEM],
        vmem=60 * MIB,
        aliases={i: i for i in range(3)},
    )

    def joined(both):
        both = both.reshape(2, 256, HALF_FF)
        pieces = [
            both[c, :, r * SLICE : (r + 1) * SLICE] for r in range(2) for c in range(2)
        ]
        return jnp.concatenate(pieces, axis=1)

    return (
        qkv.reshape(256, 2048),
        out.reshape(256, D),
        joined(gate),
        joined(up),
        down.reshape(SLICE, D),
        gains,
    )


def head_columns(head):
    return pl.ds(pl.multiple_of(head * 128, 128), 128)


def seats(here):
    me = here.ctx
    quarter, seat = (me // QUARTER, me % QUARTER)
    near = [quarter * QUARTER + (seat + s) % QUARTER for s in range(1, QUARTER)]
    far = [(me + s) % RING for s in range(1, RING)]
    return me, seat, near, far


def to_heads_kernel(query, key_value, query_out, key_value_out, sends, receives, moves):
    here = Place()
    wires = Wires(sends, receives, moves)
    me, seat, near, far = seats(here)
    greet([(k, here.fsdp) for k in far])
    copies = [
        wires.push(query.at[:, head_columns(k % QUARTER)], query_out.at[seat], (k, here.fsdp))
        for k in near
    ]
    copies += [
        wires.push(key_value.at[:, head_columns(k % QUARTER)], key_value_out.at[me], (k, here.fsdp))
        for k in far
    ]
    kept = [
        wires.move(query.at[:, head_columns(seat)], query_out.at[seat]),
        wires.move(key_value.at[:, head_columns(seat)], key_value_out.at[me]),
    ]
    arrive(copies)
    for copy in kept:
        copy.wait()
    wires.finish_sends()


def to_heads(query, key_value):
    outs = [shape(QUARTER, TOKENS, 128), shape(RING, TOKENS, 128)]
    return wired_call(to_heads_kernel, outs, [query, key_value], 3, "to_heads", 38, 2)


def grad_to_heads_kernel(grad, branch, grad_out, branch_pair, sends, receives, moves):
    here = Place()
    wires = Wires(sends, receives, moves)
    _, seat, near, _ = seats(here)
    greet([(k, here.fsdp) for k in near] + [here.sibling()])
    copies = [
        wires.push(grad.at[:, head_columns(k % QUARTER)], grad_out.at[seat], (k, here.fsdp))
        for k in near
    ]
    copies.append(wires.push(branch, branch_pair.at[here.core], here.sibling()))
    kept = [
        wires.move(grad.at[:, head_columns(seat)], grad_out.at[seat]),
        wires.move(branch, branch_pair.at[here.core]),
    ]
    arrive(copies)
    for copy in kept:
        copy.wait()
    wires.finish_sends()


def grad_to_heads(grad, branch):
    outs = [shape(QUARTER, TOKENS, 128), shape(2, TOKENS, D)]
    return wired_call(grad_to_heads_kernel, outs, [grad, branch], 4, "grad_to_heads", 8, 2)


def to_tokens_kernel(query, query_out, sends, receives, moves):
    here = Place()
    wires = Wires(sends, receives, moves)
    _, seat, near, _ = seats(here)
    greet([(k, here.fsdp) for k in near])
    columns = query_out.at[:, head_columns(seat)]
    copies = [wires.push(query.at[k % QUARTER], columns, (k, here.fsdp)) for k in near]
    kept = wires.move(query.at[seat], columns)
    arrive(copies)
    kept.wait()
    wires.finish_sends()


def to_tokens(query):
    return wired_call(to_tokens_kernel, [shape(TOKENS, D)], [query], 5, "to_tokens", 7, 1)[0]


def grads_to_tokens_kernel(*refs):
    query, key_value, pieces = (refs[0], refs[1], refs[2:5])
    query_out, key_value_out, nears = (refs[5], refs[6], refs[7:10])
    here = Place()
    wires = Wires(*refs[10:])
    me, seat, near, far = seats(here)
    greet([(k, here.fsdp) for k in far])
    held = {"zh": here.zh, "zl": here.zl, "x": here.x, "y": here.y}

    def back():
        columns = query_out.at[:, head_columns(seat)]
        copies = [wires.push(query.at[k % QUARTER], columns, (k, here.fsdp)) for k in near]
        copies += [
            wires.push(key_value.at[k], key_value_out.at[me], (k, here.fsdp)) for k in far
        ]
        kept = [
            wires.move(query.at[seat], columns),
            wires.move(key_value.at[me], key_value_out.at[me]),
        ]
        for _ in range(3):
            yield
        arrive(copies)
        for copy in kept:
            copy.wait()

    def share(p):
        _, kind, _, order = WIDE[p]
        own = wires.move(pieces[p], kind.view(nears[p], held, 1))
        own.wait()
        yield from spread(
            here, wires, kind, nears[p], held, order[:2], 1, direct=FIRST_DIRECT[p]
        )

    in_turn([share(p) for p in range(3)] + [back()])
    wires.finish_sends()


def grads_to_tokens(query, key_value, pieces):
    query_grad, key_value_grad, *nears = wired_call(
        grads_to_tokens_kernel,
        [shape(TOKENS, D), shape(RING, TOKENS, 128), *(shape(*d[1:]) for d in WIDE_DIMS)],
        [query, key_value, *pieces],
        6,
        "grads_to_tokens",
        38 + 7 + 4 + 4,
        5,
        in_specs=[ANY] * 2 + [HBM] * 3,
        out_specs=[ANY] * 2 + [HBM] * 3,
        vmem=60 * MIB,
    )
    return query_grad, key_value_grad, nears


def half_columns(r, core):
    return pl.ds(pl.multiple_of(r * 512 + core * 256, 256), 256)


def share_kernel(whole, halved, *refs):
    n = whole + halved
    ins, outs = (refs[:n], refs[n : 2 * n])
    here = Place()
    wires = Wires(*refs[2 * n :])
    core = here.core
    sibling = here.sibling()
    greet([sibling])
    copies, kept = ([], [])
    for source, target in zip(ins[:whole], outs[:whole]):
        copies.append(wires.push(source, target.at[core], sibling))
        kept.append(wires.move(source, target.at[core]))
    for source, target in zip(ins[whole:], outs[whole:]):
        for r in range(2):
            place = target.at[core, :, pl.ds(r * 256, 256)]
            copies.append(wires.push(source.at[:, half_columns(r, 1 - core)], place, sibling))
            kept.append(wires.move(source.at[:, half_columns(r, core)], place))
    arrive(copies)
    for copy in kept:
        copy.wait()
    wires.finish_sends()


def share(whole, halved, collective_id):
    outs = [shape(2, *a.shape, dtype=a.dtype) for a in whole]
    outs += [shape(2, a.shape[0], 512, dtype=a.dtype) for a in halved]
    count = len(whole) + 2 * len(halved)
    done = wired_call(
        functools.partial(share_kernel, len(whole), len(halved)),
        outs,
        [*whole, *halved],
        collective_id,
        "share",
        count,
        count,
    )
    return [a.reshape(2 * a.shape[1], a.shape[2]) for a in done]


def hand_over_kernel(count, *refs):
    ins, outs = (refs[:count], refs[count : 2 * count])
    here = Place()
    wires = Wires(*refs[2 * count :])
    sibling = here.sibling()
    greet([sibling])
    copies = [wires.push(i.at[1 - here.core], o, sibling) for i, o in zip(ins, outs)]
    arrive(copies)
    wires.finish_sends()


def hand_over(partials, collective_id):
    return wired_call(
        functools.partial(hand_over_kernel, len(partials)),
        [shape(*a.shape[1:], dtype=a.dtype) for a in partials],
        partials,
        collective_id,
        "hand_over",
        len(partials),
        0,
    )


def nt(left, right):
    return lax.dot_general(left, right, (((1,), (1,)), ((), ())), preferred_element_type=F32)


def nn(left, right):
    return lax.dot_general(left, right, (((1,), (0,)), ((), ())), preferred_element_type=F32)


def query_block(ref, t):
    block = ref[t].astype(F32)
    both = jnp.concatenate([block, pltpu.roll(block, 64, 1)], axis=0)
    low = lax.broadcasted_iota(jnp.int32, (128, 128), 1) < 64
    return jnp.where(low, both, 0.0)


def query_pair(ref, u):
    return [query_block(ref, 2 * u), query_block(ref, 2 * u + 1)]


def first_allowed(position, starts_ref):
    begin = jnp.zeros_like(position)
    for n in range(4):
        begin = jnp.maximum(begin, jnp.where(starts_ref[n] <= position, starts_ref[n], 0))
    return begin


def heads_beside(rows):
    low = lax.broadcasted_iota(jnp.int32, (64, 128), 1) < 64
    return jnp.where(low, rows[:64], pltpu.roll(rows[64:], 64, 1)).astype(BF16)


def attend_task(
    counts, first_block, starts_ref, order_ref, query_ref, key_value_ref, out_ref, exact_ref,
    sum_ref, value_ref, key_at_ref,
):
    def key_places(j, _):
        lane = lax.broadcasted_iota(jnp.int32, (1, 128), 1)
        block = jnp.where(lane < 64, order_ref[2 * j], order_ref[2 * j + 1])
        key_at_ref[:, pl.ds(pl.multiple_of(j * 128, 128), 128)] = block * 64 + lane % 64
        return 0

    def values(j, _):
        rows = pl.ds(pl.multiple_of(j * 256, 256), 256)
        block = pltpu.roll(key_value_ref[rows, :].astype(F32), 64, 1)
        low = lax.broadcasted_iota(jnp.int32, (256, 128), 1) < 64
        value_ref[rows, :] = jnp.where(low, block, 1.0).astype(BF16)
        return 0

    def blocks(u, _):
        queries = jnp.concatenate(query_pair(query_ref, u), axis=0).astype(BF16)
        inner = lax.broadcasted_iota(jnp.int32, (128, 1), 0) % 64
        block = first_block + 2 * u
        position = jnp.concatenate(
            [order_ref[block] * 64 + inner, order_ref[block + 1] * 64 + inner], axis=0
        )
        begin = first_allowed(position, starts_ref)

        def tile(j, total):
            rows = pl.ds(pl.multiple_of(j * KEY_TILE, KEY_TILE), KEY_TILE)
            scores = nt(queries, key_value_ref[rows, :])
            key = key_at_ref[:, rows]
            allowed = (key <= position) & (key >= begin)
            weight = jnp.where(allowed, jnp.exp2(scores * SCORE_TO_EXP2), 0.0)
            return total + nn(weight.astype(BF16), value_ref[rows, :])

        total = lax.fori_loop(0, SEQ // KEY_TILE, tile, jnp.zeros((256, 128), F32))
        attended = total / pltpu.roll(total, 64, 1)
        low = lax.broadcasted_iota(jnp.int32, (256, 128), 1) < 64
        attended = jnp.where(low, attended, 0.0)
        for n in range(2):
            rows = slice(128 * n, 128 * n + 128)
            exact_ref[2 * u + n] = attended[rows]
            out_ref[2 * u + n] = heads_beside(attended[rows])
            sum_ref[2 * u + n] = jnp.transpose(total[rows])[64:72]
        return 0

    lax.fori_loop(0, SEQ // 256, values, 0)
    lax.fori_loop(0, SEQ // 128, key_places, 0)
    first = 0
    for count in counts:
        lax.fori_loop(first, first + count, blocks, 0)
        first += count
        yield


def attend_kernel(
    starts, order, query, key_value, gate_in, up_in, down_in, attended, exact, sums, gate_all,
    up_all, down_all, value_ref, key_at_ref, sends, receives, moves,
):
    wires = Wires(sends, receives, moves)
    here = Place()
    greet_rings(here)
    in_turn(
        [
            *fetch_last(here, wires, (gate_all, up_all, down_all))[::-1],
            attend_task(
                (6, 2), here.ctx // QUARTER * 16, starts, order, query, key_value, attended, exact,
                sums, value_ref, key_at_ref,
            ),
        ]
    )
    wires.finish_sends()


def attend(starts, order, queries, key_values, wide):
    outs = [
        shape(16, 64, 128),
        shape(16, 128, 128, dtype=F32),
        shape(16, 8, 128, dtype=F32),
        *(shape(*a.shape) for a in wide),
    ]
    attended, exact, sums, gate, up, down = wired_call(
        attend_kernel,
        outs,
        [starts, order, queries, key_values, *wide],
        10,
        "attend",
        1 + 4 + 4,
        1,
        [pltpu.VMEM((SEQ, 128), BF16), pltpu.VMEM((1, SEQ), jnp.int32)],
        [SMEM] * 2 + [VMEM] * 2 + [HBM] * 3,
        [VMEM] * 3 + [HBM] * 3,
        vmem=40 * MIB,
        aliases={4 + i: 3 + i for i in range(3)},
    )
    weights = (gate.reshape(D, HALF_FF), up.reshape(D, HALF_FF), down.reshape(HALF_FF, D))
    return attended, exact, sums, weights


def attend_back_task(
    counts, first_block, starts_ref, order_ref, query_ref, key_value_ref, grad_ref, exact_ref,
    sum_ref, query_grad_ref, key_value_grad_ref, across_ref, total_ref, key_at_ref,
):
    total_ref[...] = jnp.zeros_like(total_ref)

    def key_places(j, _):
        inner = lax.broadcasted_iota(jnp.int32, (64, 1), 0)
        key_at_ref[pl.ds(pl.multiple_of(j * 64, 64), 64), :] = order_ref[j] * 64 + inner
        return 0

    def turn(j, _):
        rows = pl.ds(pl.multiple_of(j * 128, 128), 128)
        across_ref[:, rows] = jnp.transpose(key_value_ref[rows, :].astype(F32)).astype(BF16)
        return 0

    def blocks(u, _):
        queries, grads = (query_pair(query_ref, u), query_pair(grad_ref, u))
        delta = [
            jnp.sum(jnp.transpose(grad * exact_ref[2 * u + n]), axis=0, keepdims=True)
            for n, grad in enumerate(grads)
        ]
        delta = jnp.concatenate(delta, axis=1)
        total_exp2 = jnp.concatenate(
            [jnp.log2(sum_ref[2 * u + n][0:1]) for n in range(2)], axis=1
        )
        grads = [pltpu.roll(grad, 64, 1) for grad in grads]
        both = jnp.concatenate(queries + grads, axis=0).astype(BF16)
        inner = lax.broadcasted_iota(jnp.int32, (1, 128), 1) % 64
        block = first_block + 2 * u
        position = jnp.concatenate(
            [order_ref[block] * 64 + inner, order_ref[block + 1] * 64 + inner], axis=1
        )
        begin = first_allowed(position, starts_ref)

        def tile(j, query_grad):
            rows = pl.ds(pl.multiple_of(j * KEY_TILE_BACK, KEY_TILE_BACK), KEY_TILE_BACK)
            products = nt(key_value_ref[rows, :], both)
            key = key_at_ref[rows, :]
            allowed = (key <= position) & (key >= begin)
            prob = jnp.where(
                allowed, jnp.exp2(products[:, :256] * SCORE_TO_EXP2 - total_exp2), 0.0
            )
            score = (prob * (products[:, 256:] - delta)).astype(BF16)
            side = jnp.concatenate([score, prob.astype(BF16)], axis=1)
            total_ref[rows, :] += nn(side, both)
            return query_grad + nn(across_ref[:, rows], score)

        query_grad = lax.fori_loop(
            0, SEQ // KEY_TILE_BACK, tile, jnp.zeros((128, 256), F32)
        )
        for n in range(2):
            rows = jnp.transpose(query_grad[:, 128 * n : 128 * n + 128])
            query_grad_ref[2 * u + n] = heads_beside(rows * float(HEAD_SIZE) ** (-0.5))
        return 0

    def put_back(j, _):
        rows = pl.ds(pl.multiple_of(j * 256, 256), 256)
        low = lax.broadcasted_iota(jnp.int32, (256, 128), 1) < 64
        scale = jnp.where(low, float(HEAD_SIZE) ** (-0.5), 1.0)
        key_value_grad_ref[rows, :] = (total_ref[rows, :] * scale).astype(BF16)
        return 0

    lax.fori_loop(0, SEQ // 128, turn, 0)
    lax.fori_loop(0, 64, key_places, 0)
    first = 0
    for count in counts:
        lax.fori_loop(first, first + count, blocks, 0)
        first += count
        yield
    lax.fori_loop(0, SEQ // 256, put_back, 0)


def attend_back_kernel(*refs):
    attention, grads = (refs[:7], refs[7:10])
    outs, pieces = (refs[10:12], refs[12:15])
    scratch, totals, slots = (refs[15:18], refs[18:21], refs[21:30])
    here = Place()
    wires = Wires(*refs[30:])
    greet_rings(here)
    at = {"zh": here.zh, "zl": here.zl, "x": here.x, "y": here.y}

    def reduce(p):
        _, kind, order, _ = WIDE[p]
        yield from reduce_one(
            here, wires, kind, grads[p], totals[p], slots[3 * p : 3 * p + 3], order, 2
        )
        own = wires.move(kind.view(totals[p], at), pieces[p])
        yield
        own.wait()

    first_block = here.ctx // QUARTER * 16
    in_turn(
        [reduce(p) for p in range(3)]
        + [attend_back_task((3, 3, 1, 1), first_block, *attention, *outs, *scratch)]
    )
    wires.finish_sends()


def attend_back(starts, order, queries, key_values, grads, exact, sums, wide):
    ins = [starts, order, queries, key_values, grads]
    ins += [exact, sums, *(a.reshape(d) for a, d in zip(wide, WIDE_DIMS))]
    scratch = [
        pltpu.VMEM((128, SEQ), BF16),
        pltpu.VMEM((SEQ, 128), F32),
        pltpu.VMEM((SEQ, 1), jnp.int32),
    ]
    scratch += [pltpu.VMEM(d, BF16) for d in WIDE_DIMS]
    scratch += [pltpu.VMEM(s, BF16) for s in slot_shapes(WIDE)]
    query_grad, key_value_grad, *pieces = wired_call(
        attend_back_kernel,
        [shape(16, 64, 128), shape(SEQ, 128), *(shape(*d) for d in PIECE_DIMS)],
        ins,
        11,
        "attend_back",
        3 * 18,
        3 * 4,
        scratch,
        [SMEM] * 2 + [VMEM] * 5 + [HBM] * 3,
        [VMEM] * 2 + [HBM] * 3,
        vmem=58 * MIB,
    )
    return query_grad, key_value_grad, pieces


def low_lanes():
    return lax.broadcasted_iota(jnp.int32, (TOKENS, 128), 1) < 64


def head_mean(values):
    low = low_lanes()
    first = jnp.sum(jnp.where(low, values, 0.0), axis=1, keepdims=True)
    second = jnp.sum(jnp.where(low, 0.0, values), axis=1, keepdims=True)
    return jnp.where(low, first, second) * (1.0 / HEAD_SIZE)


def other_half(values):
    first = lax.broadcasted_iota(jnp.int32, (TOKENS, 128), 1) % 64 < 32
    return jnp.where(first, pltpu.roll(values, 96, 1), pltpu.roll(values, 32, 1))


def chunk(j):
    return slice(128 * j, 128 * j + 128)


def project_kernel(
    x_ref, gain_ref, weight_ref, query_gain_ref, key_gain_ref, cosine_ref, sine_ref, normed_ref,
    query_ref, key_value_ref, projected_ref,
):
    x = x_ref[...].astype(F32)
    normed = x * lax.rsqrt(jnp.mean(x * x, axis=-1, keepdims=True) + EPSILON) * gain_ref[...]
    normed_ref[...] = normed.astype(BF16)
    projected = nn(normed_ref[...], weight_ref[...])
    projected_ref[...] = projected[:, :1536]
    low = low_lanes()

    def turned(j, gain):
        values = projected[:, chunk(j)]
        values = values * lax.rsqrt(head_mean(values * values) + EPSILON) * gain
        return values * cosine_ref[...] + other_half(values) * sine_ref[...]

    for j in range(8):
        query_ref[:, chunk(j)] = turned(j, query_gain_ref[...]).astype(BF16)
    for j in range(4):
        keys = turned(8 + j, key_gain_ref[...])
        values = projected[:, chunk(12 + j)]
        first = jnp.where(low, keys, pltpu.roll(values, 64, 1))
        second = jnp.where(low, pltpu.roll(keys, 64, 1), values)
        key_value_ref[:, chunk(2 * j)] = first.astype(BF16)
        key_value_ref[:, chunk(2 * j + 1)] = second.astype(BF16)


def project(x, gain, weight, query_gain, key_gain, cosine, sine):
    return pl.pallas_call(
        project_kernel,
        out_shape=[
            shape(TOKENS, D),
            shape(TOKENS, D),
            shape(TOKENS, D),
            shape(TOKENS, 1536, dtype=F32),
        ],
        in_specs=[VMEM] * 7,
        out_specs=[VMEM] * 4,
        compiler_params=pltpu.CompilerParams(vmem_limit_bytes=32 * MIB),
        name="project",
    )(x, gain, weight, query_gain, key_gain, cosine, sine)


def project_back_kernel(
    query_grad_ref, key_value_grad_ref, projected_ref, x_ref, grad_resid_ref, gain_ref, weight_ref,
    query_gain_ref, key_gain_ref, cosine_ref, sine_ref, ffn_gain_grad_ref, grad_projected_ref,
    grad_inputs_ref, gains_ref,
):
    low = low_lanes()

    def back(j, grad, gain):
        grad = grad * cosine_ref[...] + other_half(grad * sine_ref[...])
        values = projected_ref[:, chunk(j)]
        scale = lax.rsqrt(head_mean(values * values) + EPSILON)
        unit = values * scale
        gain_grad = jnp.sum(grad * unit, axis=0, keepdims=True)
        grad = grad * gain
        grad = scale * (grad - unit * head_mean(grad * unit))
        grad_projected_ref[:, chunk(j)] = grad.astype(BF16)
        return gain_grad

    query_gain_grad = jnp.zeros((1, 128), F32)
    for j in range(8):
        grad = query_grad_ref[:, chunk(j)].astype(F32)
        query_gain_grad += back(j, grad, query_gain_ref[...])
    key_gain_grad = jnp.zeros((1, 128), F32)
    for j in range(4):
        first, second = [
            sum(key_value_grad_ref[8 * q + 2 * j + n].astype(F32) for q in range(4))
            for n in range(2)
        ]
        keys = jnp.where(low, first, pltpu.roll(second, 64, 1))
        values = jnp.where(low, pltpu.roll(first, 64, 1), second)
        key_gain_grad += back(8 + j, keys, key_gain_ref[...])
        grad_projected_ref[:, chunk(12 + j)] = values.astype(BF16)

    grad = nt(grad_projected_ref[...], weight_ref[...])
    x = x_ref[...].astype(F32)
    scale = lax.rsqrt(jnp.mean(x * x, axis=-1, keepdims=True) + EPSILON)
    unit = x * scale
    gain_grad = jnp.sum(grad * unit, axis=0, keepdims=True)
    grad = grad * gain_ref[...]
    grad = scale * (grad - unit * jnp.mean(grad * unit, axis=-1, keepdims=True))
    grad_inputs_ref[...] = (grad_resid_ref[...] + grad).astype(BF16)

    gains_ref[...] = jnp.zeros_like(gains_ref)
    for j in range(8):
        gains_ref[j : j + 1, :] = gain_grad[:, chunk(j)]
        gains_ref[8 + j : 9 + j, :] = ffn_gain_grad_ref[:, chunk(j)]
    gains_ref[16:17, :] = query_gain_grad + pltpu.roll(query_gain_grad, 64, 1)
    gains_ref[17:18, :] = key_gain_grad + pltpu.roll(key_gain_grad, 64, 1)


def project_back(*ins):
    return pl.pallas_call(
        project_back_kernel,
        out_shape=[shape(TOKENS, 2048), shape(TOKENS, D), shape(24, 128, dtype=F32)],
        in_specs=[VMEM] * 12,
        out_specs=[VMEM] * 3,
        compiler_params=pltpu.CompilerParams(vmem_limit_bytes=40 * MIB),
        name="project_back",
    )(*ins)


def rms_norm(values, gain_row):
    return (
        values * lax.rsqrt(jnp.mean(values * values, axis=-1, keepdims=True) + EPSILON) * gain_row
    )


def rope_tables(positions):
    lane = jnp.arange(128, dtype=jnp.int32)
    frequency = ROPE_BASE ** (-2.0 * (lane % 32).astype(F32) / HEAD_SIZE)
    angles = positions.astype(F32)[:, None] * frequency[None, :]
    sign = jnp.where(lane % 64 < 32, -1.0, 1.0)
    return jnp.cos(angles), jnp.sin(angles) * sign[None, :]


def outer_sum(left, right):
    return lax.dot_general(
        left, right, (((0,), (0,)), ((), ())), preferred_element_type=F32
    ).astype(BF16)


def matmul(left, right):
    return jnp.dot(left, right, preferred_element_type=F32)


def positions_at(block_order, first_row, total_row_count, half_rows):
    row_ids = first_row + jnp.arange(total_row_count, dtype=jnp.int32)
    blocks = row_ids // half_rows
    lookup = jnp.arange(block_order.shape[0], dtype=jnp.int32)
    picked = jnp.sum(jnp.where(blocks[:, None] == lookup[None, :], block_order[None, :], 0), axis=1)
    return picked * half_rows + row_ids % half_rows


def per_device(
    inputs,
    cotangent,
    qkv_weight,
    out_weight,
    gate_weight,
    up_weight,
    down_weight,
    gain_attn,
    gain_query,
    gain_key,
    gain_ffn,
    block_order,
    doc_starts,
):
    cycle_index = lax.axis_index("ctx")
    core = lax.axis_index("fsdp") % 2
    qkv_all, out_all, wide = gather(
        qkv_weight, out_weight, gate_weight, up_weight, down_weight
    )
    places = (doc_starts[0], block_order)
    positions = positions_at(block_order, cycle_index * TOKENS, TOKENS, TOKENS // 2)

    resid_in = inputs[0].astype(F32)
    gain_row = gain_attn.reshape(1, D)
    head_gains = [jnp.concatenate([g, g]).reshape(1, 128) for g in (gain_query, gain_key)]
    tables = rope_tables(positions)
    normed_low, queries, key_values, projected = project(
        inputs[0], gain_row, qkv_all, *head_gains, *tables
    )
    query_part, key_value_part = to_heads(queries, key_values)
    query_part = query_part.reshape(16, 64, 128)
    key_value_part = key_value_part.reshape(SEQ, 128)
    attended, exact, sums, (gate_all, up_all, down_all) = attend(
        *places, query_part, key_value_part, wide
    )
    attended_low = to_tokens(attended.reshape(QUARTER, TOKENS, 128))

    residual = resid_in + matmul(attended_low, out_all)
    normed_ffn, norm_ffn_pull = jax.vjp(rms_norm, residual, gain_ffn)
    grad_out = cotangent[0]
    ffn_pair, cotangent_pair, normed_half, attended_half = share(
        [normed_ffn.astype(BF16), grad_out], [normed_low, attended_low], 7
    )
    gate_proj = matmul(ffn_pair, gate_all)
    up_proj = matmul(ffn_pair, up_all)
    hidden, gating_pull = jax.vjp(
        lambda gate_in, up_in: jax.nn.silu(gate_in) * up_in, gate_proj, up_proj
    )
    hidden_low = hidden.astype(BF16)
    out_partial = matmul(hidden_low, down_all).reshape(2, TOKENS, D)
    grad_hidden = matmul(cotangent_pair, down_all.T)
    grad_gate, grad_up = gating_pull(grad_hidden)
    gate_low = grad_gate.astype(BF16)
    up_low = grad_up.astype(BF16)
    ffn_partial = (matmul(gate_low, gate_all.T) + matmul(up_low, up_all.T)).reshape(2, TOKENS, D)
    out_rest, ffn_rest = hand_over([out_partial, ffn_partial], 8)

    def mine(pair):
        return lax.dynamic_index_in_dim(pair, core, 0, keepdims=False)

    outputs = residual + mine(out_partial) + out_rest
    grad_resid_ffn, grad_gain_ffn = norm_ffn_pull(mine(ffn_partial) + ffn_rest)
    grad_resid = grad_out.astype(F32) + grad_resid_ffn
    branch_low = grad_resid.astype(BF16)
    grad_attended = matmul(branch_low, out_all.T).astype(BF16)
    grad_part, branch_pair = grad_to_heads(grad_attended, branch_low)
    query_grad, key_value_grad, pieces = attend_back(
        *places,
        query_part,
        key_value_part,
        grad_part.reshape(16, 64, 128),
        exact,
        sums,
        (
            outer_sum(ffn_pair, gate_low),
            outer_sum(ffn_pair, up_low),
            outer_sum(hidden_low, cotangent_pair),
        ),
    )
    query_grad, key_value_grad, nears = grads_to_tokens(
        query_grad.reshape(QUARTER, TOKENS, 128),
        key_value_grad.reshape(RING, TOKENS, 128),
        pieces,
    )
    grad_projected, grad_inputs, gains = project_back(
        query_grad,
        key_value_grad,
        projected,
        inputs[0],
        grad_resid,
        gain_row,
        qkv_all,
        *head_gains,
        *tables,
        grad_gain_ffn.reshape(1, D),
    )

    (projected_pair,) = share([grad_projected], [], 9)
    grad_qkv, grad_out_weight, grad_gate_weight, grad_up_weight, grad_down, gains = reduce_weights(
        nears,
        outer_sum(normed_half, projected_pair),
        outer_sum(attended_half, branch_pair.reshape(2 * TOKENS, D)),
        gains,
    )
    gains = gains.reshape(-1)
    return (
        outputs.astype(BF16)[None],
        grad_inputs[None],
        grad_qkv.astype(F32),
        grad_out_weight.astype(F32),
        grad_gate_weight.astype(F32),
        grad_up_weight.astype(F32),
        grad_down.astype(F32),
        gains[:D],
        gains[2 * D : 2 * D + HEAD_SIZE],
        gains[2 * D + 128 : 2 * D + 128 + HEAD_SIZE],
        gains[D : 2 * D],
    )


def solution(mesh):
    in_specs = (
        P("fsdp", "ctx", None),
        P("fsdp", "ctx", None),
        P("fsdp", None),
        P("fsdp", None),
        P("fsdp", None),
        P("fsdp", None),
        P("fsdp", None),
        P(),
        P(),
        P(),
        P(),
        P(),
        P("fsdp", None),
    )
    out_specs = (
        P("fsdp", "ctx", None),
        P("fsdp", "ctx", None),
        P("fsdp", None),
        P("fsdp", None),
        P("fsdp", None),
        P("fsdp", None),
        P("fsdp", None),
        P(),
        P(),
        P(),
        P(),
    )
    return jax.shard_map(
        per_device, mesh=mesh, in_specs=in_specs, out_specs=out_specs, check_vma=False
    )
```

```python
import functools
import math

import jax
import jax.numpy as jnp
from jax import lax
from jax.experimental import pallas as pl
from jax.experimental.pallas import tpu as pltpu
from jax.sharding import PartitionSpec as P

QUERY_HEADS = 16
KEY_VALUE_HEADS = 8
HEAD_SIZE = 64
FF = 4608
D = 1024
TOKENS = 128
RING = 32
QUARTER = 8
SLICE = 1152
HALF_FF = FF // 2
KEY_TILE = 1024
KEY_TILE_BACK = 1024
SEQ = 4096

EPSILON = 1e-05
ROPE_BASE = 1000000.0
SCORE_TO_EXP2 = float(HEAD_SIZE) ** (-0.5) * math.log2(math.e)

MESH = pl.DeviceIdType.MESH
ANY = pl.BlockSpec(memory_space=pl.ANY)
HBM = pl.BlockSpec(memory_space=pltpu.MemorySpace.HBM)
VMEM = pl.BlockSpec(memory_space=pltpu.VMEM)
SMEM = pl.BlockSpec(memory_space=pltpu.SMEM)
BF16 = jnp.bfloat16
F32 = jnp.float32
MIB = 1 << 20
STEPS = (1, 3, 2)


class Place:
    def __init__(self):
        self.ctx, self.fsdp = (lax.axis_index("ctx"), lax.axis_index("fsdp"))
        self.zl, self.x, self.y = (self.ctx // 16, (self.ctx // 4) % 4, self.ctx % 4)
        self.zh, self.core = (self.fsdp // 2, self.fsdp % 2)
        self.z = self.zh * 2 + self.zl

    def device(self, x=None, y=None, z=None, core=None):
        x = self.x if x is None else x
        y = self.y if y is None else y
        z = self.z if z is None else z
        core = self.core if core is None else core
        return ((z % 2) * 16 + x * 4 + y, (z // 2) * 2 + core)

    def sibling(self):
        return self.device(core=1 - self.core)

    def along(self, axis, step):
        coordinate = (getattr(self, axis) + step) % 4
        return coordinate, self.device(**{axis: coordinate})


class Wires:
    def __init__(self, sends, receives, locals_=None):
        self.sends, self.receives, self.locals_ = (sends, receives, locals_)
        self.pushed, self.moved = ([], 0)

    def push(self, source, target, device):
        at = len(self.pushed)
        copy = pltpu.make_async_remote_copy(
            src_ref=source,
            dst_ref=target,
            send_sem=self.sends.at[at],
            recv_sem=self.receives.at[at],
            device_id=device,
            device_id_type=MESH,
        )
        copy.start()
        self.pushed.append(copy)
        return copy

    def move(self, source, target):
        copy = pltpu.make_async_copy(source, target, self.locals_.at[self.moved])
        copy.start()
        self.moved += 1
        return copy

    def finish_sends(self):
        for copy in self.pushed:
            copy.wait_send()


def arrive(copies):
    for copy in copies:
        copy.wait_recv()


def greet(devices):
    barrier = pltpu.get_barrier_semaphore()
    for device in devices:
        pl.semaphore_signal(barrier, inc=1, device_id=device, device_id_type=MESH)
    pl.semaphore_wait(barrier, len(devices))


def wired_call(kernel, outs, ins, collective_id, name, copies, moves, scratch=(), in_specs=None,
               out_specs=None, vmem=32 * MIB, aliases=None):
    return pl.pallas_call(
        kernel,
        out_shape=outs,
        in_specs=[ANY] * len(ins) if in_specs is None else in_specs,
        out_specs=[ANY] * len(outs) if out_specs is None else out_specs,
        scratch_shapes=[
            *scratch,
            pltpu.SemaphoreType.DMA((copies,)),
            pltpu.SemaphoreType.DMA((copies,)),
            pltpu.SemaphoreType.DMA((max(moves, 1),)),
        ],
        compiler_params=pltpu.CompilerParams(
            collective_id=collective_id, has_side_effects=True, vmem_limit_bytes=vmem
        ),
        name=name,
        input_output_aliases=aliases or {},
    )(*ins)


def shape(*dims, dtype=BF16):
    return jax.ShapeDtypeStruct(dims, dtype)


class Pieces:
    def view(self, ref, at, skip=0):
        lead = [slice(None) if i is None else i for i in self.order(at)[skip:]]
        return ref.at[(*lead, *self.tail(at))]

    def open_dims(self, at):
        return tuple(n for n, i in zip(self.lead, self.order(at)) if i is None)

    def tail(self, at):
        first, width = self.columns(at)
        if not isinstance(first, int):
            first = pl.multiple_of(first, 128)
        return (slice(None), pl.ds(first, width))

    def tail_dims(self, at):
        return (self.rows, self.columns(at)[1])


def halved(first, width, at):
    if "half" not in at:
        return first, width
    return first + at["half"] * (width // 2), width // 2


class RowsByShard(Pieces):
    lead, rows = ((2, 2, 4, 4), 16)

    def __init__(self, width):
        self.width = width

    def order(self, at):
        return [at.get("zh"), at.get("zl"), at.get("x"), at.get("y")]

    def columns(self, at):
        return halved(0, self.width, at)


class RowsByPlane(Pieces):
    lead, rows = ((2, 4, 4), 16)

    def __init__(self, first, width):
        self.first, self.width = (first, width)

    def order(self, at):
        return [at.get("zh"), at.get("x"), at.get("y")]

    def columns(self, at):
        if "zl" not in at:
            return halved(self.first, self.width, at)
        half = self.width // 2
        return halved(self.first + half * at["zl"], half, at)


class ColumnsByY(Pieces):
    lead = (2, 4, 2)

    def __init__(self, rows):
        self.rows = rows

    def order(self, at):
        return [at.get("zh"), at.get("x"), at.get("zl")]

    def columns(self, at):
        return halved(at["y"] * 256, 256, at) if "y" in at else halved(0, D, at)


class ShardsByCore(Pieces):
    lead, rows = ((2, 2, 4, 4), 16)

    def __init__(self, width):
        self.width = width

    def order(self, at):
        return [at.get("zh"), at.get("half"), at.get("x"), at.get("y")]

    def columns(self, at):
        half = self.width // 2
        return (half * at["zl"], half) if "zl" in at else (0, self.width)


class OneCore(RowsByPlane):
    lead = (2, 2, 4, 4)

    def __init__(self, first, width, core):
        super().__init__(first, width)
        self.core = core

    def order(self, at):
        return [at.get("zh"), self.core, at.get("x"), at.get("y")]


def fix(at, axis, coordinate):
    if axis == "z":
        return {**at, "zh": coordinate // 2, "zl": coordinate % 2}
    return {**at, axis: coordinate}


def without(at, axis):
    return {a: i for a, i in at.items() if a != ("zl" if axis == "z" else axis)}


def in_turn(tasks):
    while tasks:
        tasks = [task for task in tasks if next(task, "over") != "over"]


def later(task, rounds):
    next(task)
    for _ in range(rounds + 1):
        yield
    yield from task


def spread(here, wires, kind, ref, at, order, skip=0, direct=""):
    for axis in order:
        piece = kind.view(ref, at, skip)
        if axis == "z":
            copies = [wires.push(piece, piece, here.device(z=here.zh * 2 + 1 - here.zl))]
            yield
            arrive(copies)
        elif axis in direct:
            copies = [wires.push(piece, piece, here.along(axis, s)[1]) for s in STEPS]
            yield
            arrive(copies)
        else:
            (_, right), (_, left) = (here.along(axis, 1), here.along(axis, 3))
            from_left = wires.push(piece, piece, right)
            from_right = wires.push(piece, piece, left)
            yield
            relays = []
            for half, copy, step, onward in ((0, from_left, 3, right), (1, from_right, 1, left)):
                arrive([copy])
                passing = fix(at, axis, here.along(axis, step)[0])
                passing = kind.view(ref, {**passing, "half": half}, skip)
                relays.append(wires.push(passing, passing, onward))
            yield
            arrive(relays)
        at = without(at, axis)


def greet_rings(here, others=()):
    rings = [here.along(a, s)[1] for a in ("x", "y", "z") for s in STEPS]
    greet([*rings, here.sibling(), *others])


class Fetch:
    def __init__(self, here, wires):
        self.here, self.wires = (here, wires)
        self.zh, self.core, self.x, self.y = (here.zh, here.core, here.x, here.y)
        self.there = 1 - here.zl
        self.cross = [here.device(z=3 - here.z, core=(here.core + t) % 2) for t in range(2)]
        self.sibling = here.sibling()
        self.held = {"zh": 1 - here.zh, "zl": here.zl, "x": here.x, "y": here.y}

    def part(self, width):
        return pl.ds(pl.multiple_of(self.there * width, 128), width)

    def ff_columns(self, r, c):
        return pl.ds(pl.multiple_of(r * HALF_FF + c * SLICE, 128), SLICE)

    def rest(self, kind, whole, crossed, order, direct):
        yield
        arrive(crossed)
        yield from spread(
            self.here, self.wires, kind, whole, self.held, order, direct=direct
        )

    def narrow(self, shard, whole, first, width, order):
        columns = pl.ds(first, width)
        source = shard.at[self.x, self.y, :, columns]
        target = whole.at[self.zh, self.core, self.x, self.y, :, columns]
        crossed = [self.wires.push(source, target, self.cross[0])]
        yield
        arrive(crossed)
        held = without(self.held, "z")
        kind = OneCore(first, width, self.core)
        yield from spread(self.here, self.wires, kind, whole, held, order, direct="xy")
        passed = whole.at[1 - self.zh, self.core, :, :, :, columns]
        beside = [self.wires.push(passed, passed, self.sibling)]
        yield
        arrive(beside)

    def wide(self, shard, whole, order):
        crossed = [
            self.wires.push(
                shard.at[self.x, self.y, :, self.ff_columns(self.there, (self.core + t) % 2)],
                whole.at[self.zh, self.core, self.x, self.y, :, self.part(SLICE)],
                self.cross[t],
            )
            for t in range(2)
        ]
        yield from self.rest(ShardsByCore(HALF_FF), whole, crossed, order, "y")

    def down(self, shard, whole, order):
        columns = pl.ds(pl.multiple_of(self.y * 256, 256), 256)
        source = shard.at[self.x, self.there, :, columns]
        target = whole.at[self.zh, self.x, self.there, :, columns]
        crossed = [self.wires.push(source, target, self.cross[0])]
        yield from self.rest(ColumnsByY(144), whole, crossed, order, "x")

    def from_this_chip(self, shards, staged, wholes):
        landed = [self.wires.move(shard, stage) for shard, stage in zip(shards, staged)]
        yield
        beside, kept = ([], [])
        for n, (stage, whole) in enumerate(zip(staged, wholes)):
            landed[n].wait()
            if n < 2:
                target = whole.at[self.zh, self.core]
                beside.append(self.wires.push(stage, target, self.sibling))
                kept.append(self.wires.move(stage, target))
            elif n < 4:
                for r in range(2):
                    target = whole.at[self.zh, self.core, :, :, :, pl.ds(r * SLICE, SLICE)]
                    theirs = stage.at[:, :, :, self.ff_columns(r, 1 - self.core)]
                    mine = stage.at[:, :, :, self.ff_columns(r, self.core)]
                    beside.append(self.wires.push(theirs, target, self.sibling))
                    kept.append(self.wires.move(mine, target))
            else:
                kept.append(self.wires.move(stage, whole.at[self.zh]))
        for _ in range(4):
            yield
        arrive(beside)
        for copy in kept:
            copy.wait()


WIDE_FETCH = (
    (ShardsByCore(HALF_FF), ("y", "x", "z")),
    (ShardsByCore(HALF_FF), ("z", "y", "x")),
    (ColumnsByY(144), ("x", "z", "y")),
)


def gather_kernel(
    qkv, out, gate, up, down, qkv_all, out_all, gate_all, up_all, down_all, *scratch
):
    staged, (sends, receives, moves) = (scratch[:5], scratch[5:])
    wires = Wires(sends, receives, moves)
    here = Place()
    fetch = Fetch(here, wires)
    greet_rings(here, fetch.cross)
    in_turn(
        [
            fetch.narrow(qkv, qkv_all, 0, 1024, ("x", "y")),
            fetch.narrow(qkv, qkv_all, 1024, 1024, ("y", "x")),
            fetch.narrow(out, out_all, 0, D, ("x", "y")),
            fetch.wide(gate, gate_all, WIDE_FETCH[0][1][:2]),
            fetch.wide(up, up_all, WIDE_FETCH[1][1][:2]),
            fetch.down(down, down_all, WIDE_FETCH[2][1][:2]),
            fetch.from_this_chip(
                (qkv, out, gate, up, down), staged, (qkv_all, out_all, gate_all, up_all, down_all)
            ),
        ]
    )
    wires.finish_sends()


def gather(qkv, out, gate, up, down):
    rows = (4, 4, 16)
    qkv, out, *wide = wired_call(
        gather_kernel,
        [
            shape(2, 2, *rows, 2048),
            shape(2, 2, *rows, D),
            shape(2, 2, *rows, HALF_FF),
            shape(2, 2, *rows, HALF_FF),
            shape(2, 4, 2, 144, D),
        ],
        (
            qkv.reshape(*rows, 2048),
            out.reshape(*rows, D),
            gate.reshape(*rows, FF),
            up.reshape(*rows, FF),
            down.reshape(4, 2, 144, D),
        ),
        1,
        "gather",
        3 * 8 + 9 + 6 + 5 + 6,
        12,
        [
            pltpu.VMEM((*rows, 2048), BF16),
            pltpu.VMEM((*rows, D), BF16),
            pltpu.VMEM((*rows, FF), BF16),
            pltpu.VMEM((*rows, FF), BF16),
            pltpu.VMEM((4, 2, 144, D), BF16),
        ],
        in_specs=[HBM] * 5,
        out_specs=[ANY] * 2 + [HBM] * 3,
        vmem=60 * MIB,
    )
    return qkv.reshape(D, 2048), out.reshape(D, D), wide


def fetch_last(here, wires, wide):
    tasks = []
    for (kind, order), whole in zip(WIDE_FETCH, wide):
        at = {"zh": 1 - here.zh, "zl": here.zl, "x": here.x, "y": here.y}
        for axis in order[:2]:
            at = without(at, axis)
        task = spread(here, wires, kind, whole, at, order[2:])
        tasks.append(later(task, 1) if order[2] == "z" else task)
    return tasks


WIDE = (
    (0, RowsByShard(HALF_FF), ("z", "x", "y"), ("y", "x", "z")),
    (1, RowsByShard(HALF_FF), ("x", "y", "z"), ("z", "y", "x")),
    (2, ColumnsByY(144), ("y", "z", "x"), ("x", "z", "y")),
)
NARROW = (
    (0, RowsByPlane(0, 1024), ("z", "x", "y"), ("z", "y", "x")),
    (0, RowsByPlane(1024, 1024), ("x", "y", "z"), ("x", "z", "y")),
    (1, ColumnsByY(32), ("y", "z", "x"), ("z", "x", "y")),
)
FIRST_DIRECT = ("y", "y", "x")
WIDE_DIMS = ((2, 2, 4, 4, 16, HALF_FF), (2, 2, 4, 4, 16, HALF_FF), (2, 4, 2, 144, D))
NARROW_DIMS = ((2, 4, 4, 16, 2048), (2, 4, 2, 32, D))


def slot_shapes(parts):
    found = []
    for _, kind, order, _ in parts:
        at = {}
        for axis in order:
            at = fix(at, axis, 0)
            found.append((6, *kind.open_dims(at), *kind.tail_dims({**at, "half": 0})))
    return found


def each_block(kind, at, body):
    dims = kind.open_dims(at)

    def step(i, _):
        inner, rest = ([], i)
        for n in reversed(dims):
            inner.insert(0, rest % n)
            rest = rest // n
        picks = iter(inner)
        lead = [next(picks) if o is None else o for o in kind.order(at)]
        body((*lead, *kind.tail(at)), (*inner, slice(None), slice(None)))
        return 0

    lax.fori_loop(0, math.prod(dims), step, 0)


def reduce_one(here, wires, kind, grad, total, slots, order, direct_from):
    at = {}
    for step, axis in enumerate(order):
        source, slot = (grad if step == 0 else total, slots[step])
        (right_place, right), (left_place, left) = (here.along(axis, 1), here.along(axis, 3))
        far_place, _ = here.along(axis, 2)
        mine = fix(at, axis, getattr(here, axis))

        def half_of(place, half):
            return {**fix(at, axis, place), "half": half}

        if step >= direct_from:
            copies = [
                wires.push(
                    kind.view(source, half_of(here.along(axis, s)[0], half)),
                    slot.at[2 * j + half],
                    here.along(axis, s)[1],
                )
                for j, s in enumerate(STEPS)
                for half in range(2)
            ]
            yield
            arrive(copies)
            for half in range(2):

                def add_all(whole, part):
                    value = total[whole].astype(F32)
                    for j in range(3):
                        value += slot[(2 * j + half, *part)].astype(F32)
                    total[whole] = value.astype(BF16)

                each_block(kind, {**mine, "half": half}, add_all)
            at = mine
            continue
        relays = [
            wires.push(kind.view(source, half_of(far_place, 0)), slot.at[4], right),
            wires.push(kind.view(source, half_of(far_place, 1)), slot.at[5], left),
        ]
        arriving = [
            wires.push(kind.view(source, half_of(right_place, 1)), slot.at[1], right),
            wires.push(kind.view(source, half_of(left_place, 0)), slot.at[2], left),
        ]
        kept = []
        if step == 0:
            for where in (half_of(right_place, 0), half_of(left_place, 1), mine):
                kept.append(wires.move(kind.view(source, where), kind.view(total, where)))
        yield
        for j, place, half, target, onward in (
            (4, right_place, 0, 0, right),
            (5, left_place, 1, 3, left),
        ):
            if kept:
                kept.pop(0).wait()
            arrive([relays[j - 4]])

            def pass_on(whole, part):
                value = slot[(j, *part)].astype(F32) + total[whole].astype(F32)
                slot[(j, *part)] = value.astype(BF16)

            each_block(kind, half_of(place, half), pass_on)
            arriving.append(wires.push(slot.at[j], slot.at[target], onward))
        yield
        if kept:
            kept.pop(0).wait()
        arrive(arriving)
        for half in range(2):

            def add_up(whole, part):
                value = total[whole].astype(F32) + slot[(half, *part)].astype(F32)
                total[whole] = (value + slot[(2 + half, *part)].astype(F32)).astype(BF16)

            each_block(kind, {**mine, "half": half}, add_up)
        at = mine


def reduce_weights_kernel(*refs):
    grads, gains = (refs[3:5], refs[5])
    nears, boths, narrow_outs, gains_out = (refs[6:9], refs[9:11], refs[11:13], refs[13])
    totals, slots, staged = (refs[14:16], refs[16:25], refs[25:27])
    gain_slots, sends, receives, moves = refs[27:]

    here = Place()
    wires = Wires(sends, receives, moves)
    core = here.core
    sibling = here.sibling()
    greet_rings(here)
    held = {"zh": here.zh, "zl": here.zl, "x": here.x, "y": here.y}

    def all_gains():
        sums = gains[...]
        for stage, axis in enumerate(("core", "x", "y", "z")):
            me = getattr(here, axis)
            gain_slots[stage, me] = sums
            source = gain_slots.at[stage, me]
            if axis == "core":
                others = [sibling]
            else:
                others = [here.along(axis, s)[1] for s in STEPS]
            copies = [wires.push(source, source, device) for device in others]
            yield
            arrive(copies)
            sums = gain_slots[stage, 0] + gain_slots[stage, 1]
            if axis != "core":
                sums = sums + gain_slots[stage, 2] + gain_slots[stage, 3]
        gains_out[...] = sums

    def narrow(p):
        g, kind, order, back = NARROW[p]
        yield from reduce_one(
            here, wires, kind, grads[g], totals[g], slots[3 * p : 3 * p + 3], order, 1
        )
        out = narrow_outs[g]
        own = wires.move(kind.view(totals[g], held), kind.view(out, held, 1))
        own.wait()
        yield from spread(here, wires, kind, out, held, back, 1, direct="xy")

    def wide(p):
        _, kind, _, back = WIDE[p]
        at = held
        for axis in back[:2]:
            at = without(at, axis)
        yield from spread(here, wires, kind, nears[p], at, back[2:], 1)
        if p < 2:
            copies = [wires.push(nears[p].at[1 - core], boths[p].at[core], sibling)]
            wires.move(nears[p].at[core], staged[p]).wait()
            own = wires.move(staged[p], boths[p].at[core])
            yield
            arrive(copies)
            own.wait()

    in_turn(
        [narrow(p) for p in range(3)]
        + [later(wide(p), rounds) for p, rounds in ((1, 2), (2, 2), (0, 4))]
        + [all_gains()]
    )
    wires.finish_sends()


def reduce_weights(nears, qkv, out, gains):
    outs = [
        *(shape(*d[1:]) for d in WIDE_DIMS),
        shape(*WIDE_DIMS[0][1:]),
        shape(*WIDE_DIMS[1][1:]),
        *(shape(*d[1:]) for d in NARROW_DIMS),
        shape(*gains.shape, dtype=F32),
    ]
    scratch = [pltpu.VMEM(d, BF16) for d in NARROW_DIMS]
    scratch += [pltpu.VMEM(s, BF16) for s in slot_shapes(NARROW)]
    scratch += [pltpu.VMEM(WIDE_DIMS[0][2:], BF16)] * 2
    scratch += [pltpu.VMEM((4, 4, *gains.shape), F32)]
    narrow = [a.reshape(d) for a, d in zip((qkv, out), NARROW_DIMS)]
    _, _, down, gate, up, qkv, out, gains = wired_call(
        reduce_weights_kernel,
        outs,
        [*nears, *narrow, gains],
        2,
        "reduce_weights",
        10 + 3 * (18 + 7) + 1 + 2 * 4 + 2,
        3 * 4 + 4,
        scratch,
        [HBM] * 3 + [ANY] * 2 + [VMEM],
        [HBM] * 7 + [VMEM],
        vmem=60 * MIB,
        aliases={i: i for i in range(3)},
    )

    def joined(both):
        both = both.reshape(2, 256, HALF_FF)
        pieces = [
            both[c, :, r * SLICE : (r + 1) * SLICE] for r in range(2) for c in range(2)
        ]
        return jnp.concatenate(pieces, axis=1)

    return (
        qkv.reshape(256, 2048),
        out.reshape(256, D),
        joined(gate),
        joined(up),
        down.reshape(SLICE, D),
        gains,
    )


def head_columns(head):
    return pl.ds(pl.multiple_of(head * 128, 128), 128)


def seats(here):
    me = here.ctx
    quarter, seat = (me // QUARTER, me % QUARTER)
    near = [quarter * QUARTER + (seat + s) % QUARTER for s in range(1, QUARTER)]
    far = [(me + s) % RING for s in range(1, RING)]
    return me, seat, near, far


def to_heads_kernel(query, key_value, query_out, key_value_out, sends, receives, moves):
    here = Place()
    wires = Wires(sends, receives, moves)
    me, seat, near, far = seats(here)
    greet([(k, here.fsdp) for k in far])
    copies = [
        wires.push(query.at[:, head_columns(k % QUARTER)], query_out.at[seat], (k, here.fsdp))
        for k in near
    ]
    copies += [
        wires.push(key_value.at[:, head_columns(k % QUARTER)], key_value_out.at[me], (k, here.fsdp))
        for k in far
    ]
    kept = [
        wires.move(query.at[:, head_columns(seat)], query_out.at[seat]),
        wires.move(key_value.at[:, head_columns(seat)], key_value_out.at[me]),
    ]
    arrive(copies)
    for copy in kept:
        copy.wait()
    wires.finish_sends()


def to_heads(query, key_value):
    outs = [shape(QUARTER, TOKENS, 128), shape(RING, TOKENS, 128)]
    return wired_call(to_heads_kernel, outs, [query, key_value], 3, "to_heads", 38, 2)


def grad_to_heads_kernel(grad, branch, grad_out, branch_pair, sends, receives, moves):
    here = Place()
    wires = Wires(sends, receives, moves)
    _, seat, near, _ = seats(here)
    greet([(k, here.fsdp) for k in near] + [here.sibling()])
    copies = [
        wires.push(grad.at[:, head_columns(k % QUARTER)], grad_out.at[seat], (k, here.fsdp))
        for k in near
    ]
    copies.append(wires.push(branch, branch_pair.at[here.core], here.sibling()))
    kept = [
        wires.move(grad.at[:, head_columns(seat)], grad_out.at[seat]),
        wires.move(branch, branch_pair.at[here.core]),
    ]
    arrive(copies)
    for copy in kept:
        copy.wait()
    wires.finish_sends()


def grad_to_heads(grad, branch):
    outs = [shape(QUARTER, TOKENS, 128), shape(2, TOKENS, D)]
    return wired_call(grad_to_heads_kernel, outs, [grad, branch], 4, "grad_to_heads", 8, 2)


def to_tokens_kernel(query, query_out, sends, receives, moves):
    here = Place()
    wires = Wires(sends, receives, moves)
    _, seat, near, _ = seats(here)
    greet([(k, here.fsdp) for k in near])
    columns = query_out.at[:, head_columns(seat)]
    copies = [wires.push(query.at[k % QUARTER], columns, (k, here.fsdp)) for k in near]
    kept = wires.move(query.at[seat], columns)
    arrive(copies)
    kept.wait()
    wires.finish_sends()


def to_tokens(query):
    return wired_call(to_tokens_kernel, [shape(TOKENS, D)], [query], 5, "to_tokens", 7, 1)[0]


def grads_to_tokens_kernel(*refs):
    query, key_value = refs[:2]
    query_out, key_value_out, nears, staged = (refs[5], refs[6], refs[7:10], refs[10:12])
    here = Place()
    wires = Wires(*refs[12:])
    me, seat, near, far = seats(here)
    greet([(k, here.fsdp) for k in far])
    held = {"zh": here.zh, "zl": here.zl, "x": here.x, "y": here.y}

    def back():
        columns = query_out.at[:, head_columns(seat)]
        landed = [
            wires.move(query.at[seat], staged[0]),
            wires.move(key_value.at[me], staged[1]),
        ]
        copies = [wires.push(query.at[k % QUARTER], columns, (k, here.fsdp)) for k in near]
        copies += [
            wires.push(key_value.at[k], key_value_out.at[me], (k, here.fsdp)) for k in far
        ]
        for copy in landed:
            copy.wait()
        kept = [
            wires.move(staged[0], columns),
            wires.move(staged[1], key_value_out.at[me]),
        ]
        for _ in range(3):
            yield
        arrive(copies)
        for copy in kept:
            copy.wait()

    def share(p):
        _, kind, _, order = WIDE[p]
        yield from spread(
            here, wires, kind, nears[p], held, order[:2], 1, direct=FIRST_DIRECT[p]
        )

    in_turn([share(p) for p in range(3)] + [back()])
    wires.finish_sends()


def grads_to_tokens(query, key_value, nears):
    query_grad, key_value_grad, *nears = wired_call(
        grads_to_tokens_kernel,
        [shape(TOKENS, D), shape(RING, TOKENS, 128), *(shape(*d[1:]) for d in WIDE_DIMS)],
        [query, key_value, *nears],
        6,
        "grads_to_tokens",
        38 + 7 + 4 + 4,
        4,
        [pltpu.VMEM((TOKENS, 128), BF16), pltpu.VMEM((TOKENS, 128), BF16)],
        in_specs=[ANY] * 2 + [HBM] * 3,
        out_specs=[ANY] * 2 + [HBM] * 3,
        vmem=60 * MIB,
        aliases={2 + i: 2 + i for i in range(3)},
    )
    return query_grad, key_value_grad, nears


def half_columns(r, core):
    return pl.ds(pl.multiple_of(r * 512 + core * 256, 256), 256)


def share_kernel(whole, halved, *refs):
    n = whole + halved
    ins, outs = (refs[:n], refs[n : 2 * n])
    here = Place()
    wires = Wires(*refs[2 * n :])
    core = here.core
    sibling = here.sibling()
    greet([sibling])
    copies, kept = ([], [])
    for source, target in zip(ins[:whole], outs[:whole]):
        copies.append(wires.push(source, target.at[core], sibling))
        kept.append(wires.move(source, target.at[core]))
    for source, target in zip(ins[whole:], outs[whole:]):
        for r in range(2):
            place = target.at[core, :, pl.ds(r * 256, 256)]
            copies.append(wires.push(source.at[:, half_columns(r, 1 - core)], place, sibling))
            kept.append(wires.move(source.at[:, half_columns(r, core)], place))
    arrive(copies)
    for copy in kept:
        copy.wait()
    wires.finish_sends()


def share(whole, halved, collective_id):
    outs = [shape(2, *a.shape, dtype=a.dtype) for a in whole]
    outs += [shape(2, a.shape[0], 512, dtype=a.dtype) for a in halved]
    count = len(whole) + 2 * len(halved)
    done = wired_call(
        functools.partial(share_kernel, len(whole), len(halved)),
        outs,
        [*whole, *halved],
        collective_id,
        "share",
        count,
        count,
    )
    return [a.reshape(2 * a.shape[1], a.shape[2]) for a in done]


def hand_over_kernel(count, *refs):
    ins, outs = (refs[:count], refs[count : 2 * count])
    here = Place()
    wires = Wires(*refs[2 * count :])
    sibling = here.sibling()
    greet([sibling])
    copies = [wires.push(i.at[1 - here.core], o, sibling) for i, o in zip(ins, outs)]
    arrive(copies)
    wires.finish_sends()


def hand_over(partials, collective_id):
    return wired_call(
        functools.partial(hand_over_kernel, len(partials)),
        [shape(*a.shape[1:], dtype=a.dtype) for a in partials],
        partials,
        collective_id,
        "hand_over",
        len(partials),
        0,
    )


def nt(left, right):
    return lax.dot_general(left, right, (((1,), (1,)), ((), ())), preferred_element_type=F32)


def nn(left, right):
    return lax.dot_general(left, right, (((1,), (0,)), ((), ())), preferred_element_type=F32)


def query_block(ref, t):
    block = ref[t].astype(F32)
    both = jnp.concatenate([block, pltpu.roll(block, 64, 1)], axis=0)
    low = lax.broadcasted_iota(jnp.int32, (128, 128), 1) < 64
    return jnp.where(low, both, 0.0)


def query_pair(ref, u):
    return [query_block(ref, 2 * u), query_block(ref, 2 * u + 1)]


def first_allowed(position, starts_ref):
    begin = jnp.zeros_like(position)
    for n in range(4):
        begin = jnp.maximum(begin, jnp.where(starts_ref[n] <= position, starts_ref[n], 0))
    return begin


def heads_beside(rows):
    low = lax.broadcasted_iota(jnp.int32, (64, 128), 1) < 64
    return jnp.where(low, rows[:64], pltpu.roll(rows[64:], 64, 1)).astype(BF16)


def attend_task(
    counts, first_block, starts_ref, order_ref, query_ref, key_value_ref, out_ref, exact_ref,
    sum_ref, value_ref, key_at_ref,
):
    def key_places(j, _):
        lane = lax.broadcasted_iota(jnp.int32, (1, 128), 1)
        block = jnp.where(lane < 64, order_ref[2 * j], order_ref[2 * j + 1])
        key_at_ref[:, pl.ds(pl.multiple_of(j * 128, 128), 128)] = block * 64 + lane % 64
        return 0

    def values(j, _):
        rows = pl.ds(pl.multiple_of(j * 256, 256), 256)
        block = pltpu.roll(key_value_ref[rows, :].astype(F32), 64, 1)
        low = lax.broadcasted_iota(jnp.int32, (256, 128), 1) < 64
        value_ref[rows, :] = jnp.where(low, block, 1.0).astype(BF16)
        return 0

    def blocks(u, _):
        queries = jnp.concatenate(query_pair(query_ref, u), axis=0).astype(BF16)
        inner = lax.broadcasted_iota(jnp.int32, (128, 1), 0) % 64
        block = first_block + 2 * u
        position = jnp.concatenate(
            [order_ref[block] * 64 + inner, order_ref[block + 1] * 64 + inner], axis=0
        )
        begin = first_allowed(position, starts_ref)

        def tile(j, total):
            rows = pl.ds(pl.multiple_of(j * KEY_TILE, KEY_TILE), KEY_TILE)
            scores = nt(queries, key_value_ref[rows, :])
            key = key_at_ref[:, rows]
            allowed = (key <= position) & (key >= begin)
            weight = jnp.where(allowed, jnp.exp2(scores * SCORE_TO_EXP2), 0.0)
            return total + nn(weight.astype(BF16), value_ref[rows, :])

        total = lax.fori_loop(0, SEQ // KEY_TILE, tile, jnp.zeros((256, 128), F32))
        attended = total / pltpu.roll(total, 64, 1)
        low = lax.broadcasted_iota(jnp.int32, (256, 128), 1) < 64
        attended = jnp.where(low, attended, 0.0)
        for n in range(2):
            rows = slice(128 * n, 128 * n + 128)
            exact_ref[2 * u + n] = attended[rows]
            out_ref[2 * u + n] = heads_beside(attended[rows])
            sum_ref[2 * u + n] = jnp.transpose(total[rows])[64:72]
        return 0

    lax.fori_loop(0, SEQ // 256, values, 0)
    lax.fori_loop(0, SEQ // 128, key_places, 0)
    first = 0
    for count in counts:
        lax.fori_loop(first, first + count, blocks, 0)
        first += count
        yield


def attend_kernel(
    starts, order, query, key_value, gate_in, up_in, down_in, attended, exact, sums, gate_all,
    up_all, down_all, value_ref, key_at_ref, sends, receives, moves,
):
    wires = Wires(sends, receives, moves)
    here = Place()
    greet_rings(here)
    in_turn(
        [
            *fetch_last(here, wires, (gate_all, up_all, down_all))[::-1],
            attend_task(
                (6, 2), here.ctx // QUARTER * 16, starts, order, query, key_value, attended, exact,
                sums, value_ref, key_at_ref,
            ),
        ]
    )
    wires.finish_sends()


def attend(starts, order, queries, key_values, wide):
    outs = [
        shape(16, 64, 128),
        shape(16, 128, 128, dtype=F32),
        shape(16, 8, 128, dtype=F32),
        *(shape(*a.shape) for a in wide),
    ]
    attended, exact, sums, gate, up, down = wired_call(
        attend_kernel,
        outs,
        [starts, order, queries, key_values, *wide],
        10,
        "attend",
        1 + 4 + 4,
        1,
        [pltpu.VMEM((SEQ, 128), BF16), pltpu.VMEM((1, SEQ), jnp.int32)],
        [SMEM] * 2 + [VMEM] * 2 + [HBM] * 3,
        [VMEM] * 3 + [HBM] * 3,
        vmem=40 * MIB,
        aliases={4 + i: 3 + i for i in range(3)},
    )
    weights = (gate.reshape(D, HALF_FF), up.reshape(D, HALF_FF), down.reshape(HALF_FF, D))
    return attended, exact, sums, weights


def attend_back_task(
    counts, first_block, starts_ref, order_ref, query_ref, key_value_ref, grad_ref, exact_ref,
    sum_ref, query_grad_ref, key_value_grad_ref, across_ref, total_ref, key_at_ref,
):
    total_ref[...] = jnp.zeros_like(total_ref)

    def key_places(j, _):
        inner = lax.broadcasted_iota(jnp.int32, (64, 1), 0)
        key_at_ref[pl.ds(pl.multiple_of(j * 64, 64), 64), :] = order_ref[j] * 64 + inner
        return 0

    def turn(j, _):
        rows = pl.ds(pl.multiple_of(j * 128, 128), 128)
        across_ref[:, rows] = jnp.transpose(key_value_ref[rows, :].astype(F32)).astype(BF16)
        return 0

    def blocks(u, _):
        queries, grads = (query_pair(query_ref, u), query_pair(grad_ref, u))
        delta = [
            jnp.sum(jnp.transpose(grad * exact_ref[2 * u + n]), axis=0, keepdims=True)
            for n, grad in enumerate(grads)
        ]
        delta = jnp.concatenate(delta, axis=1)
        total_exp2 = jnp.concatenate(
            [jnp.log2(sum_ref[2 * u + n][0:1]) for n in range(2)], axis=1
        )
        grads = [pltpu.roll(grad, 64, 1) for grad in grads]
        both = jnp.concatenate(queries + grads, axis=0).astype(BF16)
        inner = lax.broadcasted_iota(jnp.int32, (1, 128), 1) % 64
        block = first_block + 2 * u
        position = jnp.concatenate(
            [order_ref[block] * 64 + inner, order_ref[block + 1] * 64 + inner], axis=1
        )
        begin = first_allowed(position, starts_ref)

        def tile(j, query_grad):
            rows = pl.ds(pl.multiple_of(j * KEY_TILE_BACK, KEY_TILE_BACK), KEY_TILE_BACK)
            products = nt(key_value_ref[rows, :], both)
            key = key_at_ref[rows, :]
            allowed = (key <= position) & (key >= begin)
            prob = jnp.where(
                allowed, jnp.exp2(products[:, :256] * SCORE_TO_EXP2 - total_exp2), 0.0
            )
            score = (prob * (products[:, 256:] - delta)).astype(BF16)
            side = jnp.concatenate([score, prob.astype(BF16)], axis=1)
            total_ref[rows, :] += nn(side, both)
            return query_grad + nn(across_ref[:, rows], score)

        query_grad = lax.fori_loop(
            0, SEQ // KEY_TILE_BACK, tile, jnp.zeros((128, 256), F32)
        )
        for n in range(2):
            rows = jnp.transpose(query_grad[:, 128 * n : 128 * n + 128])
            query_grad_ref[2 * u + n] = heads_beside(rows * float(HEAD_SIZE) ** (-0.5))
        return 0

    def put_back(j, _):
        rows = pl.ds(pl.multiple_of(j * 256, 256), 256)
        low = lax.broadcasted_iota(jnp.int32, (256, 128), 1) < 64
        scale = jnp.where(low, float(HEAD_SIZE) ** (-0.5), 1.0)
        key_value_grad_ref[rows, :] = (total_ref[rows, :] * scale).astype(BF16)
        return 0

    lax.fori_loop(0, SEQ // 128, turn, 0)
    lax.fori_loop(0, 64, key_places, 0)
    first = 0
    for count in counts:
        lax.fori_loop(first, first + count, blocks, 0)
        first += count
        yield
    lax.fori_loop(0, SEQ // 256, put_back, 0)


def attend_back_kernel(*refs):
    attention, grads = (refs[:7], refs[7:10])
    outs, nears = (refs[10:12], refs[12:15])
    scratch, totals, slots = (refs[15:18], refs[18:21], refs[21:30])
    here = Place()
    wires = Wires(*refs[30:])
    greet_rings(here)
    at = {"zh": here.zh, "zl": here.zl, "x": here.x, "y": here.y}

    def reduce(p):
        _, kind, order, _ = WIDE[p]
        yield from reduce_one(
            here, wires, kind, grads[p], totals[p], slots[3 * p : 3 * p + 3], order, 2
        )
        own = wires.move(kind.view(totals[p], at), kind.view(nears[p], at, 1))
        yield
        own.wait()

    first_block = here.ctx // QUARTER * 16
    in_turn(
        [reduce(p) for p in range(3)]
        + [attend_back_task((3, 3, 1, 1), first_block, *attention, *outs, *scratch)]
    )
    wires.finish_sends()


def attend_back(starts, order, queries, key_values, grads, exact, sums, wide):
    ins = [starts, order, queries, key_values, grads]
    ins += [exact, sums, *(a.reshape(d) for a, d in zip(wide, WIDE_DIMS))]
    scratch = [
        pltpu.VMEM((128, SEQ), BF16),
        pltpu.VMEM((SEQ, 128), F32),
        pltpu.VMEM((SEQ, 1), jnp.int32),
    ]
    scratch += [pltpu.VMEM(d, BF16) for d in WIDE_DIMS]
    scratch += [pltpu.VMEM(s, BF16) for s in slot_shapes(WIDE)]
    query_grad, key_value_grad, *nears = wired_call(
        attend_back_kernel,
        [shape(16, 64, 128), shape(SEQ, 128), *(shape(*d[1:]) for d in WIDE_DIMS)],
        ins,
        11,
        "attend_back",
        3 * 18,
        3 * 4,
        scratch,
        [SMEM] * 2 + [VMEM] * 5 + [HBM] * 3,
        [VMEM] * 2 + [HBM] * 3,
        vmem=58 * MIB,
    )
    return query_grad, key_value_grad, nears


def low_lanes():
    return lax.broadcasted_iota(jnp.int32, (TOKENS, 128), 1) < 64


def head_mean(values):
    low = low_lanes()
    first = jnp.sum(jnp.where(low, values, 0.0), axis=1, keepdims=True)
    second = jnp.sum(jnp.where(low, 0.0, values), axis=1, keepdims=True)
    return jnp.where(low, first, second) * (1.0 / HEAD_SIZE)


def other_half(values):
    first = lax.broadcasted_iota(jnp.int32, (TOKENS, 128), 1) % 64 < 32
    return jnp.where(first, pltpu.roll(values, 96, 1), pltpu.roll(values, 32, 1))


def chunk(j):
    return slice(128 * j, 128 * j + 128)


def project_kernel(
    x_ref, gain_ref, weight_ref, query_gain_ref, key_gain_ref, cosine_ref, sine_ref, normed_ref,
    query_ref, key_value_ref, projected_ref,
):
    x = x_ref[...].astype(F32)
    normed = x * lax.rsqrt(jnp.mean(x * x, axis=-1, keepdims=True) + EPSILON) * gain_ref[...]
    normed_ref[...] = normed.astype(BF16)
    projected = nn(normed_ref[...], weight_ref[...])
    projected_ref[...] = projected[:, :1536]
    low = low_lanes()

    def turned(j, gain):
        values = projected[:, chunk(j)]
        values = values * lax.rsqrt(head_mean(values * values) + EPSILON) * gain
        return values * cosine_ref[...] + other_half(values) * sine_ref[...]

    for j in range(8):
        query_ref[:, chunk(j)] = turned(j, query_gain_ref[...]).astype(BF16)
    for j in range(4):
        keys = turned(8 + j, key_gain_ref[...])
        values = projected[:, chunk(12 + j)]
        first = jnp.where(low, keys, pltpu.roll(values, 64, 1))
        second = jnp.where(low, pltpu.roll(keys, 64, 1), values)
        key_value_ref[:, chunk(2 * j)] = first.astype(BF16)
        key_value_ref[:, chunk(2 * j + 1)] = second.astype(BF16)


def project(x, gain, weight, query_gain, key_gain, cosine, sine):
    return pl.pallas_call(
        project_kernel,
        out_shape=[
            shape(TOKENS, D),
            shape(TOKENS, D),
            shape(TOKENS, D),
            shape(TOKENS, 1536, dtype=F32),
        ],
        in_specs=[VMEM] * 7,
        out_specs=[VMEM] * 4,
        compiler_params=pltpu.CompilerParams(vmem_limit_bytes=32 * MIB),
        name="project",
    )(x, gain, weight, query_gain, key_gain, cosine, sine)


def project_back_kernel(
    query_grad_ref, key_value_grad_ref, projected_ref, x_ref, grad_resid_ref, gain_ref, weight_ref,
    query_gain_ref, key_gain_ref, cosine_ref, sine_ref, ffn_gain_grad_ref, grad_projected_ref,
    grad_inputs_ref, gains_ref,
):
    low = low_lanes()

    def back(j, grad, gain):
        grad = grad * cosine_ref[...] + other_half(grad * sine_ref[...])
        values = projected_ref[:, chunk(j)]
        scale = lax.rsqrt(head_mean(values * values) + EPSILON)
        unit = values * scale
        gain_grad = jnp.sum(grad * unit, axis=0, keepdims=True)
        grad = grad * gain
        grad = scale * (grad - unit * head_mean(grad * unit))
        grad_projected_ref[:, chunk(j)] = grad.astype(BF16)
        return gain_grad

    query_gain_grad = jnp.zeros((1, 128), F32)
    for j in range(8):
        grad = query_grad_ref[:, chunk(j)].astype(F32)
        query_gain_grad += back(j, grad, query_gain_ref[...])
    key_gain_grad = jnp.zeros((1, 128), F32)
    for j in range(4):
        first, second = [
            sum(key_value_grad_ref[8 * q + 2 * j + n].astype(F32) for q in range(4))
            for n in range(2)
        ]
        keys = jnp.where(low, first, pltpu.roll(second, 64, 1))
        values = jnp.where(low, pltpu.roll(first, 64, 1), second)
        key_gain_grad += back(8 + j, keys, key_gain_ref[...])
        grad_projected_ref[:, chunk(12 + j)] = values.astype(BF16)

    grad = nt(grad_projected_ref[...], weight_ref[...])
    x = x_ref[...].astype(F32)
    scale = lax.rsqrt(jnp.mean(x * x, axis=-1, keepdims=True) + EPSILON)
    unit = x * scale
    gain_grad = jnp.sum(grad * unit, axis=0, keepdims=True)
    grad = grad * gain_ref[...]
    grad = scale * (grad - unit * jnp.mean(grad * unit, axis=-1, keepdims=True))
    grad_inputs_ref[...] = (grad_resid_ref[...] + grad).astype(BF16)

    gains_ref[...] = jnp.zeros_like(gains_ref)
    for j in range(8):
        gains_ref[j : j + 1, :] = gain_grad[:, chunk(j)]
        gains_ref[8 + j : 9 + j, :] = ffn_gain_grad_ref[:, chunk(j)]
    gains_ref[16:17, :] = query_gain_grad + pltpu.roll(query_gain_grad, 64, 1)
    gains_ref[17:18, :] = key_gain_grad + pltpu.roll(key_gain_grad, 64, 1)


def project_back(*ins):
    return pl.pallas_call(
        project_back_kernel,
        out_shape=[shape(TOKENS, 2048), shape(TOKENS, D), shape(24, 128, dtype=F32)],
        in_specs=[VMEM] * 12,
        out_specs=[VMEM] * 3,
        compiler_params=pltpu.CompilerParams(vmem_limit_bytes=40 * MIB),
        name="project_back",
    )(*ins)


def rms_norm(values, gain_row):
    return (
        values * lax.rsqrt(jnp.mean(values * values, axis=-1, keepdims=True) + EPSILON) * gain_row
    )


def rope_tables(positions):
    lane = jnp.arange(128, dtype=jnp.int32)
    frequency = ROPE_BASE ** (-2.0 * (lane % 32).astype(F32) / HEAD_SIZE)
    angles = positions.astype(F32)[:, None] * frequency[None, :]
    sign = jnp.where(lane % 64 < 32, -1.0, 1.0)
    return jnp.cos(angles), jnp.sin(angles) * sign[None, :]


def outer_sum(left, right):
    return lax.dot_general(
        left, right, (((0,), (0,)), ((), ())), preferred_element_type=F32
    ).astype(BF16)


def matmul(left, right):
    return jnp.dot(left, right, preferred_element_type=F32)


def positions_at(block_order, first_row, total_row_count, half_rows):
    row_ids = first_row + jnp.arange(total_row_count, dtype=jnp.int32)
    blocks = row_ids // half_rows
    lookup = jnp.arange(block_order.shape[0], dtype=jnp.int32)
    picked = jnp.sum(jnp.where(blocks[:, None] == lookup[None, :], block_order[None, :], 0), axis=1)
    return picked * half_rows + row_ids % half_rows


def per_device(
    inputs,
    cotangent,
    qkv_weight,
    out_weight,
    gate_weight,
    up_weight,
    down_weight,
    gain_attn,
    gain_query,
    gain_key,
    gain_ffn,
    block_order,
    doc_starts,
):
    cycle_index = lax.axis_index("ctx")
    core = lax.axis_index("fsdp") % 2
    qkv_all, out_all, wide = gather(
        qkv_weight, out_weight, gate_weight, up_weight, down_weight
    )
    places = (doc_starts[0], block_order)
    positions = positions_at(block_order, cycle_index * TOKENS, TOKENS, TOKENS // 2)

    resid_in = inputs[0].astype(F32)
    gain_row = gain_attn.reshape(1, D)
    head_gains = [jnp.concatenate([g, g]).reshape(1, 128) for g in (gain_query, gain_key)]
    tables = rope_tables(positions)
    normed_low, queries, key_values, projected = project(
        inputs[0], gain_row, qkv_all, *head_gains, *tables
    )
    query_part, key_value_part = to_heads(queries, key_values)
    query_part = query_part.reshape(16, 64, 128)
    key_value_part = key_value_part.reshape(SEQ, 128)
    attended, exact, sums, (gate_all, up_all, down_all) = attend(
        *places, query_part, key_value_part, wide
    )
    attended_low = to_tokens(attended.reshape(QUARTER, TOKENS, 128))

    residual = resid_in + matmul(attended_low, out_all)
    normed_ffn, norm_ffn_pull = jax.vjp(rms_norm, residual, gain_ffn)
    grad_out = cotangent[0]
    ffn_pair, cotangent_pair, normed_half, attended_half = share(
        [normed_ffn.astype(BF16), grad_out], [normed_low, attended_low], 7
    )
    gate_proj = matmul(ffn_pair, gate_all)
    up_proj = matmul(ffn_pair, up_all)
    hidden, gating_pull = jax.vjp(
        lambda gate_in, up_in: jax.nn.silu(gate_in) * up_in, gate_proj, up_proj
    )
    hidden_low = hidden.astype(BF16)
    out_partial = matmul(hidden_low, down_all).reshape(2, TOKENS, D)
    grad_hidden = matmul(cotangent_pair, down_all.T)
    grad_gate, grad_up = gating_pull(grad_hidden)
    gate_low = grad_gate.astype(BF16)
    up_low = grad_up.astype(BF16)
    ffn_partial = (matmul(gate_low, gate_all.T) + matmul(up_low, up_all.T)).reshape(2, TOKENS, D)
    out_rest, ffn_rest = hand_over([out_partial, ffn_partial], 8)

    def mine(pair):
        return lax.dynamic_index_in_dim(pair, core, 0, keepdims=False)

    outputs = residual + mine(out_partial) + out_rest
    grad_resid_ffn, grad_gain_ffn = norm_ffn_pull(mine(ffn_partial) + ffn_rest)
    grad_resid = grad_out.astype(F32) + grad_resid_ffn
    branch_low = grad_resid.astype(BF16)
    grad_attended = matmul(branch_low, out_all.T).astype(BF16)
    grad_part, branch_pair = grad_to_heads(grad_attended, branch_low)
    query_grad, key_value_grad, nears = attend_back(
        *places,
        query_part,
        key_value_part,
        grad_part.reshape(16, 64, 128),
        exact,
        sums,
        (
            outer_sum(ffn_pair, gate_low),
            outer_sum(ffn_pair, up_low),
            outer_sum(hidden_low, cotangent_pair),
        ),
    )
    query_grad, key_value_grad, nears = grads_to_tokens(
        query_grad.reshape(QUARTER, TOKENS, 128),
        key_value_grad.reshape(RING, TOKENS, 128),
        nears,
    )
    grad_projected, grad_inputs, gains = project_back(
        query_grad,
        key_value_grad,
        projected,
        inputs[0],
        grad_resid,
        gain_row,
        qkv_all,
        *head_gains,
        *tables,
        grad_gain_ffn.reshape(1, D),
    )

    (projected_pair,) = share([grad_projected], [], 9)
    grad_qkv, grad_out_weight, grad_gate_weight, grad_up_weight, grad_down, gains = reduce_weights(
        nears,
        outer_sum(normed_half, projected_pair),
        outer_sum(attended_half, branch_pair.reshape(2 * TOKENS, D)),
        gains,
    )
    gains = gains.reshape(-1)
    return (
        outputs.astype(BF16)[None],
        grad_inputs[None],
        grad_qkv.astype(F32),
        grad_out_weight.astype(F32),
        grad_gate_weight.astype(F32),
        grad_up_weight.astype(F32),
        grad_down.astype(F32),
        gains[:D],
        gains[2 * D : 2 * D + HEAD_SIZE],
        gains[2 * D + 128 : 2 * D + 128 + HEAD_SIZE],
        gains[D : 2 * D],
    )


def solution(mesh):
    in_specs = (
        P("fsdp", "ctx", None),
        P("fsdp", "ctx", None),
        P("fsdp", None),
        P("fsdp", None),
        P("fsdp", None),
        P("fsdp", None),
        P("fsdp", None),
        P(),
        P(),
        P(),
        P(),
        P(),
        P("fsdp", None),
    )
    out_specs = (
        P("fsdp", "ctx", None),
        P("fsdp", "ctx", None),
        P("fsdp", None),
        P("fsdp", None),
        P("fsdp", None),
        P("fsdp", None),
        P("fsdp", None),
        P(),
        P(),
        P(),
        P(),
    )
    return jax.shard_map(
        per_device, mesh=mesh, in_specs=in_specs, out_specs=out_specs, check_vma=False
    )
```

```python
import functools
import math

import jax
import jax.numpy as jnp
from jax import lax
from jax.experimental import pallas as pl
from jax.experimental.pallas import tpu as pltpu
from jax.sharding import PartitionSpec as P

QUERY_HEADS = 16
KEY_VALUE_HEADS = 8
HEAD_SIZE = 64
FF = 4608
D = 1024
TOKENS = 128
RING = 32
QUARTER = 8
SLICE = 1152
HALF_FF = FF // 2
KEY_TILE = 1024
KEY_TILE_BACK = 1024
SEQ = 4096

EPSILON = 1e-05
ROPE_BASE = 1000000.0
SCORE_TO_EXP2 = float(HEAD_SIZE) ** (-0.5) * math.log2(math.e)

MESH = pl.DeviceIdType.MESH
ANY = pl.BlockSpec(memory_space=pl.ANY)
HBM = pl.BlockSpec(memory_space=pltpu.MemorySpace.HBM)
VMEM = pl.BlockSpec(memory_space=pltpu.VMEM)
SMEM = pl.BlockSpec(memory_space=pltpu.SMEM)
BF16 = jnp.bfloat16
F32 = jnp.float32
MIB = 1 << 20
STEPS = (1, 3, 2)


class Place:
    def __init__(self):
        self.ctx, self.fsdp = (lax.axis_index("ctx"), lax.axis_index("fsdp"))
        self.zl, self.x, self.y = (self.ctx // 16, (self.ctx // 4) % 4, self.ctx % 4)
        self.zh, self.core = (self.fsdp // 2, self.fsdp % 2)
        self.z = self.zh * 2 + self.zl

    def device(self, x=None, y=None, z=None, core=None):
        x = self.x if x is None else x
        y = self.y if y is None else y
        z = self.z if z is None else z
        core = self.core if core is None else core
        return ((z % 2) * 16 + x * 4 + y, (z // 2) * 2 + core)

    def sibling(self):
        return self.device(core=1 - self.core)

    def along(self, axis, step):
        coordinate = (getattr(self, axis) + step) % 4
        return coordinate, self.device(**{axis: coordinate})


class Wires:
    def __init__(self, sends, receives, locals_=None):
        self.sends, self.receives, self.locals_ = (sends, receives, locals_)
        self.pushed, self.moved = ([], 0)

    def push(self, source, target, device):
        at = len(self.pushed)
        copy = pltpu.make_async_remote_copy(
            src_ref=source,
            dst_ref=target,
            send_sem=self.sends.at[at],
            recv_sem=self.receives.at[at],
            device_id=device,
            device_id_type=MESH,
        )
        copy.start()
        self.pushed.append(copy)
        return copy

    def move(self, source, target):
        copy = pltpu.make_async_copy(source, target, self.locals_.at[self.moved])
        copy.start()
        self.moved += 1
        return copy

    def finish_sends(self):
        for copy in self.pushed:
            copy.wait_send()


def arrive(copies):
    for copy in copies:
        copy.wait_recv()


def greet(devices):
    barrier = pltpu.get_barrier_semaphore()
    for device in devices:
        pl.semaphore_signal(barrier, inc=1, device_id=device, device_id_type=MESH)
    pl.semaphore_wait(barrier, len(devices))


def wired_call(kernel, outs, ins, collective_id, name, copies, moves, scratch=(), in_specs=None,
               out_specs=None, vmem=32 * MIB, aliases=None):
    return pl.pallas_call(
        kernel,
        out_shape=outs,
        in_specs=[ANY] * len(ins) if in_specs is None else in_specs,
        out_specs=[ANY] * len(outs) if out_specs is None else out_specs,
        scratch_shapes=[
            *scratch,
            pltpu.SemaphoreType.DMA((copies,)),
            pltpu.SemaphoreType.DMA((copies,)),
            pltpu.SemaphoreType.DMA((max(moves, 1),)),
        ],
        compiler_params=pltpu.CompilerParams(
            collective_id=collective_id, has_side_effects=True, vmem_limit_bytes=vmem
        ),
        name=name,
        input_output_aliases=aliases or {},
    )(*ins)


def shape(*dims, dtype=BF16):
    return jax.ShapeDtypeStruct(dims, dtype)


class Pieces:
    def view(self, ref, at, skip=0):
        lead = [slice(None) if i is None else i for i in self.order(at)[skip:]]
        return ref.at[(*lead, *self.tail(at))]

    def open_dims(self, at):
        return tuple(n for n, i in zip(self.lead, self.order(at)) if i is None)

    def tail(self, at):
        first, width = self.columns(at)
        if not isinstance(first, int):
            first = pl.multiple_of(first, 128)
        return (slice(None), pl.ds(first, width))

    def tail_dims(self, at):
        return (self.rows, self.columns(at)[1])


def halved(first, width, at):
    if "half" not in at:
        return first, width
    return first + at["half"] * (width // 2), width // 2


class RowsByShard(Pieces):
    lead, rows = ((2, 2, 4, 4), 16)

    def __init__(self, width):
        self.width = width

    def order(self, at):
        return [at.get("zh"), at.get("zl"), at.get("x"), at.get("y")]

    def columns(self, at):
        return halved(0, self.width, at)


class RowsByPlane(Pieces):
    lead, rows = ((2, 4, 4), 16)

    def __init__(self, first, width):
        self.first, self.width = (first, width)

    def order(self, at):
        return [at.get("zh"), at.get("x"), at.get("y")]

    def columns(self, at):
        if "zl" not in at:
            return halved(self.first, self.width, at)
        half = self.width // 2
        return halved(self.first + half * at["zl"], half, at)


class ColumnsByY(Pieces):
    lead = (2, 4, 2)

    def __init__(self, rows):
        self.rows = rows

    def order(self, at):
        return [at.get("zh"), at.get("x"), at.get("zl")]

    def columns(self, at):
        return halved(at["y"] * 256, 256, at) if "y" in at else halved(0, D, at)


class ShardsByCore(Pieces):
    lead, rows = ((2, 2, 4, 4), 16)

    def __init__(self, width):
        self.width = width

    def order(self, at):
        return [at.get("zh"), at.get("half"), at.get("x"), at.get("y")]

    def columns(self, at):
        half = self.width // 2
        return (half * at["zl"], half) if "zl" in at else (0, self.width)


class OneCore(RowsByPlane):
    lead = (2, 2, 4, 4)

    def __init__(self, first, width, core):
        super().__init__(first, width)
        self.core = core

    def order(self, at):
        return [at.get("zh"), self.core, at.get("x"), at.get("y")]


def fix(at, axis, coordinate):
    if axis == "z":
        return {**at, "zh": coordinate // 2, "zl": coordinate % 2}
    return {**at, axis: coordinate}


def without(at, axis):
    return {a: i for a, i in at.items() if a != ("zl" if axis == "z" else axis)}


def in_turn(tasks):
    while tasks:
        tasks = [task for task in tasks if next(task, "over") != "over"]


def later(task, rounds):
    next(task)
    for _ in range(rounds + 1):
        yield
    yield from task


def delayed(task, rounds):
    for _ in range(rounds):
        yield
    yield from task


def spread(here, wires, kind, ref, at, order, skip=0, direct=""):
    for axis in order:
        piece = kind.view(ref, at, skip)
        if axis == "z":
            copies = [wires.push(piece, piece, here.device(z=here.zh * 2 + 1 - here.zl))]
            yield
            arrive(copies)
        elif axis in direct:
            copies = [wires.push(piece, piece, here.along(axis, s)[1]) for s in STEPS]
            yield
            arrive(copies)
        else:
            (_, right), (_, left) = (here.along(axis, 1), here.along(axis, 3))
            from_left = wires.push(piece, piece, right)
            from_right = wires.push(piece, piece, left)
            yield
            relays = []
            for half, copy, step, onward in ((0, from_left, 3, right), (1, from_right, 1, left)):
                arrive([copy])
                passing = fix(at, axis, here.along(axis, step)[0])
                passing = kind.view(ref, {**passing, "half": half}, skip)
                relays.append(wires.push(passing, passing, onward))
            yield
            arrive(relays)
        at = without(at, axis)


def greet_rings(here, others=()):
    rings = [here.along(a, s)[1] for a in ("x", "y", "z") for s in STEPS]
    greet([*rings, here.sibling(), *others])


class Fetch:
    def __init__(self, here, wires):
        self.here, self.wires = (here, wires)
        self.zh, self.core, self.x, self.y = (here.zh, here.core, here.x, here.y)
        self.there = 1 - here.zl
        self.cross = [here.device(z=3 - here.z, core=(here.core + t) % 2) for t in range(2)]
        self.sibling = here.sibling()
        self.held = {"zh": 1 - here.zh, "zl": here.zl, "x": here.x, "y": here.y}

    def part(self, width):
        return pl.ds(pl.multiple_of(self.there * width, 128), width)

    def ff_columns(self, r, c):
        return pl.ds(pl.multiple_of(r * HALF_FF + c * SLICE, 128), SLICE)

    def rest(self, kind, whole, crossed, order, direct):
        yield
        arrive(crossed)
        yield from spread(
            self.here, self.wires, kind, whole, self.held, order, direct=direct
        )

    def narrow(self, shard, whole, first, width, order):
        columns = pl.ds(first, width)
        source = shard.at[self.x, self.y, :, columns]
        target = whole.at[self.zh, self.core, self.x, self.y, :, columns]
        crossed = [self.wires.push(source, target, self.cross[0])]
        yield
        arrive(crossed)
        held = without(self.held, "z")
        kind = OneCore(first, width, self.core)
        yield from spread(self.here, self.wires, kind, whole, held, order, direct="xy")
        passed = whole.at[1 - self.zh, self.core, :, :, :, columns]
        beside = [self.wires.push(passed, passed, self.sibling)]
        yield
        arrive(beside)

    def wide(self, shard, whole, order):
        crossed = [
            self.wires.push(
                shard.at[self.x, self.y, :, self.ff_columns(self.there, (self.core + t) % 2)],
                whole.at[self.zh, self.core, self.x, self.y, :, self.part(SLICE)],
                self.cross[t],
            )
            for t in range(2)
        ]
        yield from self.rest(ShardsByCore(HALF_FF), whole, crossed, order, "y")

    def down(self, shard, whole, order):
        columns = pl.ds(pl.multiple_of(self.y * 256, 256), 256)
        source = shard.at[self.x, self.there, :, columns]
        target = whole.at[self.zh, self.x, self.there, :, columns]
        crossed = [self.wires.push(source, target, self.cross[0])]
        yield from self.rest(ColumnsByY(144), whole, crossed, order, "x")

    def from_this_chip(self, shards, staged, wholes):
        landed = [self.wires.move(shard, stage) for shard, stage in zip(shards, staged)]
        yield
        beside, kept = ([], [])
        for n, (stage, whole) in enumerate(zip(staged, wholes)):
            landed[n].wait()
            if n < 2:
                target = whole.at[self.zh, self.core]
                beside.append(self.wires.push(stage, target, self.sibling))
                kept.append(self.wires.move(stage, target))
            elif n < 4:
                for r in range(2):
                    target = whole.at[self.zh, self.core, :, :, :, pl.ds(r * SLICE, SLICE)]
                    theirs = stage.at[:, :, :, self.ff_columns(r, 1 - self.core)]
                    mine = stage.at[:, :, :, self.ff_columns(r, self.core)]
                    beside.append(self.wires.push(theirs, target, self.sibling))
                    kept.append(self.wires.move(mine, target))
            else:
                kept.append(self.wires.move(stage, whole.at[self.zh]))
        for _ in range(4):
            yield
        arrive(beside)
        for copy in kept:
            copy.wait()


WIDE_FETCH = (
    (ShardsByCore(HALF_FF), ("y", "x", "z")),
    (ShardsByCore(HALF_FF), ("z", "y", "x")),
    (ColumnsByY(144), ("x", "z", "y")),
)


def gather_kernel(
    qkv, out, gate, up, down, qkv_all, out_all, gate_all, up_all, down_all, *scratch
):
    staged, (sends, receives, moves) = (scratch[:5], scratch[5:])
    wires = Wires(sends, receives, moves)
    here = Place()
    fetch = Fetch(here, wires)
    greet_rings(here, fetch.cross)
    in_turn(
        [
            fetch.narrow(qkv, qkv_all, 0, 1024, ("x", "y")),
            fetch.narrow(qkv, qkv_all, 1024, 1024, ("y", "x")),
            fetch.narrow(out, out_all, 0, D, ("x", "y")),
            fetch.wide(gate, gate_all, WIDE_FETCH[0][1][:2]),
            fetch.wide(up, up_all, WIDE_FETCH[1][1][:2]),
            fetch.down(down, down_all, WIDE_FETCH[2][1][:2]),
            fetch.from_this_chip(
                (qkv, out, gate, up, down), staged, (qkv_all, out_all, gate_all, up_all, down_all)
            ),
        ]
    )
    wires.finish_sends()


def gather(qkv, out, gate, up, down):
    rows = (4, 4, 16)
    qkv, out, *wide = wired_call(
        gather_kernel,
        [
            shape(2, 2, *rows, 2048),
            shape(2, 2, *rows, D),
            shape(2, 2, *rows, HALF_FF),
            shape(2, 2, *rows, HALF_FF),
            shape(2, 4, 2, 144, D),
        ],
        (
            qkv.reshape(*rows, 2048),
            out.reshape(*rows, D),
            gate.reshape(*rows, FF),
            up.reshape(*rows, FF),
            down.reshape(4, 2, 144, D),
        ),
        1,
        "gather",
        3 * 8 + 9 + 6 + 5 + 6,
        12,
        [
            pltpu.VMEM((*rows, 2048), BF16),
            pltpu.VMEM((*rows, D), BF16),
            pltpu.VMEM((*rows, FF), BF16),
            pltpu.VMEM((*rows, FF), BF16),
            pltpu.VMEM((4, 2, 144, D), BF16),
        ],
        in_specs=[HBM] * 5,
        out_specs=[ANY] * 2 + [HBM] * 3,
        vmem=60 * MIB,
    )
    return qkv.reshape(D, 2048), out.reshape(D, D), wide


def fetch_last(here, wires, wide):
    tasks = []
    for (kind, order), whole in zip(WIDE_FETCH, wide):
        at = {"zh": 1 - here.zh, "zl": here.zl, "x": here.x, "y": here.y}
        for axis in order[:2]:
            at = without(at, axis)
        task = spread(here, wires, kind, whole, at, order[2:])
        tasks.append(later(task, 1) if order[2] == "z" else task)
    return tasks


WIDE = (
    (0, RowsByShard(HALF_FF), ("z", "x", "y"), ("y", "x", "z")),
    (1, RowsByShard(HALF_FF), ("x", "y", "z"), ("z", "y", "x")),
    (2, ColumnsByY(144), ("y", "z", "x"), ("x", "z", "y")),
)
NARROW = (
    (0, RowsByPlane(0, 1024), ("z", "x", "y"), ("z", "y", "x")),
    (0, RowsByPlane(1024, 1024), ("x", "y", "z"), ("x", "z", "y")),
    (1, ColumnsByY(32), ("y", "z", "x"), ("z", "x", "y")),
)
FIRST_DIRECT = ("y", "y", "x")
WIDE_DIMS = ((2, 2, 4, 4, 16, HALF_FF), (2, 2, 4, 4, 16, HALF_FF), (2, 4, 2, 144, D))
NARROW_DIMS = ((2, 4, 4, 16, 2048), (2, 4, 2, 32, D))


def slot_shapes(parts):
    found = []
    for _, kind, order, _ in parts:
        at = {}
        for axis in order:
            at = fix(at, axis, 0)
            found.append((6, *kind.open_dims(at), *kind.tail_dims({**at, "half": 0})))
    return found


def each_block(kind, at, body):
    dims = kind.open_dims(at)

    def step(i, _):
        inner, rest = ([], i)
        for n in reversed(dims):
            inner.insert(0, rest % n)
            rest = rest // n
        picks = iter(inner)
        lead = [next(picks) if o is None else o for o in kind.order(at)]
        body((*lead, *kind.tail(at)), (*inner, slice(None), slice(None)))
        return 0

    lax.fori_loop(0, math.prod(dims), step, 0)


def reduce_one(here, wires, kind, grad, total, slots, order, direct_from):
    at = {}
    for step, axis in enumerate(order):
        source, slot = (grad if step == 0 else total, slots[step])
        (right_place, right), (left_place, left) = (here.along(axis, 1), here.along(axis, 3))
        far_place, _ = here.along(axis, 2)
        mine = fix(at, axis, getattr(here, axis))

        def half_of(place, half):
            return {**fix(at, axis, place), "half": half}

        if step >= direct_from:
            copies = [
                wires.push(
                    kind.view(source, half_of(here.along(axis, s)[0], half)),
                    slot.at[2 * j + half],
                    here.along(axis, s)[1],
                )
                for j, s in enumerate(STEPS)
                for half in range(2)
            ]
            yield
            arrive(copies)
            for half in range(2):

                def add_all(whole, part):
                    value = total[whole].astype(F32)
                    for j in range(3):
                        value += slot[(2 * j + half, *part)].astype(F32)
                    total[whole] = value.astype(BF16)

                each_block(kind, {**mine, "half": half}, add_all)
            at = mine
            continue
        relays = [
            wires.push(kind.view(source, half_of(far_place, 0)), slot.at[4], right),
            wires.push(kind.view(source, half_of(far_place, 1)), slot.at[5], left),
        ]
        arriving = [
            wires.push(kind.view(source, half_of(right_place, 1)), slot.at[1], right),
            wires.push(kind.view(source, half_of(left_place, 0)), slot.at[2], left),
        ]
        kept = []
        if step == 0:
            for where in (half_of(right_place, 0), half_of(left_place, 1), mine):
                kept.append(wires.move(kind.view(source, where), kind.view(total, where)))
        yield
        for j, place, half, target, onward in (
            (4, right_place, 0, 0, right),
            (5, left_place, 1, 3, left),
        ):
            if kept:
                kept.pop(0).wait()
            arrive([relays[j - 4]])

            def pass_on(whole, part):
                value = slot[(j, *part)].astype(F32) + total[whole].astype(F32)
                slot[(j, *part)] = value.astype(BF16)

            each_block(kind, half_of(place, half), pass_on)
            arriving.append(wires.push(slot.at[j], slot.at[target], onward))
        yield
        if kept:
            kept.pop(0).wait()
        arrive(arriving)
        for half in range(2):

            def add_up(whole, part):
                value = total[whole].astype(F32) + slot[(half, *part)].astype(F32)
                total[whole] = (value + slot[(2 + half, *part)].astype(F32)).astype(BF16)

            each_block(kind, {**mine, "half": half}, add_up)
        at = mine


def reduce_weights_kernel(*refs):
    grads, gains = (refs[3:5], refs[5])
    nears, boths, narrow_outs, gains_out = (refs[6:9], refs[9:11], refs[11:13], refs[13])
    totals, slots, staged = (refs[14:16], refs[16:25], refs[25:27])
    gain_slots, sends, receives, moves = refs[27:]

    here = Place()
    wires = Wires(sends, receives, moves)
    core = here.core
    sibling = here.sibling()
    greet_rings(here)
    held = {"zh": here.zh, "zl": here.zl, "x": here.x, "y": here.y}

    def all_gains():
        sums = gains[...]
        for stage, axis in enumerate(("core", "x", "y", "z")):
            me = getattr(here, axis)
            gain_slots[stage, me] = sums
            source = gain_slots.at[stage, me]
            if axis == "core":
                others = [sibling]
            else:
                others = [here.along(axis, s)[1] for s in STEPS]
            copies = [wires.push(source, source, device) for device in others]
            yield
            arrive(copies)
            sums = gain_slots[stage, 0] + gain_slots[stage, 1]
            if axis != "core":
                sums = sums + gain_slots[stage, 2] + gain_slots[stage, 3]
        gains_out[...] = sums

    def narrow(p):
        g, kind, order, back = NARROW[p]
        yield from reduce_one(
            here, wires, kind, grads[g], totals[g], slots[3 * p : 3 * p + 3], order, 1
        )
        out = narrow_outs[g]
        own = wires.move(kind.view(totals[g], held), kind.view(out, held, 1))
        own.wait()
        yield from spread(here, wires, kind, out, held, back, 1, direct="xy")

    def wide(p, c):
        _, kind, _, back = WIDE[p]
        axis = back[2]
        cut = "y" if axis == "x" else "x"
        at = {"zh": here.zh, cut: c}
        if axis == "z":
            at["zl"] = here.zl
        else:
            at[axis] = getattr(here, axis)
        yield from spread(here, wires, kind, nears[p], at, (axis,), 1)
        if p < 2:
            part = (c,) if cut == "x" else (slice(None), c)
            mine = (core, *part)
            copies = [wires.push(nears[p].at[(1 - core, *part)], boths[p].at[mine], sibling)]
            wires.move(nears[p].at[mine], staged[p].at[part]).wait()
            own = wires.move(staged[p].at[part], boths[p].at[mine])
            yield
            arrive(copies)
            own.wait()

    in_turn(
        [narrow(p) for p in range(3)]
        + [delayed(later(wide(p, c), 1), c) for c in range(4) for p in (1, 2, 0)]
        + [all_gains()]
    )
    wires.finish_sends()


def widen_kernel(qkv, out, gate, up, down, qkv_out, out_out, gate_out, up_out, down_out):
    qkv_out[...] = qkv[...].astype(F32)
    out_out[...] = out[...].astype(F32)
    down_out[...] = down[...].astype(F32)
    for both, whole in ((gate, gate_out), (up, up_out)):
        for r in range(2):
            for c in range(2):
                first = r * HALF_FF + c * SLICE
                values = both[c, :, r * SLICE : (r + 1) * SLICE]
                whole[:, first : first + SLICE] = values.astype(F32)


def widen(qkv, out, gate, up, down):
    steps = 8

    def rows(n, columns):
        return pl.BlockSpec((n // steps, columns), lambda i: (i, 0))

    pair = pl.BlockSpec((2, 256 // steps, HALF_FF), lambda i: (0, i, 0))
    return pl.pallas_call(
        widen_kernel,
        grid=(steps,),
        out_shape=[
            shape(256, 2048, dtype=F32),
            shape(256, D, dtype=F32),
            shape(256, FF, dtype=F32),
            shape(256, FF, dtype=F32),
            shape(SLICE, D, dtype=F32),
        ],
        in_specs=[rows(256, 2048), rows(256, D), pair, pair, rows(SLICE, D)],
        out_specs=[
            rows(256, 2048), rows(256, D), rows(256, FF), rows(256, FF), rows(SLICE, D)
        ],
        compiler_params=pltpu.CompilerParams(vmem_limit_bytes=60 * MIB),
        name="widen",
    )(qkv, out, gate, up, down)


def reduce_weights(nears, qkv, out, gains):
    outs = [
        *(shape(*d[1:]) for d in WIDE_DIMS),
        shape(*WIDE_DIMS[0][1:]),
        shape(*WIDE_DIMS[1][1:]),
        *(shape(*d[1:]) for d in NARROW_DIMS),
        shape(*gains.shape, dtype=F32),
    ]
    scratch = [pltpu.VMEM(d, BF16) for d in NARROW_DIMS]
    scratch += [pltpu.VMEM(s, BF16) for s in slot_shapes(NARROW)]
    scratch += [pltpu.VMEM(WIDE_DIMS[0][2:], BF16)] * 2
    scratch += [pltpu.VMEM((4, 4, *gains.shape), F32)]
    narrow = [a.reshape(d) for a, d in zip((qkv, out), NARROW_DIMS)]
    _, _, down, gate, up, qkv, out, gains = wired_call(
        reduce_weights_kernel,
        outs,
        [*nears, *narrow, gains],
        2,
        "reduce_weights",
        10 + 3 * (18 + 7) + 4 * (1 + 2 * 4 + 2),
        3 * 4 + 4 * 4,
        scratch,
        [HBM] * 3 + [ANY] * 2 + [VMEM],
        [HBM] * 7 + [VMEM],
        vmem=60 * MIB,
        aliases={i: i for i in range(3)},
    )

    widened = widen(
        qkv.reshape(256, 2048),
        out.reshape(256, D),
        gate.reshape(2, 256, HALF_FF),
        up.reshape(2, 256, HALF_FF),
        down.reshape(SLICE, D),
    )
    return (*widened, gains)


def head_columns(head):
    return pl.ds(pl.multiple_of(head * 128, 128), 128)


def seats(here):
    me = here.ctx
    quarter, seat = (me // QUARTER, me % QUARTER)
    near = [quarter * QUARTER + (seat + s) % QUARTER for s in range(1, QUARTER)]
    far = [(me + s) % RING for s in range(1, RING)]
    return me, seat, near, far


def to_heads_kernel(query, key_value, query_out, key_value_out, sends, receives, moves):
    here = Place()
    wires = Wires(sends, receives, moves)
    me, seat, near, far = seats(here)
    greet([(k, here.fsdp) for k in far])
    copies = [
        wires.push(query.at[:, head_columns(k % QUARTER)], query_out.at[seat], (k, here.fsdp))
        for k in near
    ]
    copies += [
        wires.push(key_value.at[:, head_columns(k % QUARTER)], key_value_out.at[me], (k, here.fsdp))
        for k in far
    ]
    kept = [
        wires.move(query.at[:, head_columns(seat)], query_out.at[seat]),
        wires.move(key_value.at[:, head_columns(seat)], key_value_out.at[me]),
    ]
    arrive(copies)
    for copy in kept:
        copy.wait()
    wires.finish_sends()


def to_heads(query, key_value):
    outs = [shape(QUARTER, TOKENS, 128), shape(RING, TOKENS, 128)]
    return wired_call(to_heads_kernel, outs, [query, key_value], 3, "to_heads", 38, 2)


def grad_to_heads_kernel(grad, branch, grad_out, branch_pair, sends, receives, moves):
    here = Place()
    wires = Wires(sends, receives, moves)
    _, seat, near, _ = seats(here)
    greet([(k, here.fsdp) for k in near] + [here.sibling()])
    copies = [
        wires.push(grad.at[:, head_columns(k % QUARTER)], grad_out.at[seat], (k, here.fsdp))
        for k in near
    ]
    copies.append(wires.push(branch, branch_pair.at[here.core], here.sibling()))
    kept = [
        wires.move(grad.at[:, head_columns(seat)], grad_out.at[seat]),
        wires.move(branch, branch_pair.at[here.core]),
    ]
    arrive(copies)
    for copy in kept:
        copy.wait()
    wires.finish_sends()


def grad_to_heads(grad, branch):
    outs = [shape(QUARTER, TOKENS, 128), shape(2, TOKENS, D)]
    return wired_call(grad_to_heads_kernel, outs, [grad, branch], 4, "grad_to_heads", 8, 2)


def to_tokens_kernel(query, query_out, sends, receives, moves):
    here = Place()
    wires = Wires(sends, receives, moves)
    _, seat, near, _ = seats(here)
    greet([(k, here.fsdp) for k in near])
    columns = query_out.at[:, head_columns(seat)]
    copies = [wires.push(query.at[k % QUARTER], columns, (k, here.fsdp)) for k in near]
    kept = wires.move(query.at[seat], columns)
    arrive(copies)
    kept.wait()
    wires.finish_sends()


def to_tokens(query):
    return wired_call(to_tokens_kernel, [shape(TOKENS, D)], [query], 5, "to_tokens", 7, 1)[0]


def grads_to_tokens_kernel(*refs):
    query, key_value = refs[:2]
    query_out, key_value_out, nears, staged = (refs[5], refs[6], refs[7:10], refs[10:12])
    here = Place()
    wires = Wires(*refs[12:])
    me, seat, near, far = seats(here)
    greet([(k, here.fsdp) for k in far])
    held = {"zh": here.zh, "zl": here.zl, "x": here.x, "y": here.y}

    def back():
        columns = query_out.at[:, head_columns(seat)]
        landed = [
            wires.move(query.at[seat], staged[0]),
            wires.move(key_value.at[me], staged[1]),
        ]
        copies = [wires.push(query.at[k % QUARTER], columns, (k, here.fsdp)) for k in near]
        copies += [
            wires.push(key_value.at[k], key_value_out.at[me], (k, here.fsdp)) for k in far
        ]
        for copy in landed:
            copy.wait()
        kept = [
            wires.move(staged[0], columns),
            wires.move(staged[1], key_value_out.at[me]),
        ]
        for _ in range(3):
            yield
        arrive(copies)
        for copy in kept:
            copy.wait()

    def share(p):
        _, kind, _, order = WIDE[p]
        yield from spread(
            here, wires, kind, nears[p], held, order[:2], 1, direct=FIRST_DIRECT[p]
        )

    in_turn([share(p) for p in range(3)] + [back()])
    wires.finish_sends()


def grads_to_tokens(query, key_value, nears):
    query_grad, key_value_grad, *nears = wired_call(
        grads_to_tokens_kernel,
        [shape(TOKENS, D), shape(RING, TOKENS, 128), *(shape(*d[1:]) for d in WIDE_DIMS)],
        [query, key_value, *nears],
        6,
        "grads_to_tokens",
        38 + 7 + 4 + 4,
        4,
        [pltpu.VMEM((TOKENS, 128), BF16), pltpu.VMEM((TOKENS, 128), BF16)],
        in_specs=[ANY] * 2 + [HBM] * 3,
        out_specs=[ANY] * 2 + [HBM] * 3,
        vmem=60 * MIB,
        aliases={2 + i: 2 + i for i in range(3)},
    )
    return query_grad, key_value_grad, nears


def half_columns(r, core):
    return pl.ds(pl.multiple_of(r * 512 + core * 256, 256), 256)


def share_kernel(whole, halved, *refs):
    n = whole + halved
    ins, outs = (refs[:n], refs[n : 2 * n])
    here = Place()
    wires = Wires(*refs[2 * n :])
    core = here.core
    sibling = here.sibling()
    greet([sibling])
    copies, kept = ([], [])
    for source, target in zip(ins[:whole], outs[:whole]):
        copies.append(wires.push(source, target.at[core], sibling))
        kept.append(wires.move(source, target.at[core]))
    for source, target in zip(ins[whole:], outs[whole:]):
        for r in range(2):
            place = target.at[core, :, pl.ds(r * 256, 256)]
            copies.append(wires.push(source.at[:, half_columns(r, 1 - core)], place, sibling))
            kept.append(wires.move(source.at[:, half_columns(r, core)], place))
    arrive(copies)
    for copy in kept:
        copy.wait()
    wires.finish_sends()


def share(whole, halved, collective_id):
    outs = [shape(2, *a.shape, dtype=a.dtype) for a in whole]
    outs += [shape(2, a.shape[0], 512, dtype=a.dtype) for a in halved]
    count = len(whole) + 2 * len(halved)
    done = wired_call(
        functools.partial(share_kernel, len(whole), len(halved)),
        outs,
        [*whole, *halved],
        collective_id,
        "share",
        count,
        count,
    )
    return [a.reshape(2 * a.shape[1], a.shape[2]) for a in done]


def hand_over_kernel(count, *refs):
    ins, outs = (refs[:count], refs[count : 2 * count])
    here = Place()
    wires = Wires(*refs[2 * count :])
    sibling = here.sibling()
    greet([sibling])
    copies = [wires.push(i.at[1 - here.core], o, sibling) for i, o in zip(ins, outs)]
    arrive(copies)
    wires.finish_sends()


def hand_over(partials, collective_id):
    return wired_call(
        functools.partial(hand_over_kernel, len(partials)),
        [shape(*a.shape[1:], dtype=a.dtype) for a in partials],
        partials,
        collective_id,
        "hand_over",
        len(partials),
        0,
    )


def nt(left, right):
    return lax.dot_general(left, right, (((1,), (1,)), ((), ())), preferred_element_type=F32)


def nn(left, right):
    return lax.dot_general(left, right, (((1,), (0,)), ((), ())), preferred_element_type=F32)


def query_block(ref, t):
    block = ref[t].astype(F32)
    both = jnp.concatenate([block, pltpu.roll(block, 64, 1)], axis=0)
    low = lax.broadcasted_iota(jnp.int32, (128, 128), 1) < 64
    return jnp.where(low, both, 0.0)


def query_pair(ref, u):
    return [query_block(ref, 2 * u), query_block(ref, 2 * u + 1)]


def first_allowed(position, starts_ref):
    begin = jnp.zeros_like(position)
    for n in range(4):
        begin = jnp.maximum(begin, jnp.where(starts_ref[n] <= position, starts_ref[n], 0))
    return begin


def heads_beside(rows):
    low = lax.broadcasted_iota(jnp.int32, (64, 128), 1) < 64
    return jnp.where(low, rows[:64], pltpu.roll(rows[64:], 64, 1)).astype(BF16)


def attend_task(
    counts, first_block, starts_ref, order_ref, query_ref, key_value_ref, out_ref, exact_ref,
    sum_ref, value_ref, key_at_ref,
):
    def key_places(j, _):
        lane = lax.broadcasted_iota(jnp.int32, (1, 128), 1)
        block = jnp.where(lane < 64, order_ref[2 * j], order_ref[2 * j + 1])
        key_at_ref[:, pl.ds(pl.multiple_of(j * 128, 128), 128)] = block * 64 + lane % 64
        return 0

    def values(j, _):
        rows = pl.ds(pl.multiple_of(j * 256, 256), 256)
        block = pltpu.roll(key_value_ref[rows, :].astype(F32), 64, 1)
        low = lax.broadcasted_iota(jnp.int32, (256, 128), 1) < 64
        value_ref[rows, :] = jnp.where(low, block, 1.0).astype(BF16)
        return 0

    def blocks(u, _):
        queries = jnp.concatenate(query_pair(query_ref, u), axis=0).astype(BF16)
        inner = lax.broadcasted_iota(jnp.int32, (128, 1), 0) % 64
        block = first_block + 2 * u
        position = jnp.concatenate(
            [order_ref[block] * 64 + inner, order_ref[block + 1] * 64 + inner], axis=0
        )
        begin = first_allowed(position, starts_ref)

        def tile(j, total):
            rows = pl.ds(pl.multiple_of(j * KEY_TILE, KEY_TILE), KEY_TILE)
            scores = nt(queries, key_value_ref[rows, :])
            key = key_at_ref[:, rows]
            allowed = (key <= position) & (key >= begin)
            weight = jnp.where(allowed, jnp.exp2(scores * SCORE_TO_EXP2), 0.0)
            return total + nn(weight.astype(BF16), value_ref[rows, :])

        total = lax.fori_loop(0, SEQ // KEY_TILE, tile, jnp.zeros((256, 128), F32))
        attended = total / pltpu.roll(total, 64, 1)
        low = lax.broadcasted_iota(jnp.int32, (256, 128), 1) < 64
        attended = jnp.where(low, attended, 0.0)
        for n in range(2):
            rows = slice(128 * n, 128 * n + 128)
            exact_ref[2 * u + n] = attended[rows]
            out_ref[2 * u + n] = heads_beside(attended[rows])
            sum_ref[2 * u + n] = jnp.transpose(total[rows])[64:72]
        return 0

    lax.fori_loop(0, SEQ // 256, values, 0)
    lax.fori_loop(0, SEQ // 128, key_places, 0)
    first = 0
    for count in counts:
        lax.fori_loop(first, first + count, blocks, 0)
        first += count
        yield


def attend_kernel(
    starts, order, query, key_value, gate_in, up_in, down_in, attended, exact, sums, gate_all,
    up_all, down_all, value_ref, key_at_ref, sends, receives, moves,
):
    wires = Wires(sends, receives, moves)
    here = Place()
    greet_rings(here)
    in_turn(
        [
            *fetch_last(here, wires, (gate_all, up_all, down_all))[::-1],
            attend_task(
                (6, 2), here.ctx // QUARTER * 16, starts, order, query, key_value, attended, exact,
                sums, value_ref, key_at_ref,
            ),
        ]
    )
    wires.finish_sends()


def attend(starts, order, queries, key_values, wide):
    outs = [
        shape(16, 64, 128),
        shape(16, 128, 128, dtype=F32),
        shape(16, 8, 128, dtype=F32),
        *(shape(*a.shape) for a in wide),
    ]
    attended, exact, sums, gate, up, down = wired_call(
        attend_kernel,
        outs,
        [starts, order, queries, key_values, *wide],
        10,
        "attend",
        1 + 4 + 4,
        1,
        [pltpu.VMEM((SEQ, 128), BF16), pltpu.VMEM((1, SEQ), jnp.int32)],
        [SMEM] * 2 + [VMEM] * 2 + [HBM] * 3,
        [VMEM] * 3 + [HBM] * 3,
        vmem=60 * MIB,
        aliases={4 + i: 3 + i for i in range(3)},
    )
    weights = (gate.reshape(D, HALF_FF), up.reshape(D, HALF_FF), down.reshape(HALF_FF, D))
    return attended, exact, sums, weights


def attend_back_task(
    counts, first_block, starts_ref, order_ref, query_ref, key_value_ref, grad_ref, exact_ref,
    sum_ref, query_grad_ref, key_value_grad_ref, across_ref, total_ref, key_at_ref,
):
    total_ref[...] = jnp.zeros_like(total_ref)

    def key_places(j, _):
        inner = lax.broadcasted_iota(jnp.int32, (64, 1), 0)
        key_at_ref[pl.ds(pl.multiple_of(j * 64, 64), 64), :] = order_ref[j] * 64 + inner
        return 0

    def turn(j, _):
        rows = pl.ds(pl.multiple_of(j * 128, 128), 128)
        across_ref[:, rows] = jnp.transpose(key_value_ref[rows, :].astype(F32)).astype(BF16)
        return 0

    def blocks(u, _):
        queries, grads = (query_pair(query_ref, u), query_pair(grad_ref, u))
        delta = [
            jnp.sum(jnp.transpose(grad * exact_ref[2 * u + n]), axis=0, keepdims=True)
            for n, grad in enumerate(grads)
        ]
        delta = jnp.concatenate(delta, axis=1)
        total_exp2 = jnp.concatenate(
            [jnp.log2(sum_ref[2 * u + n][0:1]) for n in range(2)], axis=1
        )
        grads = [pltpu.roll(grad, 64, 1) for grad in grads]
        both = jnp.concatenate(queries + grads, axis=0).astype(BF16)
        inner = lax.broadcasted_iota(jnp.int32, (1, 128), 1) % 64
        block = first_block + 2 * u
        position = jnp.concatenate(
            [order_ref[block] * 64 + inner, order_ref[block + 1] * 64 + inner], axis=1
        )
        begin = first_allowed(position, starts_ref)

        def tile(j, query_grad):
            rows = pl.ds(pl.multiple_of(j * KEY_TILE_BACK, KEY_TILE_BACK), KEY_TILE_BACK)
            products = nt(key_value_ref[rows, :], both)
            key = key_at_ref[rows, :]
            allowed = (key <= position) & (key >= begin)
            prob = jnp.where(
                allowed, jnp.exp2(products[:, :256] * SCORE_TO_EXP2 - total_exp2), 0.0
            )
            score = (prob * (products[:, 256:] - delta)).astype(BF16)
            side = jnp.concatenate([score, prob.astype(BF16)], axis=1)
            total_ref[rows, :] += nn(side, both)
            return query_grad + nn(across_ref[:, rows], score)

        query_grad = lax.fori_loop(
            0, SEQ // KEY_TILE_BACK, tile, jnp.zeros((128, 256), F32)
        )
        for n in range(2):
            rows = jnp.transpose(query_grad[:, 128 * n : 128 * n + 128])
            query_grad_ref[2 * u + n] = heads_beside(rows * float(HEAD_SIZE) ** (-0.5))
        return 0

    def put_back(j, _):
        rows = pl.ds(pl.multiple_of(j * 256, 256), 256)
        low = lax.broadcasted_iota(jnp.int32, (256, 128), 1) < 64
        scale = jnp.where(low, float(HEAD_SIZE) ** (-0.5), 1.0)
        key_value_grad_ref[rows, :] = (total_ref[rows, :] * scale).astype(BF16)
        return 0

    lax.fori_loop(0, SEQ // 128, turn, 0)
    lax.fori_loop(0, 64, key_places, 0)
    first = 0
    for count in counts:
        lax.fori_loop(first, first + count, blocks, 0)
        first += count
        yield
    lax.fori_loop(0, SEQ // 256, put_back, 0)


def attend_back_kernel(*refs):
    attention, grads = (refs[:7], refs[7:10])
    outs, nears = (refs[10:12], refs[12:15])
    scratch, totals, slots = (refs[15:18], refs[18:21], refs[21:30])
    here = Place()
    wires = Wires(*refs[30:])
    greet_rings(here)
    at = {"zh": here.zh, "zl": here.zl, "x": here.x, "y": here.y}

    def reduce(p):
        _, kind, order, _ = WIDE[p]
        yield from reduce_one(
            here, wires, kind, grads[p], totals[p], slots[3 * p : 3 * p + 3], order, 2
        )
        own = wires.move(kind.view(totals[p], at), kind.view(nears[p], at, 1))
        yield
        own.wait()

    first_block = here.ctx // QUARTER * 16
    in_turn(
        [reduce(p) for p in range(3)]
        + [attend_back_task((3, 3, 1, 1), first_block, *attention, *outs, *scratch)]
    )
    wires.finish_sends()


def attend_back(starts, order, queries, key_values, grads, exact, sums, wide):
    ins = [starts, order, queries, key_values, grads]
    ins += [exact, sums, *(a.reshape(d) for a, d in zip(wide, WIDE_DIMS))]
    scratch = [
        pltpu.VMEM((128, SEQ), BF16),
        pltpu.VMEM((SEQ, 128), F32),
        pltpu.VMEM((SEQ, 1), jnp.int32),
    ]
    scratch += [pltpu.VMEM(d, BF16) for d in WIDE_DIMS]
    scratch += [pltpu.VMEM(s, BF16) for s in slot_shapes(WIDE)]
    query_grad, key_value_grad, *nears = wired_call(
        attend_back_kernel,
        [shape(16, 64, 128), shape(SEQ, 128), *(shape(*d[1:]) for d in WIDE_DIMS)],
        ins,
        11,
        "attend_back",
        3 * 18,
        3 * 4,
        scratch,
        [SMEM] * 2 + [VMEM] * 5 + [HBM] * 3,
        [VMEM] * 2 + [HBM] * 3,
        vmem=58 * MIB,
    )
    return query_grad, key_value_grad, nears


def low_lanes():
    return lax.broadcasted_iota(jnp.int32, (TOKENS, 128), 1) < 64


def head_mean(values):
    low = low_lanes()
    first = jnp.sum(jnp.where(low, values, 0.0), axis=1, keepdims=True)
    second = jnp.sum(jnp.where(low, 0.0, values), axis=1, keepdims=True)
    return jnp.where(low, first, second) * (1.0 / HEAD_SIZE)


def other_half(values):
    first = lax.broadcasted_iota(jnp.int32, (TOKENS, 128), 1) % 64 < 32
    return jnp.where(first, pltpu.roll(values, 96, 1), pltpu.roll(values, 32, 1))


def chunk(j):
    return slice(128 * j, 128 * j + 128)


def project_kernel(
    x_ref, gain_ref, weight_hbm, query_gain_ref, key_gain_ref, cosine_ref, sine_ref, normed_ref,
    query_ref, key_value_ref, projected_ref, weight_ref, weight_sem,
):
    fetch = pltpu.make_async_copy(weight_hbm, weight_ref, weight_sem)
    fetch.start()
    x = x_ref[...].astype(F32)
    normed = x * lax.rsqrt(jnp.mean(x * x, axis=-1, keepdims=True) + EPSILON) * gain_ref[...]
    normed_ref[...] = normed.astype(BF16)
    fetch.wait()
    projected = nn(normed_ref[...], weight_ref[...])
    projected_ref[...] = projected[:, :1536]
    low = low_lanes()

    def turned(j, gain):
        values = projected[:, chunk(j)]
        values = values * lax.rsqrt(head_mean(values * values) + EPSILON) * gain
        return values * cosine_ref[...] + other_half(values) * sine_ref[...]

    for j in range(8):
        query_ref[:, chunk(j)] = turned(j, query_gain_ref[...]).astype(BF16)
    for j in range(4):
        keys = turned(8 + j, key_gain_ref[...])
        values = projected[:, chunk(12 + j)]
        first = jnp.where(low, keys, pltpu.roll(values, 64, 1))
        second = jnp.where(low, pltpu.roll(keys, 64, 1), values)
        key_value_ref[:, chunk(2 * j)] = first.astype(BF16)
        key_value_ref[:, chunk(2 * j + 1)] = second.astype(BF16)


def project(x, gain, weight, query_gain, key_gain, cosine, sine):
    return pl.pallas_call(
        project_kernel,
        out_shape=[
            shape(TOKENS, D),
            shape(TOKENS, D),
            shape(TOKENS, D),
            shape(TOKENS, 1536, dtype=F32),
        ],
        in_specs=[VMEM] * 2 + [ANY] + [VMEM] * 4,
        out_specs=[VMEM] * 4,
        scratch_shapes=[pltpu.VMEM((D, 2048), BF16), pltpu.SemaphoreType.DMA],
        compiler_params=pltpu.CompilerParams(vmem_limit_bytes=60 * MIB),
        name="project",
    )(x, gain, weight, query_gain, key_gain, cosine, sine)


def project_back_kernel(
    query_grad_ref, key_value_grad_ref, projected_ref, x_ref, grad_resid_ref, gain_ref, weight_hbm,
    query_gain_ref, key_gain_ref, cosine_ref, sine_ref, ffn_gain_grad_ref, grad_projected_ref,
    grad_inputs_ref, gains_ref, weight_ref, weight_sem,
):
    fetch = pltpu.make_async_copy(weight_hbm, weight_ref, weight_sem)
    fetch.start()
    low = low_lanes()

    def back(j, grad, gain):
        grad = grad * cosine_ref[...] + other_half(grad * sine_ref[...])
        values = projected_ref[:, chunk(j)]
        scale = lax.rsqrt(head_mean(values * values) + EPSILON)
        unit = values * scale
        gain_grad = jnp.sum(grad * unit, axis=0, keepdims=True)
        grad = grad * gain
        grad = scale * (grad - unit * head_mean(grad * unit))
        grad_projected_ref[:, chunk(j)] = grad.astype(BF16)
        return gain_grad

    query_gain_grad = jnp.zeros((1, 128), F32)
    for j in range(8):
        grad = query_grad_ref[:, chunk(j)].astype(F32)
        query_gain_grad += back(j, grad, query_gain_ref[...])
    key_gain_grad = jnp.zeros((1, 128), F32)
    for j in range(4):
        first, second = [
            sum(key_value_grad_ref[8 * q + 2 * j + n].astype(F32) for q in range(4))
            for n in range(2)
        ]
        keys = jnp.where(low, first, pltpu.roll(second, 64, 1))
        values = jnp.where(low, pltpu.roll(first, 64, 1), second)
        key_gain_grad += back(8 + j, keys, key_gain_ref[...])
        grad_projected_ref[:, chunk(12 + j)] = values.astype(BF16)

    fetch.wait()
    grad = nt(grad_projected_ref[...], weight_ref[...])
    x = x_ref[...].astype(F32)
    scale = lax.rsqrt(jnp.mean(x * x, axis=-1, keepdims=True) + EPSILON)
    unit = x * scale
    gain_grad = jnp.sum(grad * unit, axis=0, keepdims=True)
    grad = grad * gain_ref[...]
    grad = scale * (grad - unit * jnp.mean(grad * unit, axis=-1, keepdims=True))
    grad_inputs_ref[...] = (grad_resid_ref[...] + grad).astype(BF16)

    gains_ref[...] = jnp.zeros_like(gains_ref)
    for j in range(8):
        gains_ref[j : j + 1, :] = gain_grad[:, chunk(j)]
        gains_ref[8 + j : 9 + j, :] = ffn_gain_grad_ref[:, chunk(j)]
    gains_ref[16:17, :] = query_gain_grad + pltpu.roll(query_gain_grad, 64, 1)
    gains_ref[17:18, :] = key_gain_grad + pltpu.roll(key_gain_grad, 64, 1)


def project_back(*ins):
    return pl.pallas_call(
        project_back_kernel,
        out_shape=[shape(TOKENS, 2048), shape(TOKENS, D), shape(24, 128, dtype=F32)],
        in_specs=[VMEM] * 6 + [ANY] + [VMEM] * 5,
        out_specs=[VMEM] * 3,
        scratch_shapes=[pltpu.VMEM((D, 2048), BF16), pltpu.SemaphoreType.DMA],
        compiler_params=pltpu.CompilerParams(vmem_limit_bytes=60 * MIB),
        name="project_back",
    )(*ins)


def rms_norm(values, gain_row):
    return (
        values * lax.rsqrt(jnp.mean(values * values, axis=-1, keepdims=True) + EPSILON) * gain_row
    )


def rope_tables(positions):
    lane = jnp.arange(128, dtype=jnp.int32)
    frequency = ROPE_BASE ** (-2.0 * (lane % 32).astype(F32) / HEAD_SIZE)
    angles = positions.astype(F32)[:, None] * frequency[None, :]
    sign = jnp.where(lane % 64 < 32, -1.0, 1.0)
    return jnp.cos(angles), jnp.sin(angles) * sign[None, :]


def outer_sum(left, right):
    return lax.dot_general(
        left, right, (((0,), (0,)), ((), ())), preferred_element_type=F32
    ).astype(BF16)


def matmul(left, right):
    return jnp.dot(left, right, preferred_element_type=F32)


def positions_at(block_order, first_row, total_row_count, half_rows):
    row_ids = first_row + jnp.arange(total_row_count, dtype=jnp.int32)
    blocks = row_ids // half_rows
    lookup = jnp.arange(block_order.shape[0], dtype=jnp.int32)
    picked = jnp.sum(jnp.where(blocks[:, None] == lookup[None, :], block_order[None, :], 0), axis=1)
    return picked * half_rows + row_ids % half_rows


def per_device(
    inputs,
    cotangent,
    qkv_weight,
    out_weight,
    gate_weight,
    up_weight,
    down_weight,
    gain_attn,
    gain_query,
    gain_key,
    gain_ffn,
    block_order,
    doc_starts,
):
    cycle_index = lax.axis_index("ctx")
    core = lax.axis_index("fsdp") % 2
    qkv_all, out_all, wide = gather(
        qkv_weight, out_weight, gate_weight, up_weight, down_weight
    )
    places = (doc_starts[0], block_order)
    positions = positions_at(block_order, cycle_index * TOKENS, TOKENS, TOKENS // 2)

    resid_in = inputs[0].astype(F32)
    gain_row = gain_attn.reshape(1, D)
    head_gains = [jnp.concatenate([g, g]).reshape(1, 128) for g in (gain_query, gain_key)]
    tables = rope_tables(positions)
    normed_low, queries, key_values, projected = project(
        inputs[0], gain_row, qkv_all, *head_gains, *tables
    )
    query_part, key_value_part = to_heads(queries, key_values)
    query_part = query_part.reshape(16, 64, 128)
    key_value_part = key_value_part.reshape(SEQ, 128)
    attended, exact, sums, (gate_all, up_all, down_all) = attend(
        *places, query_part, key_value_part, wide
    )
    attended_low = to_tokens(attended.reshape(QUARTER, TOKENS, 128))

    residual = resid_in + matmul(attended_low, out_all)
    normed_ffn, norm_ffn_pull = jax.vjp(rms_norm, residual, gain_ffn)
    grad_out = cotangent[0]
    ffn_pair, cotangent_pair, normed_half, attended_half = share(
        [normed_ffn.astype(BF16), grad_out], [normed_low, attended_low], 7
    )
    gate_proj = matmul(ffn_pair, gate_all)
    up_proj = matmul(ffn_pair, up_all)
    hidden, gating_pull = jax.vjp(
        lambda gate_in, up_in: jax.nn.silu(gate_in) * up_in, gate_proj, up_proj
    )
    hidden_low = hidden.astype(BF16)
    out_partial = matmul(hidden_low, down_all).reshape(2, TOKENS, D)
    grad_hidden = matmul(cotangent_pair, down_all.T)
    grad_gate, grad_up = gating_pull(grad_hidden)
    gate_low = grad_gate.astype(BF16)
    up_low = grad_up.astype(BF16)
    ffn_partial = (matmul(gate_low, gate_all.T) + matmul(up_low, up_all.T)).reshape(2, TOKENS, D)
    out_rest, ffn_rest = hand_over([out_partial, ffn_partial], 8)

    def mine(pair):
        return lax.dynamic_index_in_dim(pair, core, 0, keepdims=False)

    outputs = residual + mine(out_partial) + out_rest
    grad_resid_ffn, grad_gain_ffn = norm_ffn_pull(mine(ffn_partial) + ffn_rest)
    grad_resid = grad_out.astype(F32) + grad_resid_ffn
    branch_low = grad_resid.astype(BF16)
    grad_attended = matmul(branch_low, out_all.T).astype(BF16)
    grad_part, branch_pair = grad_to_heads(grad_attended, branch_low)
    query_grad, key_value_grad, nears = attend_back(
        *places,
        query_part,
        key_value_part,
        grad_part.reshape(16, 64, 128),
        exact,
        sums,
        (
            outer_sum(ffn_pair, gate_low),
            outer_sum(ffn_pair, up_low),
            outer_sum(hidden_low, cotangent_pair),
        ),
    )
    query_grad, key_value_grad, nears = grads_to_tokens(
        query_grad.reshape(QUARTER, TOKENS, 128),
        key_value_grad.reshape(RING, TOKENS, 128),
        nears,
    )
    grad_projected, grad_inputs, gains = project_back(
        query_grad,
        key_value_grad,
        projected,
        inputs[0],
        grad_resid,
        gain_row,
        qkv_all,
        *head_gains,
        *tables,
        grad_gain_ffn.reshape(1, D),
    )

    (projected_pair,) = share([grad_projected], [], 9)
    grad_qkv, grad_out_weight, grad_gate_weight, grad_up_weight, grad_down, gains = reduce_weights(
        nears,
        outer_sum(normed_half, projected_pair),
        outer_sum(attended_half, branch_pair.reshape(2 * TOKENS, D)),
        gains,
    )
    gains = gains.reshape(-1)
    return (
        outputs.astype(BF16)[None],
        grad_inputs[None],
        grad_qkv,
        grad_out_weight,
        grad_gate_weight,
        grad_up_weight,
        grad_down,
        gains[:D],
        gains[2 * D : 2 * D + HEAD_SIZE],
        gains[2 * D + 128 : 2 * D + 128 + HEAD_SIZE],
        gains[D : 2 * D],
    )


def solution(mesh):
    in_specs = (
        P("fsdp", "ctx", None),
        P("fsdp", "ctx", None),
        P("fsdp", None),
        P("fsdp", None),
        P("fsdp", None),
        P("fsdp", None),
        P("fsdp", None),
        P(),
        P(),
        P(),
        P(),
        P(),
        P("fsdp", None),
    )
    out_specs = (
        P("fsdp", "ctx", None),
        P("fsdp", "ctx", None),
        P("fsdp", None),
        P("fsdp", None),
        P("fsdp", None),
        P("fsdp", None),
        P("fsdp", None),
        P(),
        P(),
        P(),
        P(),
    )
    return jax.shard_map(
        per_device, mesh=mesh, in_specs=in_specs, out_specs=out_specs, check_vma=False
    )
```

```python
import functools
import math

import jax
import jax.numpy as jnp
from jax import lax
from jax.experimental import pallas as pl
from jax.experimental.pallas import tpu as pltpu
from jax.sharding import PartitionSpec as P

QUERY_HEADS = 16
KEY_VALUE_HEADS = 8
HEAD_SIZE = 64
FF = 4608
D = 1024
TOKENS = 128
RING = 32
QUARTER = 8
SLICE = 1152
HALF_FF = FF // 2
KEY_TILE = 1024
KEY_TILE_BACK = 1024
SEQ = 4096

EPSILON = 1e-05
ROPE_BASE = 1000000.0
SCORE_TO_EXP2 = float(HEAD_SIZE) ** (-0.5) * math.log2(math.e)

MESH = pl.DeviceIdType.MESH
ANY = pl.BlockSpec(memory_space=pl.ANY)
HBM = pl.BlockSpec(memory_space=pltpu.MemorySpace.HBM)
VMEM = pl.BlockSpec(memory_space=pltpu.VMEM)
SMEM = pl.BlockSpec(memory_space=pltpu.SMEM)
BF16 = jnp.bfloat16
F32 = jnp.float32
MIB = 1 << 20
STEPS = (1, 3, 2)


class Place:
    def __init__(self):
        self.ctx, self.fsdp = (lax.axis_index("ctx"), lax.axis_index("fsdp"))
        self.zl, self.x, self.y = (self.ctx // 16, (self.ctx // 4) % 4, self.ctx % 4)
        self.zh, self.core = (self.fsdp // 2, self.fsdp % 2)
        self.z = self.zh * 2 + self.zl

    def device(self, x=None, y=None, z=None, core=None):
        x = self.x if x is None else x
        y = self.y if y is None else y
        z = self.z if z is None else z
        core = self.core if core is None else core
        return ((z % 2) * 16 + x * 4 + y, (z // 2) * 2 + core)

    def sibling(self):
        return self.device(core=1 - self.core)

    def along(self, axis, step):
        coordinate = (getattr(self, axis) + step) % 4
        return coordinate, self.device(**{axis: coordinate})


class Wires:
    def __init__(self, sends, receives, locals_=None):
        self.sends, self.receives, self.locals_ = (sends, receives, locals_)
        self.pushed, self.moved = ([], 0)

    def push(self, source, target, device):
        at = len(self.pushed)
        copy = pltpu.make_async_remote_copy(
            src_ref=source,
            dst_ref=target,
            send_sem=self.sends.at[at],
            recv_sem=self.receives.at[at],
            device_id=device,
            device_id_type=MESH,
        )
        copy.start()
        self.pushed.append(copy)
        return copy

    def move(self, source, target):
        copy = pltpu.make_async_copy(source, target, self.locals_.at[self.moved])
        copy.start()
        self.moved += 1
        return copy

    def finish_sends(self):
        for copy in self.pushed:
            copy.wait_send()


def arrive(copies):
    for copy in copies:
        copy.wait_recv()


def greet(devices):
    barrier = pltpu.get_barrier_semaphore()
    for device in devices:
        pl.semaphore_signal(barrier, inc=1, device_id=device, device_id_type=MESH)
    pl.semaphore_wait(barrier, len(devices))


def wired_call(kernel, outs, ins, collective_id, name, copies, moves, scratch=(), in_specs=None,
               out_specs=None, vmem=32 * MIB, aliases=None):
    return pl.pallas_call(
        kernel,
        out_shape=outs,
        in_specs=[ANY] * len(ins) if in_specs is None else in_specs,
        out_specs=[ANY] * len(outs) if out_specs is None else out_specs,
        scratch_shapes=[
            *scratch,
            pltpu.SemaphoreType.DMA((copies,)),
            pltpu.SemaphoreType.DMA((copies,)),
            pltpu.SemaphoreType.DMA((max(moves, 1),)),
        ],
        compiler_params=pltpu.CompilerParams(
            collective_id=collective_id, has_side_effects=True, vmem_limit_bytes=vmem
        ),
        name=name,
        input_output_aliases=aliases or {},
    )(*ins)


def shape(*dims, dtype=BF16):
    return jax.ShapeDtypeStruct(dims, dtype)


class Pieces:
    def view(self, ref, at, skip=0):
        lead = [slice(None) if i is None else i for i in self.order(at)[skip:]]
        return ref.at[(*lead, *self.tail(at))]

    def open_dims(self, at):
        return tuple(n for n, i in zip(self.lead, self.order(at)) if i is None)

    def tail(self, at):
        first, width = self.columns(at)
        if not isinstance(first, int):
            first = pl.multiple_of(first, 128)
        return (slice(None), pl.ds(first, width))

    def tail_dims(self, at):
        return (self.rows, self.columns(at)[1])


def halved(first, width, at):
    if "half" not in at:
        return first, width
    return first + at["half"] * (width // 2), width // 2


class RowsByShard(Pieces):
    lead, rows = ((2, 2, 4, 4), 16)

    def __init__(self, width):
        self.width = width

    def order(self, at):
        return [at.get("zh"), at.get("zl"), at.get("x"), at.get("y")]

    def columns(self, at):
        return halved(0, self.width, at)


class RowsByPlane(Pieces):
    lead, rows = ((2, 4, 4), 16)

    def __init__(self, first, width):
        self.first, self.width = (first, width)

    def order(self, at):
        return [at.get("zh"), at.get("x"), at.get("y")]

    def columns(self, at):
        if "zl" not in at:
            return halved(self.first, self.width, at)
        half = self.width // 2
        return halved(self.first + half * at["zl"], half, at)


class ColumnsByY(Pieces):
    lead = (2, 4, 2)

    def __init__(self, rows):
        self.rows = rows

    def order(self, at):
        return [at.get("zh"), at.get("x"), at.get("zl")]

    def columns(self, at):
        return halved(at["y"] * 256, 256, at) if "y" in at else halved(0, D, at)


class ShardsByCore(Pieces):
    lead, rows = ((2, 2, 4, 4), 16)

    def __init__(self, width):
        self.width = width

    def order(self, at):
        return [at.get("zh"), at.get("half"), at.get("x"), at.get("y")]

    def columns(self, at):
        half = self.width // 2
        return (half * at["zl"], half) if "zl" in at else (0, self.width)


class OneCore(RowsByPlane):
    lead = (2, 2, 4, 4)

    def __init__(self, first, width, core):
        super().__init__(first, width)
        self.core = core

    def order(self, at):
        return [at.get("zh"), self.core, at.get("x"), at.get("y")]


def fix(at, axis, coordinate):
    if axis == "z":
        return {**at, "zh": coordinate // 2, "zl": coordinate % 2}
    return {**at, axis: coordinate}


def without(at, axis):
    return {a: i for a, i in at.items() if a != ("zl" if axis == "z" else axis)}


def in_turn(tasks):
    while tasks:
        tasks = [task for task in tasks if next(task, "over") != "over"]


def later(task, rounds):
    next(task)
    for _ in range(rounds + 1):
        yield
    yield from task


def delayed(task, rounds):
    for _ in range(rounds):
        yield
    yield from task


def spread(here, wires, kind, ref, at, order, skip=0, direct=""):
    for axis in order:
        piece = kind.view(ref, at, skip)
        if axis == "z":
            copies = [wires.push(piece, piece, here.device(z=here.zh * 2 + 1 - here.zl))]
            yield
            arrive(copies)
        elif axis in direct:
            copies = [wires.push(piece, piece, here.along(axis, s)[1]) for s in STEPS]
            yield
            arrive(copies)
        else:
            (_, right), (_, left) = (here.along(axis, 1), here.along(axis, 3))
            from_left = wires.push(piece, piece, right)
            from_right = wires.push(piece, piece, left)
            yield
            relays = []
            for half, copy, step, onward in ((0, from_left, 3, right), (1, from_right, 1, left)):
                arrive([copy])
                passing = fix(at, axis, here.along(axis, step)[0])
                passing = kind.view(ref, {**passing, "half": half}, skip)
                relays.append(wires.push(passing, passing, onward))
            yield
            arrive(relays)
        at = without(at, axis)


def greet_rings(here, others=()):
    rings = [here.along(a, s)[1] for a in ("x", "y", "z") for s in STEPS]
    greet([*rings, here.sibling(), *others])


class Fetch:
    def __init__(self, here, wires):
        self.here, self.wires = (here, wires)
        self.zh, self.core, self.x, self.y = (here.zh, here.core, here.x, here.y)
        self.there = 1 - here.zl
        self.cross = [here.device(z=3 - here.z, core=(here.core + t) % 2) for t in range(2)]
        self.sibling = here.sibling()
        self.held = {"zh": 1 - here.zh, "zl": here.zl, "x": here.x, "y": here.y}

    def part(self, width):
        return pl.ds(pl.multiple_of(self.there * width, 128), width)

    def ff_columns(self, r, c):
        return pl.ds(pl.multiple_of(r * HALF_FF + c * SLICE, 128), SLICE)

    def rest(self, kind, whole, crossed, order, direct):
        yield
        arrive(crossed)
        yield from spread(
            self.here, self.wires, kind, whole, self.held, order, direct=direct
        )

    def narrow(self, shard, whole, first, width, order):
        columns = pl.ds(first, width)
        source = shard.at[self.x, self.y, :, columns]
        target = whole.at[self.zh, self.core, self.x, self.y, :, columns]
        crossed = [self.wires.push(source, target, self.cross[0])]
        yield
        arrive(crossed)
        held = without(self.held, "z")
        kind = OneCore(first, width, self.core)
        yield from spread(self.here, self.wires, kind, whole, held, order, direct="xy")
        passed = whole.at[1 - self.zh, self.core, :, :, :, columns]
        beside = [self.wires.push(passed, passed, self.sibling)]
        yield
        arrive(beside)

    def wide(self, shard, whole, order):
        crossed = [
            self.wires.push(
                shard.at[self.x, self.y, :, self.ff_columns(self.there, (self.core + t) % 2)],
                whole.at[self.zh, self.core, self.x, self.y, :, self.part(SLICE)],
                self.cross[t],
            )
            for t in range(2)
        ]
        yield from self.rest(ShardsByCore(HALF_FF), whole, crossed, order, "y")

    def down(self, shard, whole, order):
        columns = pl.ds(pl.multiple_of(self.y * 256, 256), 256)
        source = shard.at[self.x, self.there, :, columns]
        target = whole.at[self.zh, self.x, self.there, :, columns]
        crossed = [self.wires.push(source, target, self.cross[0])]
        yield from self.rest(ColumnsByY(144), whole, crossed, order, "x")

    def from_this_chip(self, shards, staged, wholes):
        landed = [self.wires.move(shard, stage) for shard, stage in zip(shards, staged)]
        yield
        beside, kept = ([], [])
        for n, (stage, whole) in enumerate(zip(staged, wholes)):
            landed[n].wait()
            if n < 2:
                target = whole.at[self.zh, self.core]
                beside.append(self.wires.push(stage, target, self.sibling))
                kept.append(self.wires.move(stage, target))
            elif n < 4:
                for r in range(2):
                    target = whole.at[self.zh, self.core, :, :, :, pl.ds(r * SLICE, SLICE)]
                    theirs = stage.at[:, :, :, self.ff_columns(r, 1 - self.core)]
                    mine = stage.at[:, :, :, self.ff_columns(r, self.core)]
                    beside.append(self.wires.push(theirs, target, self.sibling))
                    kept.append(self.wires.move(mine, target))
            else:
                kept.append(self.wires.move(stage, whole.at[self.zh]))
        for _ in range(4):
            yield
        arrive(beside)
        for copy in kept:
            copy.wait()


WIDE_FETCH = (
    (ShardsByCore(HALF_FF), ("y", "x", "z")),
    (ShardsByCore(HALF_FF), ("z", "y", "x")),
    (ColumnsByY(144), ("x", "z", "y")),
)


def gather_kernel(
    qkv, out, gate, up, down, qkv_all, out_all, gate_all, up_all, down_all, *scratch
):
    staged, (sends, receives, moves) = (scratch[:5], scratch[5:])
    wires = Wires(sends, receives, moves)
    here = Place()
    fetch = Fetch(here, wires)
    greet_rings(here, fetch.cross)
    in_turn(
        [
            fetch.narrow(qkv, qkv_all, 0, 1024, ("x", "y")),
            fetch.narrow(qkv, qkv_all, 1024, 1024, ("y", "x")),
            fetch.narrow(out, out_all, 0, D, ("x", "y")),
            fetch.wide(gate, gate_all, WIDE_FETCH[0][1][:2]),
            fetch.wide(up, up_all, WIDE_FETCH[1][1][:2]),
            fetch.down(down, down_all, WIDE_FETCH[2][1][:2]),
            fetch.from_this_chip(
                (qkv, out, gate, up, down), staged, (qkv_all, out_all, gate_all, up_all, down_all)
            ),
        ]
    )
    wires.finish_sends()


def gather(qkv, out, gate, up, down):
    rows = (4, 4, 16)
    qkv, out, *wide = wired_call(
        gather_kernel,
        [
            shape(2, 2, *rows, 2048),
            shape(2, 2, *rows, D),
            shape(2, 2, *rows, HALF_FF),
            shape(2, 2, *rows, HALF_FF),
            shape(2, 4, 2, 144, D),
        ],
        (
            qkv.reshape(*rows, 2048),
            out.reshape(*rows, D),
            gate.reshape(*rows, FF),
            up.reshape(*rows, FF),
            down.reshape(4, 2, 144, D),
        ),
        1,
        "gather",
        3 * 8 + 9 + 6 + 5 + 6,
        12,
        [
            pltpu.VMEM((*rows, 2048), BF16),
            pltpu.VMEM((*rows, D), BF16),
            pltpu.VMEM((*rows, FF), BF16),
            pltpu.VMEM((*rows, FF), BF16),
            pltpu.VMEM((4, 2, 144, D), BF16),
        ],
        in_specs=[HBM] * 5,
        out_specs=[ANY] * 2 + [HBM] * 3,
        vmem=60 * MIB,
    )
    return qkv.reshape(D, 2048), out.reshape(D, D), wide


def fetch_last(here, wires, wide):
    tasks = []
    for (kind, order), whole in zip(WIDE_FETCH, wide):
        at = {"zh": 1 - here.zh, "zl": here.zl, "x": here.x, "y": here.y}
        for axis in order[:2]:
            at = without(at, axis)
        task = spread(here, wires, kind, whole, at, order[2:])
        tasks.append(later(task, 1) if order[2] == "z" else task)
    return tasks


WIDE = (
    (0, RowsByShard(HALF_FF), ("z", "x", "y"), ("y", "x", "z")),
    (1, RowsByShard(HALF_FF), ("x", "y", "z"), ("z", "y", "x")),
    (2, ColumnsByY(144), ("y", "z", "x"), ("x", "z", "y")),
)
NARROW = (
    (0, RowsByPlane(0, 1024), ("z", "x", "y"), ("z", "y", "x")),
    (0, RowsByPlane(1024, 1024), ("x", "y", "z"), ("x", "z", "y")),
    (1, ColumnsByY(32), ("y", "z", "x"), ("z", "x", "y")),
)
FIRST_DIRECT = ("y", "y", "x")
WIDE_DIMS = ((2, 2, 4, 4, 16, HALF_FF), (2, 2, 4, 4, 16, HALF_FF), (2, 4, 2, 144, D))
NARROW_DIMS = ((2, 4, 4, 16, 2048), (2, 4, 2, 32, D))


def slot_shapes(parts):
    found = []
    for _, kind, order, _ in parts:
        at = {}
        for axis in order:
            at = fix(at, axis, 0)
            found.append((6, *kind.open_dims(at), *kind.tail_dims({**at, "half": 0})))
    return found


def each_block(kind, at, body):
    dims = kind.open_dims(at)

    def step(i, _):
        inner, rest = ([], i)
        for n in reversed(dims):
            inner.insert(0, rest % n)
            rest = rest // n
        picks = iter(inner)
        lead = [next(picks) if o is None else o for o in kind.order(at)]
        body((*lead, *kind.tail(at)), (*inner, slice(None), slice(None)))
        return 0

    lax.fori_loop(0, math.prod(dims), step, 0)


def reduce_one(here, wires, kind, grad, total, slots, order, direct_from):
    at = {}
    for step, axis in enumerate(order):
        source, slot = (grad if step == 0 else total, slots[step])
        (right_place, right), (left_place, left) = (here.along(axis, 1), here.along(axis, 3))
        far_place, _ = here.along(axis, 2)
        mine = fix(at, axis, getattr(here, axis))

        def half_of(place, half):
            return {**fix(at, axis, place), "half": half}

        if step >= direct_from:
            copies = [
                wires.push(
                    kind.view(source, half_of(here.along(axis, s)[0], half)),
                    slot.at[2 * j + half],
                    here.along(axis, s)[1],
                )
                for j, s in enumerate(STEPS)
                for half in range(2)
            ]
            yield
            arrive(copies)
            for half in range(2):

                def add_all(whole, part):
                    value = total[whole].astype(F32)
                    for j in range(3):
                        value += slot[(2 * j + half, *part)].astype(F32)
                    total[whole] = value.astype(BF16)

                each_block(kind, {**mine, "half": half}, add_all)
            at = mine
            continue
        relays = [
            wires.push(kind.view(source, half_of(far_place, 0)), slot.at[4], right),
            wires.push(kind.view(source, half_of(far_place, 1)), slot.at[5], left),
        ]
        arriving = [
            wires.push(kind.view(source, half_of(right_place, 1)), slot.at[1], right),
            wires.push(kind.view(source, half_of(left_place, 0)), slot.at[2], left),
        ]
        kept = []
        if step == 0:
            for where in (half_of(right_place, 0), half_of(left_place, 1), mine):
                kept.append(wires.move(kind.view(source, where), kind.view(total, where)))
        yield
        for j, place, half, target, onward in (
            (4, right_place, 0, 0, right),
            (5, left_place, 1, 3, left),
        ):
            if kept:
                kept.pop(0).wait()
            arrive([relays[j - 4]])

            def pass_on(whole, part):
                value = slot[(j, *part)].astype(F32) + total[whole].astype(F32)
                slot[(j, *part)] = value.astype(BF16)

            each_block(kind, half_of(place, half), pass_on)
            arriving.append(wires.push(slot.at[j], slot.at[target], onward))
        yield
        if kept:
            kept.pop(0).wait()
        arrive(arriving)
        for half in range(2):

            def add_up(whole, part):
                value = total[whole].astype(F32) + slot[(half, *part)].astype(F32)
                total[whole] = (value + slot[(2 + half, *part)].astype(F32)).astype(BF16)

            each_block(kind, {**mine, "half": half}, add_up)
        at = mine


def reduce_weights_kernel(*refs):
    grads, gains = (refs[3:5], refs[5])
    nears, boths, narrow_outs, gains_out = (refs[6:9], refs[9:11], refs[11:13], refs[13])
    totals, slots, staged = (refs[14:16], refs[16:25], refs[25:27])
    gain_slots, sends, receives, moves = refs[27:]

    here = Place()
    wires = Wires(sends, receives, moves)
    core = here.core
    sibling = here.sibling()
    greet_rings(here)
    held = {"zh": here.zh, "zl": here.zl, "x": here.x, "y": here.y}

    def all_gains():
        sums = gains[...]
        for stage, axis in enumerate(("core", "x", "y", "z")):
            me = getattr(here, axis)
            gain_slots[stage, me] = sums
            source = gain_slots.at[stage, me]
            if axis == "core":
                others = [sibling]
            else:
                others = [here.along(axis, s)[1] for s in STEPS]
            copies = [wires.push(source, source, device) for device in others]
            yield
            arrive(copies)
            sums = gain_slots[stage, 0] + gain_slots[stage, 1]
            if axis != "core":
                sums = sums + gain_slots[stage, 2] + gain_slots[stage, 3]
        gains_out[...] = sums

    def narrow(p):
        g, kind, order, back = NARROW[p]
        yield from reduce_one(
            here, wires, kind, grads[g], totals[g], slots[3 * p : 3 * p + 3], order, 1
        )
        out = narrow_outs[g]
        own = wires.move(kind.view(totals[g], held), kind.view(out, held, 1))
        own.wait()
        yield from spread(here, wires, kind, out, held, back, 1, direct="xy")

    def wide(p, c):
        _, kind, _, back = WIDE[p]
        axis = back[2]
        cut = "y" if axis == "x" else "x"
        at = {"zh": here.zh, cut: c}
        if axis == "z":
            at["zl"] = here.zl
        else:
            at[axis] = getattr(here, axis)
        yield from spread(here, wires, kind, nears[p], at, (axis,), 1)
        if p < 2:
            part = (c,) if cut == "x" else (slice(None), c)
            mine = (core, *part)
            copies = [wires.push(nears[p].at[(1 - core, *part)], boths[p].at[mine], sibling)]
            wires.move(nears[p].at[mine], staged[p].at[part]).wait()
            own = wires.move(staged[p].at[part], boths[p].at[mine])
            yield
            arrive(copies)
            own.wait()

    in_turn(
        [narrow(p) for p in range(3)]
        + [delayed(later(wide(p, c), 1), c) for c in range(4) for p in (1, 2, 0)]
        + [all_gains()]
    )
    wires.finish_sends()


def widen_kernel(
    qkv, out, gate, up, down, gains, qkv_out, out_out, gate_out, up_out, down_out, attn_out,
    ffn_out, query_out, key_out,
):
    attn_out[...] = gains[0:8, :]
    ffn_out[...] = gains[8:16, :]
    query_out[...] = gains[16:17, :HEAD_SIZE]
    key_out[...] = gains[17:18, :HEAD_SIZE]
    qkv_out[...] = qkv[...].astype(F32)
    out_out[...] = out[...].astype(F32)
    down_out[...] = down[...].astype(F32)
    for both, whole in ((gate, gate_out), (up, up_out)):
        for r in range(2):
            for c in range(2):
                first = r * HALF_FF + c * SLICE
                values = both[c, :, r * SLICE : (r + 1) * SLICE]
                whole[:, first : first + SLICE] = values.astype(F32)


def widen(qkv, out, gate, up, down, gains):
    steps = 8

    def rows(n, columns):
        return pl.BlockSpec((n // steps, columns), lambda i: (i, 0))

    def whole(*dims):
        return pl.BlockSpec(dims, lambda i: (0, 0))

    pair = pl.BlockSpec((2, 256 // steps, HALF_FF), lambda i: (0, i, 0))
    return pl.pallas_call(
        widen_kernel,
        grid=(steps,),
        out_shape=[
            shape(256, 2048, dtype=F32),
            shape(256, D, dtype=F32),
            shape(256, FF, dtype=F32),
            shape(256, FF, dtype=F32),
            shape(SLICE, D, dtype=F32),
            shape(8, 128, dtype=F32),
            shape(8, 128, dtype=F32),
            shape(1, HEAD_SIZE, dtype=F32),
            shape(1, HEAD_SIZE, dtype=F32),
        ],
        in_specs=[rows(256, 2048), rows(256, D), pair, pair, rows(SLICE, D), whole(24, 128)],
        out_specs=[
            rows(256, 2048), rows(256, D), rows(256, FF), rows(256, FF), rows(SLICE, D),
            whole(8, 128), whole(8, 128), whole(1, HEAD_SIZE), whole(1, HEAD_SIZE),
        ],
        compiler_params=pltpu.CompilerParams(vmem_limit_bytes=60 * MIB),
        name="widen",
    )(qkv, out, gate, up, down, gains)


def reduce_weights(nears, qkv, out, gains):
    outs = [
        *(shape(*d[1:]) for d in WIDE_DIMS),
        shape(*WIDE_DIMS[0][1:]),
        shape(*WIDE_DIMS[1][1:]),
        *(shape(*d[1:]) for d in NARROW_DIMS),
        shape(*gains.shape, dtype=F32),
    ]
    scratch = [pltpu.VMEM(d, BF16) for d in NARROW_DIMS]
    scratch += [pltpu.VMEM(s, BF16) for s in slot_shapes(NARROW)]
    scratch += [pltpu.VMEM(WIDE_DIMS[0][2:], BF16)] * 2
    scratch += [pltpu.VMEM((4, 4, *gains.shape), F32)]
    narrow = [a.reshape(d) for a, d in zip((qkv, out), NARROW_DIMS)]
    _, _, down, gate, up, qkv, out, gains = wired_call(
        reduce_weights_kernel,
        outs,
        [*nears, *narrow, gains],
        2,
        "reduce_weights",
        10 + 3 * (18 + 7) + 4 * (1 + 2 * 4 + 2),
        3 * 4 + 4 * 4,
        scratch,
        [HBM] * 3 + [ANY] * 2 + [VMEM],
        [HBM] * 7 + [VMEM],
        vmem=60 * MIB,
        aliases={i: i for i in range(3)},
    )

    return widen(
        qkv.reshape(256, 2048),
        out.reshape(256, D),
        gate.reshape(2, 256, HALF_FF),
        up.reshape(2, 256, HALF_FF),
        down.reshape(SLICE, D),
        gains,
    )


def head_columns(head):
    return pl.ds(pl.multiple_of(head * 128, 128), 128)


def seats(here):
    me = here.ctx
    quarter, seat = (me // QUARTER, me % QUARTER)
    near = [quarter * QUARTER + (seat + s) % QUARTER for s in range(1, QUARTER)]
    far = [(me + s) % RING for s in range(1, RING)]
    return me, seat, near, far


def to_heads_kernel(query, key_value, query_out, key_value_out, sends, receives, moves):
    here = Place()
    wires = Wires(sends, receives, moves)
    me, seat, near, far = seats(here)
    greet([(k, here.fsdp) for k in far])
    copies = [
        wires.push(query.at[:, head_columns(k % QUARTER)], query_out.at[seat], (k, here.fsdp))
        for k in near
    ]
    copies += [
        wires.push(key_value.at[:, head_columns(k % QUARTER)], key_value_out.at[me], (k, here.fsdp))
        for k in far
    ]
    kept = [
        wires.move(query.at[:, head_columns(seat)], query_out.at[seat]),
        wires.move(key_value.at[:, head_columns(seat)], key_value_out.at[me]),
    ]
    arrive(copies)
    for copy in kept:
        copy.wait()
    wires.finish_sends()


def to_heads(query, key_value):
    outs = [shape(QUARTER, TOKENS, 128), shape(RING, TOKENS, 128)]
    return wired_call(to_heads_kernel, outs, [query, key_value], 3, "to_heads", 38, 2)


def grad_to_heads_kernel(grad, branch, grad_out, branch_pair, sends, receives, moves):
    here = Place()
    wires = Wires(sends, receives, moves)
    _, seat, near, _ = seats(here)
    greet([(k, here.fsdp) for k in near] + [here.sibling()])
    copies = [
        wires.push(grad.at[:, head_columns(k % QUARTER)], grad_out.at[seat], (k, here.fsdp))
        for k in near
    ]
    copies.append(wires.push(branch, branch_pair.at[here.core], here.sibling()))
    kept = [
        wires.move(grad.at[:, head_columns(seat)], grad_out.at[seat]),
        wires.move(branch, branch_pair.at[here.core]),
    ]
    arrive(copies)
    for copy in kept:
        copy.wait()
    wires.finish_sends()


def grad_to_heads(grad, branch):
    outs = [shape(QUARTER, TOKENS, 128), shape(2, TOKENS, D)]
    return wired_call(grad_to_heads_kernel, outs, [grad, branch], 4, "grad_to_heads", 8, 2)


def to_tokens_kernel(query, query_out, sends, receives, moves):
    here = Place()
    wires = Wires(sends, receives, moves)
    _, seat, near, _ = seats(here)
    greet([(k, here.fsdp) for k in near])
    columns = query_out.at[:, head_columns(seat)]
    copies = [wires.push(query.at[k % QUARTER], columns, (k, here.fsdp)) for k in near]
    kept = wires.move(query.at[seat], columns)
    arrive(copies)
    kept.wait()
    wires.finish_sends()


def to_tokens(query):
    return wired_call(to_tokens_kernel, [shape(TOKENS, D)], [query], 5, "to_tokens", 7, 1)[0]


def grads_to_tokens_kernel(*refs):
    query, key_value = refs[:2]
    query_out, key_value_out, nears, staged = (refs[5], refs[6], refs[7:10], refs[10:12])
    here = Place()
    wires = Wires(*refs[12:])
    me, seat, near, far = seats(here)
    greet([(k, here.fsdp) for k in far])
    held = {"zh": here.zh, "zl": here.zl, "x": here.x, "y": here.y}

    def back():
        columns = query_out.at[:, head_columns(seat)]
        landed = [
            wires.move(query.at[seat], staged[0]),
            wires.move(key_value.at[me], staged[1]),
        ]
        copies = [wires.push(query.at[k % QUARTER], columns, (k, here.fsdp)) for k in near]
        copies += [
            wires.push(key_value.at[k], key_value_out.at[me], (k, here.fsdp)) for k in far
        ]
        for copy in landed:
            copy.wait()
        kept = [
            wires.move(staged[0], columns),
            wires.move(staged[1], key_value_out.at[me]),
        ]
        for _ in range(3):
            yield
        arrive(copies)
        for copy in kept:
            copy.wait()

    def share(p):
        _, kind, _, order = WIDE[p]
        yield from spread(
            here, wires, kind, nears[p], held, order[:2], 1, direct=FIRST_DIRECT[p]
        )

    in_turn([share(p) for p in range(3)] + [back()])
    wires.finish_sends()


def grads_to_tokens(query, key_value, nears):
    query_grad, key_value_grad, *nears = wired_call(
        grads_to_tokens_kernel,
        [shape(TOKENS, D), shape(RING, TOKENS, 128), *(shape(*d[1:]) for d in WIDE_DIMS)],
        [query, key_value, *nears],
        6,
        "grads_to_tokens",
        38 + 7 + 4 + 4,
        4,
        [pltpu.VMEM((TOKENS, 128), BF16), pltpu.VMEM((TOKENS, 128), BF16)],
        in_specs=[ANY] * 2 + [HBM] * 3,
        out_specs=[ANY] * 2 + [HBM] * 3,
        vmem=60 * MIB,
        aliases={2 + i: 2 + i for i in range(3)},
    )
    return query_grad, key_value_grad, nears


def half_columns(r, core):
    return pl.ds(pl.multiple_of(r * 512 + core * 256, 256), 256)


def share_kernel(whole, halved, *refs):
    n = whole + halved
    ins, outs = (refs[:n], refs[n : 2 * n])
    here = Place()
    wires = Wires(*refs[2 * n :])
    core = here.core
    sibling = here.sibling()
    greet([sibling])
    copies, kept = ([], [])
    for source, target in zip(ins[:whole], outs[:whole]):
        copies.append(wires.push(source, target.at[core], sibling))
        kept.append(wires.move(source, target.at[core]))
    for source, target in zip(ins[whole:], outs[whole:]):
        for r in range(2):
            place = target.at[core, :, pl.ds(r * 256, 256)]
            copies.append(wires.push(source.at[:, half_columns(r, 1 - core)], place, sibling))
            kept.append(wires.move(source.at[:, half_columns(r, core)], place))
    arrive(copies)
    for copy in kept:
        copy.wait()
    wires.finish_sends()


def share(whole, halved, collective_id):
    outs = [shape(2, *a.shape, dtype=a.dtype) for a in whole]
    outs += [shape(2, a.shape[0], 512, dtype=a.dtype) for a in halved]
    count = len(whole) + 2 * len(halved)
    done = wired_call(
        functools.partial(share_kernel, len(whole), len(halved)),
        outs,
        [*whole, *halved],
        collective_id,
        "share",
        count,
        count,
    )
    return [a.reshape(2 * a.shape[1], a.shape[2]) for a in done]


def hand_over_kernel(count, *refs):
    ins, outs = (refs[:count], refs[count : 2 * count])
    here = Place()
    wires = Wires(*refs[2 * count :])
    sibling = here.sibling()
    greet([sibling])
    copies = [wires.push(i.at[1 - here.core], o, sibling) for i, o in zip(ins, outs)]
    arrive(copies)
    wires.finish_sends()


def hand_over(partials, collective_id):
    return wired_call(
        functools.partial(hand_over_kernel, len(partials)),
        [shape(*a.shape[1:], dtype=a.dtype) for a in partials],
        partials,
        collective_id,
        "hand_over",
        len(partials),
        0,
    )


def nt(left, right):
    return lax.dot_general(left, right, (((1,), (1,)), ((), ())), preferred_element_type=F32)


def nn(left, right):
    return lax.dot_general(left, right, (((1,), (0,)), ((), ())), preferred_element_type=F32)


def query_block(ref, t):
    block = ref[t].astype(F32)
    both = jnp.concatenate([block, pltpu.roll(block, 64, 1)], axis=0)
    low = lax.broadcasted_iota(jnp.int32, (128, 128), 1) < 64
    return jnp.where(low, both, 0.0)


def query_pair(ref, u):
    return [query_block(ref, 2 * u), query_block(ref, 2 * u + 1)]


def first_allowed(position, starts_ref):
    begin = jnp.zeros_like(position)
    for n in range(4):
        begin = jnp.maximum(begin, jnp.where(starts_ref[n] <= position, starts_ref[n], 0))
    return begin


def heads_beside(rows):
    low = lax.broadcasted_iota(jnp.int32, (64, 128), 1) < 64
    return jnp.where(low, rows[:64], pltpu.roll(rows[64:], 64, 1)).astype(BF16)


def attend_task(
    counts, first_block, starts_ref, order_ref, query_ref, key_value_ref, out_ref, exact_ref,
    sum_ref, value_ref, key_at_ref,
):
    def key_places(j, _):
        lane = lax.broadcasted_iota(jnp.int32, (1, 128), 1)
        block = jnp.where(lane < 64, order_ref[2 * j], order_ref[2 * j + 1])
        key_at_ref[:, pl.ds(pl.multiple_of(j * 128, 128), 128)] = block * 64 + lane % 64
        return 0

    def values(j, _):
        rows = pl.ds(pl.multiple_of(j * 256, 256), 256)
        block = pltpu.roll(key_value_ref[rows, :].astype(F32), 64, 1)
        low = lax.broadcasted_iota(jnp.int32, (256, 128), 1) < 64
        value_ref[rows, :] = jnp.where(low, block, 1.0).astype(BF16)
        return 0

    def blocks(u, _):
        queries = jnp.concatenate(query_pair(query_ref, u), axis=0).astype(BF16)
        inner = lax.broadcasted_iota(jnp.int32, (128, 1), 0) % 64
        block = first_block + 2 * u
        position = jnp.concatenate(
            [order_ref[block] * 64 + inner, order_ref[block + 1] * 64 + inner], axis=0
        )
        begin = first_allowed(position, starts_ref)

        def tile(j, total):
            rows = pl.ds(pl.multiple_of(j * KEY_TILE, KEY_TILE), KEY_TILE)
            scores = nt(queries, key_value_ref[rows, :])
            key = key_at_ref[:, rows]
            allowed = (key <= position) & (key >= begin)
            weight = jnp.where(allowed, jnp.exp2(scores * SCORE_TO_EXP2), 0.0)
            return total + nn(weight.astype(BF16), value_ref[rows, :])

        total = lax.fori_loop(0, SEQ // KEY_TILE, tile, jnp.zeros((256, 128), F32))
        attended = total / pltpu.roll(total, 64, 1)
        low = lax.broadcasted_iota(jnp.int32, (256, 128), 1) < 64
        attended = jnp.where(low, attended, 0.0)
        for n in range(2):
            rows = slice(128 * n, 128 * n + 128)
            exact_ref[2 * u + n] = attended[rows]
            out_ref[2 * u + n] = heads_beside(attended[rows])
            sum_ref[2 * u + n] = jnp.transpose(total[rows])[64:72]
        return 0

    lax.fori_loop(0, SEQ // 256, values, 0)
    lax.fori_loop(0, SEQ // 128, key_places, 0)
    first = 0
    for count in counts:
        lax.fori_loop(first, first + count, blocks, 0)
        first += count
        yield


def attend_kernel(
    starts, order, query, key_value, gate_in, up_in, down_in, attended, exact, sums, gate_all,
    up_all, down_all, value_ref, key_at_ref, sends, receives, moves,
):
    wires = Wires(sends, receives, moves)
    here = Place()
    greet_rings(here)
    in_turn(
        [
            *fetch_last(here, wires, (gate_all, up_all, down_all))[::-1],
            attend_task(
                (6, 2), here.ctx // QUARTER * 16, starts, order, query, key_value, attended, exact,
                sums, value_ref, key_at_ref,
            ),
        ]
    )
    wires.finish_sends()


def attend(starts, order, queries, key_values, wide):
    outs = [
        shape(16, 64, 128),
        shape(16, 128, 128, dtype=F32),
        shape(16, 8, 128, dtype=F32),
        *(shape(*a.shape) for a in wide),
    ]
    attended, exact, sums, gate, up, down = wired_call(
        attend_kernel,
        outs,
        [starts, order, queries, key_values, *wide],
        10,
        "attend",
        1 + 4 + 4,
        1,
        [pltpu.VMEM((SEQ, 128), BF16), pltpu.VMEM((1, SEQ), jnp.int32)],
        [SMEM] * 2 + [VMEM] * 2 + [HBM] * 3,
        [VMEM] * 3 + [HBM] * 3,
        vmem=40 * MIB,
        aliases={4 + i: 3 + i for i in range(3)},
    )
    weights = (gate.reshape(D, HALF_FF), up.reshape(D, HALF_FF), down.reshape(HALF_FF, D))
    return attended, exact, sums, weights


def attend_back_task(
    counts, first_block, starts_ref, order_ref, query_ref, key_value_ref, grad_ref, exact_ref,
    sum_ref, query_grad_ref, key_value_grad_ref, across_ref, total_ref, key_at_ref,
):
    total_ref[...] = jnp.zeros_like(total_ref)

    def key_places(j, _):
        inner = lax.broadcasted_iota(jnp.int32, (64, 1), 0)
        key_at_ref[pl.ds(pl.multiple_of(j * 64, 64), 64), :] = order_ref[j] * 64 + inner
        return 0

    def turn(j, _):
        rows = pl.ds(pl.multiple_of(j * 128, 128), 128)
        across_ref[:, rows] = jnp.transpose(key_value_ref[rows, :].astype(F32)).astype(BF16)
        return 0

    def blocks(u, _):
        queries, grads = (query_pair(query_ref, u), query_pair(grad_ref, u))
        delta = [
            jnp.sum(jnp.transpose(grad * exact_ref[2 * u + n]), axis=0, keepdims=True)
            for n, grad in enumerate(grads)
        ]
        delta = jnp.concatenate(delta, axis=1)
        total_exp2 = jnp.concatenate(
            [jnp.log2(sum_ref[2 * u + n][0:1]) for n in range(2)], axis=1
        )
        grads = [pltpu.roll(grad, 64, 1) for grad in grads]
        both = jnp.concatenate(queries + grads, axis=0).astype(BF16)
        inner = lax.broadcasted_iota(jnp.int32, (1, 128), 1) % 64
        block = first_block + 2 * u
        position = jnp.concatenate(
            [order_ref[block] * 64 + inner, order_ref[block + 1] * 64 + inner], axis=1
        )
        begin = first_allowed(position, starts_ref)

        def tile(j, query_grad):
            rows = pl.ds(pl.multiple_of(j * KEY_TILE_BACK, KEY_TILE_BACK), KEY_TILE_BACK)
            products = nt(key_value_ref[rows, :], both)
            key = key_at_ref[rows, :]
            allowed = (key <= position) & (key >= begin)
            prob = jnp.where(
                allowed, jnp.exp2(products[:, :256] * SCORE_TO_EXP2 - total_exp2), 0.0
            )
            score = (prob * (products[:, 256:] - delta)).astype(BF16)
            side = jnp.concatenate([score, prob.astype(BF16)], axis=1)
            total_ref[rows, :] += nn(side, both)
            return query_grad + nn(across_ref[:, rows], score)

        query_grad = lax.fori_loop(
            0, SEQ // KEY_TILE_BACK, tile, jnp.zeros((128, 256), F32)
        )
        for n in range(2):
            rows = jnp.transpose(query_grad[:, 128 * n : 128 * n + 128])
            query_grad_ref[2 * u + n] = heads_beside(rows * float(HEAD_SIZE) ** (-0.5))
        return 0

    def put_back(j, _):
        rows = pl.ds(pl.multiple_of(j * 256, 256), 256)
        low = lax.broadcasted_iota(jnp.int32, (256, 128), 1) < 64
        scale = jnp.where(low, float(HEAD_SIZE) ** (-0.5), 1.0)
        key_value_grad_ref[rows, :] = (total_ref[rows, :] * scale).astype(BF16)
        return 0

    lax.fori_loop(0, SEQ // 128, turn, 0)
    lax.fori_loop(0, 64, key_places, 0)
    first = 0
    for count in counts:
        lax.fori_loop(first, first + count, blocks, 0)
        first += count
        yield
    lax.fori_loop(0, SEQ // 256, put_back, 0)


def attend_back_kernel(*refs):
    attention, grads = (refs[:7], refs[7:10])
    outs, nears = (refs[10:12], refs[12:15])
    scratch, totals, slots = (refs[15:18], refs[18:21], refs[21:30])
    here = Place()
    wires = Wires(*refs[30:])
    greet_rings(here)
    at = {"zh": here.zh, "zl": here.zl, "x": here.x, "y": here.y}

    def reduce(p):
        _, kind, order, _ = WIDE[p]
        yield from reduce_one(
            here, wires, kind, grads[p], totals[p], slots[3 * p : 3 * p + 3], order, 2
        )
        own = wires.move(kind.view(totals[p], at), kind.view(nears[p], at, 1))
        yield
        own.wait()

    first_block = here.ctx // QUARTER * 16
    in_turn(
        [reduce(p) for p in range(3)]
        + [attend_back_task((3, 4, 1), first_block, *attention, *outs, *scratch)]
    )
    wires.finish_sends()


def attend_back(starts, order, queries, key_values, grads, exact, sums, wide):
    ins = [starts, order, queries, key_values, grads]
    ins += [exact, sums, *(a.reshape(d) for a, d in zip(wide, WIDE_DIMS))]
    scratch = [
        pltpu.VMEM((128, SEQ), BF16),
        pltpu.VMEM((SEQ, 128), F32),
        pltpu.VMEM((SEQ, 1), jnp.int32),
    ]
    scratch += [pltpu.VMEM(d, BF16) for d in WIDE_DIMS]
    scratch += [pltpu.VMEM(s, BF16) for s in slot_shapes(WIDE)]
    query_grad, key_value_grad, *nears = wired_call(
        attend_back_kernel,
        [shape(16, 64, 128), shape(SEQ, 128), *(shape(*d[1:]) for d in WIDE_DIMS)],
        ins,
        11,
        "attend_back",
        3 * 18,
        3 * 4,
        scratch,
        [SMEM] * 2 + [VMEM] * 5 + [HBM] * 3,
        [VMEM] * 2 + [HBM] * 3,
        vmem=58 * MIB,
    )
    return query_grad, key_value_grad, nears


def low_lanes():
    return lax.broadcasted_iota(jnp.int32, (TOKENS, 128), 1) < 64


def head_mean(values):
    low = low_lanes()
    first = jnp.sum(jnp.where(low, values, 0.0), axis=1, keepdims=True)
    second = jnp.sum(jnp.where(low, 0.0, values), axis=1, keepdims=True)
    return jnp.where(low, first, second) * (1.0 / HEAD_SIZE)


def other_half(values):
    first = lax.broadcasted_iota(jnp.int32, (TOKENS, 128), 1) % 64 < 32
    return jnp.where(first, pltpu.roll(values, 96, 1), pltpu.roll(values, 32, 1))


def chunk(j):
    return slice(128 * j, 128 * j + 128)


def project_kernel(
    x_ref, gain_ref, weight_ref, query_gain_ref, key_gain_ref, cosine_ref, sine_ref, normed_ref,
    query_ref, key_value_ref, projected_ref,
):
    x = x_ref[...].astype(F32)
    normed = x * lax.rsqrt(jnp.mean(x * x, axis=-1, keepdims=True) + EPSILON) * gain_ref[...]
    normed_ref[...] = normed.astype(BF16)
    projected = nn(normed_ref[...], weight_ref[...])
    projected_ref[...] = projected[:, :1536]
    low = low_lanes()

    def turned(j, gain):
        values = projected[:, chunk(j)]
        values = values * lax.rsqrt(head_mean(values * values) + EPSILON) * gain
        return values * cosine_ref[...] + other_half(values) * sine_ref[...]

    for j in range(8):
        query_ref[:, chunk(j)] = turned(j, query_gain_ref[...]).astype(BF16)
    for j in range(4):
        keys = turned(8 + j, key_gain_ref[...])
        values = projected[:, chunk(12 + j)]
        first = jnp.where(low, keys, pltpu.roll(values, 64, 1))
        second = jnp.where(low, pltpu.roll(keys, 64, 1), values)
        key_value_ref[:, chunk(2 * j)] = first.astype(BF16)
        key_value_ref[:, chunk(2 * j + 1)] = second.astype(BF16)


def project(x, gain, weight, query_gain, key_gain, cosine, sine):
    return pl.pallas_call(
        project_kernel,
        out_shape=[
            shape(TOKENS, D),
            shape(TOKENS, D),
            shape(TOKENS, D),
            shape(TOKENS, 1536, dtype=F32),
        ],
        in_specs=[VMEM] * 7,
        out_specs=[VMEM] * 4,
        compiler_params=pltpu.CompilerParams(vmem_limit_bytes=32 * MIB),
        name="project",
    )(x, gain, weight, query_gain, key_gain, cosine, sine)


def project_back_kernel(
    query_grad_ref, key_value_grad_ref, projected_ref, x_ref, grad_resid_ref, gain_ref, weight_hbm,
    query_gain_ref, key_gain_ref, cosine_ref, sine_ref, ffn_gain_grad_ref, grad_projected_ref,
    grad_inputs_ref, gains_ref, weight_ref, weight_sem,
):
    fetch = pltpu.make_async_copy(weight_hbm, weight_ref, weight_sem)
    fetch.start()
    low = low_lanes()

    def back(j, grad, gain):
        grad = grad * cosine_ref[...] + other_half(grad * sine_ref[...])
        values = projected_ref[:, chunk(j)]
        scale = lax.rsqrt(head_mean(values * values) + EPSILON)
        unit = values * scale
        gain_grad = jnp.sum(grad * unit, axis=0, keepdims=True)
        grad = grad * gain
        grad = scale * (grad - unit * head_mean(grad * unit))
        grad_projected_ref[:, chunk(j)] = grad.astype(BF16)
        return gain_grad

    query_gain_grad = jnp.zeros((1, 128), F32)
    for j in range(8):
        grad = query_grad_ref[:, chunk(j)].astype(F32)
        query_gain_grad += back(j, grad, query_gain_ref[...])
    key_gain_grad = jnp.zeros((1, 128), F32)
    for j in range(4):
        first, second = [
            sum(key_value_grad_ref[8 * q + 2 * j + n].astype(F32) for q in range(4))
            for n in range(2)
        ]
        keys = jnp.where(low, first, pltpu.roll(second, 64, 1))
        values = jnp.where(low, pltpu.roll(first, 64, 1), second)
        key_gain_grad += back(8 + j, keys, key_gain_ref[...])
        grad_projected_ref[:, chunk(12 + j)] = values.astype(BF16)

    fetch.wait()
    grad = nt(grad_projected_ref[...], weight_ref[...])
    x = x_ref[...].astype(F32)
    scale = lax.rsqrt(jnp.mean(x * x, axis=-1, keepdims=True) + EPSILON)
    unit = x * scale
    gain_grad = jnp.sum(grad * unit, axis=0, keepdims=True)
    grad = grad * gain_ref[...]
    grad = scale * (grad - unit * jnp.mean(grad * unit, axis=-1, keepdims=True))
    grad_inputs_ref[...] = (grad_resid_ref[...] + grad).astype(BF16)

    gains_ref[...] = jnp.zeros_like(gains_ref)
    for j in range(8):
        gains_ref[j : j + 1, :] = gain_grad[:, chunk(j)]
        gains_ref[8 + j : 9 + j, :] = ffn_gain_grad_ref[:, chunk(j)]
    gains_ref[16:17, :] = query_gain_grad + pltpu.roll(query_gain_grad, 64, 1)
    gains_ref[17:18, :] = key_gain_grad + pltpu.roll(key_gain_grad, 64, 1)


def project_back(*ins):
    return pl.pallas_call(
        project_back_kernel,
        out_shape=[shape(TOKENS, 2048), shape(TOKENS, D), shape(24, 128, dtype=F32)],
        in_specs=[VMEM] * 6 + [ANY] + [VMEM] * 5,
        out_specs=[VMEM] * 3,
        scratch_shapes=[pltpu.VMEM((D, 2048), BF16), pltpu.SemaphoreType.DMA],
        compiler_params=pltpu.CompilerParams(vmem_limit_bytes=60 * MIB),
        name="project_back",
    )(*ins)


def rms_norm(values, gain_row):
    return (
        values * lax.rsqrt(jnp.mean(values * values, axis=-1, keepdims=True) + EPSILON) * gain_row
    )


def rope_tables(positions):
    lane = jnp.arange(128, dtype=jnp.int32)
    frequency = ROPE_BASE ** (-2.0 * (lane % 32).astype(F32) / HEAD_SIZE)
    angles = positions.astype(F32)[:, None] * frequency[None, :]
    sign = jnp.where(lane % 64 < 32, -1.0, 1.0)
    return jnp.cos(angles), jnp.sin(angles) * sign[None, :]


def outer_sum(left, right):
    return lax.dot_general(
        left, right, (((0,), (0,)), ((), ())), preferred_element_type=F32
    ).astype(BF16)


def matmul(left, right):
    return jnp.dot(left, right, preferred_element_type=F32)


def positions_at(block_order, first_row, total_row_count, half_rows):
    row_ids = first_row + jnp.arange(total_row_count, dtype=jnp.int32)
    blocks = row_ids // half_rows
    lookup = jnp.arange(block_order.shape[0], dtype=jnp.int32)
    picked = jnp.sum(jnp.where(blocks[:, None] == lookup[None, :], block_order[None, :], 0), axis=1)
    return picked * half_rows + row_ids % half_rows


def per_device(
    inputs,
    cotangent,
    qkv_weight,
    out_weight,
    gate_weight,
    up_weight,
    down_weight,
    gain_attn,
    gain_query,
    gain_key,
    gain_ffn,
    block_order,
    doc_starts,
):
    cycle_index = lax.axis_index("ctx")
    core = lax.axis_index("fsdp") % 2
    qkv_all, out_all, wide = gather(
        qkv_weight, out_weight, gate_weight, up_weight, down_weight
    )
    places = (doc_starts[0], block_order)
    positions = positions_at(block_order, cycle_index * TOKENS, TOKENS, TOKENS // 2)

    resid_in = inputs[0].astype(F32)
    gain_row = gain_attn.reshape(1, D)
    head_gains = [jnp.concatenate([g, g]).reshape(1, 128) for g in (gain_query, gain_key)]
    tables = rope_tables(positions)
    normed_low, queries, key_values, projected = project(
        inputs[0], gain_row, qkv_all, *head_gains, *tables
    )
    query_part, key_value_part = to_heads(queries, key_values)
    query_part = query_part.reshape(16, 64, 128)
    key_value_part = key_value_part.reshape(SEQ, 128)
    attended, exact, sums, (gate_all, up_all, down_all) = attend(
        *places, query_part, key_value_part, wide
    )
    attended_low = to_tokens(attended.reshape(QUARTER, TOKENS, 128))

    residual = resid_in + matmul(attended_low, out_all)
    normed_ffn, norm_ffn_pull = jax.vjp(rms_norm, residual, gain_ffn)
    grad_out = cotangent[0]
    ffn_pair, cotangent_pair, normed_half, attended_half = share(
        [normed_ffn.astype(BF16), grad_out], [normed_low, attended_low], 7
    )
    gate_proj = matmul(ffn_pair, gate_all)
    up_proj = matmul(ffn_pair, up_all)
    hidden, gating_pull = jax.vjp(
        lambda gate_in, up_in: jax.nn.silu(gate_in) * up_in, gate_proj, up_proj
    )
    hidden_low = hidden.astype(BF16)
    out_partial = matmul(hidden_low, down_all).reshape(2, TOKENS, D)
    grad_hidden = matmul(cotangent_pair, down_all.T)
    grad_gate, grad_up = gating_pull(grad_hidden)
    gate_low = grad_gate.astype(BF16)
    up_low = grad_up.astype(BF16)
    ffn_partial = (matmul(gate_low, gate_all.T) + matmul(up_low, up_all.T)).reshape(2, TOKENS, D)
    out_rest, ffn_rest = hand_over([out_partial, ffn_partial], 8)

    def mine(pair):
        return lax.dynamic_index_in_dim(pair, core, 0, keepdims=False)

    outputs = residual + mine(out_partial) + out_rest
    grad_resid_ffn, grad_gain_ffn = norm_ffn_pull(mine(ffn_partial) + ffn_rest)
    grad_resid = grad_out.astype(F32) + grad_resid_ffn
    branch_low = grad_resid.astype(BF16)
    grad_attended = matmul(branch_low, out_all.T).astype(BF16)
    grad_part, branch_pair = grad_to_heads(grad_attended, branch_low)
    query_grad, key_value_grad, nears = attend_back(
        *places,
        query_part,
        key_value_part,
        grad_part.reshape(16, 64, 128),
        exact,
        sums,
        (
            outer_sum(ffn_pair, gate_low),
            outer_sum(ffn_pair, up_low),
            outer_sum(hidden_low, cotangent_pair),
        ),
    )
    query_grad, key_value_grad, nears = grads_to_tokens(
        query_grad.reshape(QUARTER, TOKENS, 128),
        key_value_grad.reshape(RING, TOKENS, 128),
        nears,
    )
    grad_projected, grad_inputs, gains = project_back(
        query_grad,
        key_value_grad,
        projected,
        inputs[0],
        grad_resid,
        gain_row,
        qkv_all,
        *head_gains,
        *tables,
        grad_gain_ffn.reshape(1, D),
    )

    (projected_pair,) = share([grad_projected], [], 9)
    *grads, attn_sum, ffn_sum, query_sum, key_sum = reduce_weights(
        nears,
        outer_sum(normed_half, projected_pair),
        outer_sum(attended_half, branch_pair.reshape(2 * TOKENS, D)),
        gains,
    )
    return (
        outputs.astype(BF16)[None],
        grad_inputs[None],
        *grads,
        attn_sum.reshape(D),
        query_sum.reshape(HEAD_SIZE),
        key_sum.reshape(HEAD_SIZE),
        ffn_sum.reshape(D),
    )


def solution(mesh):
    in_specs = (
        P("fsdp", "ctx", None),
        P("fsdp", "ctx", None),
        P("fsdp", None),
        P("fsdp", None),
        P("fsdp", None),
        P("fsdp", None),
        P("fsdp", None),
        P(),
        P(),
        P(),
        P(),
        P(),
        P("fsdp", None),
    )
    out_specs = (
        P("fsdp", "ctx", None),
        P("fsdp", "ctx", None),
        P("fsdp", None),
        P("fsdp", None),
        P("fsdp", None),
        P("fsdp", None),
        P("fsdp", None),
        P(),
        P(),
        P(),
        P(),
    )
    return jax.shard_map(
        per_device, mesh=mesh, in_specs=in_specs, out_specs=out_specs, check_vma=False
    )
```
